128 devices in a mesh: section: 4 (over x), dp: 32 (over y, z, core).
Axes of the slice: x: 4, y: 4, z: 4, core: 2. Of those that a mesh axis runs over, the one named last changes fastest.
Arguments:
- tokens: bfloat16 [24576, 768], P('dp'), may hold values from -6 to 6
- cotangent: bfloat16 [24576, 768], P('dp'), may hold values from -6 to 6
- lengths: int32 [64, 3], P('dp'), may hold values from 0 to 361, as said below
- proj_in: bfloat16 [4, 768, 5376], P('section', 'dp'), may hold values from -0.21875 to 0.21875
- proj_attn: bfloat16 [4, 768, 768], P('section', 'dp'), may hold values from -1.5 to 1.5
- proj_down: bfloat16 [4, 3072, 768], P('section', 'dp'), may hold values from -0.109375 to 0.109375
- norm_gain: bfloat16 [4, 768], P('section', 'dp'), may hold values from 0.75 to 1.25
- query_gain: bfloat16 [4, 64], P('section', 'dp'), may hold values from 0.75 to 1.25
- key_gain: bfloat16 [4, 64], P('section', 'dp'), may hold values from 0.75 to 1.25
- up_bias: bfloat16 [4, 3072], P('section', 'dp'), may hold values from -2.5 to 2.5
- out_bias: bfloat16 [4, 768], P('section', 'dp'), may hold values from -2.5 to 2.5
Outputs:
- section_outputs: float32 [4, 24576, 768], P('section', 'dp')
- section_grads: float32 [4, 24576, 768], P('section', 'dp')
- grad_proj_in: float32 [4, 768, 5376], P('section', 'dp')
- grad_proj_attn: float32 [4, 768, 768], P('section', 'dp')
- grad_proj_down: float32 [4, 3072, 768], P('section', 'dp')
- grad_norm_gain: float32 [4, 768], P('section', 'dp')
- grad_query_gain: float32 [4, 64], P('section', 'dp')
- grad_key_gain: float32 [4, 64], P('section', 'dp')
- grad_up_bias: float32 [4, 3072], P('section', 'dp')
- grad_out_bias: float32 [4, 768], P('section', 'dp')
The draws below stay inside these ranges and needn't reach their ends.
Inputs may be any that keep to these rules, and one draw needn't show every extreme that they name: `lengths`: each slot holds one image of 361 tokens, one of 256 tokens, or three of 100 tokens; unused entries are zero. The first slot holds one of 361.
All inputs are finite; a program needn't handle non-finite values.
Results may differ from the reference program's by a relative error of at most 0.035.
Values may be sent and summed in bfloat16 or wider, within the bound.
No kernel may reach another device: no remote copies, remote signals or barrier semaphores. Data moves between devices by JAX's collectives and lax.ppermute only.
A program may use at most 256 MiB of HBM per device.

```python
import math
import jax
import jax.numpy as jnp
from jax import lax

D = 768
HEADS = 12
HD = 64
FF = 3072
SLOT = 384
LONG_IMG = 361
MID_IMG = 256
SMALL_IMG = 100
LAYERS = 4
SLOTS = 64
TOKENS = 24576
JOINED = 5376


def draw_lengths(key, part):
    key = jax.random.fold_in(key, 11)
    slot_kinds = jax.random.randint(key, (SLOTS,), 0, 3)
    slot_kinds = jnp.where(jnp.arange(SLOTS) == 0, 0, slot_kinds)
    lead_length = jnp.where(slot_kinds == 0, LONG_IMG, jnp.where(slot_kinds == 1, MID_IMG, SMALL_IMG))
    tail_length = jnp.where(slot_kinds == 2, SMALL_IMG, 0)
    return jnp.stack([lead_length, tail_length, tail_length], axis=1).astype(jnp.int32)


def steps_of(own_key, shape, cuts, least, top_value):
    loudness, own = 1.0, jax.random.fold_in(own_key, 6)
    for axis_at, blocks in cuts:
        steps = jnp.exp(jax.random.uniform(jax.random.fold_in(own, axis_at), (blocks,), jnp.float32, least / len(cuts), top_value / len(cuts)))
        loudness = loudness * jnp.repeat(steps, shape[axis_at] // blocks).reshape([-1 if axis == axis_at else 1 for axis in range(len(shape))])
    return loudness


def centred(key, extent, spread, limit, cuts=(), kind=jnp.bfloat16):
    drawn = jax.random.normal(key, extent, jnp.float32) * spread
    if len(cuts) > 0:
        drawn = steps_of(key, extent, cuts, -0.22, 0.18) * drawn
    return jnp.clip(drawn, min=-limit, max=limit).astype(kind)


def setup_inputs(seed: int = 0) -> dict:
    streams_of = jax.random.split(jax.random.key(seed), 12)
    tokens = centred(streams_of[0], (TOKENS, D), 1.0, 6.0, ((0, 32),))
    cotangent = centred(streams_of[1], (TOKENS, D), 1.0, 6.0, ((0, 32),))
    lengths = draw_lengths(jax.random.fold_in(streams_of[11], 71), 0)
    proj_in = centred(streams_of[3], (LAYERS, D, JOINED), D ** -0.5, 0.21875, ((0, 4), (1, 32)))
    proj_attn = centred(streams_of[4], (LAYERS, D, D), (8 * D // LONG_IMG) ** -0.5, 1.5, ((0, 4), (1, 32)))
    proj_down = centred(streams_of[5], (LAYERS, FF, D), FF ** -0.5, 0.109375, ((0, 4), (1, 32)))
    norm_gain = jnp.clip(1.0 + 0.05 * jax.random.normal(streams_of[6], (LAYERS, D), jnp.float32), 0.75, 1.25).astype(jnp.bfloat16)
    query_gain = jnp.clip(1.0 + 0.05 * jax.random.normal(streams_of[7], (LAYERS, HD), jnp.float32), 0.75, 1.25).astype(jnp.bfloat16)
    key_gain = jnp.clip(1.0 + 0.05 * jax.random.normal(streams_of[8], (LAYERS, HD), jnp.float32), 0.75, 1.25).astype(jnp.bfloat16)
    up_bias = centred(streams_of[9], (LAYERS, FF), 0.35, 2.5, ((0, 4), (1, 32)))
    out_bias = centred(streams_of[10], (LAYERS, D), 0.35, 2.5, ((0, 4), (1, 32)))
    return dict(tokens=tokens, cotangent=cotangent, lengths=lengths, proj_in=proj_in, proj_attn=proj_attn, proj_down=proj_down, norm_gain=norm_gain, query_gain=query_gain, key_gain=key_gain, up_bias=up_bias, out_bias=out_bias)


@jax.custom_vjp
def low(v):
    return lax.optimization_barrier(v.astype(jnp.bfloat16)).astype(jnp.float32)

@jax.custom_vjp
def low_back(v):
    return v

def low_keep(v):
    return (low(v), None)

def low_pass(kept, grad):
    return (grad,)

def back_keep(v):
    return (v, None)

def back_low(kept, grad):
    return (low(grad),)
low.defvjp(low_keep, low_pass)
low_back.defvjp(back_keep, back_low)

def matmul(left, right):
    return jnp.dot(left, right, precision=lax.Precision.HIGHEST)

def normalize(values):
    centered = values - lax.optimization_barrier(jnp.mean(values, axis=-1, keepdims=True))
    return centered * lax.rsqrt(lax.optimization_barrier(jnp.mean(centered * centered, axis=-1, keepdims=True)) + 1e-06)

def slot_layout(lengths):
    boundary = jnp.cumsum(lengths, axis=-1)
    position = jnp.arange(SLOT, dtype=jnp.int32)
    image_of = lax.optimization_barrier(jnp.sum((position[None, :, None] >= boundary[:, None, :]).astype(jnp.int32), axis=-1))
    present = position[None, :] < boundary[:, 2:3]
    image_ids = jnp.where(present, image_of, 16 + position[None, :])
    return (image_ids, present)

def attend(packed):
    queries, key_rows, values, image_ids = packed
    scores = jnp.einsum('qhd,khd->hqk', queries, key_rows, precision=lax.Precision.HIGHEST)
    scores = low_back(scores * (1.0 / math.sqrt(HD)))
    allowed = image_ids[:, None] == image_ids[None, :]
    scores = jnp.where(allowed[None], scores, -1000000000.0)
    attn_probs = low(jax.nn.softmax(scores, axis=-1))
    return jnp.einsum('hqk,khd->qhd', attn_probs, values, precision=lax.Precision.HIGHEST)

def run_layer(current, layer_params, image_ids, keep_rows):
    proj_in, proj_attn, proj_down, norm_gain, query_gain, key_gain, up_bias, out_bias = layer_params
    masked = keep_rows * current
    hidden = low(normalize(masked) * norm_gain)
    joined = low_back(matmul(hidden, proj_in))
    queries = low(normalize(joined[:, :D].reshape(-1, HEADS, HD)) * query_gain)
    key_rows = low(normalize(joined[:, D:2 * D].reshape(-1, HEADS, HD)) * key_gain)
    values = low(joined[:, 2 * D:3 * D].reshape(-1, HEADS, HD))
    activated = low(jax.nn.gelu(joined[:, 3 * D:] + up_bias, approximate=False))
    attended = lax.map(jax.checkpoint(attend), (queries.reshape(-1, SLOT, HEADS, HD), key_rows.reshape(-1, SLOT, HEADS, HD), values.reshape(-1, SLOT, HEADS, HD), image_ids))
    attended = low(low_back(attended.reshape(-1, D)))
    branch = low_back(matmul(attended, proj_attn) + matmul(activated, proj_down))
    return keep_rows * (masked + branch + out_bias)

def reference(tokens, cotangent, lengths, proj_in, proj_attn, proj_down, norm_gain, query_gain, key_gain, up_bias, out_bias):
    image_ids, present = slot_layout(lengths)
    keep_rows = present.reshape(-1, 1).astype(jnp.float32)
    params = tuple((p.astype(jnp.float32) for p in (proj_in, proj_attn, proj_down, norm_gain, query_gain, key_gain, up_bias, out_bias)))
    inputs = tokens.astype(jnp.float32)
    layer_offsets = jnp.zeros((LAYERS,) + inputs.shape, jnp.float32)

    def forward(inputs, layer_offsets, params):
        current = inputs
        collected = []
        for layer_index in range(LAYERS):
            layer_params = tuple((p[layer_index] for p in params))
            current = jax.checkpoint(run_layer)(current + layer_offsets[layer_index], layer_params, image_ids, keep_rows)
            collected.append(current)
        return jnp.stack(collected)
    outputs, pullback = jax.vjp(forward, inputs, layer_offsets, params)
    seeded = jnp.zeros_like(outputs).at[LAYERS - 1].set(cotangent.astype(jnp.float32))
    unused, grad_offsets, grads = pullback(seeded)
    return (outputs, grad_offsets, grads[0], grads[1], grads[2], grads[3], grads[4], grads[5], grads[6], grads[7])
```

```python
from functools import partial
import math

import jax
import jax.numpy as jnp
from jax import lax
from jax.experimental import pallas as pl
from jax.experimental.pallas import tpu as pltpu
from jax.sharding import PartitionSpec as P

BF = jnp.bfloat16
F32 = jnp.float32
VMEM_LIMIT = 60 * 1024 * 1024
EPS = 1e-06
NN = (((1,), (0,)), ((), ()))
NT = (((1,), (1,)), ((), ()))
LANES = 128
WIDE = 256
ABSENT = 16


def mm(a, b, dims=NN):
    return lax.dot_general(a, b, dims, preferred_element_type=F32)


def head_mean(x, spread, exact):
    parts = []
    for at in range(0, x.shape[1], WIDE):
        piece = x[:, at : at + WIDE]
        top = piece.astype(BF)
        total = mm(top, spread)
        if exact:
            total = total + mm((piece - top.astype(F32)).astype(BF), spread)
        parts.append(total)
    return jnp.concatenate(parts, axis=1)


def row_norm(x):
    centered = x - jnp.mean(x, axis=-1, keepdims=True)
    rstd = lax.rsqrt(jnp.mean(centered * centered, axis=-1, keepdims=True) + EPS)
    return centered * rstd, rstd


def norm_back(grad, normal, rstd, spread):
    return rstd * (grad - head_mean(grad, spread, False) - normal * head_mean(grad * normal, spread, False))


def lane_half(x, second):
    lane = lax.broadcasted_iota(jnp.int32, x.shape, 1)
    return jnp.where((lane >= LANES // 2) if second else (lane < LANES // 2), x, jnp.zeros_like(x))


class Copies:
    def __init__(self, sems):
        self.sems, self.used = sems, 0

    def start(self, src, dst):
        copy = pltpu.make_async_copy(src, dst, self.sems.at[self.used])
        self.used += 1
        copy.start()
        return copy


def forward_kernel(d, ff, chunks, idx, tok, recv, g, g3, ids_col, ids_row, ngain, gains, ubias, obias, spread, *refs):
    refs = refs[13:]
    ybf, refs = refs[0], refs[1:]
    xs, hs, qs, ks, vs, ns, nrs, acts, gps, es, small = refs[:11]
    at_out, y_out = refs[11:13]
    (x_v, h_v, w_v, u_v, d_v, a_v, q_v, k_v, v_v, n_v, r_v, act_v, gp_v, e_v, rs_v, at_v, att_v, acc_v, y_v, ins, outs) = refs[13:]
    rows = x_v.shape[0]
    fc = ff // chunks
    which, st = idx[0], idx[1]
    cin, cout = Copies(ins), Copies(outs)

    @pl.when(idx[2] == 1)
    def _():
        pltpu.make_async_copy(tok.at[which], x_v, ins.at[0]).start()

    @pl.when(idx[2] != 1)
    def _():
        pltpu.make_async_copy(recv, x_v, ins.at[0]).start()

    cin.used = 1
    wq = [cin.start(g.at[:, pl.ds(ff + d * i, d)], w_v.at[:, pl.ds(d * i, d)]) for i in range(3)]
    groups = fc // WIDE
    wff = []
    for c in range(chunks):
        wff.append([cin.start(g.at[:, pl.ds(fc * c, fc)], u_v.at[c])] + [
            cin.start(g3.at[pl.ds(groups * c, groups), :, pl.ds(ff + 4 * d + d * j, d)], d_v.at[pl.ds(groups * c, groups), j])
            for j in range(4)
        ])
    wa = cin.start(g.at[:, pl.ds(ff + 3 * d, d)], a_v)

    pending = []
    pltpu.make_async_copy(recv, x_v, ins.at[0]).wait()
    keep = jnp.where(ids_col[0] < ABSENT, 1.0, 0.0)
    masked = keep * x_v[...].astype(F32)
    h_v[...] = (row_norm(masked)[0] * ngain[...]).astype(BF)
    pending += [cout.start(x_v, xs.at[st]), cout.start(h_v, hs.at[st])]
    bias_mask = jnp.where(ids_col[0] == ids_row[0], 0.0, -1e9)
    for i in range(3):
        wq[i].wait()
        raw = mm(h_v[...], w_v[:, d * i : d * i + d])
        if i == 2:
            v_v[...] = raw.astype(BF)
            pending.append(cout.start(v_v, vs.at[st]))
        else:
            centered = raw - head_mean(raw, spread[...], True)
            rstd = lax.rsqrt(head_mean(centered * centered, spread[...], True) + EPS)
            normal = centered * rstd
            scaled = (normal * gains[i]).astype(BF)
            n_v[:, d * i : d * i + d] = normal.astype(BF)
            r_v[:, d * i : d * i + d] = rstd.astype(BF)
            if i == 0:
                q_v[...] = scaled * jnp.asarray(0.125, BF)
                pending.append(cout.start(q_v, qs.at[st]))
            else:
                k_v[...] = scaled
                pending.append(cout.start(k_v, ks.at[st]))
    pending += [cout.start(n_v, ns.at[st]), cout.start(r_v, nrs.at[st])]
    ones = jnp.ones((16, rows), BF)
    pairs = d // LANES // chunks
    for c in range(chunks):
        for copy in wff[c]:
            copy.wait()
        pre = mm(h_v[...], u_v[c]) + ubias[:, fc * c : fc * c + fc]
        cdf = 0.5 * (1.0 + lax.erf(pre * (1.0 / math.sqrt(2.0))))
        density = jnp.exp(-0.5 * pre * pre) * (1.0 / math.sqrt(2.0 * math.pi))
        act = (pre * cdf).astype(BF)
        act_v[c] = act
        gp_v[c] = (cdf + pre * density).astype(BF)
        total = mm(act, d_v[groups * c : groups * c + groups].reshape(fc, d))
        if c == 0:
            acc_v[...] = total
        else:
            acc_v[...] += total
        for p in range(pairs * c, pairs * c + pairs):
            cols = slice(LANES * p, LANES * p + LANES)
            vals_t = v_v[:, cols].T
            pair = q_v[:, cols]
            both = []
            for half in range(2):
                h = 2 * p + half
                e = jnp.exp(mm(k_v[:, cols], lane_half(pair, half), NT) + bias_mask).astype(BF)
                e_v[h] = e
                got = mm(jnp.concatenate([vals_t[64 * half : 64 * half + 64], ones], axis=0), e)
                inv = 1.0 / got[64:65]
                rs_v[h : h + 1, :] = inv
                both.append((got[:64] * inv).astype(BF))
            both = jnp.concatenate(both, axis=0)
            at_v[cols, :] = both
            att_v[:, cols] = both.T
        pending += [cout.start(act_v.at[c], acts.at[st, c]), cout.start(gp_v.at[c], gps.at[st, c]),
                    cout.start(e_v.at[pl.ds(2 * pairs * c, 2 * pairs)], es.at[st, pl.ds(2 * pairs * c, 2 * pairs)])]
    pending += [cout.start(rs_v, small.at[st]), cout.start(at_v, at_out.at[st])]
    wa.wait()
    y = keep * (keep * x_v[...].astype(F32) + acc_v[...] + mm(att_v[...], a_v[...]) + obias[...])
    y_v[...] = y
    ybf[...] = y.astype(BF)
    pending.append(cout.start(y_v, y_out.at[st]))
    for copy in pending:
        copy.wait()


def backward_kernel(d, ff, chunks, idx, seed, recv, g, g3, ids_col, ngain, gains, spread, *refs):
    xs, qs, ks, vs, ns, nrs, gps, es, small, ats = refs[:10]
    refs = refs[10:]
    refs = refs[5 + 5 :]
    gbf, refs = refs[0], refs[1:]
    gbs, gjs, gqs, gks, gvs, refs = refs[0], refs[1], refs[2], refs[3], refs[4], refs[5:]
    grs, obs, ngs, qkgs, ubs, refs = refs[0], refs[1], refs[2], refs[3], refs[4], refs[5:]
    (g_v, gb_v, w_v, u_v, d_v, a_v, x_v, q_v, k_v, v_v, n_v, r_v, gp_v, e_v, rs_v, at_v, gat_v, gqt_v, gk_v,
     gq_b, gk_b, gv_b, gj_v, acc_v, out_v, ob_v, ng_v, qk_v, ub_v, ins, outs) = refs
    rows = x_v.shape[0]
    fc = ff // chunks
    groups = fc // WIDE
    which, st = idx[0], idx[1]
    cin, cout = Copies(ins), Copies(outs)

    @pl.when(idx[2] == 1)
    def _():
        pltpu.make_async_copy(seed.at[which], g_v, ins.at[0]).start()

    @pl.when(idx[2] != 1)
    def _():
        pltpu.make_async_copy(recv, g_v, ins.at[0]).start()

    cin.used = 1
    wa = cin.start(g.at[:, pl.ds(ff + 3 * d, d)], a_v)
    heads = [cin.start(s.at[which], v) for s, v in ((small, rs_v), (ats, at_v), (ks, k_v), (vs, v_v), (qs, q_v))]
    pairs = d // LANES // chunks
    wff = []
    for c in range(chunks):
        wff.append(
            [cin.start(g3.at[pl.ds(groups * c, groups), :, pl.ds(ff + 4 * d + d * j, d)], d_v.at[pl.ds(groups * c, groups), j])
             for j in range(4)]
            + [cin.start(gps.at[which, c], gp_v.at[c]), cin.start(g.at[:, pl.ds(fc * c, fc)], u_v.at[c]),
               cin.start(es.at[which, pl.ds(2 * pairs * c, 2 * pairs)], e_v.at[pl.ds(2 * pairs * c, 2 * pairs)])]
        )
    norms = [cin.start(ns.at[which], n_v), cin.start(nrs.at[which], r_v)]
    wq = [cin.start(g.at[:, pl.ds(ff + d * i, d)], w_v.at[:, pl.ds(d * i, d)]) for i in range(3)]
    rows_in = cin.start(xs.at[which], x_v)

    pending = []
    pltpu.make_async_copy(recv, g_v, ins.at[0]).wait()
    keep = jnp.where(ids_col[0] < ABSENT, 1.0, 0.0)
    gres = keep * g_v[...].astype(F32)
    ob_v[...] = jnp.sum(gres, axis=0, keepdims=True)
    gb_v[...] = gres.astype(BF)
    pending += [cout.start(gb_v, gbs.at[st]), cout.start(ob_v, obs.at[st])]
    wa.wait()
    gat_v[...] = mm(a_v[...], gb_v[...], NT).astype(BF)
    for copy in heads:
        copy.wait()
    zeros = jnp.zeros((LANES // 2, rows), BF)
    for c in range(chunks):
        for copy in wff[c]:
            copy.wait()
        gup = mm(gb_v[...], d_v[groups * c : groups * c + groups].reshape(fc, d), NT) * gp_v[c].astype(F32)
        ub_v[:, fc * c : fc * c + fc] = jnp.sum(gup, axis=0, keepdims=True)
        gup = gup.astype(BF)
        gj_v[c] = gup
        pending.append(cout.start(gj_v.at[c], gjs.at[st, c]))
        total = mm(gup, u_v[c], NT)
        if c == 0:
            acc_v[...] = total
        else:
            acc_v[...] += total
        for p in range(pairs * c, pairs * c + pairs):
            cols = slice(LANES * p, LANES * p + LANES)
            keys, vals, pair = k_v[:, cols], v_v[:, cols], q_v[:, cols]
            keys_t = keys.T
            gk, gv = None, None
            for half in range(2):
                h = 2 * p + half
                at_rows = slice(64 * h, 64 * h + 64)
                inv = rs_v[h : h + 1, :]
                ga = (gat_v[at_rows, :].astype(F32) * inv).astype(BF)
                ga = jnp.concatenate([zeros, ga] if half else [ga, zeros], axis=0)
                e = e_v[h]
                ef = e.astype(F32)
                gp = ef * mm(vals, ga)
                dot = jnp.sum(gp, axis=0, keepdims=True) * inv
                gs = (gp - ef * dot).astype(BF)
                gk_h = mm(gs, lane_half(pair, half))
                gv_h = mm(e, ga, NT)
                gk = gk_h if gk is None else gk + gk_h
                gv = gv_h if gv is None else gv + gv_h
                gqt_v[at_rows, :] = mm(keys_t[64 * half : 64 * half + 64], gs) * 0.125
            gk_v[:, cols] = gk
            gv_b[:, cols] = gv.astype(BF)
    pending += [cout.start(ub_v, ubs.at[st]), cout.start(gv_b, gvs.at[st])]
    for copy in norms:
        copy.wait()
    for i, (grad, out, stack) in enumerate(((gqt_v[...].T, gq_b, gqs), (gk_v[...], gk_b, gks))):
        normal = n_v[:, d * i : d * i + d].astype(F32)
        qk_v[:, d * i : d * i + d] = jnp.sum(grad * normal, axis=0, keepdims=True)
        out[...] = norm_back(grad * gains[i], normal, r_v[:, d * i : d * i + d].astype(F32), spread[...]).astype(BF)
        pending.append(cout.start(out, stack.at[st]))
    pending.append(cout.start(qk_v, qkgs.at[st]))
    for copy in wq:
        copy.wait()
    ghid = acc_v[...]
    for i, part in enumerate((gq_b, gk_b, gv_b)):
        ghid = ghid + mm(part[...], w_v[:, d * i : d * i + d], NT)
    rows_in.wait()
    xhat, rstd = row_norm(keep * x_v[...].astype(F32))
    ng_v[...] = jnp.sum(ghid * xhat, axis=0, keepdims=True)
    gx = ghid * ngain[...]
    gmask = rstd * (gx - jnp.mean(gx, axis=-1, keepdims=True) - xhat * jnp.mean(gx * xhat, axis=-1, keepdims=True))
    out = keep * (keep * g_v[...].astype(F32) + gmask)
    out_v[...] = out
    gbf[...] = out.astype(BF)
    pending += [cout.start(out_v, grs.at[st]), cout.start(ng_v, ngs.at[st])]
    for copy in pending:
        copy.wait()


ANY = pl.BlockSpec(memory_space=pl.ANY)


def whole(shape):
    return pl.BlockSpec(shape, lambda i, idx: (0,) * len(shape))


def pick(shape):
    return pl.BlockSpec((1,) + shape, lambda i, idx: (idx[0],) + (0,) * len(shape))


def call(kernel, idx, ins, fresh, stashes, scratch, flops):
    outs = pl.pallas_call(
        kernel,
        grid_spec=pltpu.PrefetchScalarGridSpec(
            num_scalar_prefetch=1,
            grid=(1,),
            in_specs=[s for _, s in ins] + [ANY] * len(stashes),
            out_specs=[whole(fresh[0])] + [ANY] * len(stashes),
            scratch_shapes=scratch,
        ),
        out_shape=[jax.ShapeDtypeStruct(*fresh)] + [jax.ShapeDtypeStruct(a.shape, a.dtype) for a in stashes],
        input_output_aliases={1 + len(ins) + i: 1 + i for i in range(len(stashes))},
        compiler_params=pltpu.CompilerParams(dimension_semantics=("arbitrary",), vmem_limit_bytes=VMEM_LIMIT),
        cost_estimate=pl.CostEstimate(flops=flops, bytes_accessed=30 << 20, transcendentals=0),
    )(idx, *[a for a, _ in ins], *stashes)
    return outs[0], outs[1:]


def shifted(x, by):
    devices = lax.axis_size("section")
    return lax.ppermute(x, "section", [(i, i + by) for i in range(devices) if 0 <= i + by < devices])


def summed_everywhere(x):
    devices = lax.axis_size("dp")
    step = 1
    while step < devices:
        x = x + lax.ppermute(x, "dp", [(i, i ^ step) for i in range(devices)])
        step *= 2
    return x


def body(tokens, cotangent, lengths, proj_in, proj_attn, proj_down, norm_gain, query_gain, key_gain, up_bias, out_bias):
    sections = lax.axis_size("section")
    ranks = lax.axis_size("dp")
    section = lax.axis_index("section")
    rank = lax.axis_index("dp")
    slots = lengths.shape[0]
    rows = tokens.shape[0] // slots
    d = tokens.shape[1]
    joined = proj_in.shape[2]
    ff = proj_down.shape[1] * ranks
    head = query_gain.shape[1] * ranks
    heads = d // head
    dshare = proj_in.shape[1]
    fshare = proj_down.shape[1] // dshare
    hshare = query_gain.shape[1]
    chunks = 3
    ticks = slots + sections - 1
    wide = joined + d + ff

    place = jnp.arange(WIDE, dtype=jnp.int32)
    source = (place % (WIDE // fshare)) * fshare + place // (WIDE // fshare)
    shuffle = (place[:, None] == source[None, :]).astype(BF)

    def shuffled(x, back=False):
        flat = x.reshape(-1, WIDE)
        out = lax.dot_general(flat, shuffle, NT if back else NN, preferred_element_type=F32)
        return out.reshape(x.shape)

    small = jnp.concatenate(
        [
            norm_gain[0][:, None],
            out_bias[0][:, None],
            up_bias[0].reshape(dshare, fshare),
            jnp.pad(query_gain[0], (0, dshare - hshare))[:, None],
            jnp.pad(key_gain[0], (0, dshare - hshare))[:, None],
            jnp.zeros((dshare, LANES - 4 - fshare), BF),
        ],
        axis=1,
    )
    heads_part = joined - ff
    local = jnp.concatenate(
        [shuffled(proj_in[0][:, heads_part:]).astype(BF), proj_in[0][:, :heads_part], proj_attn[0],
         proj_down[0].reshape(dshare, fshare * d), small],
        axis=1,
    )
    g = lax.all_gather(local, "dp", axis=0, tiled=True)
    g3 = g.reshape(ff // WIDE, WIDE // fshare, g.shape[1])
    tail = g[:, wide : wide + LANES].astype(F32)
    ngain = tail[:, 0].reshape(1, d)
    obias = tail[:, 1].reshape(1, d)
    ubias = shuffled(tail[:, 2 : 2 + fshare].reshape(1, ff).astype(BF))
    qk_gain = tail[:, 2 + fshare : 4 + fshare].reshape(ranks, dshare, 2)[:, :hshare].reshape(head, 2).T
    gains = jnp.tile(qk_gain, (1, heads)).reshape(2, 1, d)
    column = jnp.arange(WIDE, dtype=jnp.int32) // head
    spread = jnp.where(column[:, None] == column[None, :], 1.0 / head, 0.0).astype(BF)

    toks = tokens.reshape(slots, rows, d)
    seeds = cotangent.reshape(slots, rows, d)
    ends = jnp.cumsum(lengths, axis=-1)
    position = jnp.arange(rows, dtype=jnp.int32)
    image = jnp.sum((position[None, :, None] >= ends[:, None, :]).astype(jnp.int32), axis=-1)
    image = jnp.where(position[None, :] < ends[:, 2:3], image, ABSENT + position[None, :])
    ids_col, ids_row = image[:, :, None], image[:, None, :]

    def stash(*shape, dtype=BF):
        return pl.pallas_call(
            lambda out: None,
            out_shape=jax.ShapeDtypeStruct((slots + 1,) + shape, dtype),
            out_specs=pl.BlockSpec(memory_space=pl.ANY),
        )()

    fc = ff // chunks
    groups = ff // WIDE
    kept = [stash(rows, d), stash(rows, d), stash(rows, d), stash(rows, d), stash(rows, d), stash(rows, 2 * d), stash(rows, 2 * d),
            stash(chunks, rows, fc), stash(chunks, rows, fc), stash(heads, rows, rows), stash(16, rows, dtype=F32),
            stash(d, rows), stash(rows, d, dtype=F32)]

    def index_of(tick, distance, first):
        which = tick - distance
        active = (which >= 0) & (which < slots)
        return jnp.stack(
            [jnp.clip(which, 0, slots - 1), jnp.where(active, which, slots), first.astype(jnp.int32)]
        ).astype(jnp.int32)

    V = pltpu.VMEM
    weights_v = [V((d, heads_part), BF), V((chunks, d, fc), BF), V((groups, fshare, WIDE // fshare, d), BF), V((d, d), BF)]
    sems = [pltpu.SemaphoreType.DMA((48,)), pltpu.SemaphoreType.DMA((48,))]
    smalls = [(ngain, whole((1, d))), (gains, whole((2, 1, d)))]
    nothing = jnp.zeros((rows, d), BF)
    recv = nothing
    for t in range(ticks):
        ybf, kept = call(
            partial(forward_kernel, d, ff, chunks),
            index_of(t, section, section == 0),
            [(toks, ANY), (recv, ANY), (g, ANY), (g3, ANY), (ids_col, pick((rows, 1))), (ids_row, pick((1, rows)))] + smalls
            + [(ubias, whole((1, ff))), (obias, whole((1, d))), (spread, whole((WIDE, WIDE)))],
            ((rows, d), BF),
            kept,
            [V((rows, d), BF), V((rows, d), BF)] + weights_v
            + [V((rows, d), BF)] * 3 + [V((rows, 2 * d), BF)] * 2 + [V((chunks, rows, fc), BF)] * 2
            + [V((heads, rows, rows), BF), V((16, rows), F32), V((d, rows), BF), V((rows, d), BF), V((rows, d), F32), V((rows, d), F32)]
            + sems,
            2 * rows * (d * wide + 2 * rows * d),
        )
        if t < ticks - 1:
            recv = shifted(ybf, 1)

    xs, hs, qs, ks, vs, ns, nrs, acts, gps, es, rsums, ats, ys = kept
    back = [stash(rows, d), stash(chunks, rows, fc), stash(rows, d), stash(rows, d), stash(rows, d),
            stash(rows, d, dtype=F32), stash(1, d, dtype=F32), stash(1, d, dtype=F32), stash(1, 2 * d, dtype=F32), stash(1, ff, dtype=F32)]
    recv = nothing
    for t in range(ticks):
        gbf, back = call(
            partial(backward_kernel, d, ff, chunks),
            index_of(t, sections - 1 - section, section == sections - 1),
            [(seeds, ANY), (recv, ANY), (g, ANY), (g3, ANY), (ids_col, pick((rows, 1)))] + smalls + [(spread, whole((WIDE, WIDE)))]
            + [(a, ANY) for a in (xs, qs, ks, vs, ns, nrs, gps, es, rsums, ats)],
            ((rows, d), BF),
            back,
            [V((rows, d), BF), V((rows, d), BF)] + weights_v
            + [V((rows, d), BF)] * 4 + [V((rows, 2 * d), BF)] * 2
            + [V((chunks, rows, fc), BF), V((heads, rows, rows), BF), V((16, rows), F32), V((d, rows), BF)]
            + [V((d, rows), BF), V((d, rows), F32), V((rows, d), F32)]
            + [V((rows, d), BF)] * 3 + [V((chunks, rows, fc), BF), V((rows, d), F32), V((rows, d), F32)]
            + [V((1, d), F32), V((1, d), F32), V((1, 2 * d), F32), V((1, ff), F32)]
            + sems,
            2 * rows * (d * wide + 4 * rows * d),
        )
        if t < ticks - 1:
            recv = shifted(gbf, -1)

    gbs, gjs, gqs, gks, gvs, grs, obs, ngs, qkgs, ubs = back

    def over_rows(left, right):
        return jnp.einsum("md,mj->dj", left[:slots].reshape(-1, left.shape[-1]), right[:slots].reshape(-1, right.shape[-1]),
                          preferred_element_type=F32).astype(BF)

    g_up = [jnp.einsum("smd,smj->dj", hs[:slots], gjs[:slots, c], preferred_element_type=F32).astype(BF) for c in range(chunks)]
    g_heads = [over_rows(hs, v) for v in (gqs, gks, gvs)]
    g_attn = jnp.einsum("sdm,smj->dj", ats[:slots], gbs[:slots], preferred_element_type=F32).astype(BF)
    g_down = [jnp.einsum("smf,smj->fj", acts[:slots, c], gbs[:slots], preferred_element_type=F32).astype(BF) for c in range(chunks)]
    g_down = jnp.concatenate(g_down).reshape(groups, fshare, WIDE // fshare, d).transpose(0, 2, 1, 3).reshape(d, fshare * d)
    flat = jnp.concatenate([jnp.sum(v[:slots], axis=0)[0] for v in (ngs, obs, qkgs, ubs)]).reshape(-1, LANES)
    flat = summed_everywhere(flat).reshape(-1)
    g_ng, g_ob, g_q, g_k, g_ub = (flat[:d], flat[d : 2 * d], flat[2 * d : 3 * d], flat[3 * d : 4 * d], flat[4 * d :])
    g_q, g_k = (jnp.sum(v.reshape(heads, head), axis=0) for v in (g_q, g_k))
    g_ub = g_ub.reshape(-1, fshare, WIDE // fshare).transpose(0, 2, 1).reshape(-1)

    def share(v):
        size = v.shape[0] // ranks
        return lax.dynamic_slice_in_dim(v, rank * size, size)[None]

    total = lax.optimization_barrier(
        lax.psum_scatter(jnp.concatenate(g_up + g_heads + [g_attn, g_down], axis=1), "dp", scatter_dimension=0, tiled=True)
    )
    g_in = jnp.concatenate([total[:, ff:joined].astype(F32), shuffled(total[:, :ff], back=True)], axis=1)
    return (
        ys[:slots].reshape(1, slots * rows, d),
        grs[:slots].reshape(1, slots * rows, d),
        g_in[None],
        total[None, :, joined : joined + d].astype(F32),
        total[:, joined + d : wide].astype(F32).reshape(1, dshare * fshare, d),
        share(g_ng),
        share(g_q),
        share(g_k),
        share(g_ub),
        share(g_ob),
    )


def solution(mesh):
    in_specs = (P("dp", None),) * 3 + (P("section", "dp", None),) * 3 + (P("section", "dp"),) * 5
    out_specs = (P("section", "dp", None),) * 5 + (P("section", "dp"),) * 5
    return jax.shard_map(body, mesh=mesh, in_specs=in_specs, out_specs=out_specs, check_vma=False)
```

```python
from functools import partial
import math

import jax
import jax.numpy as jnp
from jax import lax
from jax.experimental import pallas as pl
from jax.experimental.pallas import tpu as pltpu
from jax.sharding import PartitionSpec as P

BF = jnp.bfloat16
F32 = jnp.float32
VMEM_LIMIT = 60 * 1024 * 1024
EPS = 1e-06
NN = (((1,), (0,)), ((), ()))
NT = (((1,), (1,)), ((), ()))
TN = (((0,), (0,)), ((), ()))
LANES = 128
WIDE = 256
ABSENT = 16


def mm(a, b, dims=NN):
    return lax.dot_general(a, b, dims, preferred_element_type=F32)


def head_mean(x, spread, exact):
    parts = []
    for at in range(0, x.shape[1], WIDE):
        piece = x[:, at : at + WIDE]
        top = piece.astype(BF)
        total = mm(top, spread)
        if exact:
            total = total + mm((piece - top.astype(F32)).astype(BF), spread)
        parts.append(total)
    return jnp.concatenate(parts, axis=1)


def row_norm(x):
    centered = x - jnp.mean(x, axis=-1, keepdims=True)
    rstd = lax.rsqrt(jnp.mean(centered * centered, axis=-1, keepdims=True) + EPS)
    return centered * rstd, rstd


def norm_back(grad, normal, rstd, spread):
    return rstd * (grad - head_mean(grad, spread, False) - normal * head_mean(grad * normal, spread, False))


def lane_half(x, second):
    lane = lax.broadcasted_iota(jnp.int32, x.shape, 1)
    return jnp.where((lane >= LANES // 2) if second else (lane < LANES // 2), x, jnp.zeros_like(x))


class Copies:
    def __init__(self, sems):
        self.sems, self.used = sems, 0

    def start(self, src, dst):
        copy = pltpu.make_async_copy(src, dst, self.sems.at[self.used])
        self.used += 1
        copy.start()
        return copy


def forward_kernel(d, ff, chunks, idx, tok, recv, g, g3, ids_col, ids_row, ngain, gains, ubias, obias, spread, *refs):
    refs = refs[13:]
    ybf, refs = refs[0], refs[1:]
    xs, hs, qs, ks, vs, ns, nrs, acts, gps, es, small = refs[:11]
    at_out, y_out = refs[11:13]
    (x_v, h_v, w_v, u_v, d_v, a_v, q_v, k_v, v_v, n_v, r_v, act_v, gp_v, e_v, rs_v, at_v, att_v, acc_v, y_v, ins, outs) = refs[13:]
    rows = x_v.shape[0]
    fc = ff // chunks
    which, st = idx[0], idx[1]
    cin, cout = Copies(ins), Copies(outs)

    @pl.when(idx[2] == 1)
    def _():
        pltpu.make_async_copy(tok.at[which], x_v, ins.at[0]).start()

    @pl.when(idx[2] != 1)
    def _():
        pltpu.make_async_copy(recv, x_v, ins.at[0]).start()

    cin.used = 1
    wq = [cin.start(g.at[:, pl.ds(ff + d * i, d)], w_v.at[:, pl.ds(d * i, d)]) for i in range(3)]
    groups = fc // WIDE
    wff = []
    for c in range(chunks):
        wff.append([cin.start(g.at[:, pl.ds(fc * c, fc)], u_v.at[c])] + [
            cin.start(g3.at[pl.ds(groups * c, groups), :, pl.ds(ff + 4 * d + d * j, d)], d_v.at[pl.ds(groups * c, groups), j])
            for j in range(4)
        ])
    wa = cin.start(g.at[:, pl.ds(ff + 3 * d, d)], a_v)

    pending = []
    pltpu.make_async_copy(recv, x_v, ins.at[0]).wait()
    keep = jnp.where(ids_col[0] < ABSENT, 1.0, 0.0)
    masked = keep * x_v[...].astype(F32)
    h_v[...] = (row_norm(masked)[0] * ngain[...]).astype(BF)
    pending += [cout.start(x_v, xs.at[st]), cout.start(h_v, hs.at[st])]
    bias_mask = jnp.where(ids_col[0] == ids_row[0], 0.0, -1e9)
    for i in range(3):
        wq[i].wait()
        raw = mm(h_v[...], w_v[:, d * i : d * i + d])
        if i == 2:
            v_v[...] = raw.astype(BF)
            pending.append(cout.start(v_v, vs.at[st]))
        else:
            centered = raw - head_mean(raw, spread[...], True)
            rstd = lax.rsqrt(head_mean(centered * centered, spread[...], True) + EPS)
            normal = centered * rstd
            scaled = (normal * gains[i]).astype(BF)
            n_v[:, d * i : d * i + d] = normal.astype(BF)
            r_v[:, d * i : d * i + d] = rstd.astype(BF)
            if i == 0:
                q_v[...] = scaled * jnp.asarray(0.125, BF)
                pending.append(cout.start(q_v, qs.at[st]))
            else:
                k_v[...] = scaled
                pending.append(cout.start(k_v, ks.at[st]))
    pending += [cout.start(n_v, ns.at[st]), cout.start(r_v, nrs.at[st])]
    ones = jnp.ones((16, rows), BF)
    pairs = d // LANES // chunks
    for c in range(chunks):
        for copy in wff[c]:
            copy.wait()
        pre = mm(h_v[...], u_v[c]) + ubias[:, fc * c : fc * c + fc]
        cdf = 0.5 * (1.0 + lax.erf(pre * (1.0 / math.sqrt(2.0))))
        density = jnp.exp(-0.5 * pre * pre) * (1.0 / math.sqrt(2.0 * math.pi))
        act = (pre * cdf).astype(BF)
        act_v[c] = act
        gp_v[c] = (cdf + pre * density).astype(BF)
        total = mm(act, d_v[groups * c : groups * c + groups].reshape(fc, d))
        if c == 0:
            acc_v[...] = total
        else:
            acc_v[...] += total
        for p in range(pairs * c, pairs * c + pairs):
            cols = slice(LANES * p, LANES * p + LANES)
            vals_t = v_v[:, cols].T
            pair = q_v[:, cols]
            both = []
            for half in range(2):
                h = 2 * p + half
                e = jnp.exp(mm(k_v[:, cols], lane_half(pair, half), NT) + bias_mask).astype(BF)
                e_v[h] = e
                got = mm(jnp.concatenate([vals_t[64 * half : 64 * half + 64], ones], axis=0), e)
                inv = 1.0 / got[64:65]
                rs_v[h : h + 1, :] = inv
                both.append((got[:64] * inv).astype(BF))
            both = jnp.concatenate(both, axis=0)
            at_v[cols, :] = both
            att_v[:, cols] = both.T
        pending += [cout.start(act_v.at[c], acts.at[st, c]), cout.start(gp_v.at[c], gps.at[st, c]),
                    cout.start(e_v.at[pl.ds(2 * pairs * c, 2 * pairs)], es.at[st, pl.ds(2 * pairs * c, 2 * pairs)])]
    pending += [cout.start(rs_v, small.at[st]), cout.start(at_v, at_out.at[st])]
    wa.wait()
    y = keep * (keep * x_v[...].astype(F32) + acc_v[...] + mm(att_v[...], a_v[...]) + obias[...])
    y_v[...] = y
    ybf[...] = y.astype(BF)
    pending.append(cout.start(y_v, y_out.at[st]))
    for copy in pending:
        copy.wait()


def backward_kernel(d, ff, chunks, idx, seed, recv, g, g3, ids_col, ngain, gains, spread, *refs):
    xs, qs, ks, vs, ns, nrs, gps, es, small, ats = refs[:10]
    refs = refs[10:]
    refs = refs[5 + 5 :]
    gbf, refs = refs[0], refs[1:]
    gbs, gjs, gqs, gks, gvs, refs = refs[0], refs[1], refs[2], refs[3], refs[4], refs[5:]
    grs, obs, ngs, qkgs, ubs, refs = refs[0], refs[1], refs[2], refs[3], refs[4], refs[5:]
    (g_v, gb_v, w_v, u_v, d_v, a_v, x_v, q_v, k_v, v_v, n_v, r_v, gp_v, e_v, rs_v, at_v, gat_v, gqt_v, gk_v,
     gq_b, gk_b, gv_b, gj_v, acc_v, out_v, ob_v, ng_v, qk_v, ub_v, ins, outs) = refs
    rows = x_v.shape[0]
    fc = ff // chunks
    groups = fc // WIDE
    which, st = idx[0], idx[1]
    cin, cout = Copies(ins), Copies(outs)

    @pl.when(idx[2] == 1)
    def _():
        pltpu.make_async_copy(seed.at[which], g_v, ins.at[0]).start()

    @pl.when(idx[2] != 1)
    def _():
        pltpu.make_async_copy(recv, g_v, ins.at[0]).start()

    cin.used = 1
    wa = cin.start(g.at[:, pl.ds(ff + 3 * d, d)], a_v)
    heads = [cin.start(s.at[which], v) for s, v in ((small, rs_v), (ats, at_v), (ks, k_v), (vs, v_v), (qs, q_v))]
    pairs = d // LANES // chunks
    wff = []
    for c in range(chunks):
        wff.append(
            [cin.start(g3.at[pl.ds(groups * c, groups), :, pl.ds(ff + 4 * d + d * j, d)], d_v.at[pl.ds(groups * c, groups), j])
             for j in range(4)]
            + [cin.start(gps.at[which, c], gp_v.at[c]), cin.start(g.at[:, pl.ds(fc * c, fc)], u_v.at[c]),
               cin.start(es.at[which, pl.ds(2 * pairs * c, 2 * pairs)], e_v.at[pl.ds(2 * pairs * c, 2 * pairs)])]
        )
    norms = [cin.start(ns.at[which], n_v), cin.start(nrs.at[which], r_v)]
    wq = [cin.start(g.at[:, pl.ds(ff + d * i, d)], w_v.at[:, pl.ds(d * i, d)]) for i in range(3)]
    rows_in = cin.start(xs.at[which], x_v)

    pending = []
    pltpu.make_async_copy(recv, g_v, ins.at[0]).wait()
    keep = jnp.where(ids_col[0] < ABSENT, 1.0, 0.0)
    gres = keep * g_v[...].astype(F32)
    ob_v[...] = jnp.sum(gres, axis=0, keepdims=True)
    gb_v[...] = gres.astype(BF)
    pending += [cout.start(gb_v, gbs.at[st]), cout.start(ob_v, obs.at[st])]
    wa.wait()
    gat_v[...] = mm(a_v[...], gb_v[...], NT).astype(BF)
    for copy in heads:
        copy.wait()
    zeros = jnp.zeros((LANES // 2, rows), BF)
    for c in range(chunks):
        for copy in wff[c]:
            copy.wait()
        gup = mm(gb_v[...], d_v[groups * c : groups * c + groups].reshape(fc, d), NT) * gp_v[c].astype(F32)
        ub_v[:, fc * c : fc * c + fc] = jnp.sum(gup, axis=0, keepdims=True)
        gup = gup.astype(BF)
        gj_v[c] = gup
        pending.append(cout.start(gj_v.at[c], gjs.at[st, c]))
        total = mm(gup, u_v[c], NT)
        if c == 0:
            acc_v[...] = total
        else:
            acc_v[...] += total
        for p in range(pairs * c, pairs * c + pairs):
            cols = slice(LANES * p, LANES * p + LANES)
            keys, vals, pair = k_v[:, cols], v_v[:, cols], q_v[:, cols]
            keys_t = keys.T
            gk, gv = None, None
            for half in range(2):
                h = 2 * p + half
                at_rows = slice(64 * h, 64 * h + 64)
                inv = rs_v[h : h + 1, :]
                ga = (gat_v[at_rows, :].astype(F32) * inv).astype(BF)
                ga = jnp.concatenate([zeros, ga] if half else [ga, zeros], axis=0)
                e = e_v[h]
                ef = e.astype(F32)
                gp = ef * mm(vals, ga)
                dot = jnp.sum(gp, axis=0, keepdims=True) * inv
                gs = (gp - ef * dot).astype(BF)
                gk_h = mm(gs, lane_half(pair, half))
                gv_h = mm(e, ga, NT)
                gk = gk_h if gk is None else gk + gk_h
                gv = gv_h if gv is None else gv + gv_h
                gqt_v[at_rows, :] = mm(keys_t[64 * half : 64 * half + 64], gs) * 0.125
            gk_v[:, cols] = gk
            gv_b[:, cols] = gv.astype(BF)
    pending += [cout.start(ub_v, ubs.at[st]), cout.start(gv_b, gvs.at[st])]
    for copy in norms:
        copy.wait()
    for i, (grad, out, stack) in enumerate(((gqt_v[...].T, gq_b, gqs), (gk_v[...], gk_b, gks))):
        normal = n_v[:, d * i : d * i + d].astype(F32)
        qk_v[:, d * i : d * i + d] = jnp.sum(grad * normal, axis=0, keepdims=True)
        out[...] = norm_back(grad * gains[i], normal, r_v[:, d * i : d * i + d].astype(F32), spread[...]).astype(BF)
        pending.append(cout.start(out, stack.at[st]))
    pending.append(cout.start(qk_v, qkgs.at[st]))
    for copy in wq:
        copy.wait()
    ghid = acc_v[...]
    for i, part in enumerate((gq_b, gk_b, gv_b)):
        ghid = ghid + mm(part[...], w_v[:, d * i : d * i + d], NT)
    rows_in.wait()
    xhat, rstd = row_norm(keep * x_v[...].astype(F32))
    ng_v[...] = jnp.sum(ghid * xhat, axis=0, keepdims=True)
    gx = ghid * ngain[...]
    gmask = rstd * (gx - jnp.mean(gx, axis=-1, keepdims=True) - xhat * jnp.mean(gx * xhat, axis=-1, keepdims=True))
    out = keep * (keep * g_v[...].astype(F32) + gmask)
    out_v[...] = out
    gbf[...] = out.astype(BF)
    pending += [cout.start(out_v, grs.at[st]), cout.start(ng_v, ngs.at[st])]
    for copy in pending:
        copy.wait()


def weight_grad_kernel(d, ff, chunks, idx, place, hs, acts, ats, gbs, gjs, gqs, gks, gvs, obs, ngs, qkgs, ubs, out,
                       h_v, big_v, side_v, at_v, gb_v, out_v, ins, outs):
    slots, rows = h_v.shape[0], h_v.shape[1]
    fc = ff // chunks
    cin, cout = Copies(ins), Copies(outs)
    hidden = cin.start(hs.at[pl.ds(0, slots)], h_v)

    @pl.when(idx[0] == 0)
    def _():
        cin.used = 1
        copies = [cin.start(gbs.at[pl.ds(0, slots)], gb_v)]
        parts = [cin.start(acts.at[pl.ds(0, slots), c], big_v.at[c]) for c in range(chunks)]
        copies.append(cin.start(ats.at[pl.ds(0, slots)], at_v))
        values = cin.start(gvs.at[pl.ds(0, slots)], side_v.at[0])
        pending = []
        for copy in copies:
            copy.wait()
        gb = gb_v[...].reshape(slots * rows, d)
        quarter = WIDE // 4
        for c in range(chunks):
            parts[c].wait()
            got = lax.dot_general(big_v[c].reshape(slots * rows, fc), gb, TN, preferred_element_type=F32).astype(BF)
            for b in range(fc // WIDE):
                for j in range(4):
                    at = quarter * (fc // WIDE * c + b)
                    out_v[at : at + quarter, d * j : d * j + d] = got[WIDE * b + quarter * j : WIDE * b + quarter * (j + 1)]
            span = pl.ds(quarter * (fc // WIDE) * c, quarter * (fc // WIDE))
            pending.append(cout.start(out_v.at[span, pl.ds(0, 4 * d)], out.at[span, pl.ds(0, 4 * d)]))
        total = mm(at_v[0], gb_v[0])
        for s in range(1, slots):
            total = total + mm(at_v[s], gb_v[s])
        out_v[:, 4 * d : 5 * d] = total.astype(BF)
        hidden.wait()
        values.wait()
        flat = h_v[...].reshape(slots * rows, d)
        out_v[:, 5 * d : 6 * d] = lax.dot_general(
            flat, side_v[0].reshape(slots * rows, d), TN, preferred_element_type=F32
        ).astype(BF)
        def over_slots(ref):
            total = ref[0]
            for s in range(1, slots):
                total = total + ref[s]
            return total

        ub = over_slots(ubs)
        up_rows = []
        for j in range(4):
            pieces = [ub[:, WIDE * b + quarter * j : WIDE * b + quarter * (j + 1)] for b in range(ff // WIDE)]
            up_rows.append(jnp.concatenate(pieces, axis=1))
        qk = over_slots(qkgs)
        head_rows = []
        for i in range(2):
            lanes = qk[:, d * i : d * i + LANES]
            for p in range(1, d // LANES):
                lanes = lanes + qk[:, d * i + LANES * p : d * i + LANES * (p + 1)]
            head_rows.append(lanes)
        both = jnp.concatenate(head_rows + [jnp.zeros((6, LANES), F32)], axis=0)
        placed = lax.dot_general(both, place[...], NN, precision=lax.Precision.HIGHEST, preferred_element_type=F32)
        values8 = jnp.concatenate([over_slots(ngs), over_slots(obs)] + up_rows + [placed[0:1], placed[1:2]], axis=0)
        top = values8.astype(BF).astype(F32)
        table = jnp.concatenate([top, values8 - top, jnp.zeros((LANES - 16, d), F32)], axis=0)
        out_v[:, 6 * d :] = table.T.astype(BF)
        pending.append(cout.start(out_v.at[:, pl.ds(4 * d, 2 * d + LANES)], out.at[:, pl.ds(4 * d, 2 * d + LANES)]))
        for copy in pending:
            copy.wait()

    @pl.when(idx[0] == 1)
    def _():
        cin.used, cout.used = 1, 0
        parts = [cin.start(gjs.at[pl.ds(0, slots), c], big_v.at[c]) for c in range(chunks)]
        sides = [cin.start(v.at[pl.ds(0, slots)], side_v.at[i]) for i, v in enumerate((gqs, gks))]
        pending = []
        hidden.wait()
        turned = h_v[...].reshape(slots * rows, d).T
        for c in range(chunks):
            parts[c].wait()
            span = pl.ds(fc * c, fc)
            out_v[:, fc * c : fc * c + fc] = mm(turned, big_v[c].reshape(slots * rows, fc)).astype(BF)
            pending.append(cout.start(out_v.at[:, span], out.at[:, span]))
        for i in range(2):
            sides[i].wait()
            at = ff + d * i
            out_v[:, at : at + d] = mm(turned, side_v[i].reshape(slots * rows, d)).astype(BF)
        out_v[:, 6 * d :] = jnp.zeros((d, LANES), BF)
        pending.append(cout.start(out_v.at[:, pl.ds(ff, 2 * d + LANES)], out.at[:, pl.ds(ff, 2 * d + LANES)]))
        for copy in pending:
            copy.wait()


def pair_kernel(cut, idx, own, got, own4, got4, *refs):
    firsts, seconds, (a_v, b_v, c_v, d_v, ins, outs) = refs[:4], refs[4:8], refs[8:]
    y, z = idx[1], idx[2]
    width = own.shape[2]
    cin, cout = Copies(ins), Copies(outs)
    loads = []
    for s in range(4):
        to_y, to_z = lax.rem(y + s, 4), lax.rem(z + s, 4)
        loads.append((
            cin.start(own.at[to_y, :, pl.ds(0, cut)], a_v.at[s]),
            cin.start(got.at[to_y, :, pl.ds(0, cut)], b_v.at[s]),
            cin.start(own4.at[:, to_z, :, pl.ds(cut, width - cut)], c_v.at[s]),
            cin.start(got4.at[:, to_z, :, pl.ds(cut, width - cut)], d_v.at[s]),
        ))
    pending = []
    for s in (1, 2, 3, 0):
        for copy in loads[s]:
            copy.wait()
        a_v[s] = (a_v[s].astype(F32) + b_v[s].astype(F32)).astype(BF)
        pending.append(cout.start(a_v.at[s], firsts[s]))
        c_v[s] = added([c_v[s], d_v[s]])
        pending.append(cout.start(c_v.at[s], seconds[s]))
    for copy in pending:
        copy.wait()


def added(parts):
    total = parts[0].astype(F32)
    for part in parts[1:]:
        total = total + part.astype(F32)
    shape = total.shape
    total = total.reshape(-1, shape[-1])
    main, last = total[:, : shape[-1] - LANES], total[:, shape[-1] - LANES :]
    last = last + pltpu.roll(last, LANES - 8, 1)
    top = last.astype(BF).astype(F32)
    lane = lax.broadcasted_iota(jnp.int32, last.shape, 1)
    last = jnp.where(lane < 8, top, jnp.where(lane < 16, pltpu.roll(last - top, 8, 1), 0.0))
    return jnp.concatenate([main, last], axis=1).astype(BF).reshape(shape)


def mid_kernel(idx, *refs):
    firsts, seconds, a_out, b_out, (a_v, b_v) = refs[:4], refs[4:8], refs[8:12], refs[12:16], refs[16:]
    y, z = idx[1], idx[2]
    total = firsts[0][...].astype(F32)
    for part in firsts[1:]:
        total = total + part[...].astype(F32)
    a_v[...] = total.astype(BF).reshape(a_v.shape)
    b_v[...] = added([part[...].reshape(-1, part.shape[-1]) for part in seconds]).reshape(b_v.shape)
    for s in range(4):
        a_out[s][...] = a_v[lax.rem(z + s, 4)]
        b_out[s][...] = b_v[lax.rem(y + s, 4)]


def last_kernel(idx, *refs):
    firsts, seconds, mine, theirs, hold = refs[:4], refs[4:8], refs[8], refs[9], refs[10]
    cut = firsts[0].shape[-1]
    for group, at in ((firsts, 0), (seconds, cut)):
        total = group[0][...].astype(F32)
        for part in group[1:]:
            total = total + part[...].astype(F32)
        hold[:, at : at + total.shape[1]] = total
    count = mine.shape[0]
    core = idx[3]
    mine[...] = hold[pl.ds(pl.multiple_of(core * count, 8), count), :]
    theirs[...] = hold[pl.ds(pl.multiple_of((1 - core) * count, 8), count), :]


ANY = pl.BlockSpec(memory_space=pl.ANY)


def whole(shape):
    return pl.BlockSpec(shape, lambda i, idx: (0,) * len(shape))


def pick(shape):
    return pl.BlockSpec((1,) + shape, lambda i, idx: (idx[0],) + (0,) * len(shape))


def call(kernel, idx, ins, fresh, stashes, scratch, flops):
    outs = pl.pallas_call(
        kernel,
        grid_spec=pltpu.PrefetchScalarGridSpec(
            num_scalar_prefetch=1,
            grid=(1,),
            in_specs=[s for _, s in ins] + [ANY] * len(stashes),
            out_specs=[whole(fresh[0])] + [ANY] * len(stashes),
            scratch_shapes=scratch,
        ),
        out_shape=[jax.ShapeDtypeStruct(*fresh)] + [jax.ShapeDtypeStruct(a.shape, a.dtype) for a in stashes],
        input_output_aliases={1 + len(ins) + i: 1 + i for i in range(len(stashes))},
        compiler_params=pltpu.CompilerParams(dimension_semantics=("arbitrary",), vmem_limit_bytes=VMEM_LIMIT),
        cost_estimate=pl.CostEstimate(flops=flops, bytes_accessed=30 << 20, transcendentals=0),
    )(idx, *[a for a, _ in ins], *stashes)
    return outs[0], outs[1:]


def simple(kernel, idx, arrays, specs, out_shapes, out_specs, scratch, flops=1 << 24):
    return pl.pallas_call(
        kernel,
        grid_spec=pltpu.PrefetchScalarGridSpec(
            num_scalar_prefetch=1, grid=(1,), in_specs=specs, out_specs=out_specs, scratch_shapes=scratch
        ),
        out_shape=out_shapes,
        compiler_params=pltpu.CompilerParams(dimension_semantics=("arbitrary",), vmem_limit_bytes=VMEM_LIMIT),
        cost_estimate=pl.CostEstimate(flops=flops, bytes_accessed=16 << 20, transcendentals=0),
    )(idx, *arrays)


def along(x, step, size, by):
    devices = lax.axis_size("dp")

    def to(i):
        digit = i // step % size
        return i + ((digit + by) % size - digit) * step

    return lax.ppermute(x, "dp", [(i, to(i)) for i in range(devices)])


def shifted(x, by):
    devices = lax.axis_size("section")
    return lax.ppermute(x, "section", [(i, i + by) for i in range(devices) if 0 <= i + by < devices])


def body(tokens, cotangent, lengths, proj_in, proj_attn, proj_down, norm_gain, query_gain, key_gain, up_bias, out_bias):
    sections = lax.axis_size("section")
    ranks = lax.axis_size("dp")
    section = lax.axis_index("section")
    rank = lax.axis_index("dp")
    slots = lengths.shape[0]
    rows = tokens.shape[0] // slots
    d = tokens.shape[1]
    joined = proj_in.shape[2]
    ff = proj_down.shape[1] * ranks
    head = query_gain.shape[1] * ranks
    heads = d // head
    dshare = proj_in.shape[1]
    fshare = proj_down.shape[1] // dshare
    hshare = query_gain.shape[1]
    chunks = 3
    ticks = slots + sections - 1
    wide = joined + d + ff

    place = jnp.arange(WIDE, dtype=jnp.int32)
    source = (place % (WIDE // fshare)) * fshare + place // (WIDE // fshare)
    shuffle = (place[:, None] == source[None, :]).astype(BF)

    def shuffled(x, back=False):
        flat = x.reshape(-1, WIDE)
        out = lax.dot_general(flat, shuffle.astype(x.dtype), NT if back else NN, precision=lax.Precision.HIGHEST, preferred_element_type=F32)
        return out.reshape(x.shape)

    small = jnp.concatenate(
        [
            norm_gain[0][:, None],
            out_bias[0][:, None],
            up_bias[0].reshape(dshare, fshare),
            jnp.pad(query_gain[0], (0, dshare - hshare))[:, None],
            jnp.pad(key_gain[0], (0, dshare - hshare))[:, None],
            jnp.zeros((dshare, LANES - 4 - fshare), BF),
        ],
        axis=1,
    )
    heads_part = joined - ff
    local = jnp.concatenate(
        [shuffled(proj_in[0][:, heads_part:]).astype(BF), proj_in[0][:, :heads_part], proj_attn[0],
         proj_down[0].reshape(dshare, fshare * d), small],
        axis=1,
    )
    g = lax.all_gather(local, "dp", axis=0, tiled=True)
    g3 = g.reshape(ff // WIDE, WIDE // fshare, g.shape[1])
    tail = g[:, wide : wide + LANES].astype(F32)
    ngain = tail[:, 0].reshape(1, d)
    obias = tail[:, 1].reshape(1, d)
    ubias = shuffled(tail[:, 2 : 2 + fshare].reshape(1, ff).astype(BF))
    qk_gain = tail[:, 2 + fshare : 4 + fshare].reshape(ranks, dshare, 2)[:, :hshare].reshape(head, 2).T
    gains = jnp.tile(qk_gain, (1, heads)).reshape(2, 1, d)
    column = jnp.arange(WIDE, dtype=jnp.int32) // head
    spread = jnp.where(column[:, None] == column[None, :], 1.0 / head, 0.0).astype(BF)

    toks = tokens.reshape(slots, rows, d)
    seeds = cotangent.reshape(slots, rows, d)
    ends = jnp.cumsum(lengths, axis=-1)
    position = jnp.arange(rows, dtype=jnp.int32)
    image = jnp.sum((position[None, :, None] >= ends[:, None, :]).astype(jnp.int32), axis=-1)
    image = jnp.where(position[None, :] < ends[:, 2:3], image, ABSENT + position[None, :])
    ids_col, ids_row = image[:, :, None], image[:, None, :]

    def stash(*shape, dtype=BF):
        return pl.pallas_call(
            lambda out: None,
            out_shape=jax.ShapeDtypeStruct((slots + 1,) + shape, dtype),
            out_specs=pl.BlockSpec(memory_space=pl.ANY),
        )()

    fc = ff // chunks
    groups = ff // WIDE
    kept = [stash(rows, d), stash(rows, d), stash(rows, d), stash(rows, d), stash(rows, d), stash(rows, 2 * d), stash(rows, 2 * d),
            stash(chunks, rows, fc), stash(chunks, rows, fc), stash(heads, rows, rows), stash(16, rows, dtype=F32),
            stash(d, rows), stash(rows, d, dtype=F32)]

    def index_of(tick, distance, first):
        which = tick - distance
        active = (which >= 0) & (which < slots)
        return jnp.stack(
            [jnp.clip(which, 0, slots - 1), jnp.where(active, which, slots), first.astype(jnp.int32)]
        ).astype(jnp.int32)

    V = pltpu.VMEM
    weights_v = [V((d, heads_part), BF), V((chunks, d, fc), BF), V((groups, fshare, WIDE // fshare, d), BF), V((d, d), BF)]
    sems = [pltpu.SemaphoreType.DMA((48,)), pltpu.SemaphoreType.DMA((48,))]
    smalls = [(ngain, whole((1, d))), (gains, whole((2, 1, d)))]
    nothing = jnp.zeros((rows, d), BF)
    recv = nothing
    for t in range(ticks):
        ybf, kept = call(
            partial(forward_kernel, d, ff, chunks),
            index_of(t, section, section == 0),
            [(toks, ANY), (recv, ANY), (g, ANY), (g3, ANY), (ids_col, pick((rows, 1))), (ids_row, pick((1, rows)))] + smalls
            + [(ubias, whole((1, ff))), (obias, whole((1, d))), (spread, whole((WIDE, WIDE)))],
            ((rows, d), BF),
            kept,
            [V((rows, d), BF), V((rows, d), BF)] + weights_v
            + [V((rows, d), BF)] * 3 + [V((rows, 2 * d), BF)] * 2 + [V((chunks, rows, fc), BF)] * 2
            + [V((heads, rows, rows), BF), V((16, rows), F32), V((d, rows), BF), V((rows, d), BF), V((rows, d), F32), V((rows, d), F32)]
            + sems,
            2 * rows * (d * wide + 2 * rows * d),
        )
        if t < ticks - 1:
            recv = shifted(ybf, 1)

    xs, hs, qs, ks, vs, ns, nrs, acts, gps, es, rsums, ats, ys = kept
    back = [stash(rows, d), stash(chunks, rows, fc), stash(rows, d), stash(rows, d), stash(rows, d),
            stash(rows, d, dtype=F32), stash(1, d, dtype=F32), stash(1, d, dtype=F32), stash(1, 2 * d, dtype=F32), stash(1, ff, dtype=F32)]
    recv = nothing
    for t in range(ticks):
        gbf, back = call(
            partial(backward_kernel, d, ff, chunks),
            index_of(t, sections - 1 - section, section == sections - 1),
            [(seeds, ANY), (recv, ANY), (g, ANY), (g3, ANY), (ids_col, pick((rows, 1)))] + smalls + [(spread, whole((WIDE, WIDE)))]
            + [(a, ANY) for a in (xs, qs, ks, vs, ns, nrs, gps, es, rsums, ats)],
            ((rows, d), BF),
            back,
            [V((rows, d), BF), V((rows, d), BF)] + weights_v
            + [V((rows, d), BF)] * 4 + [V((rows, 2 * d), BF)] * 2
            + [V((chunks, rows, fc), BF), V((heads, rows, rows), BF), V((16, rows), F32), V((d, rows), BF)]
            + [V((d, rows), BF), V((d, rows), F32), V((rows, d), F32)]
            + [V((rows, d), BF)] * 3 + [V((chunks, rows, fc), BF), V((rows, d), F32), V((rows, d), F32)]
            + [V((1, d), F32), V((1, d), F32), V((1, 2 * d), F32), V((1, ff), F32)]
            + sems,
            2 * rows * (d * wide + 4 * rows * d),
        )
        if t < ticks - 1:
            recv = shifted(gbf, -1)

    gbs, gjs, gqs, gks, gvs, grs, obs, ngs, qkgs, ubs = back

    side = math.isqrt(ranks // 2)
    core, z, y = lax.rem(rank, 2), lax.rem(rank // 2, side), rank // (2 * side)
    width = 6 * d + LANES
    cut = 3 * d
    share = 2 * dshare
    position = jnp.arange(LANES, dtype=jnp.int32)[:, None] % head
    place = (position // hshare * dshare + position % hshare == jnp.arange(d, dtype=jnp.int32)[None, :]).astype(F32)

    def weight_grads(half):
        return simple(
            partial(weight_grad_kernel, d, ff, chunks),
            jnp.stack([half, y, z, core]).astype(jnp.int32),
            [place, hs, acts, ats, gbs, gjs, gqs, gks, gvs, obs, ngs, qkgs, ubs],
            [whole((LANES, d))] + [ANY] * 8 + [whole(a.shape) for a in (obs, ngs, qkgs, ubs)],
            jax.ShapeDtypeStruct((d, width), BF),
            ANY,
            [V((slots, rows, d), BF), V((chunks, slots, rows, fc), BF), V((2, slots, rows, d), BF), V((slots, d, rows), BF),
             V((slots, rows, d), BF), V((d, width), BF), pltpu.SemaphoreType.DMA((16,)), pltpu.SemaphoreType.DMA((16,))],
            2 * d * slots * rows * 6 * d,
        )

    here = jnp.stack([core, y, z, core]).astype(jnp.int32)
    theirs = weight_grads(1 - core)
    got = along(theirs, 1, 2, 1)
    own = weight_grads(core)
    by_y, by_z = (side, side * share, width), (side, side, share, width)
    outs = simple(
        partial(pair_kernel, cut), here,
        [own.reshape(by_y), got.reshape(by_y), own.reshape(by_z), got.reshape(by_z)],
        [ANY] * 4,
        [jax.ShapeDtypeStruct((side * share, cut), BF)] * side + [jax.ShapeDtypeStruct((side, share, width - cut), BF)] * side,
        [ANY] * 8,
        [V((side, side * share, cut), BF)] * 2 + [V((side, side, share, width - cut), BF)] * 2
        + [pltpu.SemaphoreType.DMA((16,)), pltpu.SemaphoreType.DMA((8,))],
    )
    firsts = [outs[0]] + [along(outs[s], 2 * side, side, s) for s in range(1, side)]
    seconds = [outs[side]] + [along(outs[side + s], 2, side, s) for s in range(1, side)]
    shapes = [(share, cut)] * side + [(share, width - cut)] * side
    outs = simple(
        mid_kernel, here, firsts + seconds, [whole(a.shape) for a in firsts + seconds],
        [jax.ShapeDtypeStruct(s, BF) for s in shapes], [whole(s) for s in shapes],
        [V((side, share, cut), BF), V((side, share, width - cut), BF)],
    )
    firsts = [outs[0]] + [along(outs[s], 2, side, s) for s in range(1, side)]
    seconds = [outs[side]] + [along(outs[side + s], 2 * side, side, s) for s in range(1, side)]
    mine, other = simple(
        last_kernel, here, firsts + seconds, [whole(a.shape) for a in firsts + seconds],
        [jax.ShapeDtypeStruct((dshare, width), F32)] * 2, [whole((dshare, width))] * 2,
        [V((share, width), F32)],
    )
    other = along(other, 1, 2, 1)
    half0, half1 = jnp.where(core == 0, mine, other), jnp.where(core == 0, other, mine)
    g_in = jnp.concatenate([half1[:, ff : 6 * d], half0[:, 5 * d : 6 * d], shuffled(half1[:, :ff], back=True)], axis=1)
    last = half0[:, 6 * d : 6 * d + 8] + half0[:, 6 * d + 8 : 6 * d + 16]
    return (
        ys[:slots].reshape(1, slots * rows, d),
        grs[:slots].reshape(1, slots * rows, d),
        g_in[None],
        half0[None, :, 4 * d : 5 * d],
        half0[:, : 4 * d].reshape(1, dshare * fshare, d),
        last[None, :, 0],
        last[None, :hshare, 6],
        last[None, :hshare, 7],
        last[:, 2:6].reshape(1, dshare * fshare),
        last[None, :, 1],
    )


def solution(mesh):
    in_specs = (P("dp", None),) * 3 + (P("section", "dp", None),) * 3 + (P("section", "dp"),) * 5
    out_specs = (P("section", "dp", None),) * 5 + (P("section", "dp"),) * 5
    return jax.shard_map(body, mesh=mesh, in_specs=in_specs, out_specs=out_specs, check_vma=False)
```

```python
from functools import partial
import math

import jax
import jax.numpy as jnp
from jax import lax
from jax.experimental import pallas as pl
from jax.experimental.pallas import tpu as pltpu
from jax.sharding import PartitionSpec as P

BF = jnp.bfloat16
F32 = jnp.float32
VMEM_LIMIT = 60 * 1024 * 1024
EPS = 1e-06
NN = (((1,), (0,)), ((), ()))
NT = (((1,), (1,)), ((), ()))
TN = (((0,), (0,)), ((), ()))
LANES = 128
WIDE = 256
ABSENT = 16


def mm(a, b, dims=NN):
    return lax.dot_general(a, b, dims, preferred_element_type=F32)


def head_mean(x, spread, exact):
    parts = []
    for at in range(0, x.shape[1], WIDE):
        piece = x[:, at : at + WIDE]
        top = piece.astype(BF)
        total = mm(top, spread)
        if exact:
            total = total + mm((piece - top.astype(F32)).astype(BF), spread)
        parts.append(total)
    return jnp.concatenate(parts, axis=1)


def row_norm(x):
    centered = x - jnp.mean(x, axis=-1, keepdims=True)
    rstd = lax.rsqrt(jnp.mean(centered * centered, axis=-1, keepdims=True) + EPS)
    return centered * rstd, rstd


def norm_back(grad, normal, rstd, spread):
    return rstd * (grad - head_mean(grad, spread, False) - normal * head_mean(grad * normal, spread, False))


def lane_half(x, second):
    lane = lax.broadcasted_iota(jnp.int32, x.shape, 1)
    return jnp.where((lane >= LANES // 2) if second else (lane < LANES // 2), x, jnp.zeros_like(x))


class Copies:
    def __init__(self, sems):
        self.sems, self.used = sems, 0

    def start(self, src, dst):
        copy = pltpu.make_async_copy(src, dst, self.sems.at[self.used])
        self.used += 1
        copy.start()
        return copy


def result_out(value, stack, entry, copies):
    @pl.when(entry < stack.shape[0])
    def _():
        copy = copies.start(value, stack.at[entry])
        copy.wait()


def forward_kernel(d, ff, chunks, idx, tok, recv, g, g3, ids_col, ids_row, ngain, gains, ubias, obias, spread, *refs):
    refs = refs[13:]
    ybf, refs = refs[0], refs[1:]
    xs, hs, qs, ks, vs, ns, nrs, acts, gps, es, small = refs[:11]
    at_out, y_out = refs[11:13]
    (x_v, h_v, w_v, u_v, d_v, a_v, q_v, k_v, v_v, n_v, r_v, act_v, gp_v, e_v, rs_v, at_v, att_v, acc_v, y_v, ins, outs) = refs[13:]
    rows = x_v.shape[0]
    fc = ff // chunks
    which, st = idx[0], idx[1]
    cin, cout = Copies(ins), Copies(outs)

    @pl.when(idx[2] == 1)
    def _():
        pltpu.make_async_copy(tok.at[which], x_v, ins.at[0]).start()

    @pl.when(idx[2] != 1)
    def _():
        pltpu.make_async_copy(recv, x_v, ins.at[0]).start()

    cin.used = 1
    wq = [cin.start(g.at[:, pl.ds(ff + d * i, d)], w_v.at[:, pl.ds(d * i, d)]) for i in range(3)]
    groups = fc // WIDE
    wff = []
    for c in range(chunks):
        wff.append([cin.start(g.at[:, pl.ds(fc * c, fc)], u_v.at[c])] + [
            cin.start(g3.at[pl.ds(groups * c, groups), :, pl.ds(ff + 4 * d + d * j, d)], d_v.at[pl.ds(groups * c, groups), j])
            for j in range(4)
        ])
    wa = cin.start(g.at[:, pl.ds(ff + 3 * d, d)], a_v)

    pending = []
    pltpu.make_async_copy(recv, x_v, ins.at[0]).wait()
    keep = jnp.where(ids_col[0] < ABSENT, 1.0, 0.0)
    masked = keep * x_v[...].astype(F32)
    h_v[...] = (row_norm(masked)[0] * ngain[...]).astype(BF)
    pending += [cout.start(x_v, xs.at[st]), cout.start(h_v, hs.at[st])]
    bias_mask = jnp.where(ids_col[0] == ids_row[0], 0.0, -1e9)
    for i in range(3):
        wq[i].wait()
        raw = mm(h_v[...], w_v[:, d * i : d * i + d])
        if i == 2:
            v_v[...] = raw.astype(BF)
            pending.append(cout.start(v_v, vs.at[st]))
        else:
            centered = raw - head_mean(raw, spread[...], True)
            rstd = lax.rsqrt(head_mean(centered * centered, spread[...], True) + EPS)
            normal = centered * rstd
            scaled = (normal * gains[i]).astype(BF)
            n_v[:, d * i : d * i + d] = normal.astype(BF)
            r_v[:, d * i : d * i + d] = rstd.astype(BF)
            if i == 0:
                q_v[...] = scaled * jnp.asarray(0.125, BF)
                pending.append(cout.start(q_v, qs.at[st]))
            else:
                k_v[...] = scaled
                pending.append(cout.start(k_v, ks.at[st]))
    pending += [cout.start(n_v, ns.at[st]), cout.start(r_v, nrs.at[st])]
    ones = jnp.ones((16, rows), BF)
    pairs = d // LANES // chunks
    for c in range(chunks):
        for copy in wff[c]:
            copy.wait()
        pre = mm(h_v[...], u_v[c]) + ubias[:, fc * c : fc * c + fc]
        cdf = 0.5 * (1.0 + lax.erf(pre * (1.0 / math.sqrt(2.0))))
        density = jnp.exp(-0.5 * pre * pre) * (1.0 / math.sqrt(2.0 * math.pi))
        act = (pre * cdf).astype(BF)
        act_v[c] = act
        gp_v[c] = (cdf + pre * density).astype(BF)
        total = mm(act, d_v[groups * c : groups * c + groups].reshape(fc, d))
        if c == 0:
            acc_v[...] = total
        else:
            acc_v[...] += total
        for p in range(pairs * c, pairs * c + pairs):
            cols = slice(LANES * p, LANES * p + LANES)
            vals_t = v_v[:, cols].T
            pair = q_v[:, cols]
            both = []
            for half in range(2):
                h = 2 * p + half
                e = jnp.exp(mm(k_v[:, cols], lane_half(pair, half), NT) + bias_mask).astype(BF)
                e_v[h] = e
                got = mm(jnp.concatenate([vals_t[64 * half : 64 * half + 64], ones], axis=0), e)
                inv = 1.0 / got[64:65]
                rs_v[h : h + 1, :] = inv
                both.append((got[:64] * inv).astype(BF))
            both = jnp.concatenate(both, axis=0)
            at_v[cols, :] = both
            att_v[:, cols] = both.T
        pending += [cout.start(act_v.at[c], acts.at[st, c]), cout.start(gp_v.at[c], gps.at[st, c]),
                    cout.start(e_v.at[pl.ds(2 * pairs * c, 2 * pairs)], es.at[st, pl.ds(2 * pairs * c, 2 * pairs)])]
    pending += [cout.start(rs_v, small.at[st]), cout.start(at_v, at_out.at[st])]
    wa.wait()
    y = keep * (keep * x_v[...].astype(F32) + acc_v[...] + mm(att_v[...], a_v[...]) + obias[...])
    y_v[...] = y
    ybf[...] = y.astype(BF)
    result_out(y_v, y_out, st, cout)
    for copy in pending:
        copy.wait()


def backward_kernel(d, ff, chunks, idx, seed, recv, g, g3, ids_col, ngain, gains, spread, *refs):
    xs, qs, ks, vs, ns, nrs, gps, es, small, ats = refs[:10]
    refs = refs[10:]
    refs = refs[5 + 5 :]
    gbf, refs = refs[0], refs[1:]
    gbs, gjs, gqs, gks, gvs, refs = refs[0], refs[1], refs[2], refs[3], refs[4], refs[5:]
    grs, obs, ngs, qkgs, ubs, refs = refs[0], refs[1], refs[2], refs[3], refs[4], refs[5:]
    (g_v, gb_v, w_v, u_v, d_v, a_v, x_v, q_v, k_v, v_v, n_v, r_v, gp_v, e_v, rs_v, at_v, gat_v, gqt_v, gk_v,
     gq_b, gk_b, gv_b, gj_v, acc_v, out_v, ob_v, ng_v, qk_v, ub_v, ins, outs) = refs
    rows = x_v.shape[0]
    fc = ff // chunks
    groups = fc // WIDE
    which, st = idx[0], idx[1]
    cin, cout = Copies(ins), Copies(outs)

    @pl.when(idx[2] == 1)
    def _():
        pltpu.make_async_copy(seed.at[which], g_v, ins.at[0]).start()

    @pl.when(idx[2] != 1)
    def _():
        pltpu.make_async_copy(recv, g_v, ins.at[0]).start()

    cin.used = 1
    wa = cin.start(g.at[:, pl.ds(ff + 3 * d, d)], a_v)
    heads = [cin.start(s.at[which], v) for s, v in ((small, rs_v), (ats, at_v), (ks, k_v), (vs, v_v), (qs, q_v))]
    pairs = d // LANES // chunks
    wff = []
    for c in range(chunks):
        wff.append(
            [cin.start(g3.at[pl.ds(groups * c, groups), :, pl.ds(ff + 4 * d + d * j, d)], d_v.at[pl.ds(groups * c, groups), j])
             for j in range(4)]
            + [cin.start(gps.at[which, c], gp_v.at[c]), cin.start(g.at[:, pl.ds(fc * c, fc)], u_v.at[c]),
               cin.start(es.at[which, pl.ds(2 * pairs * c, 2 * pairs)], e_v.at[pl.ds(2 * pairs * c, 2 * pairs)])]
        )
    norms = [cin.start(ns.at[which], n_v), cin.start(nrs.at[which], r_v)]
    wq = [cin.start(g.at[:, pl.ds(ff + d * i, d)], w_v.at[:, pl.ds(d * i, d)]) for i in range(3)]
    rows_in = cin.start(xs.at[which], x_v)

    pending = []
    pltpu.make_async_copy(recv, g_v, ins.at[0]).wait()
    keep = jnp.where(ids_col[0] < ABSENT, 1.0, 0.0)
    gres = keep * g_v[...].astype(F32)
    ob_v[...] = jnp.sum(gres, axis=0, keepdims=True)
    gb_v[...] = gres.astype(BF)
    pending += [cout.start(gb_v, gbs.at[st]), cout.start(ob_v, obs.at[st])]
    wa.wait()
    gat_v[...] = mm(a_v[...], gb_v[...], NT).astype(BF)
    for copy in heads:
        copy.wait()
    zeros = jnp.zeros((LANES // 2, rows), BF)
    for c in range(chunks):
        for copy in wff[c]:
            copy.wait()
        gup = mm(gb_v[...], d_v[groups * c : groups * c + groups].reshape(fc, d), NT) * gp_v[c].astype(F32)
        ub_v[:, fc * c : fc * c + fc] = jnp.sum(gup, axis=0, keepdims=True)
        gup = gup.astype(BF)
        gj_v[c] = gup
        pending.append(cout.start(gj_v.at[c], gjs.at[st, c]))
        total = mm(gup, u_v[c], NT)
        if c == 0:
            acc_v[...] = total
        else:
            acc_v[...] += total
        for p in range(pairs * c, pairs * c + pairs):
            cols = slice(LANES * p, LANES * p + LANES)
            keys, vals, pair = k_v[:, cols], v_v[:, cols], q_v[:, cols]
            keys_t = keys.T
            gk, gv = None, None
            for half in range(2):
                h = 2 * p + half
                at_rows = slice(64 * h, 64 * h + 64)
                inv = rs_v[h : h + 1, :]
                ga = (gat_v[at_rows, :].astype(F32) * inv).astype(BF)
                ga = jnp.concatenate([zeros, ga] if half else [ga, zeros], axis=0)
                e = e_v[h]
                ef = e.astype(F32)
                gp = ef * mm(vals, ga)
                dot = jnp.sum(gp, axis=0, keepdims=True) * inv
                gs = (gp - ef * dot).astype(BF)
                gk_h = mm(gs, lane_half(pair, half))
                gv_h = mm(e, ga, NT)
                gk = gk_h if gk is None else gk + gk_h
                gv = gv_h if gv is None else gv + gv_h
                gqt_v[at_rows, :] = mm(keys_t[64 * half : 64 * half + 64], gs) * 0.125
            gk_v[:, cols] = gk
            gv_b[:, cols] = gv.astype(BF)
    pending += [cout.start(ub_v, ubs.at[st]), cout.start(gv_b, gvs.at[st])]
    for copy in norms:
        copy.wait()
    for i, (grad, out, stack) in enumerate(((gqt_v[...].T, gq_b, gqs), (gk_v[...], gk_b, gks))):
        normal = n_v[:, d * i : d * i + d].astype(F32)
        qk_v[:, d * i : d * i + d] = jnp.sum(grad * normal, axis=0, keepdims=True)
        out[...] = norm_back(grad * gains[i], normal, r_v[:, d * i : d * i + d].astype(F32), spread[...]).astype(BF)
        pending.append(cout.start(out, stack.at[st]))
    pending.append(cout.start(qk_v, qkgs.at[st]))
    for copy in wq:
        copy.wait()
    ghid = acc_v[...]
    for i, part in enumerate((gq_b, gk_b, gv_b)):
        ghid = ghid + mm(part[...], w_v[:, d * i : d * i + d], NT)
    rows_in.wait()
    xhat, rstd = row_norm(keep * x_v[...].astype(F32))
    ng_v[...] = jnp.sum(ghid * xhat, axis=0, keepdims=True)
    gx = ghid * ngain[...]
    gmask = rstd * (gx - jnp.mean(gx, axis=-1, keepdims=True) - xhat * jnp.mean(gx * xhat, axis=-1, keepdims=True))
    out = keep * (keep * g_v[...].astype(F32) + gmask)
    out_v[...] = out
    gbf[...] = out.astype(BF)
    pending.append(cout.start(ng_v, ngs.at[st]))
    result_out(out_v, grs, st, cout)
    for copy in pending:
        copy.wait()


def split_small(values):
    top = values.astype(BF).astype(F32)
    lane = lax.broadcasted_iota(jnp.int32, values.shape, 1)
    return jnp.where(lane < 8, top, jnp.where(lane < 16, pltpu.roll(values - top, 8, 1), 0.0)).astype(BF)


def joined_small(parts):
    return parts + pltpu.roll(parts, LANES - 8, 1)


def small_table(d, ff, place, obs, ngs, qkgs, ubs):
    def over_slots(ref):
        total = ref[0]
        for s in range(1, ref.shape[0] - 1):
            total = total + ref[s]
        return total

    quarter = WIDE // 4
    ub = over_slots(ubs)
    up_rows = []
    for j in range(4):
        pieces = [ub[:, WIDE * b + quarter * j : WIDE * b + quarter * (j + 1)] for b in range(ff // WIDE)]
        up_rows.append(jnp.concatenate(pieces, axis=1))
    qk = over_slots(qkgs)
    head_rows = []
    for i in range(2):
        lanes = qk[:, d * i : d * i + LANES]
        for p in range(1, d // LANES):
            lanes = lanes + qk[:, d * i + LANES * p : d * i + LANES * (p + 1)]
        head_rows.append(lanes)
    both = jnp.concatenate(head_rows + [jnp.zeros((6, LANES), F32)], axis=0)
    placed = lax.dot_general(both, place[...], NN, precision=lax.Precision.HIGHEST, preferred_element_type=F32)
    rows = [over_slots(ngs), over_slots(obs)] + up_rows + [placed[0:1], placed[1:2], jnp.zeros((LANES - 8, d), F32)]
    return jnp.concatenate(rows, axis=0).T


def weight_grad_kernel(d, ff, chunks, part, mine, idx, place, hs, acts, ats, gbs, gjs, gqk, gvs, obs, ngs, qkgs, ubs, *refs):
    if mine:
        got, refs = refs[0], refs[1:]
    outs_hbm, (h_v, big_v, side_v, at_v, out_v, got_v, ins, outs) = refs[:-8], refs[-8:]
    slots, rows = h_v.shape[0], h_v.shape[1]
    fc = ff // chunks
    blocks, quarter, half = fc // WIDE, WIDE // 4, ff // 2
    y, z = idx[1], idx[2]
    live = pl.ds(0, slots)
    tokens = slots * rows
    arrive = pltpu.make_async_copy(got, got_v, ins.at[15]) if mine else None
    if mine:
        arrive.start()

    def put(rows_at, cols_at, value):
        if mine:
            value = value + got_v[rows_at, cols_at].astype(F32)
        out_v[rows_at, cols_at] = value.astype(BF)

    def send():
        cout = Copies(outs)
        if not mine:
            return [cout.start(out_v, outs_hbm[0])]
        share = d // 16
        if part == 0:
            return [cout.start(out_v.at[pl.ds(pl.multiple_of(lax.rem(y + s, 4) * 4 * share, 16), 4 * share)], outs_hbm[s])
                    for s in (1, 2, 3, 0)]
        return [
            cout.start(out_v.at[pl.ds(pl.multiple_of((4 * i + lax.rem(z + s, 4)) * share, 16), share)], outs_hbm[s].at[i])
            for s in (1, 2, 3, 0) for i in range(4)
        ]

    @pl.when(idx[0] == 0)
    def _():
        cin = Copies(ins)
        grads = cin.start(gbs.at[live], h_v)
        loads = [
            [cin.start(acts.at[live, c, :, pl.ds(WIDE * b + LANES * part, LANES)],
                       big_v.at[:, :, pl.ds(LANES * (blocks * c + b), LANES)]) for b in range(blocks)]
            for c in range(chunks)
        ]
        last = [cin.start(ats.at[live], at_v)] if part == 0 else [
            cin.start(hs.at[live], side_v.at[0]), cin.start(gvs.at[live], side_v.at[1])]
        grads.wait()
        gb = h_v[...].reshape(tokens, d)
        if mine:
            arrive.wait()
        for c in range(chunks):
            for copy in loads[c]:
                copy.wait()
            left = big_v[:, :, LANES * blocks * c : LANES * blocks * (c + 1)].reshape(tokens, LANES * blocks)
            got_c = lax.dot_general(left, gb, TN, preferred_element_type=F32)
            for b in range(blocks):
                for j in range(2):
                    at = quarter * (blocks * c + b)
                    put(slice(at, at + quarter), slice(d * j, d * j + d),
                        got_c[LANES * b + quarter * j : LANES * b + quarter * (j + 1)])
        for copy in last:
            copy.wait()
        everything = slice(0, d)
        if part == 0:
            total = mm(at_v[0], h_v[0])
            for s in range(1, slots):
                total = total + mm(at_v[s], h_v[s])
            put(everything, slice(2 * d, 3 * d), total)
        else:
            put(everything, slice(2 * d, 3 * d), lax.dot_general(
                side_v[0].reshape(tokens, d), side_v[1].reshape(tokens, d), TN, preferred_element_type=F32))
            table = small_table(d, ff, place, obs, ngs, qkgs, ubs)
            if mine:
                table = table + joined_small(got_v[:, 3 * d :].astype(F32))
            out_v[:, 3 * d :] = split_small(table)
        for copy in send():
            copy.wait()

    @pl.when(idx[0] == 1)
    def _():
        cin = Copies(ins)
        hidden = cin.start(hs.at[live], h_v)
        if part == 0:
            loads = [cin.start(gjs.at[live, 0], big_v.at[:, :, pl.ds(0, fc)]),
                     cin.start(gjs.at[live, 1, :, pl.ds(0, fc // 2)], big_v.at[:, :, pl.ds(fc, fc // 2)])]
        else:
            loads = [cin.start(gjs.at[live, 1, :, pl.ds(fc // 2, fc // 2)], big_v.at[:, :, pl.ds(0, fc // 2)]),
                     cin.start(gjs.at[live, 2], big_v.at[:, :, pl.ds(fc // 2, fc)])]
        loads.append(cin.start(gqk.at[live], side_v.at[0]))
        hidden.wait()
        turned = h_v[...].reshape(tokens, d).T
        if mine:
            arrive.wait()
        for copy in loads:
            copy.wait()
        everything = slice(0, d)
        for at in range(0, half, fc // 2):
            put(everything, slice(at, at + fc // 2), mm(turned, big_v[:, :, at : at + fc // 2].reshape(tokens, fc // 2)))
        put(everything, slice(half, half + d), mm(turned, side_v[0].reshape(tokens, d)))
        if part == 1:
            out_v[:, 3 * d :] = jnp.zeros((d, LANES), BF)
        for copy in send():
            copy.wait()


def added(parts):
    total = parts[0][...].astype(F32)
    for part in parts[1:]:
        total = total + part[...].astype(F32)
    shape = total.shape
    total = total.reshape(-1, shape[-1])
    main, last = total[:, : shape[-1] - LANES], split_small(joined_small(total[:, shape[-1] - LANES :]))
    return jnp.concatenate([main.astype(BF), last], axis=1).reshape(shape)


def mid_kernel(part, idx, *refs):
    came, outs, hold = refs[:4], refs[4:8], refs[8]
    if part == 0:
        total = came[0][...].astype(F32)
        for piece in came[1:]:
            total = total + piece[...].astype(F32)
        hold[...] = total.astype(BF).reshape(hold.shape)
    else:
        hold[...] = added(came)
    at = idx[2] if part == 0 else idx[1]
    for s in range(4):
        outs[s][...] = hold[lax.rem(at + s, 4)]


def last_kernel(idx, *refs):
    firsts, seconds, mine, theirs, hold = refs[:4], refs[4:8], refs[8], refs[9], refs[10]
    cut = firsts[0].shape[-1]
    for group, at in ((firsts, 0), (seconds, cut)):
        total = group[0][...].astype(F32)
        for part in group[1:]:
            total = total + part[...].astype(F32)
        hold[:, at : at + total.shape[1]] = total
    count = mine.shape[0]
    core = idx[3]
    mine[...] = hold[pl.ds(pl.multiple_of(core * count, 8), count), :]
    theirs[...] = hold[pl.ds(pl.multiple_of((1 - core) * count, 8), count), :]


ANY = pl.BlockSpec(memory_space=pl.ANY)


def whole(shape):
    return pl.BlockSpec(shape, lambda i, idx: (0,) * len(shape))


def pick(shape):
    return pl.BlockSpec((1,) + shape, lambda i, idx: (idx[0],) + (0,) * len(shape))


def call(kernel, idx, ins, fresh, stashes, scratch, flops):
    outs = pl.pallas_call(
        kernel,
        grid_spec=pltpu.PrefetchScalarGridSpec(
            num_scalar_prefetch=1,
            grid=(1,),
            in_specs=[s for _, s in ins] + [ANY] * len(stashes),
            out_specs=[whole(fresh[0])] + [ANY] * len(stashes),
            scratch_shapes=scratch,
        ),
        out_shape=[jax.ShapeDtypeStruct(*fresh)] + [jax.ShapeDtypeStruct(a.shape, a.dtype) for a in stashes],
        input_output_aliases={1 + len(ins) + i: 1 + i for i in range(len(stashes))},
        compiler_params=pltpu.CompilerParams(dimension_semantics=("arbitrary",), vmem_limit_bytes=VMEM_LIMIT),
        cost_estimate=pl.CostEstimate(flops=flops, bytes_accessed=30 << 20, transcendentals=0),
    )(idx, *[a for a, _ in ins], *stashes)
    return outs[0], outs[1:]


def simple(kernel, idx, arrays, specs, out_shapes, out_specs, scratch, flops=1 << 24):
    return pl.pallas_call(
        kernel,
        grid_spec=pltpu.PrefetchScalarGridSpec(
            num_scalar_prefetch=1, grid=(1,), in_specs=specs, out_specs=out_specs, scratch_shapes=scratch
        ),
        out_shape=out_shapes,
        compiler_params=pltpu.CompilerParams(dimension_semantics=("arbitrary",), vmem_limit_bytes=VMEM_LIMIT),
        cost_estimate=pl.CostEstimate(flops=flops, bytes_accessed=16 << 20, transcendentals=0),
    )(idx, *arrays)


def along(x, step, size, by):
    devices = lax.axis_size("dp")

    def to(i):
        digit = i // step % size
        return i + ((digit + by) % size - digit) * step

    return lax.ppermute(x, "dp", [(i, to(i)) for i in range(devices)])


def shifted(x, by):
    devices = lax.axis_size("section")
    return lax.ppermute(x, "section", [(i, i + by) for i in range(devices) if 0 <= i + by < devices])


def body(tokens, cotangent, lengths, proj_in, proj_attn, proj_down, norm_gain, query_gain, key_gain, up_bias, out_bias):
    sections = lax.axis_size("section")
    ranks = lax.axis_size("dp")
    section = lax.axis_index("section")
    rank = lax.axis_index("dp")
    slots = lengths.shape[0]
    rows = tokens.shape[0] // slots
    d = tokens.shape[1]
    joined = proj_in.shape[2]
    ff = proj_down.shape[1] * ranks
    head = query_gain.shape[1] * ranks
    heads = d // head
    dshare = proj_in.shape[1]
    fshare = proj_down.shape[1] // dshare
    hshare = query_gain.shape[1]
    chunks = 3
    ticks = slots + sections - 1
    wide = joined + d + ff

    place = jnp.arange(WIDE, dtype=jnp.int32)
    source = (place % (WIDE // fshare)) * fshare + place // (WIDE // fshare)
    shuffle = (place[:, None] == source[None, :]).astype(BF)

    def shuffled(x, back=False):
        flat = x.reshape(-1, WIDE)
        out = lax.dot_general(flat, shuffle.astype(x.dtype), NT if back else NN, precision=lax.Precision.HIGHEST, preferred_element_type=F32)
        return out.reshape(x.shape)

    small = jnp.concatenate(
        [
            norm_gain[0][:, None],
            out_bias[0][:, None],
            up_bias[0].reshape(dshare, fshare),
            jnp.pad(query_gain[0], (0, dshare - hshare))[:, None],
            jnp.pad(key_gain[0], (0, dshare - hshare))[:, None],
            jnp.zeros((dshare, LANES - 4 - fshare), BF),
        ],
        axis=1,
    )
    heads_part = joined - ff
    local = jnp.concatenate(
        [shuffled(proj_in[0][:, heads_part:]).astype(BF), proj_in[0][:, :heads_part], proj_attn[0],
         proj_down[0].reshape(dshare, fshare * d), small],
        axis=1,
    )
    g = lax.all_gather(local, "dp", axis=0, tiled=True)
    g3 = g.reshape(ff // WIDE, WIDE // fshare, g.shape[1])
    tail = g[:, wide : wide + LANES].astype(F32)
    ngain = tail[:, 0].reshape(1, d)
    obias = tail[:, 1].reshape(1, d)
    ubias = shuffled(tail[:, 2 : 2 + fshare].reshape(1, ff).astype(BF))
    qk_gain = tail[:, 2 + fshare : 4 + fshare].reshape(ranks, dshare, 2)[:, :hshare].reshape(head, 2).T
    gains = jnp.tile(qk_gain, (1, heads)).reshape(2, 1, d)
    column = jnp.arange(WIDE, dtype=jnp.int32) // head
    spread = jnp.where(column[:, None] == column[None, :], 1.0 / head, 0.0).astype(BF)

    toks = tokens.reshape(slots, rows, d)
    seeds = cotangent.reshape(slots, rows, d)
    ends = jnp.cumsum(lengths, axis=-1)
    position = jnp.arange(rows, dtype=jnp.int32)
    image = jnp.sum((position[None, :, None] >= ends[:, None, :]).astype(jnp.int32), axis=-1)
    image = jnp.where(position[None, :] < ends[:, 2:3], image, ABSENT + position[None, :])
    ids_col, ids_row = image[:, :, None], image[:, None, :]

    def stash(*shape, dtype=BF, spare=1):
        return pl.pallas_call(
            lambda out: None,
            out_shape=jax.ShapeDtypeStruct((slots + spare,) + shape, dtype),
            out_specs=pl.BlockSpec(memory_space=pl.ANY),
        )()

    fc = ff // chunks
    groups = ff // WIDE
    kept = [stash(rows, d), stash(rows, d), stash(rows, d), stash(rows, d), stash(rows, d), stash(rows, 2 * d), stash(rows, 2 * d),
            stash(chunks, rows, fc), stash(chunks, rows, fc), stash(heads, rows, rows), stash(16, rows, dtype=F32),
            stash(d, rows), stash(rows, d, dtype=F32, spare=0)]

    def index_of(tick, distance, first):
        which = tick - distance
        active = (which >= 0) & (which < slots)
        return jnp.stack(
            [jnp.clip(which, 0, slots - 1), jnp.where(active, which, slots), first.astype(jnp.int32)]
        ).astype(jnp.int32)

    V = pltpu.VMEM
    weights_v = [V((d, heads_part), BF), V((chunks, d, fc), BF), V((groups, fshare, WIDE // fshare, d), BF), V((d, d), BF)]
    sems = [pltpu.SemaphoreType.DMA((48,)), pltpu.SemaphoreType.DMA((48,))]
    smalls = [(ngain, whole((1, d))), (gains, whole((2, 1, d)))]
    nothing = jnp.zeros((rows, d), BF)
    recv = nothing
    for t in range(ticks):
        ybf, kept = call(
            partial(forward_kernel, d, ff, chunks),
            index_of(t, section, section == 0),
            [(toks, ANY), (recv, ANY), (g, ANY), (g3, ANY), (ids_col, pick((rows, 1))), (ids_row, pick((1, rows)))] + smalls
            + [(ubias, whole((1, ff))), (obias, whole((1, d))), (spread, whole((WIDE, WIDE)))],
            ((rows, d), BF),
            kept,
            [V((rows, d), BF), V((rows, d), BF)] + weights_v
            + [V((rows, d), BF)] * 3 + [V((rows, 2 * d), BF)] * 2 + [V((chunks, rows, fc), BF)] * 2
            + [V((heads, rows, rows), BF), V((16, rows), F32), V((d, rows), BF), V((rows, d), BF), V((rows, d), F32), V((rows, d), F32)]
            + sems,
            2 * rows * (d * wide + 2 * rows * d),
        )
        if t < ticks - 1:
            recv = shifted(ybf, 1)

    xs, hs, qs, ks, vs, ns, nrs, acts, gps, es, rsums, ats, ys = kept
    back = [stash(rows, d), stash(chunks, rows, fc), stash(rows, d), stash(rows, d), stash(rows, d),
            stash(rows, d, dtype=F32, spare=0), stash(1, d, dtype=F32), stash(1, d, dtype=F32), stash(1, 2 * d, dtype=F32), stash(1, ff, dtype=F32)]
    recv = nothing
    for t in range(ticks):
        gbf, back = call(
            partial(backward_kernel, d, ff, chunks),
            index_of(t, sections - 1 - section, section == sections - 1),
            [(seeds, ANY), (recv, ANY), (g, ANY), (g3, ANY), (ids_col, pick((rows, 1)))] + smalls + [(spread, whole((WIDE, WIDE)))]
            + [(a, ANY) for a in (xs, qs, ks, vs, ns, nrs, gps, es, rsums, ats)],
            ((rows, d), BF),
            back,
            [V((rows, d), BF), V((rows, d), BF)] + weights_v
            + [V((rows, d), BF)] * 4 + [V((rows, 2 * d), BF)] * 2
            + [V((chunks, rows, fc), BF), V((heads, rows, rows), BF), V((16, rows), F32), V((d, rows), BF)]
            + [V((d, rows), BF), V((d, rows), F32), V((rows, d), F32)]
            + [V((rows, d), BF)] * 3 + [V((chunks, rows, fc), BF), V((rows, d), F32), V((rows, d), F32)]
            + [V((1, d), F32), V((1, d), F32), V((1, 2 * d), F32), V((1, ff), F32)]
            + sems,
            2 * rows * (d * wide + 4 * rows * d),
        )
        if t < ticks - 1:
            recv = shifted(gbf, -1)

    gbs, gjs, gqs, gks, gvs, grs, obs, ngs, qkgs, ubs = back

    side = math.isqrt(ranks // 2)
    core, z, y = lax.rem(rank, 2), lax.rem(rank // 2, side), rank // (2 * side)
    width = 6 * d + LANES
    widths = (3 * d, 3 * d + LANES)
    share = 2 * dshare
    position = jnp.arange(LANES, dtype=jnp.int32)[:, None] % head
    place = (position // hshare * dshare + position % hshare == jnp.arange(d, dtype=jnp.int32)[None, :]).astype(F32)
    here = jnp.stack([core, y, z, core]).astype(jnp.int32)
    there = jnp.stack([1 - core, y, z, core]).astype(jnp.int32)

    def weight_grads(idx, part, got=None):
        w = widths[part]
        mine = got is not None
        if not mine:
            shapes = [jax.ShapeDtypeStruct((d, w), BF)]
        else:
            shapes = [jax.ShapeDtypeStruct((side * share, w) if part == 0 else (side, share, w), BF)] * side
        smalls = [obs, ngs, qkgs, ubs]
        return simple(
            partial(weight_grad_kernel, d, ff, chunks, part, mine), idx,
            [place, hs, acts, ats, gbs, gjs, (gqs, gks)[part], gvs] + smalls + ([got] if mine else []),
            [whole((LANES, d))] + [ANY] * 7 + [whole(a.shape) for a in smalls] + ([ANY] if mine else []),
            shapes, [ANY] * len(shapes),
            [V((slots, rows, d), BF), V((slots, rows, ff // 2), BF), V((2, slots, rows, d), BF), V((slots, d, rows), BF),
             V((d, w), BF), V((d, w), BF),
             pltpu.SemaphoreType.DMA((16,)), pltpu.SemaphoreType.DMA((16,))],
            2 * d * slots * rows * 3 * d,
        )

    steps = ((2 * side, 2), (2, 2 * side))
    got = [along(weight_grads(there, part)[0], 1, 2, 1) for part in range(2)]
    arrived = []
    for part in range(2):
        outs = weight_grads(here, part, got[part])
        first, second = steps[part]
        came = [outs[0]] + [along(outs[s], first, side, s) for s in (1, 2, 3)]
        outs = simple(
            partial(mid_kernel, part), here, came, [whole(a.shape) for a in came],
            [jax.ShapeDtypeStruct((share, widths[part]), BF)] * side, [whole((share, widths[part]))] * side,
            [V((side, share, widths[part]), BF)],
        )
        arrived += [outs[0]] + [along(outs[s], second, side, s) for s in (1, 2, 3)]
    mine, other = simple(
        last_kernel, here, arrived, [whole(a.shape) for a in arrived],
        [jax.ShapeDtypeStruct((dshare, width), F32)] * 2, [whole((dshare, width))] * 2,
        [V((share, width), F32)],
    )
    other = along(other, 1, 2, 1)
    half0, half1 = jnp.where(core == 0, mine, other), jnp.where(core == 0, other, mine)
    ups = shuffled(jnp.concatenate([half1[:, : 2 * d], half1[:, 3 * d : 5 * d]], axis=1), back=True)
    g_in = jnp.concatenate([half1[:, 2 * d : 3 * d], half1[:, 5 * d : 6 * d], half0[:, 5 * d : 6 * d], ups], axis=1)
    g_down = jnp.concatenate([half0[:, : 2 * d], half0[:, 3 * d : 5 * d]], axis=1)
    last = half0[:, 6 * d : 6 * d + 8] + half0[:, 6 * d + 8 : 6 * d + 16]
    return (
        ys.reshape(1, slots * rows, d),
        grs.reshape(1, slots * rows, d),
        g_in[None],
        half0[None, :, 2 * d : 3 * d],
        g_down.reshape(1, dshare * fshare, d),
        last[None, :, 0],
        last[None, :hshare, 6],
        last[None, :hshare, 7],
        last[:, 2:6].reshape(1, dshare * fshare),
        last[None, :, 1],
    )


def solution(mesh):
    in_specs = (P("dp", None),) * 3 + (P("section", "dp", None),) * 3 + (P("section", "dp"),) * 5
    out_specs = (P("section", "dp", None),) * 5 + (P("section", "dp"),) * 5
    return jax.shard_map(body, mesh=mesh, in_specs=in_specs, out_specs=out_specs, check_vma=False)
```

```python
from functools import partial
import math

import jax
import jax.numpy as jnp
from jax import lax
from jax.experimental import pallas as pl
from jax.experimental.pallas import tpu as pltpu
from jax.sharding import PartitionSpec as P

BF = jnp.bfloat16
F32 = jnp.float32
VMEM_LIMIT = 60 * 1024 * 1024
EPS = 1e-06
NN = (((1,), (0,)), ((), ()))
NT = (((1,), (1,)), ((), ()))
TN = (((0,), (0,)), ((), ()))
LANES = 128
WIDE = 256
ABSENT = 16


def mm(a, b, dims=NN):
    return lax.dot_general(a, b, dims, preferred_element_type=F32)


def head_mean(x, spread, exact):
    parts = []
    for at in range(0, x.shape[1], WIDE):
        piece = x[:, at : at + WIDE]
        top = piece.astype(BF)
        total = mm(top, spread)
        if exact:
            total = total + mm((piece - top.astype(F32)).astype(BF), spread)
        parts.append(total)
    return jnp.concatenate(parts, axis=1)


def row_norm(x):
    centered = x - jnp.mean(x, axis=-1, keepdims=True)
    rstd = lax.rsqrt(jnp.mean(centered * centered, axis=-1, keepdims=True) + EPS)
    return centered * rstd, rstd


def norm_back(grad, normal, rstd, spread):
    return rstd * (grad - head_mean(grad, spread, False) - normal * head_mean(grad * normal, spread, False))


def lane_half(x, second):
    lane = lax.broadcasted_iota(jnp.int32, x.shape, 1)
    return jnp.where((lane >= LANES // 2) if second else (lane < LANES // 2), x, jnp.zeros_like(x))


class Copies:
    def __init__(self, sems):
        self.sems, self.used = sems, 0

    def start(self, src, dst):
        copy = pltpu.make_async_copy(src, dst, self.sems.at[self.used])
        self.used += 1
        copy.start()
        return copy

    def either(self, flag, src, yes, no):
        sem = self.sems.at[self.used]
        self.used += 1

        @pl.when(flag == 1)
        def _():
            pltpu.make_async_copy(src, yes, sem).start()

        @pl.when(flag != 1)
        def _():
            pltpu.make_async_copy(src, no, sem).start()

        return pltpu.make_async_copy(src, yes, sem)


def forward_kernel(d, ff, chunks, base, first, idx, x_in, g, g3, ids_col, ids_row, ngain, gains, ubias, obias, spread, *refs):
    @pl.when(idx[0] == 1)
    def _():
        forward_work(d, ff, chunks, base, first, idx, x_in, g, g3, ids_col, ids_row, ngain, gains, ubias, obias, spread, *refs)


def forward_work(d, ff, chunks, base, first, idx, x_in, g, g3, ids_col, ids_row, ngain, gains, ubias, obias, spread, *refs):
    refs = refs[13:]
    ybf, xs, qs, ks, vs, ns, nrs, gps, es, small, kept, sent, y_out, y_send = refs[:14]
    (x_v, h_v, w_v, u_v, d_v, a_v, q_v, k_v, v_v, n_v, r_v, act_v, gp_v, e_v, rs_v, att_v, acc_v, y_v, ins, outs) = refs[14:]
    rows = x_v.shape[0]
    fc = ff // chunks
    core, slot, home = idx[1], idx[2], idx[3]
    cin, cout = Copies(ins), Copies(outs)
    x_copy = cin.start(x_in.at[slot] if first else x_in, x_v)
    wq = [cin.start(g.at[:, pl.ds(base + ff + d * i, d)], w_v.at[:, pl.ds(d * i, d)]) for i in range(3)]
    groups = fc // WIDE
    wff = []
    for c in range(chunks):
        wff.append([cin.start(g.at[:, pl.ds(base + fc * c, fc)], u_v.at[c])] + [
            cin.start(g3.at[pl.ds(groups * c, groups), :, pl.ds(base + ff + 4 * d + d * j, d)], d_v.at[pl.ds(groups * c, groups), j])
            for j in range(4)
        ])
    wa = cin.start(g.at[:, pl.ds(base + ff + 3 * d, d)], a_v)

    pending = []

    def side(i):
        return pl.ds(ff + d * i, d)

    x_copy.wait()
    keep = jnp.where(ids_col[0] < ABSENT, 1.0, 0.0)
    masked = keep * x_v[...].astype(F32)
    h_v[...] = (row_norm(masked)[0] * ngain[...]).astype(BF)
    pending += [cout.start(x_v, xs), cout.start(h_v, kept.at[:, side(2)]), cout.start(h_v, sent.at[:, side(2)])]
    bias_mask = jnp.where(ids_col[0] == ids_row[0], 0.0, -1e9)
    for i in range(3):
        wq[i].wait()
        raw = mm(h_v[...], w_v[:, d * i : d * i + d])
        if i == 2:
            v_v[...] = raw.astype(BF)
            pending.append(cout.start(v_v, vs))
        else:
            centered = raw - head_mean(raw, spread[...], True)
            rstd = lax.rsqrt(head_mean(centered * centered, spread[...], True) + EPS)
            normal = centered * rstd
            scaled = (normal * gains[i]).astype(BF)
            n_v[:, d * i : d * i + d] = normal.astype(BF)
            r_v[:, d * i : d * i + d] = rstd.astype(BF)
            if i == 0:
                q_v[...] = scaled * jnp.asarray(0.125, BF)
                pending.append(cout.start(q_v, qs))
            else:
                k_v[...] = scaled
                pending.append(cout.start(k_v, ks))
    pending += [cout.start(n_v, ns), cout.start(r_v, nrs)]
    ones = jnp.ones((16, rows), BF)
    pairs = d // LANES // chunks
    for c in range(chunks):
        for copy in wff[c]:
            copy.wait()
        pre = mm(h_v[...], u_v[c]) + ubias[:, fc * c : fc * c + fc]
        cdf = 0.5 * (1.0 + lax.erf(pre * (1.0 / math.sqrt(2.0))))
        density = jnp.exp(-0.5 * pre * pre) * (1.0 / math.sqrt(2.0 * math.pi))
        act = (pre * cdf).astype(BF)
        act_v[c] = act
        gp_v[c] = (cdf + pre * density).astype(BF)
        total = mm(act, d_v[groups * c : groups * c + groups].reshape(fc, d))
        if c == 0:
            acc_v[...] = total
        else:
            acc_v[...] += total
        for p in range(pairs * c, pairs * c + pairs):
            cols = slice(LANES * p, LANES * p + LANES)
            vals_t = v_v[:, cols].T
            pair = q_v[:, cols]
            both = []
            for half in range(2):
                h = 2 * p + half
                e = jnp.exp(mm(k_v[:, cols], lane_half(pair, half), NT) + bias_mask).astype(BF)
                e_v[h] = e
                got = mm(jnp.concatenate([vals_t[64 * half : 64 * half + 64], ones], axis=0), e)
                inv = 1.0 / got[64:65]
                rs_v[h : h + 1, :] = inv
                both.append((got[:64] * inv).astype(BF))
            att_v[:, cols] = jnp.concatenate(both, axis=0).T
        span = pl.ds(fc * c, fc)
        pending += [cout.either(core, act_v.at[c], sent.at[:, span], kept.at[:, span]), cout.start(gp_v.at[c], gps.at[c]),
                    cout.start(e_v.at[pl.ds(2 * pairs * c, 2 * pairs)], es.at[pl.ds(2 * pairs * c, 2 * pairs)])]
    pending += [cout.start(rs_v, small), cout.either(core, att_v, sent.at[:, side(3)], kept.at[:, side(3)])]
    wa.wait()
    y = keep * (keep * x_v[...].astype(F32) + acc_v[...] + mm(att_v[...], a_v[...]) + obias[...])
    y_v[...] = y
    ybf[...] = y.astype(BF)
    pending.append(cout.either(home, y_v, y_out.at[slot], y_send))
    for copy in pending:
        copy.wait()


def backward_kernel(d, ff, chunks, base, first, idx, g_in, g, g3, ids_col, ngain, gains, spread, *refs):
    @pl.when(idx[0] == 1)
    def _():
        backward_work(d, ff, chunks, base, first, idx, g_in, g, g3, ids_col, ngain, gains, spread, *refs)


def backward_work(d, ff, chunks, base, first, idx, g_in, g, g3, ids_col, ngain, gains, spread, *refs):
    xs, qs, ks, vs, ns, nrs, gps, es, small = refs[:9]
    refs = refs[9 + 5 :]
    gbf, kept, sent, table, gr_out, gr_send = refs[:6]
    (g_v, gb_v, w_v, u_v, d_v, a_v, x_v, q_v, k_v, v_v, n_v, r_v, gp_v, e_v, rs_v, gat_v, gqt_v, gk_v,
     gq_b, gk_b, gv_b, gj_v, acc_v, out_v, sm_v, ins, outs) = refs[6:]
    rows = x_v.shape[0]
    fc = ff // chunks
    groups = fc // WIDE
    core, slot, home = idx[1], idx[2], idx[3]
    cin, cout = Copies(ins), Copies(outs)
    g_copy = cin.start(g_in.at[slot] if first else g_in, g_v)
    wa = cin.start(g.at[:, pl.ds(base + ff + 3 * d, d)], a_v)
    heads = [cin.start(s, v) for s, v in ((small, rs_v), (ks, k_v), (vs, v_v), (qs, q_v))]
    pairs = d // LANES // chunks
    wff = []
    for c in range(chunks):
        wff.append(
            [cin.start(g3.at[pl.ds(groups * c, groups), :, pl.ds(base + ff + 4 * d + d * j, d)], d_v.at[pl.ds(groups * c, groups), j])
             for j in range(4)]
            + [cin.start(gps.at[c], gp_v.at[c]), cin.start(g.at[:, pl.ds(base + fc * c, fc)], u_v.at[c]),
               cin.start(es.at[pl.ds(2 * pairs * c, 2 * pairs)], e_v.at[pl.ds(2 * pairs * c, 2 * pairs)])]
        )
    norms = [cin.start(ns, n_v), cin.start(nrs, r_v)]
    wq = [cin.start(g.at[:, pl.ds(base + ff + d * i, d)], w_v.at[:, pl.ds(d * i, d)]) for i in range(3)]
    rows_in = cin.start(xs, x_v)

    pending = []

    def side(i):
        return pl.ds(ff + d * i, d)

    def summed(at, value):
        sm_v[:, at : at + value.shape[1]] = jnp.sum(value, axis=0, keepdims=True)

    g_copy.wait()
    keep = jnp.where(ids_col[0] < ABSENT, 1.0, 0.0)
    gres = keep * g_v[...].astype(F32)
    summed(d, gres)
    gb_v[...] = gres.astype(BF)
    pending.append(cout.either(core, gb_v, sent.at[:, side(0)], kept.at[:, side(0)]))
    wa.wait()
    gat_v[...] = mm(a_v[...], gb_v[...], NT).astype(BF)
    for copy in heads:
        copy.wait()
    zeros = jnp.zeros((LANES // 2, rows), BF)
    for c in range(chunks):
        for copy in wff[c]:
            copy.wait()
        gup = mm(gb_v[...], d_v[groups * c : groups * c + groups].reshape(fc, d), NT) * gp_v[c].astype(F32)
        summed(4 * d + fc * c, gup)
        gup = gup.astype(BF)
        gj_v[c] = gup
        span = pl.ds(fc * c, fc)
        pending.append(cout.either(core, gj_v.at[c], kept.at[:, span], sent.at[:, span]))
        total = mm(gup, u_v[c], NT)
        if c == 0:
            acc_v[...] = total
        else:
            acc_v[...] += total
        for p in range(pairs * c, pairs * c + pairs):
            cols = slice(LANES * p, LANES * p + LANES)
            keys, vals, pair = k_v[:, cols], v_v[:, cols], q_v[:, cols]
            keys_t = keys.T
            gk, gv = None, None
            for half in range(2):
                h = 2 * p + half
                at_rows = slice(64 * h, 64 * h + 64)
                inv = rs_v[h : h + 1, :]
                ga = (gat_v[at_rows, :].astype(F32) * inv).astype(BF)
                ga = jnp.concatenate([zeros, ga] if half else [ga, zeros], axis=0)
                e = e_v[h]
                ef = e.astype(F32)
                gp = ef * mm(vals, ga)
                dot = jnp.sum(gp, axis=0, keepdims=True) * inv
                gs = (gp - ef * dot).astype(BF)
                gk_h = mm(gs, lane_half(pair, half))
                gv_h = mm(e, ga, NT)
                gk = gk_h if gk is None else gk + gk_h
                gv = gv_h if gv is None else gv + gv_h
                gqt_v[at_rows, :] = mm(keys_t[64 * half : 64 * half + 64], gs) * 0.125
            gk_v[:, cols] = gk
            gv_b[:, cols] = gv.astype(BF)
    pending.append(cout.either(core, gv_b, sent.at[:, side(1)], kept.at[:, side(1)]))
    for copy in norms:
        copy.wait()
    for i, (grad, out) in enumerate(((gqt_v[...].T, gq_b), (gk_v[...], gk_b))):
        normal = n_v[:, d * i : d * i + d].astype(F32)
        summed(2 * d + d * i, grad * normal)
        out[...] = norm_back(grad * gains[i], normal, r_v[:, d * i : d * i + d].astype(F32), spread[...]).astype(BF)
        pending.append(cout.either(core, out, kept.at[:, side(i)], sent.at[:, side(i)]))
    for copy in wq:
        copy.wait()
    ghid = acc_v[...]
    for i, part in enumerate((gq_b, gk_b, gv_b)):
        ghid = ghid + mm(part[...], w_v[:, d * i : d * i + d], NT)
    rows_in.wait()
    xhat, rstd = row_norm(keep * x_v[...].astype(F32))
    summed(0, ghid * xhat)
    pending.append(cout.start(sm_v, table))
    gx = ghid * ngain[...]
    gmask = rstd * (gx - jnp.mean(gx, axis=-1, keepdims=True) - xhat * jnp.mean(gx * xhat, axis=-1, keepdims=True))
    out = keep * (keep * g_v[...].astype(F32) + gmask)
    out_v[...] = out
    gbf[...] = out.astype(BF)
    pending.append(cout.either(home, out_v, gr_out.at[slot], gr_send))
    for copy in pending:
        copy.wait()


def split_small(values):
    top = values.astype(BF).astype(F32)
    lane = lax.broadcasted_iota(jnp.int32, values.shape, 1)
    return jnp.where(lane < 8, top, jnp.where(lane < 16, pltpu.roll(values - top, 8, 1), 0.0)).astype(BF)


def joined_small(parts):
    return parts + pltpu.roll(parts, LANES - 8, 1)


def small_table(d, ff, place, mine, theirs):
    total = mine[...] + theirs[...]
    quarter = WIDE // 4
    ub = total[:, 4 * d :]
    up_rows = []
    for j in range(4):
        pieces = [ub[:, WIDE * b + quarter * j : WIDE * b + quarter * (j + 1)] for b in range(ff // WIDE)]
        up_rows.append(jnp.concatenate(pieces, axis=1))
    head_rows = []
    for i in range(2, 4):
        lanes = total[:, d * i : d * i + LANES]
        for p in range(1, d // LANES):
            lanes = lanes + total[:, d * i + LANES * p : d * i + LANES * (p + 1)]
        head_rows.append(lanes)
    both = jnp.concatenate(head_rows + [jnp.zeros((6, LANES), F32)], axis=0)
    placed = lax.dot_general(both, place[...], NN, precision=lax.Precision.HIGHEST, preferred_element_type=F32)
    rows = [total[:, :d], total[:, d : 2 * d]] + up_rows + [placed[0:1], placed[1:2], jnp.zeros((LANES - 8, d), F32)]
    return jnp.concatenate(rows, axis=0).T


def weight_grad_kernel(d, ff, part, idx, place, mine, theirs, kept, got, *refs):
    outs_hbm, (big_v, a_v, b_v, out_v, ins, outs) = refs[:-6], refs[-6:]
    rows = kept.shape[0]
    tokens = 2 * rows
    quarter, half, blocks = WIDE // 4, ff // 2, ff // WIDE
    y, z, core = idx[0], idx[1], idx[2]

    def load(cin, at, width, to, to_at):
        return [cin.start(src.at[:, pl.ds(at, width)], to.at[i, :, pl.ds(to_at, width)]) for i, src in enumerate((kept, got))]

    def put(rows_at, cols_at, value):
        out_v[rows_at, cols_at] = value.astype(BF)

    def send():
        cout = Copies(outs)
        share = d // 16
        if part == 0:
            return [cout.start(out_v.at[pl.ds(pl.multiple_of(lax.rem(y + s, 4) * 4 * share, 16), 4 * share)], outs_hbm[s])
                    for s in (1, 2, 3, 0)]
        return [
            cout.start(out_v.at[pl.ds(pl.multiple_of((4 * i + lax.rem(z + s, 4)) * share, 16), share)], outs_hbm[s].at[i])
            for s in (1, 2, 3, 0) for i in range(4)
        ]

    everything = slice(0, d)

    @pl.when(core == 0)
    def _():
        cin = Copies(ins)
        grads = load(cin, ff, d, a_v, 0)
        third = blocks // 3
        loads = [[c for b in range(third * k, third * k + third) for c in load(cin, WIDE * b + LANES * part, LANES, big_v, LANES * b)]
                 for k in range(3)]
        if part == 0:
            last = load(cin, ff + 3 * d, d, b_v, 0)
        else:
            last = load(cin, ff + 2 * d, d, b_v, 0) + load(cin, ff + d, d, big_v, LANES * blocks)
        for copy in grads:
            copy.wait()
        gb = a_v[...].reshape(tokens, d)
        for k in range(3):
            for copy in loads[k]:
                copy.wait()
            left = big_v[:, :, LANES * third * k : LANES * third * (k + 1)].reshape(tokens, LANES * third)
            found = lax.dot_general(left, gb, TN, preferred_element_type=F32)
            for b in range(third):
                for j in range(2):
                    at = quarter * (third * k + b)
                    put(slice(at, at + quarter), slice(d * j, d * j + d),
                        found[LANES * b + quarter * j : LANES * b + quarter * (j + 1)])
        for copy in last:
            copy.wait()
        if part == 0:
            put(everything, slice(2 * d, 3 * d), lax.dot_general(b_v[...].reshape(tokens, d), gb, TN, preferred_element_type=F32))
        else:
            values = big_v[:, :, LANES * blocks :].reshape(tokens, d)
            put(everything, slice(2 * d, 3 * d), lax.dot_general(
                b_v[...].reshape(tokens, d), values, TN, preferred_element_type=F32))
            out_v[:, 3 * d :] = split_small(small_table(d, ff, place, mine, theirs))
        for copy in send():
            copy.wait()

    @pl.when(core == 1)
    def _():
        cin = Copies(ins)
        hidden = load(cin, ff + 2 * d, d, a_v, 0)
        step = half // 3
        loads = [load(cin, half * part + step * k, step, big_v, step * k) for k in range(3)]
        loads.append(load(cin, ff + d * part, d, b_v, 0))
        for copy in hidden:
            copy.wait()
        turned = a_v[...].reshape(tokens, d).T
        for k in range(3):
            for copy in loads[k]:
                copy.wait()
            put(everything, slice(step * k, step * k + step), mm(turned, big_v[:, :, step * k : step * k + step].reshape(tokens, step)))
        for copy in loads[3]:
            copy.wait()
        put(everything, slice(half, half + d), mm(turned, b_v[...].reshape(tokens, d)))
        if part == 1:
            out_v[:, 3 * d :] = jnp.zeros((d, LANES), BF)
        for copy in send():
            copy.wait()


def added(parts):
    total = parts[0][...].astype(F32)
    for part in parts[1:]:
        total = total + part[...].astype(F32)
    shape = total.shape
    total = total.reshape(-1, shape[-1])
    main, last = total[:, : shape[-1] - LANES], split_small(joined_small(total[:, shape[-1] - LANES :]))
    return jnp.concatenate([main.astype(BF), last], axis=1).reshape(shape)


def mid_kernel(part, idx, *refs):
    came, outs, hold = refs[:4], refs[4:8], refs[8]
    if part == 0:
        total = came[0][...].astype(F32)
        for piece in came[1:]:
            total = total + piece[...].astype(F32)
        hold[...] = total.astype(BF).reshape(hold.shape)
    else:
        hold[...] = added(came)
    at = idx[1] if part == 0 else idx[0]
    for s in range(4):
        outs[s][...] = hold[lax.rem(at + s, 4)]


def last_kernel(idx, *refs):
    firsts, seconds, mine, theirs, hold = refs[:4], refs[4:8], refs[8], refs[9], refs[10]
    cut = firsts[0].shape[-1]
    total = firsts[0][...].astype(F32)
    for piece in firsts[1:]:
        total = total + piece[...].astype(F32)
    hold[:, :cut] = total
    hold[:, cut:] = added(seconds).astype(F32)
    count = mine.shape[0]
    core = idx[2]
    mine[...] = hold[pl.ds(pl.multiple_of(core * count, 8), count), :]
    theirs[...] = hold[pl.ds(pl.multiple_of((1 - core) * count, 8), count), :]


def place_kernel(idx, y_in, y_got, g_in, g_got, y_out, g_out, sems):
    copies = Copies(sems)
    for copy in [copies.start(y_got, y_out.at[1 - idx[3]]), copies.start(g_got, g_out.at[1 - idx[3]])]:
        copy.wait()


ANY = pl.BlockSpec(memory_space=pl.ANY)


def whole(shape):
    return pl.BlockSpec(shape, lambda i, idx: (0,) * len(shape))


def pick(shape):
    return pl.BlockSpec((1,) + shape, lambda i, idx: (idx[2],) + (0,) * len(shape))


def call(kernel, idx, ins, fresh, stashes, scratch, flops):
    outs = pl.pallas_call(
        kernel,
        grid_spec=pltpu.PrefetchScalarGridSpec(
            num_scalar_prefetch=1,
            grid=(1,),
            in_specs=[s for _, s in ins] + [ANY] * len(stashes),
            out_specs=[whole(fresh[0])] + [ANY] * len(stashes),
            scratch_shapes=scratch,
        ),
        out_shape=[jax.ShapeDtypeStruct(*fresh)] + [jax.ShapeDtypeStruct(a.shape, a.dtype) for a in stashes],
        input_output_aliases={1 + len(ins) + i: 1 + i for i in range(len(stashes))},
        compiler_params=pltpu.CompilerParams(dimension_semantics=("arbitrary",), vmem_limit_bytes=VMEM_LIMIT),
        cost_estimate=pl.CostEstimate(flops=flops, bytes_accessed=1 << 10, transcendentals=0),
    )(idx, *[a for a, _ in ins], *stashes)
    return outs[0], list(outs[1:])


def simple(kernel, idx, arrays, specs, out_shapes, out_specs, scratch, flops=1 << 10):
    return pl.pallas_call(
        kernel,
        grid_spec=pltpu.PrefetchScalarGridSpec(
            num_scalar_prefetch=1, grid=(1,), in_specs=specs, out_specs=out_specs, scratch_shapes=scratch
        ),
        out_shape=out_shapes,
        compiler_params=pltpu.CompilerParams(dimension_semantics=("arbitrary",), vmem_limit_bytes=VMEM_LIMIT),
        cost_estimate=pl.CostEstimate(flops=flops, bytes_accessed=1 << 10, transcendentals=0),
    )(idx, *arrays)


def along(x, step, size, by):
    devices = lax.axis_size("dp")

    def to(i):
        digit = i // step % size
        return i + ((digit + by) % size - digit) * step

    return lax.ppermute(x, "dp", [(i, to(i)) for i in range(devices)])


def paired(x):
    return lax.ppermute(x, "section", [(0, 1), (1, 0), (2, 3), (3, 2)])


def body(tokens, cotangent, lengths, proj_in, proj_attn, proj_down, norm_gain, query_gain, key_gain, up_bias, out_bias):
    ranks = lax.axis_size("dp")
    section = lax.axis_index("section")
    rank = lax.axis_index("dp")
    slots = lengths.shape[0]
    rows = tokens.shape[0] // slots
    d = tokens.shape[1]
    joined = proj_in.shape[2]
    ff = proj_down.shape[1] * ranks
    head = query_gain.shape[1] * ranks
    heads = d // head
    dshare = proj_in.shape[1]
    fshare = proj_down.shape[1] // dshare
    hshare = query_gain.shape[1]
    chunks = 3
    wide = joined + d + ff
    stride = wide + LANES
    side = math.isqrt(ranks // 2)
    core, z, y = lax.rem(rank, 2), lax.rem(rank // 2, side), rank // (2 * side)
    stage, odd = section // 2, lax.rem(section, 2)
    slot = lax.rem(stage + odd, 2)

    place = jnp.arange(WIDE, dtype=jnp.int32)
    source = (place % (WIDE // fshare)) * fshare + place // (WIDE // fshare)
    shuffle = (place[:, None] == source[None, :]).astype(BF)

    def shuffled(x, back=False):
        flat = x.reshape(-1, WIDE)
        out = lax.dot_general(
            flat, shuffle.astype(x.dtype), NT if back else NN, precision=lax.Precision.HIGHEST, preferred_element_type=F32
        )
        return out.reshape(x.shape)

    small = jnp.concatenate(
        [
            norm_gain[0][:, None],
            out_bias[0][:, None],
            up_bias[0].reshape(dshare, fshare),
            jnp.pad(query_gain[0], (0, dshare - hshare))[:, None],
            jnp.pad(key_gain[0], (0, dshare - hshare))[:, None],
            jnp.zeros((dshare, LANES - 4 - fshare), BF),
        ],
        axis=1,
    )
    heads_part = joined - ff
    local = jnp.concatenate(
        [shuffled(proj_in[0][:, heads_part:]).astype(BF), proj_in[0][:, :heads_part], proj_attn[0],
         proj_down[0].reshape(dshare, fshare * d), small],
        axis=1,
    )
    other = paired(local)
    both = jnp.where(odd == 0, jnp.concatenate([local, other], axis=1), jnp.concatenate([other, local], axis=1))
    g = lax.all_gather(both, "dp", axis=0, tiled=True)
    g3 = g.reshape(ff // WIDE, WIDE // fshare, g.shape[1])
    smalls = []
    for layer in range(2):
        at = stride * layer + wide
        tail = g[:, at : at + LANES].astype(F32)
        qk_gain = tail[:, 2 + fshare : 4 + fshare].reshape(ranks, dshare, 2)[:, :hshare].reshape(head, 2).T
        smalls.append((
            tail[:, 0].reshape(1, d),
            jnp.tile(qk_gain, (1, heads)).reshape(2, 1, d),
            shuffled(tail[:, 2 : 2 + fshare].reshape(1, ff).astype(BF)),
            tail[:, 1].reshape(1, d),
        ))
    column = jnp.arange(WIDE, dtype=jnp.int32) // head
    spread = jnp.where(column[:, None] == column[None, :], 1.0 / head, 0.0).astype(BF)

    toks = tokens.reshape(slots, rows, d)
    seeds = cotangent.reshape(slots, rows, d)
    ends = jnp.cumsum(lengths, axis=-1)
    position = jnp.arange(rows, dtype=jnp.int32)
    image = jnp.sum((position[None, :, None] >= ends[:, None, :]).astype(jnp.int32), axis=-1)
    image = jnp.where(position[None, :] < ends[:, 2:3], image, ABSENT + position[None, :])
    ids_col, ids_row = image[:, :, None], image[:, None, :]

    def stash(*shape, dtype=BF):
        return pl.pallas_call(
            lambda out: None, out_shape=jax.ShapeDtypeStruct(shape, dtype), out_specs=pl.BlockSpec(memory_space=pl.ANY)
        )()

    fc = ff // chunks
    groups = ff // WIDE

    def index_of(layer, active_stage):
        return jnp.stack([stage == active_stage, core, slot, odd == layer]).astype(jnp.int32)

    V = pltpu.VMEM
    weights_v = [V((d, heads_part), BF), V((chunks, d, fc), BF), V((groups, fshare, WIDE // fshare, d), BF), V((d, d), BF)]
    sems = [pltpu.SemaphoreType.DMA((48,)), pltpu.SemaphoreType.DMA((48,))]
    stacked = ff + 4 * d
    operands = [[stash(rows, stacked), stash(rows, stacked)] for _ in range(2)]
    kept = [[stash(rows, d) for _ in range(4)] + [stash(rows, 2 * d), stash(rows, 2 * d), stash(chunks, rows, fc),
             stash(heads, rows, rows), stash(16, rows, dtype=F32)] for _ in range(2)]
    results = [stash(slots, rows, d, dtype=F32), stash(rows, d, dtype=F32)]
    here_x = toks
    for t in range(4):
        layer = t % 2
        ngain, gains, ubias, obias = smalls[layer]
        ybf, done = call(
            partial(forward_kernel, d, ff, chunks, stride * layer, t == 0),
            index_of(layer, t // 2),
            [(here_x, ANY), (g, ANY), (g3, ANY), (ids_col, pick((rows, 1))), (ids_row, pick((1, rows))),
             (ngain, whole((1, d))), (gains, whole((2, 1, d))), (ubias, whole((1, ff))), (obias, whole((1, d))),
             (spread, whole((WIDE, WIDE)))],
            ((rows, d), BF),
            kept[layer][:9] + operands[layer] + results,
            [V((rows, d), BF), V((rows, d), BF)] + weights_v
            + [V((rows, d), BF)] * 3 + [V((rows, 2 * d), BF)] * 2 + [V((chunks, rows, fc), BF)] * 2
            + [V((heads, rows, rows), BF), V((16, rows), F32), V((rows, d), BF), V((rows, d), F32), V((rows, d), F32)]
            + sems,
            1 << 10,
        )
        kept[layer], operands[layer], results = done[:9], done[9:11], done[11:]
        here_x = lax.ppermute(ybf, "section", [(0, 3), (1, 2)]) if t == 1 else ybf
    y_out, y_send = results
    y_got = paired(y_send)

    results = [stash(slots, rows, d, dtype=F32), stash(rows, d, dtype=F32)]
    tables = [stash(1, stacked, dtype=F32) for _ in range(2)]
    steps = ((2 * side, 2), (2, 2 * side))
    widths = (3 * d, 3 * d + LANES)
    width = widths[0] + widths[1]
    share = 2 * dshare
    position = jnp.arange(LANES, dtype=jnp.int32)[:, None] % head
    place = (position // hshare * dshare + position % hshare == jnp.arange(d, dtype=jnp.int32)[None, :]).astype(F32)
    here = jnp.stack([y, z, core, slot]).astype(jnp.int32)

    def grads_by_place(layer, ahead=None):
        mine, sent = operands[layer]
        if ahead is not None:
            sent, ahead = lax.optimization_barrier((sent, ahead))
        got, table_got = along(sent, 1, 2, 1), along(tables[layer], 1, 2, 1)
        made = []
        for part in range(2):
            w = widths[part]
            shape = (side * share, w) if part == 0 else (side, share, w)
            made.append(simple(
                partial(weight_grad_kernel, d, ff, part), here,
                [place, tables[layer], table_got, mine, got],
                [whole((LANES, d)), whole(table_got.shape), whole(table_got.shape), ANY, ANY],
                [jax.ShapeDtypeStruct(shape, BF)] * side, [ANY] * side,
                [V((2, rows, ff // 2 + d), BF), V((2, rows, d), BF), V((2, rows, d), BF), V((d, w), BF),
                 pltpu.SemaphoreType.DMA((32,)), pltpu.SemaphoreType.DMA((16,))],
                1 << 10,
            ))
        return made, ahead

    def first_leg(made):
        return [[outs[0]] + [along(outs[s], steps[part][0], side, s) for s in (1, 2, 3)] for part, outs in enumerate(made)]

    def second_leg(legs):
        arrived = []
        for part, came in enumerate(legs):
            w = widths[part]
            outs = simple(
                partial(mid_kernel, part), here, came, [whole(a.shape) for a in came],
                [jax.ShapeDtypeStruct((share, w), BF)] * side, [whole((share, w))] * side, [V((side, share, w), BF)],
            )
            arrived += [outs[0]] + [along(outs[s], steps[part][1], side, s) for s in (1, 2, 3)]
        return simple(
            last_kernel, here, arrived, [whole(a.shape) for a in arrived],
            [jax.ShapeDtypeStruct((dshare, width), F32)] * 2, [whole((dshare, width))] * 2, [V((share, width), F32)],
        )

    sums = [None, None]
    here_g = seeds
    for t in range(4):
        layer = 1 - t % 2
        ngain, gains, ubias, obias = smalls[layer]
        gbf, done = call(
            partial(backward_kernel, d, ff, chunks, stride * layer, t == 0),
            index_of(layer, 1 - t // 2),
            [(here_g, ANY), (g, ANY), (g3, ANY), (ids_col, pick((rows, 1))), (ngain, whole((1, d))), (gains, whole((2, 1, d))),
             (spread, whole((WIDE, WIDE)))] + [(a, ANY) for a in kept[layer]],
            ((rows, d), BF),
            operands[layer] + [tables[layer]] + results,
            [V((rows, d), BF), V((rows, d), BF)] + weights_v
            + [V((rows, d), BF)] * 4 + [V((rows, 2 * d), BF)] * 2
            + [V((chunks, rows, fc), BF), V((heads, rows, rows), BF), V((16, rows), F32)]
            + [V((d, rows), BF), V((d, rows), F32), V((rows, d), F32)]
            + [V((rows, d), BF)] * 3 + [V((chunks, rows, fc), BF), V((rows, d), F32), V((rows, d), F32), V((1, stacked), F32)]
            + sems,
            1 << 10,
        )
        operands[layer], tables[layer], results = done[:2], done[2], done[3:]
        here_g = lax.ppermute(gbf, "section", [(3, 0), (2, 1)]) if t == 1 else gbf
        if t == 1:
            here_g, y_got = lax.optimization_barrier((here_g, y_got))
        if t == 2:
            made, _ = grads_by_place(layer)
            here_g, made = lax.optimization_barrier((here_g, made))
            legs = first_leg(made)
        if t == 3:
            made, early = grads_by_place(layer, [legs[p][s] for p in (0, 1) for s in (1, 3)])
            (legs[0][1], legs[0][3], legs[1][1], legs[1][3]) = early
            sums[1 - layer] = second_leg(legs)
            gr_got = paired(results[1])
            legs, gr_got = lax.optimization_barrier((first_leg(made), gr_got))
            sums[layer] = second_leg(legs)
    gr_out = results[0]
    y_out, gr_out = pl.pallas_call(
        place_kernel,
        grid_spec=pltpu.PrefetchScalarGridSpec(
            num_scalar_prefetch=1, grid=(1,), in_specs=[ANY] * 4, out_specs=[ANY] * 2,
            scratch_shapes=[pltpu.SemaphoreType.DMA((2,))],
        ),
        out_shape=[jax.ShapeDtypeStruct(y_out.shape, F32)] * 2,
        input_output_aliases={1: 0, 3: 1},
    )(here, y_out, y_got, gr_out, gr_got)

    home = [jnp.where(odd == 1, b, a) for a, b in zip(*sums)]
    away = [jnp.where(odd == 1, a, b).astype(BF) for a, b in zip(*sums)]
    sections = lax.axis_size("section")
    cross = [(s * ranks + i, (s ^ 1) * ranks + (i ^ 1)) for s in range(sections) for i in range(ranks)]
    mine = home[0] + paired(away[0]).astype(F32)
    other = along(home[1].astype(BF), 1, 2, 1).astype(F32) + lax.ppermute(away[1], ("section", "dp"), cross).astype(F32)
    half0, half1 = jnp.where(core == 0, mine, other), jnp.where(core == 0, other, mine)
    ups = shuffled(jnp.concatenate([half1[:, : 2 * d], half1[:, 3 * d : 5 * d]], axis=1), back=True)
    g_in = jnp.concatenate([half1[:, 2 * d : 3 * d], half1[:, 5 * d : 6 * d], half0[:, 5 * d : 6 * d], ups], axis=1)
    g_down = jnp.concatenate([half0[:, : 2 * d], half0[:, 3 * d : 5 * d]], axis=1)
    last = half0[:, 6 * d : 6 * d + 8] + half0[:, 6 * d + 8 : 6 * d + 16]
    return (
        y_out.reshape(1, slots * rows, d),
        gr_out.reshape(1, slots * rows, d),
        g_in[None],
        half0[None, :, 2 * d : 3 * d],
        g_down.reshape(1, dshare * fshare, d),
        last[None, :, 0],
        last[None, :hshare, 6],
        last[None, :hshare, 7],
        last[:, 2:6].reshape(1, dshare * fshare),
        last[None, :, 1],
    )


def solution(mesh):
    in_specs = (P("dp", None),) * 3 + (P("section", "dp", None),) * 3 + (P("section", "dp"),) * 5
    out_specs = (P("section", "dp", None),) * 5 + (P("section", "dp"),) * 5
    return jax.shard_map(body, mesh=mesh, in_specs=in_specs, out_specs=out_specs, check_vma=False)
```

```python
from functools import partial
import math

import jax
import jax.numpy as jnp
from jax import lax
from jax.experimental import pallas as pl
from jax.experimental.pallas import tpu as pltpu
from jax.sharding import PartitionSpec as P

BF = jnp.bfloat16
F32 = jnp.float32
VMEM_LIMIT = 60 * 1024 * 1024
EPS = 1e-06
NN = (((1,), (0,)), ((), ()))
NT = (((1,), (1,)), ((), ()))
TN = (((0,), (0,)), ((), ()))
LANES = 128
WIDE = 256
ABSENT = 16


def mm(a, b, dims=NN):
    return lax.dot_general(a, b, dims, preferred_element_type=F32)


def head_mean(x, spread, exact):
    parts = []
    for at in range(0, x.shape[1], WIDE):
        piece = x[:, at : at + WIDE]
        top = piece.astype(BF)
        total = mm(top, spread)
        if exact:
            total = total + mm((piece - top.astype(F32)).astype(BF), spread)
        parts.append(total)
    return jnp.concatenate(parts, axis=1)


def row_norm(x):
    centered = x - jnp.mean(x, axis=-1, keepdims=True)
    rstd = lax.rsqrt(jnp.mean(centered * centered, axis=-1, keepdims=True) + EPS)
    return centered * rstd, rstd


def norm_back(grad, normal, rstd, spread):
    return rstd * (grad - head_mean(grad, spread, False) - normal * head_mean(grad * normal, spread, False))


def lane_half(x, second):
    lane = lax.broadcasted_iota(jnp.int32, x.shape, 1)
    return jnp.where((lane >= LANES // 2) if second else (lane < LANES // 2), x, jnp.zeros_like(x))


class Copies:
    def __init__(self, sems):
        self.sems, self.used = sems, 0

    def start(self, src, dst):
        copy = pltpu.make_async_copy(src, dst, self.sems.at[self.used])
        self.used += 1
        copy.start()
        return copy

    def either(self, flag, src, yes, no):
        sem = self.sems.at[self.used]
        self.used += 1

        @pl.when(flag == 1)
        def _():
            pltpu.make_async_copy(src, yes, sem).start()

        @pl.when(flag != 1)
        def _():
            pltpu.make_async_copy(src, no, sem).start()

        return pltpu.make_async_copy(src, yes, sem)


def forward_kernel(d, ff, chunks, base, first, idx, x_in, g, g3, ids_col, ids_row, ngain, gains, ubias, obias, spread, *refs):
    @pl.when(idx[0] == 1)
    def _():
        forward_work(d, ff, chunks, base, first, idx, x_in, g, g3, ids_col, ids_row, ngain, gains, ubias, obias, spread, *refs)


def forward_work(d, ff, chunks, base, first, idx, x_in, g, g3, ids_col, ids_row, ngain, gains, ubias, obias, spread, *refs):
    refs = refs[13:]
    ybf, xs, qs, ks, vs, ns, nrs, gps, es, small, kept, sent, y_out, y_send = refs[:14]
    (x_v, h_v, w_v, u_v, d_v, a_v, q_v, k_v, v_v, n_v, r_v, act_v, gp_v, e_v, rs_v, att_v, acc_v, y_v, ins, outs) = refs[14:]
    rows = x_v.shape[0]
    fc = ff // chunks
    core, slot, home = idx[1], idx[2], idx[3]
    cin, cout = Copies(ins), Copies(outs)
    x_copy = cin.start(x_in.at[slot] if first else x_in, x_v)
    wq = [cin.start(g.at[:, pl.ds(base + ff + d * i, d)], w_v.at[:, pl.ds(d * i, d)]) for i in range(3)]
    groups = fc // WIDE
    wff = []
    for c in range(chunks):
        wff.append([cin.start(g.at[:, pl.ds(base + fc * c, fc)], u_v.at[c])] + [
            cin.start(g3.at[pl.ds(groups * c, groups), :, pl.ds(base + ff + 4 * d + d * j, d)], d_v.at[pl.ds(groups * c, groups), j])
            for j in range(4)
        ])
    wa = cin.start(g.at[:, pl.ds(base + ff + 3 * d, d)], a_v)

    pending = []

    def side(i):
        return pl.ds(ff + d * i, d)

    x_copy.wait()
    keep = jnp.where(ids_col[0] < ABSENT, 1.0, 0.0)
    masked = keep * x_v[...].astype(F32)
    h_v[...] = (row_norm(masked)[0] * ngain[...]).astype(BF)
    pending += [cout.start(x_v, xs), cout.start(h_v, kept.at[:, side(2)]), cout.start(h_v, sent.at[:, side(2)])]
    bias_mask = jnp.where(ids_col[0] == ids_row[0], 0.0, -1e9)
    for i in range(3):
        wq[i].wait()
        raw = mm(h_v[...], w_v[:, d * i : d * i + d])
        if i == 2:
            v_v[...] = raw.astype(BF)
            pending.append(cout.start(v_v, vs))
        else:
            centered = raw - head_mean(raw, spread[...], True)
            rstd = lax.rsqrt(head_mean(centered * centered, spread[...], True) + EPS)
            normal = centered * rstd
            scaled = (normal * gains[i]).astype(BF)
            n_v[:, d * i : d * i + d] = normal.astype(BF)
            r_v[:, d * i : d * i + d] = rstd.astype(BF)
            if i == 0:
                q_v[...] = scaled * jnp.asarray(0.125, BF)
                pending.append(cout.start(q_v, qs))
            else:
                k_v[...] = scaled
                pending.append(cout.start(k_v, ks))
    pending += [cout.start(n_v, ns), cout.start(r_v, nrs)]
    ones = jnp.ones((16, rows), BF)
    pairs = d // LANES // chunks
    for c in range(chunks):
        for copy in wff[c]:
            copy.wait()
        pre = mm(h_v[...], u_v[c]) + ubias[:, fc * c : fc * c + fc]
        cdf = 0.5 * (1.0 + lax.erf(pre * (1.0 / math.sqrt(2.0))))
        density = jnp.exp(-0.5 * pre * pre) * (1.0 / math.sqrt(2.0 * math.pi))
        act = (pre * cdf).astype(BF)
        act_v[c] = act
        gp_v[c] = (cdf + pre * density).astype(BF)
        total = mm(act, d_v[groups * c : groups * c + groups].reshape(fc, d))
        if c == 0:
            acc_v[...] = total
        else:
            acc_v[...] += total
        for p in range(pairs * c, pairs * c + pairs):
            cols = slice(LANES * p, LANES * p + LANES)
            vals_t = v_v[:, cols].T
            pair = q_v[:, cols]
            both = []
            for half in range(2):
                h = 2 * p + half
                e = jnp.exp(mm(k_v[:, cols], lane_half(pair, half), NT) + bias_mask).astype(BF)
                e_v[h] = e
                got = mm(jnp.concatenate([vals_t[64 * half : 64 * half + 64], ones], axis=0), e)
                inv = 1.0 / got[64:65]
                rs_v[h : h + 1, :] = inv
                both.append((got[:64] * inv).astype(BF))
            att_v[:, cols] = jnp.concatenate(both, axis=0).T
        span = pl.ds(fc * c, fc)
        pending += [cout.either(core, act_v.at[c], sent.at[:, span], kept.at[:, span]), cout.start(gp_v.at[c], gps.at[c]),
                    cout.start(e_v.at[pl.ds(2 * pairs * c, 2 * pairs)], es.at[pl.ds(2 * pairs * c, 2 * pairs)])]
    pending += [cout.start(rs_v, small), cout.either(core, att_v, sent.at[:, side(3)], kept.at[:, side(3)])]
    wa.wait()
    y = keep * (keep * x_v[...].astype(F32) + acc_v[...] + mm(att_v[...], a_v[...]) + obias[...])
    y_v[...] = y
    ybf[...] = y.astype(BF)
    pending.append(cout.either(home, y_v, y_out.at[slot], y_send))
    for copy in pending:
        copy.wait()


def backward_kernel(d, ff, chunks, base, first, idx, g_in, g, g3, ids_col, ngain, gains, spread, *refs):
    @pl.when(idx[0] == 1)
    def _():
        backward_work(d, ff, chunks, base, first, idx, g_in, g, g3, ids_col, ngain, gains, spread, *refs)


def backward_work(d, ff, chunks, base, first, idx, g_in, g, g3, ids_col, ngain, gains, spread, *refs):
    xs, qs, ks, vs, ns, nrs, gps, es, small = refs[:9]
    refs = refs[9 + 5 :]
    gbf, kept, sent, table, gr_out, gr_send = refs[:6]
    (g_v, gb_v, w_v, u_v, d_v, a_v, x_v, q_v, k_v, v_v, n_v, r_v, gp_v, e_v, rs_v, gat_v, gqt_v, gk_v,
     gq_b, gk_b, gv_b, gj_v, acc_v, out_v, sm_v, ins, outs) = refs[6:]
    rows = x_v.shape[0]
    fc = ff // chunks
    groups = fc // WIDE
    core, slot, home = idx[1], idx[2], idx[3]
    cin, cout = Copies(ins), Copies(outs)
    g_copy = cin.start(g_in.at[slot] if first else g_in, g_v)
    wa = cin.start(g.at[:, pl.ds(base + ff + 3 * d, d)], a_v)
    heads = [cin.start(s, v) for s, v in ((small, rs_v), (ks, k_v), (vs, v_v), (qs, q_v))]
    pairs = d // LANES // chunks
    wff = []
    for c in range(chunks):
        wff.append(
            [cin.start(g3.at[pl.ds(groups * c, groups), :, pl.ds(base + ff + 4 * d + d * j, d)], d_v.at[pl.ds(groups * c, groups), j])
             for j in range(4)]
            + [cin.start(gps.at[c], gp_v.at[c]), cin.start(g.at[:, pl.ds(base + fc * c, fc)], u_v.at[c]),
               cin.start(es.at[pl.ds(2 * pairs * c, 2 * pairs)], e_v.at[pl.ds(2 * pairs * c, 2 * pairs)])]
        )
    norms = [cin.start(ns, n_v), cin.start(nrs, r_v)]
    wq = [cin.start(g.at[:, pl.ds(base + ff + d * i, d)], w_v.at[:, pl.ds(d * i, d)]) for i in range(3)]
    rows_in = cin.start(xs, x_v)

    pending = []

    def side(i):
        return pl.ds(ff + d * i, d)

    def summed(at, value):
        sm_v[:, at : at + value.shape[1]] = jnp.sum(value, axis=0, keepdims=True)

    g_copy.wait()
    keep = jnp.where(ids_col[0] < ABSENT, 1.0, 0.0)
    gres = keep * g_v[...].astype(F32)
    summed(d, gres)
    gb_v[...] = gres.astype(BF)
    pending.append(cout.either(core, gb_v, sent.at[:, side(0)], kept.at[:, side(0)]))
    wa.wait()
    gat_v[...] = mm(a_v[...], gb_v[...], NT).astype(BF)
    for copy in heads:
        copy.wait()
    zeros = jnp.zeros((LANES // 2, rows), BF)
    for c in range(chunks):
        for copy in wff[c]:
            copy.wait()
        gup = mm(gb_v[...], d_v[groups * c : groups * c + groups].reshape(fc, d), NT) * gp_v[c].astype(F32)
        summed(4 * d + fc * c, gup)
        gup = gup.astype(BF)
        gj_v[c] = gup
        span = pl.ds(fc * c, fc)
        pending.append(cout.either(core, gj_v.at[c], kept.at[:, span], sent.at[:, span]))
        total = mm(gup, u_v[c], NT)
        if c == 0:
            acc_v[...] = total
        else:
            acc_v[...] += total
        for p in range(pairs * c, pairs * c + pairs):
            cols = slice(LANES * p, LANES * p + LANES)
            keys, vals, pair = k_v[:, cols], v_v[:, cols], q_v[:, cols]
            keys_t = keys.T
            gk, gv = None, None
            for half in range(2):
                h = 2 * p + half
                at_rows = slice(64 * h, 64 * h + 64)
                inv = rs_v[h : h + 1, :]
                ga = (gat_v[at_rows, :].astype(F32) * inv).astype(BF)
                ga = jnp.concatenate([zeros, ga] if half else [ga, zeros], axis=0)
                e = e_v[h]
                ef = e.astype(F32)
                gp = ef * mm(vals, ga)
                dot = jnp.sum(gp, axis=0, keepdims=True) * inv
                gs = (gp - ef * dot).astype(BF)
                gk_h = mm(gs, lane_half(pair, half))
                gv_h = mm(e, ga, NT)
                gk = gk_h if gk is None else gk + gk_h
                gv = gv_h if gv is None else gv + gv_h
                gqt_v[at_rows, :] = mm(keys_t[64 * half : 64 * half + 64], gs) * 0.125
            gk_v[:, cols] = gk
            gv_b[:, cols] = gv.astype(BF)
    pending.append(cout.either(core, gv_b, sent.at[:, side(1)], kept.at[:, side(1)]))
    for copy in norms:
        copy.wait()
    for i, (grad, out) in enumerate(((gqt_v[...].T, gq_b), (gk_v[...], gk_b))):
        normal = n_v[:, d * i : d * i + d].astype(F32)
        summed(2 * d + d * i, grad * normal)
        out[...] = norm_back(grad * gains[i], normal, r_v[:, d * i : d * i + d].astype(F32), spread[...]).astype(BF)
        pending.append(cout.either(core, out, kept.at[:, side(i)], sent.at[:, side(i)]))
    for copy in wq:
        copy.wait()
    ghid = acc_v[...]
    for i, part in enumerate((gq_b, gk_b, gv_b)):
        ghid = ghid + mm(part[...], w_v[:, d * i : d * i + d], NT)
    rows_in.wait()
    xhat, rstd = row_norm(keep * x_v[...].astype(F32))
    summed(0, ghid * xhat)
    pending.append(cout.start(sm_v, table))
    gx = ghid * ngain[...]
    gmask = rstd * (gx - jnp.mean(gx, axis=-1, keepdims=True) - xhat * jnp.mean(gx * xhat, axis=-1, keepdims=True))
    out = keep * (keep * g_v[...].astype(F32) + gmask)
    out_v[...] = out
    gbf[...] = out.astype(BF)
    pending.append(cout.either(home, out_v, gr_out.at[slot], gr_send))
    for copy in pending:
        copy.wait()


def split_small(values):
    top = values.astype(BF).astype(F32)
    lane = lax.broadcasted_iota(jnp.int32, values.shape, 1)
    return jnp.where(lane < 8, top, jnp.where(lane < 16, pltpu.roll(values - top, 8, 1), 0.0)).astype(BF)


def joined_small(parts):
    return parts + pltpu.roll(parts, LANES - 8, 1)


def small_table(d, ff, place, mine, theirs):
    total = mine[...] + theirs[...]
    quarter = WIDE // 4
    ub = total[:, 4 * d :]
    up_rows = []
    for j in range(4):
        pieces = [ub[:, WIDE * b + quarter * j : WIDE * b + quarter * (j + 1)] for b in range(ff // WIDE)]
        up_rows.append(jnp.concatenate(pieces, axis=1))
    head_rows = []
    for i in range(2, 4):
        lanes = total[:, d * i : d * i + LANES]
        for p in range(1, d // LANES):
            lanes = lanes + total[:, d * i + LANES * p : d * i + LANES * (p + 1)]
        head_rows.append(lanes)
    both = jnp.concatenate(head_rows + [jnp.zeros((6, LANES), F32)], axis=0)
    placed = lax.dot_general(both, place[...], NN, precision=lax.Precision.HIGHEST, preferred_element_type=F32)
    rows = [total[:, :d], total[:, d : 2 * d]] + up_rows + [placed[0:1], placed[1:2], jnp.zeros((LANES - 8, d), F32)]
    return jnp.concatenate(rows, axis=0).T


def weight_grad_kernel(d, ff, idx, place, mine, theirs, kept, got, *refs):
    firsts, seconds, (big_v, a_v, b_v, c_v, p_v, q_v, ins, outs) = refs[:4], refs[4:8], refs[8:]
    rows = kept.shape[0]
    tokens = 2 * rows
    quarter, half, third = WIDE // 4, ff // 2, ff // 3
    blocks = third // WIDE
    share = d // 16
    y, z, core = idx[0], idx[1], idx[2]

    def load(cin, at, width, to, to_at):
        return [cin.start(src.at[:, pl.ds(at, width)], to.at[i, :, pl.ds(to_at, width)]) for i, src in enumerate((kept, got))]

    def wait(copies):
        for copy in copies:
            copy.wait()

    def both(ref, at=0, width=d):
        return ref[:, :, at : at + width].reshape(tokens, width)

    def send_first(cout):
        return [cout.start(p_v.at[pl.ds(pl.multiple_of(lax.rem(y + s, 4) * 4 * share, 16), 4 * share)], firsts[s])
                for s in (2, 1, 3, 0)]

    def send_second(cout):
        return [
            cout.start(q_v.at[pl.ds(pl.multiple_of((4 * i + lax.rem(z + s, 4)) * share, 16), share)], seconds[s].at[i])
            for s in (2, 1, 3, 0) for i in range(4)
        ]

    @pl.when(core == 0)
    def _():
        cin, cout = Copies(ins), Copies(outs)
        grads = load(cin, ff, d, a_v, 0)
        loads = [load(cin, third * k, third, big_v, third * k) for k in range(3)]
        attended = load(cin, ff + 3 * d, d, b_v, 0)
        hidden, values = load(cin, ff + 2 * d, d, c_v, 0), load(cin, ff + d, d, c_v, d)
        wait(grads)
        gb = both(a_v)
        for k in range(3):
            wait(loads[k])
            found = lax.dot_general(both(big_v, third * k, third), gb, TN, preferred_element_type=F32).astype(BF)
            for b in range(blocks):
                at = quarter * (blocks * k + b)
                for j in range(4):
                    to = p_v if j < 2 else q_v
                    to[at : at + quarter, d * (j % 2) : d * (j % 2) + d] = found[WIDE * b + quarter * j : WIDE * b + quarter * (j + 1)]
        wait(attended)
        p_v[:, 2 * d :] = lax.dot_general(both(b_v), gb, TN, preferred_element_type=F32).astype(BF)
        pending = send_first(cout)
        wait(hidden + values)
        q_v[:, 2 * d : 3 * d] = lax.dot_general(both(c_v), both(c_v, d), TN, preferred_element_type=F32).astype(BF)
        q_v[:, 3 * d :] = split_small(small_table(d, ff, place, mine, theirs))
        wait(pending + send_second(cout))

    @pl.when(core == 1)
    def _():
        cin, cout = Copies(ins), Copies(outs)
        hidden = load(cin, ff + 2 * d, d, a_v, 0)
        loads = [load(cin, third * k, third, big_v, third * k) for k in range(2)]
        queries = load(cin, ff, d, b_v, 0)
        loads.append(load(cin, 2 * third, third, big_v, 2 * third))
        keys = load(cin, ff + d, d, c_v, 0)
        wait(hidden)
        turned = both(a_v).T
        wait(loads[0])
        p_v[:, :third] = mm(turned, both(big_v, 0, third)).astype(BF)
        wait(loads[1])
        found = mm(turned, both(big_v, third, third)).astype(BF)
        p_v[:, third:half] = found[:, : half - third]
        q_v[:, : 2 * third - half] = found[:, half - third :]
        wait(queries)
        p_v[:, half:] = mm(turned, both(b_v)).astype(BF)
        pending = send_first(cout)
        wait(loads[2])
        q_v[:, 2 * third - half : half] = mm(turned, both(big_v, 2 * third, third)).astype(BF)
        wait(keys)
        q_v[:, half : half + d] = mm(turned, both(c_v)).astype(BF)
        q_v[:, half + d :] = jnp.zeros((d, LANES), BF)
        wait(pending + send_second(cout))


def added(parts):
    total = parts[0][...].astype(F32)
    for part in parts[1:]:
        total = total + part[...].astype(F32)
    shape = total.shape
    total = total.reshape(-1, shape[-1])
    main, last = total[:, : shape[-1] - LANES], split_small(joined_small(total[:, shape[-1] - LANES :]))
    return jnp.concatenate([main.astype(BF), last], axis=1).reshape(shape)


def mid_kernel(part, idx, *refs):
    came, outs, hold = refs[:4], refs[4:8], refs[8]
    if part == 0:
        total = came[0][...].astype(F32)
        for piece in came[1:]:
            total = total + piece[...].astype(F32)
        hold[...] = total.astype(BF).reshape(hold.shape)
    else:
        hold[...] = added(came)
    at = idx[1] if part == 0 else idx[0]
    for s in range(4):
        outs[s][...] = hold[lax.rem(at + s, 4)]


def last_kernel(idx, *refs):
    firsts, seconds, mine, theirs, hold = refs[:4], refs[4:8], refs[8], refs[9], refs[10]
    cut = firsts[0].shape[-1]
    total = firsts[0][...].astype(F32)
    for piece in firsts[1:]:
        total = total + piece[...].astype(F32)
    hold[:, :cut] = total
    hold[:, cut:] = added(seconds).astype(F32)
    count = mine.shape[0]
    core = idx[2]
    mine[...] = hold[pl.ds(pl.multiple_of(core * count, 8), count), :]
    theirs[...] = hold[pl.ds(pl.multiple_of((1 - core) * count, 8), count), :]


def place_kernel(idx, y_in, y_got, g_in, g_got, y_out, g_out, sems):
    copies = Copies(sems)
    for copy in [copies.start(y_got, y_out.at[1 - idx[3]]), copies.start(g_got, g_out.at[1 - idx[3]])]:
        copy.wait()


def picked(rows, columns, wanted):
    row = lax.broadcasted_iota(jnp.int32, (rows, columns), 0)
    column = lax.broadcasted_iota(jnp.int32, (rows, columns), 1)
    return row, column, jnp.where(column == wanted(row), 1.0, 0.0)


def prepare_kernel(d, ff, p_in, p_attn, p_down, n_gain, o_bias, u_bias, q_gain, k_gain, shuffle, out):
    share = p_in.shape[0]
    heads_part = p_in.shape[1] - ff
    for at in range(0, ff, WIDE):
        out[:, at : at + WIDE] = mm(p_in[:, heads_part + at : heads_part + at + WIDE], shuffle[...]).astype(BF)
    out[:, ff : ff + heads_part] = p_in[:, :heads_part]
    at = ff + heads_part
    out[:, at : at + d] = p_attn[...]
    down = p_down[...]
    for j in range(4):
        take = picked(share, down.shape[0], lambda row: 4 * row + j)[2].astype(BF)
        out[:, at + d * (j + 1) : at + d * (j + 2)] = mm(take, down).astype(BF)

    def column_of(ref, wanted, where):
        values = ref[...].astype(F32)
        take = picked(share, values.shape[1], wanted)[2]
        lane = lax.broadcasted_iota(jnp.int32, (share, LANES), 1)
        return jnp.where(lane == where, jnp.sum(take * values, axis=1, keepdims=True), 0.0)

    table = column_of(n_gain, lambda row: row, 0) + column_of(o_bias, lambda row: row, 1)
    for j in range(4):
        table = table + column_of(u_bias, lambda row: 4 * row + j, 2 + j)
    table = table + column_of(q_gain, lambda row: row, 6) + column_of(k_gain, lambda row: row, 7)
    out[:, at + 5 * d :] = table.astype(BF)


def smalls_kernel(d, ff, base, stride, g, place, ngain, gains, ubias, obias, t_v, sems):
    copies = Copies(sems)
    loads = [copies.start(g.at[:, pl.ds(base + stride * layer, LANES)], t_v.at[layer]) for layer in range(2)]
    quarter = WIDE // 4
    for layer in range(2):
        loads[layer].wait()
        table = t_v[layer].astype(F32).T
        ngain[layer] = table[0:1]
        obias[layer] = table[1:2]
        pieces = [table[2 + j : 3 + j, quarter * b : quarter * (b + 1)] for b in range(ff // WIDE) for j in range(4)]
        ubias[layer] = jnp.concatenate(pieces, axis=1)
        both = mm(table[0:8].astype(BF), place[...])
        gains[layer, 0] = both[6:7]
        gains[layer, 1] = both[7:8]


def finish_kernel(d, ff, idx, own, a_in, b_in, c_in, shuffle, g_in, g_attn, g_down, g_ng, g_q, g_k, g_ub, g_ob):
    core = idx[2]
    share = own.shape[0]
    mine = own[...] + a_in[...].astype(F32)
    theirs = b_in[...].astype(F32) + c_in[...].astype(F32)
    half0 = jnp.where(core == 0, mine, theirs)
    half1 = jnp.where(core == 0, theirs, mine)
    g_in[:, :d] = half1[:, 2 * d : 3 * d]
    g_in[:, d : 2 * d] = half1[:, 5 * d : 6 * d]
    g_in[:, 2 * d : 3 * d] = half0[:, 5 * d : 6 * d]
    for at in range(0, ff, WIDE):
        start = at if at < 2 * d else at + d
        g_in[:, 3 * d + at : 3 * d + at + WIDE] = lax.dot_general(
            half1[:, start : start + WIDE], shuffle[...], NT, precision=lax.Precision.HIGHEST, preferred_element_type=F32)
    g_attn[...] = half0[:, 2 * d : 3 * d]
    stacked = jnp.concatenate([half0[:, at : at + d] for at in (0, d, 3 * d, 4 * d)], axis=0)
    row, column, _ = picked(4 * share, 4 * share, lambda row: row)
    turn = jnp.where(column == lax.rem(row, 4) * share + row // 4, 1.0, 0.0)
    g_down[...] = lax.dot_general(turn, stacked, NN, precision=lax.Precision.HIGHEST, preferred_element_type=F32)
    small = joined_small(half0[:, 6 * d :])
    turned = jnp.concatenate([small, jnp.zeros((LANES - share, LANES), F32)], axis=0).T
    g_ng[...] = turned[0:1, :share]
    g_ob[...] = turned[1:2, :share]
    g_q[...] = turned[6:7, : g_q.shape[1]]
    g_k[...] = turned[7:8, : g_k.shape[1]]
    total = jnp.zeros((8, 4 * share), F32)
    for j in range(4):
        row, column, _ = picked(LANES, 4 * share, lambda row: row)
        spread_out = jnp.where(column == 4 * row + j, 1.0, 0.0)
        total = total + jnp.where(lax.broadcasted_iota(jnp.int32, (8, 4 * share), 0) == 2 + j, 1.0, 0.0) * lax.dot_general(
            turned[0:8], spread_out, NN, precision=lax.Precision.HIGHEST, preferred_element_type=F32)
    g_ub[...] = jnp.sum(total, axis=0, keepdims=True)


ANY = pl.BlockSpec(memory_space=pl.ANY)


def whole(shape):
    return pl.BlockSpec(shape, lambda i, idx: (0,) * len(shape))


def pick(shape):
    return pl.BlockSpec((1,) + shape, lambda i, idx: (idx[2],) + (0,) * len(shape))


def call(kernel, idx, ins, fresh, stashes, scratch, flops):
    outs = pl.pallas_call(
        kernel,
        grid_spec=pltpu.PrefetchScalarGridSpec(
            num_scalar_prefetch=1,
            grid=(1,),
            in_specs=[s for _, s in ins] + [ANY] * len(stashes),
            out_specs=[whole(fresh[0])] + [ANY] * len(stashes),
            scratch_shapes=scratch,
        ),
        out_shape=[jax.ShapeDtypeStruct(*fresh)] + [jax.ShapeDtypeStruct(a.shape, a.dtype) for a in stashes],
        input_output_aliases={1 + len(ins) + i: 1 + i for i in range(len(stashes))},
        compiler_params=pltpu.CompilerParams(dimension_semantics=("arbitrary",), vmem_limit_bytes=VMEM_LIMIT),
        cost_estimate=pl.CostEstimate(flops=flops, bytes_accessed=1 << 10, transcendentals=0),
    )(idx, *[a for a, _ in ins], *stashes)
    return outs[0], list(outs[1:])


def plain(kernel, arrays, specs, out_shapes, out_specs, scratch):
    return pl.pallas_call(
        kernel, grid=(1,), in_specs=specs, out_specs=out_specs, scratch_shapes=scratch, out_shape=out_shapes,
        compiler_params=pltpu.CompilerParams(dimension_semantics=("arbitrary",), vmem_limit_bytes=VMEM_LIMIT),
        cost_estimate=pl.CostEstimate(flops=1 << 10, bytes_accessed=1 << 10, transcendentals=0),
    )(*arrays)


def simple(kernel, idx, arrays, specs, out_shapes, out_specs, scratch, flops=1 << 10):
    return pl.pallas_call(
        kernel,
        grid_spec=pltpu.PrefetchScalarGridSpec(
            num_scalar_prefetch=1, grid=(1,), in_specs=specs, out_specs=out_specs, scratch_shapes=scratch
        ),
        out_shape=out_shapes,
        compiler_params=pltpu.CompilerParams(dimension_semantics=("arbitrary",), vmem_limit_bytes=VMEM_LIMIT),
        cost_estimate=pl.CostEstimate(flops=flops, bytes_accessed=1 << 10, transcendentals=0),
    )(idx, *arrays)


def along(x, step, size, by):
    devices = lax.axis_size("dp")

    def to(i):
        digit = i // step % size
        return i + ((digit + by) % size - digit) * step

    return lax.ppermute(x, "dp", [(i, to(i)) for i in range(devices)])


def paired(x):
    return lax.ppermute(x, "section", [(0, 1), (1, 0), (2, 3), (3, 2)])


def body(tokens, cotangent, lengths, proj_in, proj_attn, proj_down, norm_gain, query_gain, key_gain, up_bias, out_bias):
    ranks = lax.axis_size("dp")
    section = lax.axis_index("section")
    rank = lax.axis_index("dp")
    slots = lengths.shape[0]
    rows = tokens.shape[0] // slots
    d = tokens.shape[1]
    joined = proj_in.shape[2]
    ff = proj_down.shape[1] * ranks
    head = query_gain.shape[1] * ranks
    heads = d // head
    dshare = proj_in.shape[1]
    fshare = proj_down.shape[1] // dshare
    hshare = query_gain.shape[1]
    chunks = 3
    wide = joined + d + ff
    stride = wide + LANES
    side = math.isqrt(ranks // 2)
    core, z, y = lax.rem(rank, 2), lax.rem(rank // 2, side), rank // (2 * side)
    stage, odd = section // 2, lax.rem(section, 2)
    slot = lax.rem(stage + odd, 2)

    place = jnp.arange(WIDE, dtype=jnp.int32)
    source = (place % (WIDE // fshare)) * fshare + place // (WIDE // fshare)
    shuffle = (place[:, None] == source[None, :]).astype(BF)

    def full(a):
        return pl.BlockSpec(a.shape, lambda i: (0,) * a.ndim)

    shares = [proj_in[0], proj_attn[0], proj_down[0], norm_gain, out_bias, up_bias, query_gain, key_gain, shuffle]
    heads_part = joined - ff
    local = jax.ShapeDtypeStruct((dshare, stride), BF)
    local = plain(partial(prepare_kernel, d, ff), shares, [full(a) for a in shares], local, full(local), [])
    other = paired(local)
    both = jnp.where(odd == 0, jnp.concatenate([local, other], axis=1), jnp.concatenate([other, local], axis=1))
    g = lax.all_gather(both, "dp", axis=0, tiled=True)
    g3 = g.reshape(ff // WIDE, WIDE // fshare, g.shape[1])
    element = jnp.arange(d, dtype=jnp.int32) % head
    spread_gain = (jnp.arange(d, dtype=jnp.int32)[:, None] == (element // hshare * dshare + element % hshare)[None, :]).astype(BF)
    tables = [jax.ShapeDtypeStruct(s, F32) for s in ((2, 1, d), (2, 2, 1, d), (2, 1, ff), (2, 1, d))]
    ngain, gains, ubias, obias = plain(
        partial(smalls_kernel, d, ff, wide, stride), [g, spread_gain], [ANY, full(spread_gain)], tables,
        [full(a) for a in tables], [pltpu.VMEM((2, d, LANES), BF), pltpu.SemaphoreType.DMA((2,))],
    )

    def of_layer(a, layer):
        return (a, pl.BlockSpec((None,) + a.shape[1:], lambda i, idx: (layer,) + (0,) * (a.ndim - 1)))

    column = jnp.arange(WIDE, dtype=jnp.int32) // head
    spread = jnp.where(column[:, None] == column[None, :], 1.0 / head, 0.0).astype(BF)

    toks = tokens.reshape(slots, rows, d)
    seeds = cotangent.reshape(slots, rows, d)
    ends = jnp.cumsum(lengths, axis=-1)
    position = jnp.arange(rows, dtype=jnp.int32)
    image = jnp.sum((position[None, :, None] >= ends[:, None, :]).astype(jnp.int32), axis=-1)
    image = jnp.where(position[None, :] < ends[:, 2:3], image, ABSENT + position[None, :])
    ids_col, ids_row = image[:, :, None], image[:, None, :]

    def stash(*shape, dtype=BF):
        return pl.pallas_call(
            lambda out: None, out_shape=jax.ShapeDtypeStruct(shape, dtype), out_specs=pl.BlockSpec(memory_space=pl.ANY)
        )()

    fc = ff // chunks
    groups = ff // WIDE

    def index_of(layer, active_stage):
        return jnp.stack([stage == active_stage, core, slot, odd == layer]).astype(jnp.int32)

    V = pltpu.VMEM
    weights_v = [V((d, heads_part), BF), V((chunks, d, fc), BF), V((groups, fshare, WIDE // fshare, d), BF), V((d, d), BF)]
    sems = [pltpu.SemaphoreType.DMA((48,)), pltpu.SemaphoreType.DMA((48,))]
    stacked = ff + 4 * d
    operands = [[stash(rows, stacked), stash(rows, stacked)] for _ in range(2)]
    kept = [[stash(rows, d) for _ in range(4)] + [stash(rows, 2 * d), stash(rows, 2 * d), stash(chunks, rows, fc),
             stash(heads, rows, rows), stash(16, rows, dtype=F32)] for _ in range(2)]
    results = [stash(slots, rows, d, dtype=F32), stash(rows, d, dtype=F32)]
    here_x = toks
    for t in range(4):
        layer = t % 2
        ybf, done = call(
            partial(forward_kernel, d, ff, chunks, stride * layer, t == 0),
            index_of(layer, t // 2),
            [(here_x, ANY), (g, ANY), (g3, ANY), (ids_col, pick((rows, 1))), (ids_row, pick((1, rows))),
             of_layer(ngain, layer), of_layer(gains, layer), of_layer(ubias, layer), of_layer(obias, layer),
             (spread, whole((WIDE, WIDE)))],
            ((rows, d), BF),
            kept[layer][:9] + operands[layer] + results,
            [V((rows, d), BF), V((rows, d), BF)] + weights_v
            + [V((rows, d), BF)] * 3 + [V((rows, 2 * d), BF)] * 2 + [V((chunks, rows, fc), BF)] * 2
            + [V((heads, rows, rows), BF), V((16, rows), F32), V((rows, d), BF), V((rows, d), F32), V((rows, d), F32)]
            + sems,
            1 << 10,
        )
        kept[layer], operands[layer], results = done[:9], done[9:11], done[11:]
        here_x = lax.ppermute(ybf, "section", [(0, 3), (1, 2)]) if t == 1 else ybf
    y_out, y_send = results
    y_got = paired(y_send)

    results = [stash(slots, rows, d, dtype=F32), stash(rows, d, dtype=F32)]
    tables = [stash(1, stacked, dtype=F32) for _ in range(2)]
    steps = ((2 * side, 2), (2, 2 * side))
    widths = (3 * d, 3 * d + LANES)
    width = widths[0] + widths[1]
    share = 2 * dshare
    position = jnp.arange(LANES, dtype=jnp.int32)[:, None] % head
    place = (position // hshare * dshare + position % hshare == jnp.arange(d, dtype=jnp.int32)[None, :]).astype(F32)
    here = jnp.stack([y, z, core, slot]).astype(jnp.int32)

    def grads_by_place(layer, ahead=None):
        mine, sent = operands[layer]
        if ahead is not None:
            sent, ahead = lax.optimization_barrier((sent, ahead))
        got, table_got = along(sent, 1, 2, 1), along(tables[layer], 1, 2, 1)
        shapes = [(side * share, widths[0])] * side + [(side, share, widths[1])] * side
        outs = simple(
            partial(weight_grad_kernel, d, ff), here,
            [place, tables[layer], table_got, mine, got],
            [whole((LANES, d)), whole(table_got.shape), whole(table_got.shape), ANY, ANY],
            [jax.ShapeDtypeStruct(s, BF) for s in shapes], [ANY] * (2 * side),
            [V((2, rows, ff), BF), V((2, rows, d), BF), V((2, rows, d), BF), V((2, rows, 2 * d), BF),
             V((d, widths[0]), BF), V((d, widths[1]), BF), pltpu.SemaphoreType.DMA((32,)), pltpu.SemaphoreType.DMA((32,))],
        )
        made = [outs[:side], outs[side:]]
        return made, ahead

    def first_leg(made):
        return [[outs[0]] + [along(outs[s], steps[part][0], side, s) for s in (1, 2, 3)] for part, outs in enumerate(made)]

    def second_leg(legs):
        arrived = []
        for part, came in enumerate(legs):
            w = widths[part]
            outs = simple(
                partial(mid_kernel, part), here, came, [whole(a.shape) for a in came],
                [jax.ShapeDtypeStruct((share, w), BF)] * side, [whole((share, w))] * side, [V((side, share, w), BF)],
            )
            arrived += [outs[0]] + [along(outs[s], steps[part][1], side, s) for s in (1, 2, 3)]
        return simple(
            last_kernel, here, arrived, [whole(a.shape) for a in arrived],
            [jax.ShapeDtypeStruct((dshare, width), F32)] * 2, [whole((dshare, width))] * 2, [V((share, width), F32)],
        )

    sums = [None, None]
    here_g = seeds
    for t in range(4):
        layer = 1 - t % 2
        gbf, done = call(
            partial(backward_kernel, d, ff, chunks, stride * layer, t == 0),
            index_of(layer, 1 - t // 2),
            [(here_g, ANY), (g, ANY), (g3, ANY), (ids_col, pick((rows, 1))), of_layer(ngain, layer), of_layer(gains, layer),
             (spread, whole((WIDE, WIDE)))] + [(a, ANY) for a in kept[layer]],
            ((rows, d), BF),
            operands[layer] + [tables[layer]] + results,
            [V((rows, d), BF), V((rows, d), BF)] + weights_v
            + [V((rows, d), BF)] * 4 + [V((rows, 2 * d), BF)] * 2
            + [V((chunks, rows, fc), BF), V((heads, rows, rows), BF), V((16, rows), F32)]
            + [V((d, rows), BF), V((d, rows), F32), V((rows, d), F32)]
            + [V((rows, d), BF)] * 3 + [V((chunks, rows, fc), BF), V((rows, d), F32), V((rows, d), F32), V((1, stacked), F32)]
            + sems,
            1 << 10,
        )
        operands[layer], tables[layer], results = done[:2], done[2], done[3:]
        here_g = lax.ppermute(gbf, "section", [(3, 0), (2, 1)]) if t == 1 else gbf
        if t == 1:
            here_g, y_got = lax.optimization_barrier((here_g, y_got))
        if t == 2:
            made, _ = grads_by_place(layer)
            here_g, made = lax.optimization_barrier((here_g, made))
            legs = first_leg(made)
        if t == 3:
            made, early = grads_by_place(layer, [legs[p][s] for p in (0, 1) for s in (1, 3)])
            (legs[0][1], legs[0][3], legs[1][1], legs[1][3]) = early
            sums[1 - layer] = second_leg(legs)
            gr_got = paired(results[1])
            legs, gr_got = lax.optimization_barrier((first_leg(made), gr_got))
            sums[layer] = second_leg(legs)
    gr_out = results[0]
    y_out, gr_out = pl.pallas_call(
        place_kernel,
        grid_spec=pltpu.PrefetchScalarGridSpec(
            num_scalar_prefetch=1, grid=(1,), in_specs=[ANY, whole((rows, d)), ANY, whole((rows, d))], out_specs=[ANY] * 2,
            scratch_shapes=[pltpu.SemaphoreType.DMA((2,))],
        ),
        out_shape=[jax.ShapeDtypeStruct(y_out.shape, F32)] * 2,
        input_output_aliases={1: 0, 3: 1},
    )(here, y_out, y_got, gr_out, gr_got)

    home = [jnp.where(odd == 1, b, a) for a, b in zip(*sums)]
    away = [jnp.where(odd == 1, a, b).astype(BF) for a, b in zip(*sums)]
    sections = lax.axis_size("section")
    cross = [(s * ranks + i, (s ^ 1) * ranks + (i ^ 1)) for s in range(sections) for i in range(ranks)]
    arrays = [home[0], paired(away[0]), along(home[1].astype(BF), 1, 2, 1), lax.ppermute(away[1], ("section", "dp"), cross),
              shuffle.astype(F32)]
    shapes = [(dshare, joined), (dshare, d), (dshare * fshare, d), (1, dshare), (1, hshare), (1, hshare), (1, dshare * fshare),
              (1, dshare)]
    g_in, g_attn, g_down, g_ng, g_q, g_k, g_ub, g_ob = simple(
        partial(finish_kernel, d, ff), here, arrays, [whole(a.shape) for a in arrays],
        [jax.ShapeDtypeStruct(s, F32) for s in shapes], [whole(s) for s in shapes], [],
    )
    return (y_out.reshape(1, slots * rows, d), gr_out.reshape(1, slots * rows, d), g_in[None], g_attn[None], g_down[None],
            g_ng, g_q, g_k, g_ub, g_ob)


def solution(mesh):
    in_specs = (P("dp", None),) * 3 + (P("section", "dp", None),) * 3 + (P("section", "dp"),) * 5
    out_specs = (P("section", "dp", None),) * 5 + (P("section", "dp"),) * 5
    return jax.shard_map(body, mesh=mesh, in_specs=in_specs, out_specs=out_specs, check_vma=False)
```

```python
from functools import partial
import math

import jax
import jax.numpy as jnp
from jax import lax
from jax.experimental import pallas as pl
from jax.experimental.pallas import tpu as pltpu
from jax.sharding import PartitionSpec as P

BF = jnp.bfloat16
F32 = jnp.float32
VMEM_LIMIT = 60 * 1024 * 1024
EPS = 1e-06
NN = (((1,), (0,)), ((), ()))
NT = (((1,), (1,)), ((), ()))
TN = (((0,), (0,)), ((), ()))
LANES = 128
WIDE = 256
ABSENT = 16


def mm(a, b, dims=NN):
    return lax.dot_general(a, b, dims, preferred_element_type=F32)


def head_mean(x, spread, exact):
    parts = []
    for at in range(0, x.shape[1], WIDE):
        piece = x[:, at : at + WIDE]
        top = piece.astype(BF)
        total = mm(top, spread)
        if exact:
            total = total + mm((piece - top.astype(F32)).astype(BF), spread)
        parts.append(total)
    return jnp.concatenate(parts, axis=1)


def row_norm(x):
    centered = x - jnp.mean(x, axis=-1, keepdims=True)
    rstd = lax.rsqrt(jnp.mean(centered * centered, axis=-1, keepdims=True) + EPS)
    return centered * rstd, rstd


def norm_back(grad, normal, rstd, spread):
    return rstd * (grad - head_mean(grad, spread, False) - normal * head_mean(grad * normal, spread, False))


def lane_half(x, second):
    lane = lax.broadcasted_iota(jnp.int32, x.shape, 1)
    return jnp.where((lane >= LANES // 2) if second else (lane < LANES // 2), x, jnp.zeros_like(x))


class Copies:
    def __init__(self, sems):
        self.sems, self.used = sems, 0

    def start(self, src, dst):
        copy = pltpu.make_async_copy(src, dst, self.sems.at[self.used])
        self.used += 1
        copy.start()
        return copy

    def either(self, flag, src, yes, no):
        sem = self.sems.at[self.used]
        self.used += 1

        @pl.when(flag == 1)
        def _():
            pltpu.make_async_copy(src, yes, sem).start()

        @pl.when(flag != 1)
        def _():
            pltpu.make_async_copy(src, no, sem).start()

        return pltpu.make_async_copy(src, yes, sem)


def forward_kernel(d, ff, chunks, base, first, idx, x_in, g, g3, ids_col, ids_row, ngain, gains, ubias, obias, spread, *refs):
    @pl.when(idx[0] == 1)
    def _():
        forward_work(d, ff, chunks, base, first, idx, x_in, g, g3, ids_col, ids_row, ngain, gains, ubias, obias, spread, *refs)


def forward_work(d, ff, chunks, base, first, idx, x_in, g, g3, ids_col, ids_row, ngain, gains, ubias, obias, spread, *refs):
    refs = refs[13:]
    ybf, xs, qs, ks, vs, ns, nrs, gps, es, small, kept, sent, y_out, y_send = refs[:14]
    (x_v, h_v, w_v, u_v, d_v, a_v, q_v, k_v, v_v, n_v, r_v, act_v, gp_v, e_v, rs_v, att_v, acc_v, y_v, ins, outs) = refs[14:]
    rows = x_v.shape[0]
    fc = ff // chunks
    core, slot, home = idx[1], idx[2], idx[3]
    cin, cout = Copies(ins), Copies(outs)
    x_copy = cin.start(x_in.at[slot] if first else x_in, x_v)
    wq = [cin.start(g.at[:, pl.ds(base + ff + d * i, d)], w_v.at[:, pl.ds(d * i, d)]) for i in range(3)]
    groups = fc // WIDE
    wff = []
    for c in range(chunks):
        wff.append([cin.start(g.at[:, pl.ds(base + fc * c, fc)], u_v.at[c])] + [
            cin.start(g3.at[pl.ds(groups * c, groups), :, pl.ds(base + ff + 4 * d + d * j, d)], d_v.at[pl.ds(groups * c, groups), j])
            for j in range(4)
        ])
    wa = cin.start(g.at[:, pl.ds(base + ff + 3 * d, d)], a_v)

    pending = []

    def side(i):
        return pl.ds(ff + d * i, d)

    x_copy.wait()
    keep = jnp.where(ids_col[0] < ABSENT, 1.0, 0.0)
    masked = keep * x_v[...].astype(F32)
    h_v[...] = (row_norm(masked)[0] * ngain[...]).astype(BF)
    pending += [cout.start(x_v, xs), cout.start(h_v, kept.at[:, side(2)]), cout.start(h_v, sent.at[:, side(2)])]
    bias_mask = jnp.where(ids_col[0] == ids_row[0], 0.0, -1e9)
    for i in range(3):
        wq[i].wait()
        raw = mm(h_v[...], w_v[:, d * i : d * i + d])
        if i == 2:
            v_v[...] = raw.astype(BF)
            pending.append(cout.start(v_v, vs))
        else:
            centered = raw - head_mean(raw, spread[...], True)
            rstd = lax.rsqrt(head_mean(centered * centered, spread[...], True) + EPS)
            normal = centered * rstd
            scaled = (normal * gains[i]).astype(BF)
            n_v[:, d * i : d * i + d] = normal.astype(BF)
            r_v[:, d * i : d * i + d] = rstd.astype(BF)
            if i == 0:
                q_v[...] = scaled * jnp.asarray(0.125, BF)
                pending.append(cout.start(q_v, qs))
            else:
                k_v[...] = scaled
                pending.append(cout.start(k_v, ks))
    pending += [cout.start(n_v, ns), cout.start(r_v, nrs)]
    ones = jnp.ones((16, rows), BF)
    pairs = d // LANES // chunks
    for c in range(chunks):
        for copy in wff[c]:
            copy.wait()
        pre = mm(h_v[...], u_v[c]) + ubias[:, fc * c : fc * c + fc]
        cdf = 0.5 * (1.0 + lax.erf(pre * (1.0 / math.sqrt(2.0))))
        density = jnp.exp(-0.5 * pre * pre) * (1.0 / math.sqrt(2.0 * math.pi))
        act = (pre * cdf).astype(BF)
        act_v[c] = act
        gp_v[c] = (cdf + pre * density).astype(BF)
        total = mm(act, d_v[groups * c : groups * c + groups].reshape(fc, d))
        if c == 0:
            acc_v[...] = total
        else:
            acc_v[...] += total
        for p in range(pairs * c, pairs * c + pairs):
            cols = slice(LANES * p, LANES * p + LANES)
            vals_t = v_v[:, cols].T
            pair = q_v[:, cols]
            both = []
            for half in range(2):
                h = 2 * p + half
                e = jnp.exp(mm(k_v[:, cols], lane_half(pair, half), NT) + bias_mask).astype(BF)
                e_v[h] = e
                got = mm(jnp.concatenate([vals_t[64 * half : 64 * half + 64], ones], axis=0), e)
                inv = 1.0 / got[64:65]
                rs_v[h : h + 1, :] = inv
                both.append((got[:64] * inv).astype(BF))
            att_v[:, cols] = jnp.concatenate(both, axis=0).T
        span = pl.ds(fc * c, fc)
        pending += [cout.either(core, act_v.at[c], sent.at[:, span], kept.at[:, span]), cout.start(gp_v.at[c], gps.at[c]),
                    cout.start(e_v.at[pl.ds(2 * pairs * c, 2 * pairs)], es.at[pl.ds(2 * pairs * c, 2 * pairs)])]
    pending += [cout.start(rs_v, small), cout.either(core, att_v, sent.at[:, side(3)], kept.at[:, side(3)])]
    wa.wait()
    y = keep * (keep * x_v[...].astype(F32) + acc_v[...] + mm(att_v[...], a_v[...]) + obias[...])
    y_v[...] = y
    ybf[...] = y.astype(BF)
    pending.append(cout.either(home, y_v, y_out.at[slot], y_send))
    for copy in pending:
        copy.wait()


def backward_kernel(d, ff, chunks, base, first, idx, g_in, g, g3, ids_col, ngain, gains, spread, *refs):
    @pl.when(idx[0] == 1)
    def _():
        backward_work(d, ff, chunks, base, first, idx, g_in, g, g3, ids_col, ngain, gains, spread, *refs)


def backward_work(d, ff, chunks, base, first, idx, g_in, g, g3, ids_col, ngain, gains, spread, *refs):
    xs, qs, ks, vs, ns, nrs, gps, es, small = refs[:9]
    refs = refs[9 + 5 :]
    gbf, kept, sent, table, gr_out, gr_send = refs[:6]
    (g_v, gb_v, w_v, u_v, d_v, a_v, x_v, q_v, k_v, v_v, n_v, r_v, gp_v, e_v, rs_v, gat_v, gqt_v, gk_v,
     gq_b, gk_b, gv_b, gj_v, acc_v, out_v, sm_v, ins, outs) = refs[6:]
    rows = x_v.shape[0]
    fc = ff // chunks
    groups = fc // WIDE
    core, slot, home = idx[1], idx[2], idx[3]
    cin, cout = Copies(ins), Copies(outs)
    g_copy = cin.start(g_in.at[slot] if first else g_in, g_v)
    wa = cin.start(g.at[:, pl.ds(base + ff + 3 * d, d)], a_v)
    heads = [cin.start(s, v) for s, v in ((small, rs_v), (ks, k_v), (vs, v_v), (qs, q_v))]
    pairs = d // LANES // chunks
    wff = []
    for c in range(chunks):
        wff.append(
            [cin.start(g3.at[pl.ds(groups * c, groups), :, pl.ds(base + ff + 4 * d + d * j, d)], d_v.at[pl.ds(groups * c, groups), j])
             for j in range(4)]
            + [cin.start(gps.at[c], gp_v.at[c]), cin.start(g.at[:, pl.ds(base + fc * c, fc)], u_v.at[c]),
               cin.start(es.at[pl.ds(2 * pairs * c, 2 * pairs)], e_v.at[pl.ds(2 * pairs * c, 2 * pairs)])]
        )
    norms = [cin.start(ns, n_v), cin.start(nrs, r_v)]
    wq = [cin.start(g.at[:, pl.ds(base + ff + d * i, d)], w_v.at[:, pl.ds(d * i, d)]) for i in range(3)]
    rows_in = cin.start(xs, x_v)

    pending = []

    def side(i):
        return pl.ds(ff + d * i, d)

    def summed(at, value):
        sm_v[:, at : at + value.shape[1]] = jnp.sum(value, axis=0, keepdims=True)

    g_copy.wait()
    keep = jnp.where(ids_col[0] < ABSENT, 1.0, 0.0)
    gres = keep * g_v[...].astype(F32)
    summed(d, gres)
    gb_v[...] = gres.astype(BF)
    pending.append(cout.either(core, gb_v, sent.at[:, side(0)], kept.at[:, side(0)]))
    wa.wait()
    gat_v[...] = mm(a_v[...], gb_v[...], NT).astype(BF)
    for copy in heads:
        copy.wait()
    zeros = jnp.zeros((LANES // 2, rows), BF)
    for c in range(chunks):
        for copy in wff[c]:
            copy.wait()
        gup = mm(gb_v[...], d_v[groups * c : groups * c + groups].reshape(fc, d), NT) * gp_v[c].astype(F32)
        summed(4 * d + fc * c, gup)
        gup = gup.astype(BF)
        gj_v[c] = gup
        span = pl.ds(fc * c, fc)
        pending.append(cout.either(core, gj_v.at[c], kept.at[:, span], sent.at[:, span]))
        total = mm(gup, u_v[c], NT)
        if c == 0:
            acc_v[...] = total
        else:
            acc_v[...] += total
        for p in range(pairs * c, pairs * c + pairs):
            cols = slice(LANES * p, LANES * p + LANES)
            keys, vals, pair = k_v[:, cols], v_v[:, cols], q_v[:, cols]
            keys_t = keys.T
            gk, gv = None, None
            for half in range(2):
                h = 2 * p + half
                at_rows = slice(64 * h, 64 * h + 64)
                inv = rs_v[h : h + 1, :]
                ga = (gat_v[at_rows, :].astype(F32) * inv).astype(BF)
                ga = jnp.concatenate([zeros, ga] if half else [ga, zeros], axis=0)
                e = e_v[h]
                ef = e.astype(F32)
                gp = ef * mm(vals, ga)
                dot = jnp.sum(gp, axis=0, keepdims=True) * inv
                gs = (gp - ef * dot).astype(BF)
                gk_h = mm(gs, lane_half(pair, half))
                gv_h = mm(e, ga, NT)
                gk = gk_h if gk is None else gk + gk_h
                gv = gv_h if gv is None else gv + gv_h
                gqt_v[at_rows, :] = mm(keys_t[64 * half : 64 * half + 64], gs) * 0.125
            gk_v[:, cols] = gk
            gv_b[:, cols] = gv.astype(BF)
    pending.append(cout.either(core, gv_b, sent.at[:, side(1)], kept.at[:, side(1)]))
    for copy in norms:
        copy.wait()
    for i, (grad, out) in enumerate(((gqt_v[...].T, gq_b), (gk_v[...], gk_b))):
        normal = n_v[:, d * i : d * i + d].astype(F32)
        summed(2 * d + d * i, grad * normal)
        out[...] = norm_back(grad * gains[i], normal, r_v[:, d * i : d * i + d].astype(F32), spread[...]).astype(BF)
        pending.append(cout.either(core, out, kept.at[:, side(i)], sent.at[:, side(i)]))
    for copy in wq:
        copy.wait()
    ghid = acc_v[...]
    for i, part in enumerate((gq_b, gk_b, gv_b)):
        ghid = ghid + mm(part[...], w_v[:, d * i : d * i + d], NT)
    rows_in.wait()
    xhat, rstd = row_norm(keep * x_v[...].astype(F32))
    summed(0, ghid * xhat)
    pending.append(cout.start(sm_v, table))
    gx = ghid * ngain[...]
    gmask = rstd * (gx - jnp.mean(gx, axis=-1, keepdims=True) - xhat * jnp.mean(gx * xhat, axis=-1, keepdims=True))
    out = keep * (keep * g_v[...].astype(F32) + gmask)
    out_v[...] = out
    gbf[...] = out.astype(BF)
    pending.append(cout.either(home, out_v, gr_out.at[slot], gr_send))
    for copy in pending:
        copy.wait()


def split_small(values):
    top = values.astype(BF).astype(F32)
    lane = lax.broadcasted_iota(jnp.int32, values.shape, 1)
    return jnp.where(lane < 8, top, jnp.where(lane < 16, pltpu.roll(values - top, 8, 1), 0.0)).astype(BF)


def joined_small(parts):
    return parts + pltpu.roll(parts, LANES - 8, 1)


def small_table(d, ff, place, mine, theirs):
    total = mine[...] + theirs[...]
    quarter = WIDE // 4
    ub = total[:, 4 * d :]
    up_rows = []
    for j in range(4):
        pieces = [ub[:, WIDE * b + quarter * j : WIDE * b + quarter * (j + 1)] for b in range(ff // WIDE)]
        up_rows.append(jnp.concatenate(pieces, axis=1))
    head_rows = []
    for i in range(2, 4):
        lanes = total[:, d * i : d * i + LANES]
        for p in range(1, d // LANES):
            lanes = lanes + total[:, d * i + LANES * p : d * i + LANES * (p + 1)]
        head_rows.append(lanes)
    both = jnp.concatenate(head_rows + [jnp.zeros((6, LANES), F32)], axis=0)
    placed = lax.dot_general(both, place[...], NN, precision=lax.Precision.HIGHEST, preferred_element_type=F32)
    rows = [total[:, :d], total[:, d : 2 * d]] + up_rows + [placed[0:1], placed[1:2], jnp.zeros((LANES - 8, d), F32)]
    return jnp.concatenate(rows, axis=0).T


def weight_grad_kernel(d, ff, idx, place, mine, theirs, kept, got, *refs):
    results, (big_v, a_v, b_v, c_v, out_v, ins, outs) = refs[:4], refs[4:]
    rows = kept.shape[0]
    tokens = 2 * rows
    quarter, half, third = WIDE // 4, ff // 2, ff // 3
    blocks = third // WIDE
    share = d // 16
    cut = 3 * d
    y, z, core = idx[0], idx[1], idx[2]

    def load(cin, at, width, to, to_at):
        return [cin.start(src.at[:, pl.ds(at, width)], to.at[i, :, pl.ds(to_at, width)]) for i, src in enumerate((kept, got))]

    def wait(copies):
        for copy in copies:
            copy.wait()

    def both(ref, at=0, width=d):
        return ref[:, :, at : at + width].reshape(tokens, width)

    def put(rows_at, cols_at, value):
        out_v[rows_at, cols_at] = value.astype(BF)

    def send_by_y(cout, at, width):
        cols = pl.ds(at, width)
        return [cout.start(out_v.at[pl.ds(pl.multiple_of(lax.rem(y + s, 4) * 4 * share, 16), 4 * share), cols], results[s].at[:, cols])
                for s in (2, 1, 3, 0)]

    def send_by_z(cout, at, width):
        cols = pl.ds(at, width)
        return [
            cout.start(out_v.at[pl.ds(pl.multiple_of((4 * i + lax.rem(z + s, 4)) * share, 16), share), cols],
                       results[s].at[pl.ds(share * i, share), cols])
            for s in (2, 1, 3, 0) for i in range(4)
        ]

    everything = slice(0, d)

    @pl.when(core == 0)
    def _():
        cin, cout = Copies(ins), Copies(outs)
        grads = load(cin, ff, d, a_v, 0)
        loads = [load(cin, third * k, third, big_v, third * k) for k in range(3)]
        attended = load(cin, ff + 3 * d, d, b_v, 0)
        hidden, values = load(cin, ff + 2 * d, d, c_v, 0), load(cin, ff + d, d, c_v, d)
        wait(grads)
        gb = both(a_v)
        for k in range(3):
            wait(loads[k])
            found = lax.dot_general(both(big_v, third * k, third), gb, TN, preferred_element_type=F32).astype(BF)
            for b in range(blocks):
                at = quarter * (blocks * k + b)
                for j in range(4):
                    put(slice(at, at + quarter), slice(d * j, d * j + d), found[WIDE * b + quarter * j : WIDE * b + quarter * (j + 1)])
        pending = send_by_y(cout, 0, 4 * d)
        wait(attended)
        put(everything, slice(4 * d, 5 * d), lax.dot_general(both(b_v), gb, TN, preferred_element_type=F32))
        wait(hidden + values)
        put(everything, slice(5 * d, 6 * d), lax.dot_general(both(c_v), both(c_v, d), TN, preferred_element_type=F32))
        put(everything, slice(6 * d, 6 * d + LANES), split_small(small_table(d, ff, place, mine, theirs)))
        wait(pending + send_by_y(cout, 4 * d, 2 * d + LANES))

    @pl.when(core == 1)
    def _():
        cin, cout = Copies(ins), Copies(outs)
        hidden = load(cin, ff + 2 * d, d, a_v, 0)
        loads = [load(cin, third * k, third, big_v, third * k) for k in range(2)]
        queries = load(cin, ff, d, b_v, 0)
        loads.append(load(cin, 2 * third, third, big_v, 2 * third))
        keys = load(cin, ff + d, d, c_v, 0)
        wait(hidden)
        turned = both(a_v).T
        pending = []
        for k in range(2):
            wait(loads[k])
            put(everything, slice(third * k, third * k + third), mm(turned, both(big_v, third * k, third)))
        pending = send_by_z(cout, 0, 2 * third)
        wait(queries)
        put(everything, slice(ff, ff + d), mm(turned, both(b_v)))
        wait(loads[2])
        put(everything, slice(2 * third, ff), mm(turned, both(big_v, 2 * third, third)))
        wait(keys)
        put(everything, slice(ff + d, ff + 2 * d), mm(turned, both(c_v)))
        out_v[:, 6 * d :] = jnp.zeros((d, LANES), BF)
        wait(pending + send_by_z(cout, 2 * third, 6 * d + LANES - 2 * third))


def added(parts):
    total = parts[0][...].astype(F32)
    for part in parts[1:]:
        total = total + part[...].astype(F32)
    shape = total.shape
    total = total.reshape(-1, shape[-1])
    main, last = total[:, : shape[-1] - LANES], split_small(joined_small(total[:, shape[-1] - LANES :]))
    return jnp.concatenate([main.astype(BF), last], axis=1).reshape(shape)


def mid_kernel(idx, *refs):
    came, outs, hold = refs[:4], refs[4:8], refs[8]
    hold[...] = added(came).reshape(hold.shape)
    at = jnp.where(idx[2] == 0, idx[1], idx[0])
    for s in range(4):
        outs[s][...] = hold[lax.rem(at + s, 4)]


def last_kernel(idx, *refs):
    layers, (home_mine, home_other, away_mine, away_other), holds = (refs[:4], refs[4:8]), refs[8:12], refs[12:]
    core, odd = idx[2], idx[4]
    for came, hold in zip(layers, holds):
        hold[...] = added(came).astype(F32)
    count = home_mine.shape[0]

    def rows_of(hold, which):
        return hold[pl.ds(pl.multiple_of(which * count, 8), count), :]

    for which, home, away in ((core, home_mine, away_mine), (1 - core, home_other, away_other)):
        lower, upper = rows_of(holds[0], which), rows_of(holds[1], which)
        home[...] = jnp.where(odd == 1, upper, lower).astype(home.dtype)
        away[...] = jnp.where(odd == 1, lower, upper).astype(away.dtype)


def place_kernel(idx, y_in, y_got, g_in, g_got, y_out, g_out, sems):
    copies = Copies(sems)
    for copy in [copies.start(y_got, y_out.at[1 - idx[3]]), copies.start(g_got, g_out.at[1 - idx[3]])]:
        copy.wait()


def picked(rows, columns, wanted):
    row = lax.broadcasted_iota(jnp.int32, (rows, columns), 0)
    column = lax.broadcasted_iota(jnp.int32, (rows, columns), 1)
    return row, column, jnp.where(column == wanted(row), 1.0, 0.0)


def prepare_kernel(d, ff, p_in, p_attn, p_down, n_gain, o_bias, u_bias, q_gain, k_gain, shuffle, out):
    share = p_in.shape[0]
    heads_part = p_in.shape[1] - ff
    for at in range(0, ff, WIDE):
        out[:, at : at + WIDE] = mm(p_in[:, heads_part + at : heads_part + at + WIDE], shuffle[...]).astype(BF)
    out[:, ff : ff + heads_part] = p_in[:, :heads_part]
    at = ff + heads_part
    out[:, at : at + d] = p_attn[...]
    down = p_down[...]
    for j in range(4):
        take = picked(share, down.shape[0], lambda row: 4 * row + j)[2].astype(BF)
        out[:, at + d * (j + 1) : at + d * (j + 2)] = mm(take, down).astype(BF)

    def column_of(ref, wanted, where):
        values = ref[...].astype(F32)
        take = picked(share, values.shape[1], wanted)[2]
        lane = lax.broadcasted_iota(jnp.int32, (share, LANES), 1)
        return jnp.where(lane == where, jnp.sum(take * values, axis=1, keepdims=True), 0.0)

    table = column_of(n_gain, lambda row: row, 0) + column_of(o_bias, lambda row: row, 1)
    for j in range(4):
        table = table + column_of(u_bias, lambda row: 4 * row + j, 2 + j)
    table = table + column_of(q_gain, lambda row: row, 6) + column_of(k_gain, lambda row: row, 7)
    out[:, at + 5 * d :] = table.astype(BF)


def smalls_kernel(d, ff, base, stride, g, place, ngain, gains, ubias, obias, t_v, sems):
    copies = Copies(sems)
    loads = [copies.start(g.at[:, pl.ds(base + stride * layer, LANES)], t_v.at[layer]) for layer in range(2)]
    quarter = WIDE // 4
    for layer in range(2):
        loads[layer].wait()
        table = t_v[layer].astype(F32).T
        ngain[layer] = table[0:1]
        obias[layer] = table[1:2]
        pieces = [table[2 + j : 3 + j, quarter * b : quarter * (b + 1)] for b in range(ff // WIDE) for j in range(4)]
        ubias[layer] = jnp.concatenate(pieces, axis=1)
        both = mm(table[0:8].astype(BF), place[...])
        gains[layer, 0] = both[6:7]
        gains[layer, 1] = both[7:8]


def finish_kernel(d, ff, idx, own, a_in, b_in, c_in, shuffle, g_in, g_attn, g_down, g_ng, g_q, g_k, g_ub, g_ob):
    core = idx[2]
    share = own.shape[0]
    mine = own[...] + a_in[...].astype(F32)
    theirs = b_in[...].astype(F32) + c_in[...].astype(F32)
    half0 = jnp.where(core == 0, mine, theirs)
    half1 = jnp.where(core == 0, theirs, mine)
    g_in[:, : 2 * d] = half1[:, ff : ff + 2 * d]
    g_in[:, 2 * d : 3 * d] = half0[:, 5 * d : 6 * d]
    for at in range(0, ff, WIDE):
        g_in[:, 3 * d + at : 3 * d + at + WIDE] = lax.dot_general(
            half1[:, at : at + WIDE], shuffle[...], NT, precision=lax.Precision.HIGHEST, preferred_element_type=F32)
    g_attn[...] = half0[:, 4 * d : 5 * d]
    stacked = jnp.concatenate([half0[:, at : at + d] for at in range(0, 4 * d, d)], axis=0)
    row, column, _ = picked(4 * share, 4 * share, lambda row: row)
    turn = jnp.where(column == lax.rem(row, 4) * share + row // 4, 1.0, 0.0)
    g_down[...] = lax.dot_general(turn, stacked, NN, precision=lax.Precision.HIGHEST, preferred_element_type=F32)
    small = joined_small(half0[:, 6 * d :])
    turned = jnp.concatenate([small, jnp.zeros((LANES - share, LANES), F32)], axis=0).T
    g_ng[...] = turned[0:1, :share]
    g_ob[...] = turned[1:2, :share]
    g_q[...] = turned[6:7, : g_q.shape[1]]
    g_k[...] = turned[7:8, : g_k.shape[1]]
    total = jnp.zeros((8, 4 * share), F32)
    for j in range(4):
        row, column, _ = picked(LANES, 4 * share, lambda row: row)
        spread_out = jnp.where(column == 4 * row + j, 1.0, 0.0)
        total = total + jnp.where(lax.broadcasted_iota(jnp.int32, (8, 4 * share), 0) == 2 + j, 1.0, 0.0) * lax.dot_general(
            turned[0:8], spread_out, NN, precision=lax.Precision.HIGHEST, preferred_element_type=F32)
    g_ub[...] = jnp.sum(total, axis=0, keepdims=True)


ANY = pl.BlockSpec(memory_space=pl.ANY)


def whole(shape):
    return pl.BlockSpec(shape, lambda i, idx: (0,) * len(shape))


def pick(shape):
    return pl.BlockSpec((1,) + shape, lambda i, idx: (idx[2],) + (0,) * len(shape))


def call(kernel, idx, ins, fresh, stashes, scratch, flops):
    outs = pl.pallas_call(
        kernel,
        grid_spec=pltpu.PrefetchScalarGridSpec(
            num_scalar_prefetch=1,
            grid=(1,),
            in_specs=[s for _, s in ins] + [ANY] * len(stashes),
            out_specs=[whole(fresh[0])] + [ANY] * len(stashes),
            scratch_shapes=scratch,
        ),
        out_shape=[jax.ShapeDtypeStruct(*fresh)] + [jax.ShapeDtypeStruct(a.shape, a.dtype) for a in stashes],
        input_output_aliases={1 + len(ins) + i: 1 + i for i in range(len(stashes))},
        compiler_params=pltpu.CompilerParams(dimension_semantics=("arbitrary",), vmem_limit_bytes=VMEM_LIMIT),
        cost_estimate=pl.CostEstimate(flops=flops, bytes_accessed=1 << 10, transcendentals=0),
    )(idx, *[a for a, _ in ins], *stashes)
    return outs[0], list(outs[1:])


def plain(kernel, arrays, specs, out_shapes, out_specs, scratch):
    return pl.pallas_call(
        kernel, grid=(1,), in_specs=specs, out_specs=out_specs, scratch_shapes=scratch, out_shape=out_shapes,
        compiler_params=pltpu.CompilerParams(dimension_semantics=("arbitrary",), vmem_limit_bytes=VMEM_LIMIT),
        cost_estimate=pl.CostEstimate(flops=1 << 10, bytes_accessed=1 << 10, transcendentals=0),
    )(*arrays)


def simple(kernel, idx, arrays, specs, out_shapes, out_specs, scratch, flops=1 << 10):
    return pl.pallas_call(
        kernel,
        grid_spec=pltpu.PrefetchScalarGridSpec(
            num_scalar_prefetch=1, grid=(1,), in_specs=specs, out_specs=out_specs, scratch_shapes=scratch
        ),
        out_shape=out_shapes,
        compiler_params=pltpu.CompilerParams(dimension_semantics=("arbitrary",), vmem_limit_bytes=VMEM_LIMIT),
        cost_estimate=pl.CostEstimate(flops=flops, bytes_accessed=1 << 10, transcendentals=0),
    )(idx, *arrays)


def along(x, step, size, by):
    devices = lax.axis_size("dp")

    def to(i):
        digit = i // step % size
        return i + ((digit + by) % size - digit) * step

    return lax.ppermute(x, "dp", [(i, to(i)) for i in range(devices)])


def paired(x):
    return lax.ppermute(x, "section", [(0, 1), (1, 0), (2, 3), (3, 2)])


def body(tokens, cotangent, lengths, proj_in, proj_attn, proj_down, norm_gain, query_gain, key_gain, up_bias, out_bias):
    ranks = lax.axis_size("dp")
    section = lax.axis_index("section")
    rank = lax.axis_index("dp")
    slots = lengths.shape[0]
    rows = tokens.shape[0] // slots
    d = tokens.shape[1]
    joined = proj_in.shape[2]
    ff = proj_down.shape[1] * ranks
    head = query_gain.shape[1] * ranks
    heads = d // head
    dshare = proj_in.shape[1]
    fshare = proj_down.shape[1] // dshare
    hshare = query_gain.shape[1]
    chunks = 3
    wide = joined + d + ff
    stride = wide + LANES
    side = math.isqrt(ranks // 2)
    core, z, y = lax.rem(rank, 2), lax.rem(rank // 2, side), rank // (2 * side)
    stage, odd = section // 2, lax.rem(section, 2)
    slot = lax.rem(stage + odd, 2)

    place = jnp.arange(WIDE, dtype=jnp.int32)
    source = (place % (WIDE // fshare)) * fshare + place // (WIDE // fshare)
    shuffle = (place[:, None] == source[None, :]).astype(BF)

    def full(a):
        return pl.BlockSpec(a.shape, lambda i: (0,) * a.ndim)

    shares = [proj_in[0], proj_attn[0], proj_down[0], norm_gain, out_bias, up_bias, query_gain, key_gain, shuffle]
    heads_part = joined - ff
    local = jax.ShapeDtypeStruct((dshare, stride), BF)
    local = plain(partial(prepare_kernel, d, ff), shares, [full(a) for a in shares], local, full(local), [])
    other = paired(local)
    both = jnp.where(odd == 0, jnp.concatenate([local, other], axis=1), jnp.concatenate([other, local], axis=1))
    g = lax.all_gather(both, "dp", axis=0, tiled=True)
    g3 = g.reshape(ff // WIDE, WIDE // fshare, g.shape[1])
    element = jnp.arange(d, dtype=jnp.int32) % head
    spread_gain = (jnp.arange(d, dtype=jnp.int32)[:, None] == (element // hshare * dshare + element % hshare)[None, :]).astype(BF)
    tables = [jax.ShapeDtypeStruct(s, F32) for s in ((2, 1, d), (2, 2, 1, d), (2, 1, ff), (2, 1, d))]
    ngain, gains, ubias, obias = plain(
        partial(smalls_kernel, d, ff, wide, stride), [g, spread_gain], [ANY, full(spread_gain)], tables,
        [full(a) for a in tables], [pltpu.VMEM((2, d, LANES), BF), pltpu.SemaphoreType.DMA((2,))],
    )

    def of_layer(a, layer):
        return (a, pl.BlockSpec((None,) + a.shape[1:], lambda i, idx: (layer,) + (0,) * (a.ndim - 1)))

    column = jnp.arange(WIDE, dtype=jnp.int32) // head
    spread = jnp.where(column[:, None] == column[None, :], 1.0 / head, 0.0).astype(BF)

    toks = tokens.reshape(slots, rows, d)
    seeds = cotangent.reshape(slots, rows, d)
    ends = jnp.cumsum(lengths, axis=-1)
    position = jnp.arange(rows, dtype=jnp.int32)
    image = jnp.sum((position[None, :, None] >= ends[:, None, :]).astype(jnp.int32), axis=-1)
    image = jnp.where(position[None, :] < ends[:, 2:3], image, ABSENT + position[None, :])
    ids_col, ids_row = image[:, :, None], image[:, None, :]

    def stash(*shape, dtype=BF):
        return pl.pallas_call(
            lambda out: None, out_shape=jax.ShapeDtypeStruct(shape, dtype), out_specs=pl.BlockSpec(memory_space=pl.ANY)
        )()

    fc = ff // chunks
    groups = ff // WIDE

    def index_of(layer, active_stage):
        return jnp.stack([stage == active_stage, core, slot, odd == layer]).astype(jnp.int32)

    V = pltpu.VMEM
    weights_v = [V((d, heads_part), BF), V((chunks, d, fc), BF), V((groups, fshare, WIDE // fshare, d), BF), V((d, d), BF)]
    sems = [pltpu.SemaphoreType.DMA((48,)), pltpu.SemaphoreType.DMA((48,))]
    stacked = ff + 4 * d
    operands = [[stash(rows, stacked), stash(rows, stacked)] for _ in range(2)]
    kept = [[stash(rows, d) for _ in range(4)] + [stash(rows, 2 * d), stash(rows, 2 * d), stash(chunks, rows, fc),
             stash(heads, rows, rows), stash(16, rows, dtype=F32)] for _ in range(2)]
    results = [stash(slots, rows, d, dtype=F32), stash(rows, d, dtype=F32)]
    here_x = toks
    for t in range(4):
        layer = t % 2
        ybf, done = call(
            partial(forward_kernel, d, ff, chunks, stride * layer, t == 0),
            index_of(layer, t // 2),
            [(here_x, ANY), (g, ANY), (g3, ANY), (ids_col, pick((rows, 1))), (ids_row, pick((1, rows))),
             of_layer(ngain, layer), of_layer(gains, layer), of_layer(ubias, layer), of_layer(obias, layer),
             (spread, whole((WIDE, WIDE)))],
            ((rows, d), BF),
            kept[layer][:9] + operands[layer] + results,
            [V((rows, d), BF), V((rows, d), BF)] + weights_v
            + [V((rows, d), BF)] * 3 + [V((rows, 2 * d), BF)] * 2 + [V((chunks, rows, fc), BF)] * 2
            + [V((heads, rows, rows), BF), V((16, rows), F32), V((rows, d), BF), V((rows, d), F32), V((rows, d), F32)]
            + sems,
            1 << 10,
        )
        kept[layer], operands[layer], results = done[:9], done[9:11], done[11:]
        here_x = lax.ppermute(ybf, "section", [(0, 3), (1, 2)]) if t == 1 else ybf
    y_out, y_send = results
    y_got = paired(y_send)

    results = [stash(slots, rows, d, dtype=F32), stash(rows, d, dtype=F32)]
    tables = [stash(1, stacked, dtype=F32) for _ in range(2)]
    width = 6 * d + LANES
    share = 2 * dshare
    position = jnp.arange(LANES, dtype=jnp.int32)[:, None] % head
    place = (position // hshare * dshare + position % hshare == jnp.arange(d, dtype=jnp.int32)[None, :]).astype(F32)
    here = jnp.stack([y, z, core, slot, odd]).astype(jnp.int32)

    def moved(x, leg, by):
        def to(i):
            step = 2 * side if i % 2 == leg else 2
            digit = i // step % side
            return i + ((digit + by) % side - digit) * step

        return lax.ppermute(x, "dp", [(i, to(i)) for i in range(ranks)])

    def grads_by_place(layer, got, table_got):
        return simple(
            partial(weight_grad_kernel, d, ff), here,
            [place, tables[layer], table_got, operands[layer][0], got],
            [whole((LANES, d)), whole(table_got.shape), whole(table_got.shape), ANY, ANY],
            [jax.ShapeDtypeStruct((side * share, width), BF)] * side, [ANY] * side,
            [V((2, rows, ff), BF), V((2, rows, d), BF), V((2, rows, d), BF), V((2, rows, 2 * d), BF), V((d, width), BF),
             pltpu.SemaphoreType.DMA((32,)), pltpu.SemaphoreType.DMA((32,))],
        )

    def leg(outs, which):
        far, near, back = (moved(outs[s], which, s) for s in (2, 1, 3))
        return [outs[0], near, far, back]

    def by_second_axis(came):
        return simple(
            mid_kernel, here, came, [whole(a.shape) for a in came],
            [jax.ShapeDtypeStruct((share, width), BF)] * side, [whole((share, width))] * side, [V((side, share, width), BF)],
        )

    here_g = seeds
    swaps = []
    for t in range(4):
        layer = 1 - t % 2
        gbf, done = call(
            partial(backward_kernel, d, ff, chunks, stride * layer, t == 0),
            index_of(layer, 1 - t // 2),
            [(here_g, ANY), (g, ANY), (g3, ANY), (ids_col, pick((rows, 1))), of_layer(ngain, layer), of_layer(gains, layer),
             (spread, whole((WIDE, WIDE)))] + [(a, ANY) for a in kept[layer]],
            ((rows, d), BF),
            operands[layer] + [tables[layer]] + results,
            [V((rows, d), BF), V((rows, d), BF)] + weights_v
            + [V((rows, d), BF)] * 4 + [V((rows, 2 * d), BF)] * 2
            + [V((chunks, rows, fc), BF), V((heads, rows, rows), BF), V((16, rows), F32)]
            + [V((d, rows), BF), V((d, rows), F32), V((rows, d), F32)]
            + [V((rows, d), BF)] * 3 + [V((chunks, rows, fc), BF), V((rows, d), F32), V((rows, d), F32), V((1, stacked), F32)]
            + sems,
            1 << 10,
        )
        operands[layer], tables[layer], results = done[:2], done[2], done[3:]
        here_g = lax.ppermute(gbf, "section", [(3, 0), (2, 1)]) if t == 1 else gbf
        if t == 1:
            here_g, y_got = lax.optimization_barrier((here_g, y_got))
        if t == 3:
            operands[layer][1], swaps[0] = lax.optimization_barrier((operands[layer][1], swaps[0]))
        if t >= 2:
            swaps.append((along(operands[layer][1], 1, 2, 1), along(tables[layer], 1, 2, 1)))
    gr_got = paired(results[1])
    legs = [leg(grads_by_place(1, *swaps[0]), 0), leg(grads_by_place(0, *swaps[1]), 0)]
    legs[1], gr_got = lax.optimization_barrier((legs[1], gr_got))
    arrived = [leg(by_second_axis(came), 1) for came in legs]
    gr_out = results[0]
    y_out, gr_out = pl.pallas_call(
        place_kernel,
        grid_spec=pltpu.PrefetchScalarGridSpec(
            num_scalar_prefetch=1, grid=(1,), in_specs=[ANY, whole((rows, d)), ANY, whole((rows, d))], out_specs=[ANY] * 2,
            scratch_shapes=[pltpu.SemaphoreType.DMA((2,))],
        ),
        out_shape=[jax.ShapeDtypeStruct(y_out.shape, F32)] * 2,
        input_output_aliases={1: 0, 3: 1},
    )(here, y_out, y_got, gr_out, gr_got)

    both = arrived[1] + arrived[0]
    home_mine, home_other, away_mine, away_other = simple(
        last_kernel, here, both, [whole(a.shape) for a in both],
        [jax.ShapeDtypeStruct((dshare, width), t) for t in (F32, BF, BF, BF)], [whole((dshare, width))] * 4,
        [V((share, width), F32)] * 2,
    )
    sections = lax.axis_size("section")
    cross = [(s * ranks + i, (s ^ 1) * ranks + (i ^ 1)) for s in range(sections) for i in range(ranks)]
    arrays = [home_mine, paired(away_mine), along(home_other, 1, 2, 1), lax.ppermute(away_other, ("section", "dp"), cross),
              shuffle.astype(F32)]
    shapes = [(dshare, joined), (dshare, d), (dshare * fshare, d), (1, dshare), (1, hshare), (1, hshare), (1, dshare * fshare),
              (1, dshare)]
    g_in, g_attn, g_down, g_ng, g_q, g_k, g_ub, g_ob = simple(
        partial(finish_kernel, d, ff), here, arrays, [whole(a.shape) for a in arrays],
        [jax.ShapeDtypeStruct(s, F32) for s in shapes], [whole(s) for s in shapes], [],
    )
    return (y_out.reshape(1, slots * rows, d), gr_out.reshape(1, slots * rows, d), g_in[None], g_attn[None], g_down[None],
            g_ng, g_q, g_k, g_ub, g_ob)


def solution(mesh):
    in_specs = (P("dp", None),) * 3 + (P("section", "dp", None),) * 3 + (P("section", "dp"),) * 5
    out_specs = (P("section", "dp", None),) * 5 + (P("section", "dp"),) * 5
    return jax.shard_map(body, mesh=mesh, in_specs=in_specs, out_specs=out_specs, check_vma=False)
```

```python
from functools import partial
import math

import jax
import jax.numpy as jnp
from jax import lax
from jax.experimental import pallas as pl
from jax.experimental.pallas import tpu as pltpu
from jax.sharding import PartitionSpec as P

BF = jnp.bfloat16
F32 = jnp.float32
VMEM_LIMIT = 60 * 1024 * 1024
EPS = 1e-06
NN = (((1,), (0,)), ((), ()))
NT = (((1,), (1,)), ((), ()))
TN = (((0,), (0,)), ((), ()))
LANES = 128
WIDE = 256
ABSENT = 16


def mm(a, b, dims=NN):
    return lax.dot_general(a, b, dims, preferred_element_type=F32)


def head_mean(x, spread, exact):
    parts = []
    for at in range(0, x.shape[1], WIDE):
        piece = x[:, at : at + WIDE]
        top = piece.astype(BF)
        total = mm(top, spread)
        if exact:
            total = total + mm((piece - top.astype(F32)).astype(BF), spread)
        parts.append(total)
    return jnp.concatenate(parts, axis=1)


def row_norm(x):
    centered = x - jnp.mean(x, axis=-1, keepdims=True)
    rstd = lax.rsqrt(jnp.mean(centered * centered, axis=-1, keepdims=True) + EPS)
    return centered * rstd, rstd


def norm_back(grad, normal, rstd, spread):
    return rstd * (grad - head_mean(grad, spread, False) - normal * head_mean(grad * normal, spread, False))


def lane_half(x, second):
    lane = lax.broadcasted_iota(jnp.int32, x.shape, 1)
    return jnp.where((lane >= LANES // 2) if second else (lane < LANES // 2), x, jnp.zeros_like(x))


class Copies:
    def __init__(self, sems):
        self.sems, self.used = sems, 0

    def start(self, src, dst):
        copy = pltpu.make_async_copy(src, dst, self.sems.at[self.used])
        self.used += 1
        copy.start()
        return copy

    def either(self, flag, src, yes, no):
        sem = self.sems.at[self.used]
        self.used += 1

        @pl.when(flag == 1)
        def _():
            pltpu.make_async_copy(src, yes, sem).start()

        @pl.when(flag != 1)
        def _():
            pltpu.make_async_copy(src, no, sem).start()

        return pltpu.make_async_copy(src, yes, sem)


def result_out(home, value, result, rounded, send, copies):
    sem = copies.sems.at[copies.used]
    copies.used += 1

    @pl.when(home == 1)
    def _():
        copy = pltpu.make_async_copy(value, result, sem)
        copy.start()
        copy.wait()

    @pl.when(home != 1)
    def _():
        copy = pltpu.make_async_copy(rounded, send, sem)
        copy.start()
        copy.wait()


def forward_kernel(d, ff, chunks, base, first, idx, x_in, g, g3, ids_col, ids_row, ngain, gains, ubias, obias, spread, *refs):
    @pl.when(idx[0] == 1)
    def _():
        forward_work(d, ff, chunks, base, first, idx, x_in, g, g3, ids_col, ids_row, ngain, gains, ubias, obias, spread, *refs)


def forward_work(d, ff, chunks, base, first, idx, x_in, g, g3, ids_col, ids_row, ngain, gains, ubias, obias, spread, *refs):
    refs = refs[13:]
    ybf, xs, qs, ks, vs, ns, nrs, gps, es, small, kept, sent, y_out, y_send = refs[:14]
    (x_v, h_v, w_v, u_v, d_v, a_v, q_v, k_v, v_v, n_v, r_v, act_v, gp_v, e_v, rs_v, att_v, acc_v, y_v, yb_v, ins, outs) = refs[14:]
    rows = x_v.shape[0]
    fc = ff // chunks
    core, slot, home = idx[1], idx[2], idx[3]
    cin, cout = Copies(ins), Copies(outs)
    x_copy = cin.start(x_in.at[slot] if first else x_in, x_v)
    wq = [cin.start(g.at[:, pl.ds(base + ff + d * i, d)], w_v.at[:, pl.ds(d * i, d)]) for i in range(3)]
    groups = fc // WIDE
    wff = []
    for c in range(chunks):
        wff.append([cin.start(g.at[:, pl.ds(base + fc * c, fc)], u_v.at[c])] + [
            cin.start(g3.at[pl.ds(groups * c, groups), :, pl.ds(base + ff + 4 * d + d * j, d)], d_v.at[pl.ds(groups * c, groups), j])
            for j in range(4)
        ])
    wa = cin.start(g.at[:, pl.ds(base + ff + 3 * d, d)], a_v)

    pending = []

    def side(i):
        return pl.ds(ff + d * i, d)

    x_copy.wait()
    keep = jnp.where(ids_col[0] < ABSENT, 1.0, 0.0)
    masked = keep * x_v[...].astype(F32)
    h_v[...] = (row_norm(masked)[0] * ngain[...]).astype(BF)
    pending += [cout.start(x_v, xs), cout.start(h_v, kept.at[:, side(2)]), cout.start(h_v, sent.at[:, side(2)])]
    bias_mask = jnp.where(ids_col[0] == ids_row[0], 0.0, -1e9)
    for i in range(3):
        wq[i].wait()
        raw = mm(h_v[...], w_v[:, d * i : d * i + d])
        if i == 2:
            v_v[...] = raw.astype(BF)
            pending.append(cout.start(v_v, vs))
        else:
            centered = raw - head_mean(raw, spread[...], True)
            rstd = lax.rsqrt(head_mean(centered * centered, spread[...], True) + EPS)
            normal = centered * rstd
            scaled = (normal * gains[i]).astype(BF)
            n_v[:, d * i : d * i + d] = normal.astype(BF)
            r_v[:, d * i : d * i + d] = rstd.astype(BF)
            if i == 0:
                q_v[...] = scaled * jnp.asarray(0.125, BF)
                pending.append(cout.start(q_v, qs))
            else:
                k_v[...] = scaled
                pending.append(cout.start(k_v, ks))
    pending += [cout.start(n_v, ns), cout.start(r_v, nrs)]
    ones = jnp.ones((16, rows), BF)
    pairs = d // LANES // chunks
    for c in range(chunks):
        for copy in wff[c]:
            copy.wait()
        pre = mm(h_v[...], u_v[c]) + ubias[:, fc * c : fc * c + fc]
        cdf = 0.5 * (1.0 + lax.erf(pre * (1.0 / math.sqrt(2.0))))
        density = jnp.exp(-0.5 * pre * pre) * (1.0 / math.sqrt(2.0 * math.pi))
        act = (pre * cdf).astype(BF)
        act_v[c] = act
        gp_v[c] = (cdf + pre * density).astype(BF)
        total = mm(act, d_v[groups * c : groups * c + groups].reshape(fc, d))
        if c == 0:
            acc_v[...] = total
        else:
            acc_v[...] += total
        for p in range(pairs * c, pairs * c + pairs):
            cols = slice(LANES * p, LANES * p + LANES)
            vals_t = v_v[:, cols].T
            pair = q_v[:, cols]
            both = []
            for half in range(2):
                h = 2 * p + half
                e = jnp.exp(mm(k_v[:, cols], lane_half(pair, half), NT) + bias_mask).astype(BF)
                e_v[h] = e
                got = mm(jnp.concatenate([vals_t[64 * half : 64 * half + 64], ones], axis=0), e)
                inv = 1.0 / got[64:65]
                rs_v[h : h + 1, :] = inv
                both.append((got[:64] * inv).astype(BF))
            att_v[:, cols] = jnp.concatenate(both, axis=0).T
        span = pl.ds(fc * c, fc)
        pending += [cout.either(core, act_v.at[c], sent.at[:, span], kept.at[:, span]), cout.start(gp_v.at[c], gps.at[c]),
                    cout.start(e_v.at[pl.ds(2 * pairs * c, 2 * pairs)], es.at[pl.ds(2 * pairs * c, 2 * pairs)])]
    pending += [cout.start(rs_v, small), cout.either(core, att_v, sent.at[:, side(3)], kept.at[:, side(3)])]
    wa.wait()
    y = keep * (keep * x_v[...].astype(F32) + acc_v[...] + mm(att_v[...], a_v[...]) + obias[...])
    y_v[...] = y
    ybf[...] = y.astype(BF)
    yb_v[...] = y.astype(BF)
    result_out(home, y_v, y_out.at[slot], yb_v, y_send, cout)
    for copy in pending:
        copy.wait()


def backward_kernel(d, ff, chunks, base, first, idx, g_in, g, g3, ids_col, ngain, gains, spread, *refs):
    @pl.when(idx[0] == 1)
    def _():
        backward_work(d, ff, chunks, base, first, idx, g_in, g, g3, ids_col, ngain, gains, spread, *refs)


def backward_work(d, ff, chunks, base, first, idx, g_in, g, g3, ids_col, ngain, gains, spread, *refs):
    xs, qs, ks, vs, ns, nrs, gps, es, small = refs[:9]
    refs = refs[9 + 5 :]
    gbf, kept, sent, table, gr_out, gr_send = refs[:6]
    (g_v, gb_v, w_v, u_v, d_v, a_v, x_v, q_v, k_v, v_v, n_v, r_v, gp_v, e_v, rs_v, gat_v, gqt_v, gk_v,
     gq_b, gk_b, gv_b, gj_v, acc_v, out_v, ob_v, sm_v, ins, outs) = refs[6:]
    rows = x_v.shape[0]
    fc = ff // chunks
    groups = fc // WIDE
    core, slot, home = idx[1], idx[2], idx[3]
    cin, cout = Copies(ins), Copies(outs)
    g_copy = cin.start(g_in.at[slot] if first else g_in, g_v)
    wa = cin.start(g.at[:, pl.ds(base + ff + 3 * d, d)], a_v)
    heads = [cin.start(s, v) for s, v in ((small, rs_v), (ks, k_v), (vs, v_v), (qs, q_v))]
    pairs = d // LANES // chunks
    wff = []
    for c in range(chunks):
        wff.append(
            [cin.start(g3.at[pl.ds(groups * c, groups), :, pl.ds(base + ff + 4 * d + d * j, d)], d_v.at[pl.ds(groups * c, groups), j])
             for j in range(4)]
            + [cin.start(gps.at[c], gp_v.at[c]), cin.start(g.at[:, pl.ds(base + fc * c, fc)], u_v.at[c]),
               cin.start(es.at[pl.ds(2 * pairs * c, 2 * pairs)], e_v.at[pl.ds(2 * pairs * c, 2 * pairs)])]
        )
    norms = [cin.start(ns, n_v), cin.start(nrs, r_v)]
    wq = [cin.start(g.at[:, pl.ds(base + ff + d * i, d)], w_v.at[:, pl.ds(d * i, d)]) for i in range(3)]
    rows_in = cin.start(xs, x_v)

    pending = []

    def side(i):
        return pl.ds(ff + d * i, d)

    def summed(at, value):
        sm_v[:, at : at + value.shape[1]] = jnp.sum(value, axis=0, keepdims=True)

    g_copy.wait()
    keep = jnp.where(ids_col[0] < ABSENT, 1.0, 0.0)
    gres = keep * g_v[...].astype(F32)
    summed(d, gres)
    gb_v[...] = gres.astype(BF)
    pending.append(cout.either(core, gb_v, sent.at[:, side(0)], kept.at[:, side(0)]))
    wa.wait()
    gat_v[...] = mm(a_v[...], gb_v[...], NT).astype(BF)
    for copy in heads:
        copy.wait()
    zeros = jnp.zeros((LANES // 2, rows), BF)
    for c in range(chunks):
        for copy in wff[c]:
            copy.wait()
        gup = mm(gb_v[...], d_v[groups * c : groups * c + groups].reshape(fc, d), NT) * gp_v[c].astype(F32)
        summed(4 * d + fc * c, gup)
        gup = gup.astype(BF)
        gj_v[c] = gup
        span = pl.ds(fc * c, fc)
        pending.append(cout.either(core, gj_v.at[c], kept.at[:, span], sent.at[:, span]))
        total = mm(gup, u_v[c], NT)
        if c == 0:
            acc_v[...] = total
        else:
            acc_v[...] += total
        for p in range(pairs * c, pairs * c + pairs):
            cols = slice(LANES * p, LANES * p + LANES)
            keys, vals, pair = k_v[:, cols], v_v[:, cols], q_v[:, cols]
            keys_t = keys.T
            gk, gv = None, None
            for half in range(2):
                h = 2 * p + half
                at_rows = slice(64 * h, 64 * h + 64)
                inv = rs_v[h : h + 1, :]
                ga = (gat_v[at_rows, :].astype(F32) * inv).astype(BF)
                ga = jnp.concatenate([zeros, ga] if half else [ga, zeros], axis=0)
                e = e_v[h]
                ef = e.astype(F32)
                gp = ef * mm(vals, ga)
                dot = jnp.sum(gp, axis=0, keepdims=True) * inv
                gs = (gp - ef * dot).astype(BF)
                gk_h = mm(gs, lane_half(pair, half))
                gv_h = mm(e, ga, NT)
                gk = gk_h if gk is None else gk + gk_h
                gv = gv_h if gv is None else gv + gv_h
                gqt_v[at_rows, :] = mm(keys_t[64 * half : 64 * half + 64], gs) * 0.125
            gk_v[:, cols] = gk
            gv_b[:, cols] = gv.astype(BF)
    pending.append(cout.either(core, gv_b, sent.at[:, side(1)], kept.at[:, side(1)]))
    for copy in norms:
        copy.wait()
    for i, (grad, out) in enumerate(((gqt_v[...].T, gq_b), (gk_v[...], gk_b))):
        normal = n_v[:, d * i : d * i + d].astype(F32)
        summed(2 * d + d * i, grad * normal)
        out[...] = norm_back(grad * gains[i], normal, r_v[:, d * i : d * i + d].astype(F32), spread[...]).astype(BF)
        pending.append(cout.either(core, out, kept.at[:, side(i)], sent.at[:, side(i)]))
    for copy in wq:
        copy.wait()
    ghid = acc_v[...]
    for i, part in enumerate((gq_b, gk_b, gv_b)):
        ghid = ghid + mm(part[...], w_v[:, d * i : d * i + d], NT)
    rows_in.wait()
    xhat, rstd = row_norm(keep * x_v[...].astype(F32))
    summed(0, ghid * xhat)
    pending.append(cout.start(sm_v, table))
    gx = ghid * ngain[...]
    gmask = rstd * (gx - jnp.mean(gx, axis=-1, keepdims=True) - xhat * jnp.mean(gx * xhat, axis=-1, keepdims=True))
    out = keep * (keep * g_v[...].astype(F32) + gmask)
    out_v[...] = out
    gbf[...] = out.astype(BF)
    ob_v[...] = out.astype(BF)
    result_out(home, out_v, gr_out.at[slot], ob_v, gr_send, cout)
    for copy in pending:
        copy.wait()


def split_small(values):
    top = values.astype(BF).astype(F32)
    lane = lax.broadcasted_iota(jnp.int32, values.shape, 1)
    return jnp.where(lane < 8, top, jnp.where(lane < 16, pltpu.roll(values - top, 8, 1), 0.0)).astype(BF)


def joined_small(parts):
    return parts + pltpu.roll(parts, LANES - 8, 1)


def small_table(d, ff, place, mine, theirs):
    total = mine[...] + theirs[...]
    quarter = WIDE // 4
    ub = total[:, 4 * d :]
    up_rows = []
    for j in range(4):
        pieces = [ub[:, WIDE * b + quarter * j : WIDE * b + quarter * (j + 1)] for b in range(ff // WIDE)]
        up_rows.append(jnp.concatenate(pieces, axis=1))
    head_rows = []
    for i in range(2, 4):
        lanes = total[:, d * i : d * i + LANES]
        for p in range(1, d // LANES):
            lanes = lanes + total[:, d * i + LANES * p : d * i + LANES * (p + 1)]
        head_rows.append(lanes)
    both = jnp.concatenate(head_rows + [jnp.zeros((6, LANES), F32)], axis=0)
    placed = lax.dot_general(both, place[...], NN, precision=lax.Precision.HIGHEST, preferred_element_type=F32)
    rows = [total[:, :d], total[:, d : 2 * d]] + up_rows + [placed[0:1], placed[1:2], jnp.zeros((LANES - 8, d), F32)]
    return jnp.concatenate(rows, axis=0).T


def weight_grad_kernel(d, ff, idx, place, mine, theirs, kept, got, *refs):
    results, (big_v, a_v, b_v, c_v, out_v, ins, outs) = refs[:4], refs[4:]
    rows = kept.shape[0]
    tokens = 2 * rows
    quarter, half, third = WIDE // 4, ff // 2, ff // 3
    blocks = third // WIDE
    share = d // 16
    cut = 3 * d
    y, z, core = idx[0], idx[1], idx[2]

    def load(cin, at, width, to, to_at):
        return [cin.start(src.at[:, pl.ds(at, width)], to.at[i, :, pl.ds(to_at, width)]) for i, src in enumerate((kept, got))]

    def wait(copies):
        for copy in copies:
            copy.wait()

    def both(ref, at=0, width=d):
        return ref[:, :, at : at + width].reshape(tokens, width)

    def put(rows_at, cols_at, value):
        out_v[rows_at, cols_at] = value.astype(BF)

    def send_by_y(cout, at, width):
        cols = pl.ds(at, width)
        return [cout.start(out_v.at[pl.ds(pl.multiple_of(lax.rem(y + s, 4) * 4 * share, 16), 4 * share), cols], results[s].at[:, cols])
                for s in (2, 1, 3, 0)]

    def send_by_z(cout, at, width):
        cols = pl.ds(at, width)
        return [
            cout.start(out_v.at[pl.ds(pl.multiple_of((4 * i + lax.rem(z + s, 4)) * share, 16), share), cols],
                       results[s].at[pl.ds(share * i, share), cols])
            for s in (2, 1, 3, 0) for i in range(4)
        ]

    everything = slice(0, d)

    @pl.when(core == 0)
    def _():
        cin, cout = Copies(ins), Copies(outs)
        grads = load(cin, ff, d, a_v, 0)
        loads = [load(cin, third * k, third, big_v, third * k) for k in range(3)]
        attended = load(cin, ff + 3 * d, d, b_v, 0)
        hidden, values = load(cin, ff + 2 * d, d, c_v, 0), load(cin, ff + d, d, c_v, d)
        wait(grads)
        gb = both(a_v)
        for k in range(3):
            wait(loads[k])
            found = lax.dot_general(both(big_v, third * k, third), gb, TN, preferred_element_type=F32).astype(BF)
            for b in range(blocks):
                at = quarter * (blocks * k + b)
                for j in range(4):
                    put(slice(at, at + quarter), slice(d * j, d * j + d), found[WIDE * b + quarter * j : WIDE * b + quarter * (j + 1)])
        pending = send_by_y(cout, 0, 4 * d)
        wait(attended)
        put(everything, slice(4 * d, 5 * d), lax.dot_general(both(b_v), gb, TN, preferred_element_type=F32))
        wait(hidden + values)
        put(everything, slice(5 * d, 6 * d), lax.dot_general(both(c_v), both(c_v, d), TN, preferred_element_type=F32))
        put(everything, slice(6 * d, 6 * d + LANES), split_small(small_table(d, ff, place, mine, theirs)))
        wait(pending + send_by_y(cout, 4 * d, 2 * d + LANES))

    @pl.when(core == 1)
    def _():
        cin, cout = Copies(ins), Copies(outs)
        hidden = load(cin, ff + 2 * d, d, a_v, 0)
        loads = [load(cin, third * k, third, big_v, third * k) for k in range(2)]
        queries = load(cin, ff, d, b_v, 0)
        loads.append(load(cin, 2 * third, third, big_v, 2 * third))
        keys = load(cin, ff + d, d, c_v, 0)
        wait(hidden)
        turned = both(a_v).T
        pending = []
        for k in range(2):
            wait(loads[k])
            put(everything, slice(third * k, third * k + third), mm(turned, both(big_v, third * k, third)))
        pending = send_by_z(cout, 0, 2 * third)
        wait(queries)
        put(everything, slice(ff, ff + d), mm(turned, both(b_v)))
        wait(loads[2])
        put(everything, slice(2 * third, ff), mm(turned, both(big_v, 2 * third, third)))
        wait(keys)
        put(everything, slice(ff + d, ff + 2 * d), mm(turned, both(c_v)))
        out_v[:, 6 * d :] = jnp.zeros((d, LANES), BF)
        wait(pending + send_by_z(cout, 2 * third, 6 * d + LANES - 2 * third))


def added(parts):
    total = parts[0][...].astype(F32)
    for part in parts[1:]:
        total = total + part[...].astype(F32)
    shape = total.shape
    total = total.reshape(-1, shape[-1])
    main, last = total[:, : shape[-1] - LANES], split_small(joined_small(total[:, shape[-1] - LANES :]))
    return jnp.concatenate([main.astype(BF), last], axis=1).reshape(shape)


def mid_kernel(idx, *refs):
    came, outs, hold = refs[:4], refs[4:8], refs[8]
    hold[...] = added(came).reshape(hold.shape)
    at = jnp.where(idx[2] == 0, idx[1], idx[0])
    for s in range(4):
        outs[s][...] = hold[lax.rem(at + s, 4)]


def last_kernel(idx, *refs):
    layers, (home_mine, home_other, away_mine, away_other), holds = (refs[:4], refs[4:8]), refs[8:12], refs[12:]
    core, odd = idx[2], idx[4]
    for came, hold in zip(layers, holds):
        hold[...] = added(came).astype(F32)
    count = home_mine.shape[0]

    def rows_of(hold, which):
        return hold[pl.ds(pl.multiple_of(which * count, 8), count), :]

    for which, home, away in ((core, home_mine, away_mine), (1 - core, home_other, away_other)):
        lower, upper = rows_of(holds[0], which), rows_of(holds[1], which)
        home[...] = jnp.where(odd == 1, upper, lower).astype(home.dtype)
        away[...] = jnp.where(odd == 1, lower, upper).astype(away.dtype)


def place_kernel(idx, y_in, y_got, g_in, g_got, y_out, g_out, y_v, g_v, sems):
    copies = Copies(sems)
    pending = []
    for got, wide_v, out in ((y_got, y_v, y_out), (g_got, g_v, g_out)):
        wide_v[...] = got[...].astype(F32)
        pending.append(copies.start(wide_v, out.at[1 - idx[3]]))
    for copy in pending:
        copy.wait()


def picked(rows, columns, wanted):
    row = lax.broadcasted_iota(jnp.int32, (rows, columns), 0)
    column = lax.broadcasted_iota(jnp.int32, (rows, columns), 1)
    return row, column, jnp.where(column == wanted(row), 1.0, 0.0)


def prepare_kernel(d, ff, p_in, p_attn, p_down, n_gain, o_bias, u_bias, q_gain, k_gain, shuffle, out):
    share = p_in.shape[0]
    heads_part = p_in.shape[1] - ff
    for at in range(0, ff, WIDE):
        out[:, at : at + WIDE] = mm(p_in[:, heads_part + at : heads_part + at + WIDE], shuffle[...]).astype(BF)
    out[:, ff : ff + heads_part] = p_in[:, :heads_part]
    at = ff + heads_part
    out[:, at : at + d] = p_attn[...]
    down = p_down[...]
    for j in range(4):
        take = picked(share, down.shape[0], lambda row: 4 * row + j)[2].astype(BF)
        out[:, at + d * (j + 1) : at + d * (j + 2)] = mm(take, down).astype(BF)

    def column_of(ref, wanted, where):
        values = ref[...].astype(F32)
        take = picked(share, values.shape[1], wanted)[2]
        lane = lax.broadcasted_iota(jnp.int32, (share, LANES), 1)
        return jnp.where(lane == where, jnp.sum(take * values, axis=1, keepdims=True), 0.0)

    table = column_of(n_gain, lambda row: row, 0) + column_of(o_bias, lambda row: row, 1)
    for j in range(4):
        table = table + column_of(u_bias, lambda row: 4 * row + j, 2 + j)
    table = table + column_of(q_gain, lambda row: row, 6) + column_of(k_gain, lambda row: row, 7)
    out[:, at + 5 * d :] = table.astype(BF)


def smalls_kernel(d, ff, base, stride, g, place, ngain, gains, ubias, obias, t_v, sems):
    copies = Copies(sems)
    loads = [copies.start(g.at[:, pl.ds(base + stride * layer, LANES)], t_v.at[layer]) for layer in range(2)]
    quarter = WIDE // 4
    for layer in range(2):
        loads[layer].wait()
        table = t_v[layer].astype(F32).T
        ngain[layer] = table[0:1]
        obias[layer] = table[1:2]
        pieces = [table[2 + j : 3 + j, quarter * b : quarter * (b + 1)] for b in range(ff // WIDE) for j in range(4)]
        ubias[layer] = jnp.concatenate(pieces, axis=1)
        both = mm(table[0:8].astype(BF), place[...])
        gains[layer, 0] = both[6:7]
        gains[layer, 1] = both[7:8]


def finish_kernel(d, ff, idx, own, a_in, b_in, c_in, shuffle, g_in, g_attn, g_down, g_ng, g_q, g_k, g_ub, g_ob):
    core = idx[2]
    share = own.shape[0]
    mine = own[...] + a_in[...].astype(F32)
    theirs = b_in[...].astype(F32) + c_in[...].astype(F32)
    half0 = jnp.where(core == 0, mine, theirs)
    half1 = jnp.where(core == 0, theirs, mine)
    g_in[:, : 2 * d] = half1[:, ff : ff + 2 * d]
    g_in[:, 2 * d : 3 * d] = half0[:, 5 * d : 6 * d]
    for at in range(0, ff, WIDE):
        g_in[:, 3 * d + at : 3 * d + at + WIDE] = lax.dot_general(
            half1[:, at : at + WIDE], shuffle[...], NT, precision=lax.Precision.HIGHEST, preferred_element_type=F32)
    g_attn[...] = half0[:, 4 * d : 5 * d]
    stacked = jnp.concatenate([half0[:, at : at + d] for at in range(0, 4 * d, d)], axis=0)
    row, column, _ = picked(4 * share, 4 * share, lambda row: row)
    turn = jnp.where(column == lax.rem(row, 4) * share + row // 4, 1.0, 0.0)
    g_down[...] = lax.dot_general(turn, stacked, NN, precision=lax.Precision.HIGHEST, preferred_element_type=F32)
    small = joined_small(half0[:, 6 * d :])
    turned = jnp.concatenate([small, jnp.zeros((LANES - share, LANES), F32)], axis=0).T
    g_ng[...] = turned[0:1, :share]
    g_ob[...] = turned[1:2, :share]
    g_q[...] = turned[6:7, : g_q.shape[1]]
    g_k[...] = turned[7:8, : g_k.shape[1]]
    total = jnp.zeros((8, 4 * share), F32)
    for j in range(4):
        row, column, _ = picked(LANES, 4 * share, lambda row: row)
        spread_out = jnp.where(column == 4 * row + j, 1.0, 0.0)
        total = total + jnp.where(lax.broadcasted_iota(jnp.int32, (8, 4 * share), 0) == 2 + j, 1.0, 0.0) * lax.dot_general(
            turned[0:8], spread_out, NN, precision=lax.Precision.HIGHEST, preferred_element_type=F32)
    g_ub[...] = jnp.sum(total, axis=0, keepdims=True)


ANY = pl.BlockSpec(memory_space=pl.ANY)


def whole(shape):
    return pl.BlockSpec(shape, lambda i, idx: (0,) * len(shape))


def pick(shape):
    return pl.BlockSpec((1,) + shape, lambda i, idx: (idx[2],) + (0,) * len(shape))


def call(kernel, idx, ins, fresh, stashes, scratch, flops):
    outs = pl.pallas_call(
        kernel,
        grid_spec=pltpu.PrefetchScalarGridSpec(
            num_scalar_prefetch=1,
            grid=(1,),
            in_specs=[s for _, s in ins] + [ANY] * len(stashes),
            out_specs=[whole(fresh[0])] + [ANY] * len(stashes),
            scratch_shapes=scratch,
        ),
        out_shape=[jax.ShapeDtypeStruct(*fresh)] + [jax.ShapeDtypeStruct(a.shape, a.dtype) for a in stashes],
        input_output_aliases={1 + len(ins) + i: 1 + i for i in range(len(stashes))},
        compiler_params=pltpu.CompilerParams(dimension_semantics=("arbitrary",), vmem_limit_bytes=VMEM_LIMIT),
        cost_estimate=pl.CostEstimate(flops=flops, bytes_accessed=1 << 10, transcendentals=0),
    )(idx, *[a for a, _ in ins], *stashes)
    return outs[0], list(outs[1:])


def plain(kernel, arrays, specs, out_shapes, out_specs, scratch):
    return pl.pallas_call(
        kernel, grid=(1,), in_specs=specs, out_specs=out_specs, scratch_shapes=scratch, out_shape=out_shapes,
        compiler_params=pltpu.CompilerParams(dimension_semantics=("arbitrary",), vmem_limit_bytes=VMEM_LIMIT),
        cost_estimate=pl.CostEstimate(flops=1 << 10, bytes_accessed=1 << 10, transcendentals=0),
    )(*arrays)


def simple(kernel, idx, arrays, specs, out_shapes, out_specs, scratch, flops=1 << 10):
    return pl.pallas_call(
        kernel,
        grid_spec=pltpu.PrefetchScalarGridSpec(
            num_scalar_prefetch=1, grid=(1,), in_specs=specs, out_specs=out_specs, scratch_shapes=scratch
        ),
        out_shape=out_shapes,
        compiler_params=pltpu.CompilerParams(dimension_semantics=("arbitrary",), vmem_limit_bytes=VMEM_LIMIT),
        cost_estimate=pl.CostEstimate(flops=flops, bytes_accessed=1 << 10, transcendentals=0),
    )(idx, *arrays)


def along(x, step, size, by):
    devices = lax.axis_size("dp")

    def to(i):
        digit = i // step % size
        return i + ((digit + by) % size - digit) * step

    return lax.ppermute(x, "dp", [(i, to(i)) for i in range(devices)])


def paired(x):
    return lax.ppermute(x, "section", [(0, 1), (1, 0), (2, 3), (3, 2)])


def body(tokens, cotangent, lengths, proj_in, proj_attn, proj_down, norm_gain, query_gain, key_gain, up_bias, out_bias):
    ranks = lax.axis_size("dp")
    section = lax.axis_index("section")
    rank = lax.axis_index("dp")
    slots = lengths.shape[0]
    rows = tokens.shape[0] // slots
    d = tokens.shape[1]
    joined = proj_in.shape[2]
    ff = proj_down.shape[1] * ranks
    head = query_gain.shape[1] * ranks
    heads = d // head
    dshare = proj_in.shape[1]
    fshare = proj_down.shape[1] // dshare
    hshare = query_gain.shape[1]
    chunks = 3
    wide = joined + d + ff
    stride = wide + LANES
    side = math.isqrt(ranks // 2)
    core, z, y = lax.rem(rank, 2), lax.rem(rank // 2, side), rank // (2 * side)
    stage, odd = section // 2, lax.rem(section, 2)
    slot = lax.rem(stage + odd, 2)

    place = jnp.arange(WIDE, dtype=jnp.int32)
    source = (place % (WIDE // fshare)) * fshare + place // (WIDE // fshare)
    shuffle = (place[:, None] == source[None, :]).astype(BF)

    def full(a):
        return pl.BlockSpec(a.shape, lambda i: (0,) * a.ndim)

    shares = [proj_in[0], proj_attn[0], proj_down[0], norm_gain, out_bias, up_bias, query_gain, key_gain, shuffle]
    heads_part = joined - ff
    local = jax.ShapeDtypeStruct((dshare, stride), BF)
    local = plain(partial(prepare_kernel, d, ff), shares, [full(a) for a in shares], local, full(local), [])
    other = paired(local)
    both = jnp.where(odd == 0, jnp.concatenate([local, other], axis=1), jnp.concatenate([other, local], axis=1))
    g = lax.all_gather(both, "dp", axis=0, tiled=True)
    g3 = g.reshape(ff // WIDE, WIDE // fshare, g.shape[1])
    element = jnp.arange(d, dtype=jnp.int32) % head
    spread_gain = (jnp.arange(d, dtype=jnp.int32)[:, None] == (element // hshare * dshare + element % hshare)[None, :]).astype(BF)
    tables = [jax.ShapeDtypeStruct(s, F32) for s in ((2, 1, d), (2, 2, 1, d), (2, 1, ff), (2, 1, d))]
    ngain, gains, ubias, obias = plain(
        partial(smalls_kernel, d, ff, wide, stride), [g, spread_gain], [ANY, full(spread_gain)], tables,
        [full(a) for a in tables], [pltpu.VMEM((2, d, LANES), BF), pltpu.SemaphoreType.DMA((2,))],
    )

    def of_layer(a, layer):
        return (a, pl.BlockSpec((None,) + a.shape[1:], lambda i, idx: (layer,) + (0,) * (a.ndim - 1)))

    column = jnp.arange(WIDE, dtype=jnp.int32) // head
    spread = jnp.where(column[:, None] == column[None, :], 1.0 / head, 0.0).astype(BF)

    toks = tokens.reshape(slots, rows, d)
    seeds = cotangent.reshape(slots, rows, d)
    ends = jnp.cumsum(lengths, axis=-1)
    position = jnp.arange(rows, dtype=jnp.int32)
    image = jnp.sum((position[None, :, None] >= ends[:, None, :]).astype(jnp.int32), axis=-1)
    image = jnp.where(position[None, :] < ends[:, 2:3], image, ABSENT + position[None, :])
    ids_col, ids_row = image[:, :, None], image[:, None, :]

    def stash(*shape, dtype=BF):
        return pl.pallas_call(
            lambda out: None, out_shape=jax.ShapeDtypeStruct(shape, dtype), out_specs=pl.BlockSpec(memory_space=pl.ANY)
        )()

    fc = ff // chunks
    groups = ff // WIDE

    def index_of(layer, active_stage):
        return jnp.stack([stage == active_stage, core, slot, odd == layer]).astype(jnp.int32)

    V = pltpu.VMEM
    weights_v = [V((d, heads_part), BF), V((chunks, d, fc), BF), V((groups, fshare, WIDE // fshare, d), BF), V((d, d), BF)]
    sems = [pltpu.SemaphoreType.DMA((48,)), pltpu.SemaphoreType.DMA((48,))]
    stacked = ff + 4 * d
    operands = [[stash(rows, stacked), stash(rows, stacked)] for _ in range(2)]
    kept = [[stash(rows, d) for _ in range(4)] + [stash(rows, 2 * d), stash(rows, 2 * d), stash(chunks, rows, fc),
             stash(heads, rows, rows), stash(16, rows, dtype=F32)] for _ in range(2)]
    results = [stash(slots, rows, d, dtype=F32), stash(rows, d)]
    here_x = toks
    for t in range(4):
        layer = t % 2
        ybf, done = call(
            partial(forward_kernel, d, ff, chunks, stride * layer, t == 0),
            index_of(layer, t // 2),
            [(here_x, ANY), (g, ANY), (g3, ANY), (ids_col, pick((rows, 1))), (ids_row, pick((1, rows))),
             of_layer(ngain, layer), of_layer(gains, layer), of_layer(ubias, layer), of_layer(obias, layer),
             (spread, whole((WIDE, WIDE)))],
            ((rows, d), BF),
            kept[layer][:9] + operands[layer] + results,
            [V((rows, d), BF), V((rows, d), BF)] + weights_v
            + [V((rows, d), BF)] * 3 + [V((rows, 2 * d), BF)] * 2 + [V((chunks, rows, fc), BF)] * 2
            + [V((heads, rows, rows), BF), V((16, rows), F32), V((rows, d), BF), V((rows, d), F32), V((rows, d), F32), V((rows, d), BF)]
            + sems,
            1 << 10,
        )
        kept[layer], operands[layer], results = done[:9], done[9:11], done[11:]
        here_x = lax.ppermute(ybf, "section", [(0, 3), (1, 2)]) if t == 1 else ybf
    y_out, y_send = results
    y_got = paired(y_send)

    results = [stash(slots, rows, d, dtype=F32), stash(rows, d)]
    tables = [stash(1, stacked, dtype=F32) for _ in range(2)]
    width = 6 * d + LANES
    share = 2 * dshare
    position = jnp.arange(LANES, dtype=jnp.int32)[:, None] % head
    place = (position // hshare * dshare + position % hshare == jnp.arange(d, dtype=jnp.int32)[None, :]).astype(F32)
    here = jnp.stack([y, z, core, slot, odd]).astype(jnp.int32)

    def moved(x, leg, by):
        def to(i):
            step = 2 * side if i % 2 == leg else 2
            digit = i // step % side
            return i + ((digit + by) % side - digit) * step

        return lax.ppermute(x, "dp", [(i, to(i)) for i in range(ranks)])

    def grads_by_place(layer, got, table_got):
        return simple(
            partial(weight_grad_kernel, d, ff), here,
            [place, tables[layer], table_got, operands[layer][0], got],
            [whole((LANES, d)), whole(table_got.shape), whole(table_got.shape), ANY, ANY],
            [jax.ShapeDtypeStruct((side * share, width), BF)] * side, [ANY] * side,
            [V((2, rows, ff), BF), V((2, rows, d), BF), V((2, rows, d), BF), V((2, rows, 2 * d), BF), V((d, width), BF),
             pltpu.SemaphoreType.DMA((32,)), pltpu.SemaphoreType.DMA((32,))],
        )

    def leg(outs, which):
        far, near, back = (moved(outs[s], which, s) for s in (2, 1, 3))
        return [outs[0], near, far, back]

    def by_second_axis(came):
        return simple(
            mid_kernel, here, came, [whole(a.shape) for a in came],
            [jax.ShapeDtypeStruct((share, width), BF)] * side, [whole((share, width))] * side, [V((side, share, width), BF)],
        )

    here_g = seeds
    swaps = []
    for t in range(4):
        layer = 1 - t % 2
        gbf, done = call(
            partial(backward_kernel, d, ff, chunks, stride * layer, t == 0),
            index_of(layer, 1 - t // 2),
            [(here_g, ANY), (g, ANY), (g3, ANY), (ids_col, pick((rows, 1))), of_layer(ngain, layer), of_layer(gains, layer),
             (spread, whole((WIDE, WIDE)))] + [(a, ANY) for a in kept[layer]],
            ((rows, d), BF),
            operands[layer] + [tables[layer]] + results,
            [V((rows, d), BF), V((rows, d), BF)] + weights_v
            + [V((rows, d), BF)] * 4 + [V((rows, 2 * d), BF)] * 2
            + [V((chunks, rows, fc), BF), V((heads, rows, rows), BF), V((16, rows), F32)]
            + [V((d, rows), BF), V((d, rows), F32), V((rows, d), F32)]
            + [V((rows, d), BF)] * 3 + [V((chunks, rows, fc), BF), V((rows, d), F32), V((rows, d), F32), V((rows, d), BF), V((1, stacked), F32)]
            + sems,
            1 << 10,
        )
        operands[layer], tables[layer], results = done[:2], done[2], done[3:]
        here_g = lax.ppermute(gbf, "section", [(3, 0), (2, 1)]) if t == 1 else gbf
        if t == 1:
            here_g, y_got = lax.optimization_barrier((here_g, y_got))
        if t == 3:
            operands[layer][1], swaps[0] = lax.optimization_barrier((operands[layer][1], swaps[0]))
        if t >= 2:
            swaps.append((along(operands[layer][1], 1, 2, 1), along(tables[layer], 1, 2, 1)))
    gr_got = paired(results[1])
    upper, gr_got = lax.optimization_barrier((grads_by_place(1, *swaps[0]), gr_got))
    legs = [leg(upper, 0), leg(grads_by_place(0, *swaps[1]), 0)]
    arrived = [leg(by_second_axis(came), 1) for came in legs]
    gr_out = results[0]
    y_out, gr_out = pl.pallas_call(
        place_kernel,
        grid_spec=pltpu.PrefetchScalarGridSpec(
            num_scalar_prefetch=1, grid=(1,), in_specs=[ANY, whole((rows, d)), ANY, whole((rows, d))], out_specs=[ANY] * 2,
            scratch_shapes=[V((rows, d), F32), V((rows, d), F32), pltpu.SemaphoreType.DMA((2,))],
        ),
        out_shape=[jax.ShapeDtypeStruct(y_out.shape, F32)] * 2,
        input_output_aliases={1: 0, 3: 1},
    )(here, y_out, y_got, gr_out, gr_got)

    both = arrived[1] + arrived[0]
    home_mine, home_other, away_mine, away_other = simple(
        last_kernel, here, both, [whole(a.shape) for a in both],
        [jax.ShapeDtypeStruct((dshare, width), t) for t in (F32, BF, BF, BF)], [whole((dshare, width))] * 4,
        [V((share, width), F32)] * 2,
    )
    sections = lax.axis_size("section")
    cross = [(s * ranks + i, (s ^ 1) * ranks + (i ^ 1)) for s in range(sections) for i in range(ranks)]
    arrays = [home_mine, paired(away_mine), along(home_other, 1, 2, 1), lax.ppermute(away_other, ("section", "dp"), cross),
              shuffle.astype(F32)]
    shapes = [(dshare, joined), (dshare, d), (dshare * fshare, d), (1, dshare), (1, hshare), (1, hshare), (1, dshare * fshare),
              (1, dshare)]
    g_in, g_attn, g_down, g_ng, g_q, g_k, g_ub, g_ob = simple(
        partial(finish_kernel, d, ff), here, arrays, [whole(a.shape) for a in arrays],
        [jax.ShapeDtypeStruct(s, F32) for s in shapes], [whole(s) for s in shapes], [],
    )
    return (y_out.reshape(1, slots * rows, d), gr_out.reshape(1, slots * rows, d), g_in[None], g_attn[None], g_down[None],
            g_ng, g_q, g_k, g_ub, g_ob)


def solution(mesh):
    in_specs = (P("dp", None),) * 3 + (P("section", "dp", None),) * 3 + (P("section", "dp"),) * 5
    out_specs = (P("section", "dp", None),) * 5 + (P("section", "dp"),) * 5
    return jax.shard_map(body, mesh=mesh, in_specs=in_specs, out_specs=out_specs, check_vma=False)
```

```python
from functools import partial
import math

import jax
import jax.numpy as jnp
from jax import lax
from jax.experimental import pallas as pl
from jax.experimental.pallas import tpu as pltpu
from jax.sharding import PartitionSpec as P

BF = jnp.bfloat16
F32 = jnp.float32
VMEM_LIMIT = 60 * 1024 * 1024
EPS = 1e-06
NN = (((1,), (0,)), ((), ()))
NT = (((1,), (1,)), ((), ()))
TN = (((0,), (0,)), ((), ()))
LANES = 128
WIDE = 256
ABSENT = 16


def mm(a, b, dims=NN):
    return lax.dot_general(a, b, dims, preferred_element_type=F32)


def head_mean(x, spread, exact):
    parts = []
    for at in range(0, x.shape[1], WIDE):
        piece = x[:, at : at + WIDE]
        top = piece.astype(BF)
        total = mm(top, spread)
        if exact:
            total = total + mm((piece - top.astype(F32)).astype(BF), spread)
        parts.append(total)
    return jnp.concatenate(parts, axis=1)


def row_norm(x):
    centered = x - jnp.mean(x, axis=-1, keepdims=True)
    rstd = lax.rsqrt(jnp.mean(centered * centered, axis=-1, keepdims=True) + EPS)
    return centered * rstd, rstd


def norm_back(grad, normal, rstd, spread):
    return rstd * (grad - head_mean(grad, spread, False) - normal * head_mean(grad * normal, spread, False))


def lane_half(x, second):
    lane = lax.broadcasted_iota(jnp.int32, x.shape, 1)
    return jnp.where((lane >= LANES // 2) if second else (lane < LANES // 2), x, jnp.zeros_like(x))


class Copies:
    def __init__(self, sems):
        self.sems, self.used = sems, 0

    def start(self, src, dst):
        copy = pltpu.make_async_copy(src, dst, self.sems.at[self.used])
        self.used += 1
        copy.start()
        return copy

    def either(self, flag, src, yes, no):
        sem = self.sems.at[self.used]
        self.used += 1

        @pl.when(flag == 1)
        def _():
            pltpu.make_async_copy(src, yes, sem).start()

        @pl.when(flag != 1)
        def _():
            pltpu.make_async_copy(src, no, sem).start()

        return pltpu.make_async_copy(src, yes, sem)


def result_out(home, value, result, rounded, send, copies):
    sem = copies.sems.at[copies.used]
    copies.used += 1

    @pl.when(home == 1)
    def _():
        copy = pltpu.make_async_copy(value, result, sem)
        copy.start()
        copy.wait()

    @pl.when(home != 1)
    def _():
        copy = pltpu.make_async_copy(rounded, send, sem)
        copy.start()
        copy.wait()


def forward_kernel(d, ff, chunks, base, first, idx, x_in, g, g3, ids_col, ids_row, ngain, gains, ubias, obias, spread, *refs):
    @pl.when(idx[0] == 1)
    def _():
        forward_work(d, ff, chunks, base, first, idx, x_in, g, g3, ids_col, ids_row, ngain, gains, ubias, obias, spread, *refs)


def forward_work(d, ff, chunks, base, first, idx, x_in, g, g3, ids_col, ids_row, ngain, gains, ubias, obias, spread, *refs):
    refs = refs[13:]
    ybf, xs, qs, ks, vs, ns, nrs, gps, es, small, kept, sent, y_out, y_send = refs[:14]
    (x_v, h_v, w_v, u_v, d_v, a_v, q_v, k_v, v_v, n_v, r_v, act_v, gp_v, e_v, rs_v, att_v, acc_v, y_v, yb_v, ins, outs) = refs[14:]
    rows = x_v.shape[0]
    fc = ff // chunks
    core, slot, home = idx[1], idx[2], idx[3]
    cin, cout = Copies(ins), Copies(outs)
    x_copy = cin.start(x_in.at[slot] if first else x_in, x_v)
    wq = [cin.start(g.at[:, pl.ds(base + ff + d * i, d)], w_v.at[:, pl.ds(d * i, d)]) for i in range(3)]
    groups = fc // WIDE
    wff = []
    for c in range(chunks):
        wff.append([cin.start(g.at[:, pl.ds(base + fc * c, fc)], u_v.at[c])] + [
            cin.start(g3.at[pl.ds(groups * c, groups), :, pl.ds(base + ff + 4 * d + d * j, d)], d_v.at[pl.ds(groups * c, groups), j])
            for j in range(4)
        ])
    wa = cin.start(g.at[:, pl.ds(base + ff + 3 * d, d)], a_v)

    pending = []

    def side(i):
        return pl.ds(ff + d * i, d)

    x_copy.wait()
    keep = jnp.where(ids_col[0] < ABSENT, 1.0, 0.0)
    masked = keep * x_v[...].astype(F32)
    h_v[...] = (row_norm(masked)[0] * ngain[...]).astype(BF)
    pending += [cout.start(x_v, xs), cout.start(h_v, kept.at[:, side(2)]), cout.start(h_v, sent.at[:, side(2)])]
    bias_mask = jnp.where(ids_col[0] == ids_row[0], 0.0, -1e9)
    for i in range(3):
        wq[i].wait()
        raw = mm(h_v[...], w_v[:, d * i : d * i + d])
        if i == 2:
            v_v[...] = raw.astype(BF)
            pending.append(cout.start(v_v, vs))
        else:
            centered = raw - head_mean(raw, spread[...], True)
            rstd = lax.rsqrt(head_mean(centered * centered, spread[...], True) + EPS)
            normal = centered * rstd
            scaled = (normal * gains[i]).astype(BF)
            n_v[:, d * i : d * i + d] = normal.astype(BF)
            r_v[:, d * i : d * i + d] = rstd.astype(BF)
            if i == 0:
                q_v[...] = scaled * jnp.asarray(0.125, BF)
                pending.append(cout.start(q_v, qs))
            else:
                k_v[...] = scaled
                pending.append(cout.start(k_v, ks))
    pending += [cout.start(n_v, ns), cout.start(r_v, nrs)]
    ones = jnp.ones((16, rows), BF)
    pairs = d // LANES // chunks
    for c in range(chunks):
        for copy in wff[c]:
            copy.wait()
        pre = mm(h_v[...], u_v[c]) + ubias[:, fc * c : fc * c + fc]
        cdf = 0.5 * (1.0 + lax.erf(pre * (1.0 / math.sqrt(2.0))))
        density = jnp.exp(-0.5 * pre * pre) * (1.0 / math.sqrt(2.0 * math.pi))
        act = (pre * cdf).astype(BF)
        act_v[c] = act
        gp_v[c] = (cdf + pre * density).astype(BF)
        total = mm(act, d_v[groups * c : groups * c + groups].reshape(fc, d))
        if c == 0:
            acc_v[...] = total
        else:
            acc_v[...] += total
        for p in range(pairs * c, pairs * c + pairs):
            cols = slice(LANES * p, LANES * p + LANES)
            vals_t = v_v[:, cols].T
            pair = q_v[:, cols]
            both = []
            for half in range(2):
                h = 2 * p + half
                e = jnp.exp(mm(k_v[:, cols], lane_half(pair, half), NT) + bias_mask).astype(BF)
                e_v[h] = e
                got = mm(jnp.concatenate([vals_t[64 * half : 64 * half + 64], ones], axis=0), e)
                inv = 1.0 / got[64:65]
                rs_v[h : h + 1, :] = inv
                both.append((got[:64] * inv).astype(BF))
            att_v[:, cols] = jnp.concatenate(both, axis=0).T
        span = pl.ds(fc * c, fc)
        pending += [cout.either(core, act_v.at[c], sent.at[:, span], kept.at[:, span]), cout.start(gp_v.at[c], gps.at[c]),
                    cout.start(e_v.at[pl.ds(2 * pairs * c, 2 * pairs)], es.at[pl.ds(2 * pairs * c, 2 * pairs)])]
    pending += [cout.start(rs_v, small), cout.either(core, att_v, sent.at[:, side(3)], kept.at[:, side(3)])]
    wa.wait()
    y = keep * (keep * x_v[...].astype(F32) + acc_v[...] + mm(att_v[...], a_v[...]) + obias[...])
    y_v[...] = y
    ybf[...] = y.astype(BF)
    yb_v[...] = y.astype(BF)
    result_out(home, y_v, y_out.at[slot], yb_v, y_send, cout)
    for copy in pending:
        copy.wait()


def backward_kernel(d, ff, chunks, base, first, idx, g_in, g, g3, ids_col, ngain, gains, spread, *refs):
    @pl.when(idx[0] == 1)
    def _():
        backward_work(d, ff, chunks, base, first, idx, g_in, g, g3, ids_col, ngain, gains, spread, *refs)


def backward_work(d, ff, chunks, base, first, idx, g_in, g, g3, ids_col, ngain, gains, spread, *refs):
    xs, qs, ks, vs, ns, nrs, gps, es, small = refs[:9]
    refs = refs[9 + 5 :]
    gbf, kept, sent, table, gr_out, gr_send = refs[:6]
    (g_v, gb_v, w_v, u_v, d_v, a_v, x_v, q_v, k_v, v_v, n_v, r_v, gp_v, e_v, rs_v, gat_v, gqt_v, gk_v,
     gq_b, gk_b, gv_b, gj_v, acc_v, out_v, ob_v, sm_v, ins, outs) = refs[6:]
    rows = x_v.shape[0]
    fc = ff // chunks
    groups = fc // WIDE
    core, slot, home = idx[1], idx[2], idx[3]
    cin, cout = Copies(ins), Copies(outs)
    g_copy = cin.start(g_in.at[slot] if first else g_in, g_v)
    wa = cin.start(g.at[:, pl.ds(base + ff + 3 * d, d)], a_v)
    heads = [cin.start(s, v) for s, v in ((small, rs_v), (ks, k_v), (vs, v_v), (qs, q_v))]
    pairs = d // LANES // chunks
    wff = []
    for c in range(chunks):
        wff.append(
            [cin.start(g3.at[pl.ds(groups * c, groups), :, pl.ds(base + ff + 4 * d + d * j, d)], d_v.at[pl.ds(groups * c, groups), j])
             for j in range(4)]
            + [cin.start(gps.at[c], gp_v.at[c]), cin.start(g.at[:, pl.ds(base + fc * c, fc)], u_v.at[c]),
               cin.start(es.at[pl.ds(2 * pairs * c, 2 * pairs)], e_v.at[pl.ds(2 * pairs * c, 2 * pairs)])]
        )
    norms = [cin.start(ns, n_v), cin.start(nrs, r_v)]
    wq = [cin.start(g.at[:, pl.ds(base + ff + d * i, d)], w_v.at[:, pl.ds(d * i, d)]) for i in range(3)]
    rows_in = cin.start(xs, x_v)

    pending = []

    def side(i):
        return pl.ds(ff + d * i, d)

    def summed(at, value):
        sm_v[:, at : at + value.shape[1]] = jnp.sum(value, axis=0, keepdims=True)

    g_copy.wait()
    keep = jnp.where(ids_col[0] < ABSENT, 1.0, 0.0)
    gres = keep * g_v[...].astype(F32)
    summed(d, gres)
    gb_v[...] = gres.astype(BF)
    pending.append(cout.either(core, gb_v, sent.at[:, side(0)], kept.at[:, side(0)]))
    wa.wait()
    gat_v[...] = mm(a_v[...], gb_v[...], NT).astype(BF)
    for copy in heads:
        copy.wait()
    zeros = jnp.zeros((LANES // 2, rows), BF)
    for c in range(chunks):
        for copy in wff[c]:
            copy.wait()
        gup = mm(gb_v[...], d_v[groups * c : groups * c + groups].reshape(fc, d), NT) * gp_v[c].astype(F32)
        summed(4 * d + fc * c, gup)
        gup = gup.astype(BF)
        gj_v[c] = gup
        span = pl.ds(fc * c, fc)
        pending.append(cout.either(core, gj_v.at[c], kept.at[:, span], sent.at[:, span]))
        total = mm(gup, u_v[c], NT)
        if c == 0:
            acc_v[...] = total
        else:
            acc_v[...] += total
        for p in range(pairs * c, pairs * c + pairs):
            cols = slice(LANES * p, LANES * p + LANES)
            keys, vals, pair = k_v[:, cols], v_v[:, cols], q_v[:, cols]
            keys_t = keys.T
            gk, gv = None, None
            for half in range(2):
                h = 2 * p + half
                at_rows = slice(64 * h, 64 * h + 64)
                inv = rs_v[h : h + 1, :]
                ga = (gat_v[at_rows, :].astype(F32) * inv).astype(BF)
                ga = jnp.concatenate([zeros, ga] if half else [ga, zeros], axis=0)
                e = e_v[h]
                ef = e.astype(F32)
                gp = ef * mm(vals, ga)
                dot = jnp.sum(gp, axis=0, keepdims=True) * inv
                gs = (gp - ef * dot).astype(BF)
                gk_h = mm(gs, lane_half(pair, half))
                gv_h = mm(e, ga, NT)
                gk = gk_h if gk is None else gk + gk_h
                gv = gv_h if gv is None else gv + gv_h
                gqt_v[at_rows, :] = mm(keys_t[64 * half : 64 * half + 64], gs) * 0.125
            gk_v[:, cols] = gk
            gv_b[:, cols] = gv.astype(BF)
    pending.append(cout.either(core, gv_b, sent.at[:, side(1)], kept.at[:, side(1)]))
    for copy in norms:
        copy.wait()
    for i, (grad, out) in enumerate(((gqt_v[...].T, gq_b), (gk_v[...], gk_b))):
        normal = n_v[:, d * i : d * i + d].astype(F32)
        summed(2 * d + d * i, grad * normal)
        out[...] = norm_back(grad * gains[i], normal, r_v[:, d * i : d * i + d].astype(F32), spread[...]).astype(BF)
        pending.append(cout.either(core, out, kept.at[:, side(i)], sent.at[:, side(i)]))
    for copy in wq:
        copy.wait()
    ghid = acc_v[...]
    for i, part in enumerate((gq_b, gk_b, gv_b)):
        ghid = ghid + mm(part[...], w_v[:, d * i : d * i + d], NT)
    rows_in.wait()
    xhat, rstd = row_norm(keep * x_v[...].astype(F32))
    summed(0, ghid * xhat)
    pending.append(cout.start(sm_v, table))
    gx = ghid * ngain[...]
    gmask = rstd * (gx - jnp.mean(gx, axis=-1, keepdims=True) - xhat * jnp.mean(gx * xhat, axis=-1, keepdims=True))
    out = keep * (keep * g_v[...].astype(F32) + gmask)
    out_v[...] = out
    gbf[...] = out.astype(BF)
    ob_v[...] = out.astype(BF)
    result_out(home, out_v, gr_out.at[slot], ob_v, gr_send, cout)
    for copy in pending:
        copy.wait()


def split_small(values):
    top = values.astype(BF).astype(F32)
    lane = lax.broadcasted_iota(jnp.int32, values.shape, 1)
    return jnp.where(lane < 8, top, jnp.where(lane < 16, pltpu.roll(values - top, 8, 1), 0.0)).astype(BF)


def joined_small(parts):
    return parts + pltpu.roll(parts, LANES - 8, 1)


def small_table(d, ff, place, mine, theirs):
    total = mine[...] + theirs[...]
    quarter = WIDE // 4
    ub = total[:, 4 * d :]
    up_rows = []
    for j in range(4):
        pieces = [ub[:, WIDE * b + quarter * j : WIDE * b + quarter * (j + 1)] for b in range(ff // WIDE)]
        up_rows.append(jnp.concatenate(pieces, axis=1))
    head_rows = []
    for i in range(2, 4):
        lanes = total[:, d * i : d * i + LANES]
        for p in range(1, d // LANES):
            lanes = lanes + total[:, d * i + LANES * p : d * i + LANES * (p + 1)]
        head_rows.append(lanes)
    both = jnp.concatenate(head_rows + [jnp.zeros((6, LANES), F32)], axis=0)
    placed = lax.dot_general(both, place[...], NN, precision=lax.Precision.HIGHEST, preferred_element_type=F32)
    rows = [total[:, :d], total[:, d : 2 * d]] + up_rows + [placed[0:1], placed[1:2], jnp.zeros((LANES - 8, d), F32)]
    return jnp.concatenate(rows, axis=0).T


def weight_grad_kernel(d, ff, idx, place, mine, theirs, kept, got, *refs):
    results, (big_v, a_v, b_v, c_v, out_v, ins, outs) = refs[:5], refs[5:]
    rows = kept.shape[0]
    tokens = 2 * rows
    quarter, half, third = WIDE // 4, ff // 2, ff // 3
    blocks = third // WIDE
    share = d // 16
    cut = 3 * d
    y, z, core = idx[0], idx[1], idx[2]

    def load(cin, at, width, to, to_at):
        return [cin.start(src.at[:, pl.ds(at, width)], to.at[i, :, pl.ds(to_at, width)]) for i, src in enumerate((kept, got))]

    def wait(copies):
        for copy in copies:
            copy.wait()

    def both(ref, at=0, width=d):
        return ref[:, :, at : at + width].reshape(tokens, width)

    def put(rows_at, cols_at, value):
        out_v[rows_at, cols_at] = value.astype(BF)

    def send_by_y(cout, at, width):
        cols = pl.ds(at, width)

        def rows_of(s, first, count):
            return out_v.at[pl.ds(pl.multiple_of(lax.rem(y + s, 4) * 4 * share + first, 16), count), cols]

        return [cout.start(rows_of(2, 0, 2 * share), results[3].at[:, cols]),
                cout.start(rows_of(2, 2 * share, 2 * share), results[4].at[:, cols])] + [
            cout.start(rows_of(s, 0, 4 * share), results[r].at[:, cols]) for r, s in ((1, 1), (2, 3), (0, 0))]

    def send_by_z(cout, at, width):
        cols = pl.ds(at, width)

        def rows_of(i, s):
            return out_v.at[pl.ds(pl.multiple_of((4 * i + lax.rem(z + s, 4)) * share, 16), share), cols]

        return [
            cout.start(rows_of(i, s), results[r].at[pl.ds(share * (i - base), share), cols])
            for r, s, base, count in ((3, 2, 0, 2), (4, 2, 2, 2), (1, 1, 0, 4), (2, 3, 0, 4), (0, 0, 0, 4))
            for i in range(base, base + count)
        ]

    everything = slice(0, d)

    @pl.when(core == 0)
    def _():
        cin, cout = Copies(ins), Copies(outs)
        grads = load(cin, ff, d, a_v, 0)
        loads = [load(cin, third * k, third, big_v, third * k) for k in range(3)]
        attended = load(cin, ff + 3 * d, d, b_v, 0)
        hidden, values = load(cin, ff + 2 * d, d, c_v, 0), load(cin, ff + d, d, c_v, d)
        wait(grads)
        gb = both(a_v)
        for k in range(3):
            wait(loads[k])
            found = lax.dot_general(both(big_v, third * k, third), gb, TN, preferred_element_type=F32).astype(BF)
            for b in range(blocks):
                at = quarter * (blocks * k + b)
                for j in range(4):
                    put(slice(at, at + quarter), slice(d * j, d * j + d), found[WIDE * b + quarter * j : WIDE * b + quarter * (j + 1)])
        pending = send_by_y(cout, 0, 4 * d)
        wait(attended)
        put(everything, slice(4 * d, 5 * d), lax.dot_general(both(b_v), gb, TN, preferred_element_type=F32))
        wait(hidden + values)
        put(everything, slice(5 * d, 6 * d), lax.dot_general(both(c_v), both(c_v, d), TN, preferred_element_type=F32))
        put(everything, slice(6 * d, 6 * d + LANES), split_small(small_table(d, ff, place, mine, theirs)))
        wait(pending + send_by_y(cout, 4 * d, 2 * d + LANES))

    @pl.when(core == 1)
    def _():
        cin, cout = Copies(ins), Copies(outs)
        hidden = load(cin, ff + 2 * d, d, a_v, 0)
        loads = [load(cin, third * k, third, big_v, third * k) for k in range(2)]
        queries = load(cin, ff, d, b_v, 0)
        loads.append(load(cin, 2 * third, third, big_v, 2 * third))
        keys = load(cin, ff + d, d, c_v, 0)
        wait(hidden)
        turned = both(a_v).T
        pending = []
        for k in range(2):
            wait(loads[k])
            put(everything, slice(third * k, third * k + third), mm(turned, both(big_v, third * k, third)))
        pending = send_by_z(cout, 0, 2 * third)
        wait(queries)
        put(everything, slice(ff, ff + d), mm(turned, both(b_v)))
        wait(loads[2])
        put(everything, slice(2 * third, ff), mm(turned, both(big_v, 2 * third, third)))
        wait(keys)
        put(everything, slice(ff + d, ff + 2 * d), mm(turned, both(c_v)))
        out_v[:, 6 * d :] = jnp.zeros((d, LANES), BF)
        wait(pending + send_by_z(cout, 2 * third, 6 * d + LANES - 2 * third))


def added(parts):
    total = parts[0][...].astype(F32)
    for part in parts[1:]:
        total = total + part[...].astype(F32)
    shape = total.shape
    total = total.reshape(-1, shape[-1])
    main, last = total[:, : shape[-1] - LANES], split_small(joined_small(total[:, shape[-1] - LANES :]))
    return jnp.concatenate([main.astype(BF), last], axis=1).reshape(shape)


def relay_kernel(idx, up_in, down_in, up_got, down_got, up, down, up_v, down_v, ins, outs):
    half = up_got.shape[0]
    cin, cout = Copies(ins), Copies(outs)
    pending = []
    loads = [(cin.start(block.at[pl.ds(at, half)], hold), got, hold, out.at[pl.ds(at, half)])
             for block, at, got, hold, out in ((up_in, 0, up_got, up_v, up), (down_in, half, down_got, down_v, down))]
    for copy, got, hold, out in loads:
        copy.wait()
        hold[...] = added([hold, got])
        pending.append(cout.start(hold, out))
    for copy in pending:
        copy.wait()


def mid_kernel(idx, *refs):
    came, outs, hold = refs[:3], refs[3:7], refs[7]
    hold[...] = added(came).reshape(hold.shape)
    at = jnp.where(idx[2] == 0, idx[1], idx[0])
    for s in range(4):
        outs[s][...] = hold[lax.rem(at + s, 4)]


def last_kernel(idx, *refs):
    layers, (home_mine, home_other, away_mine, away_other), holds = (refs[:4], refs[4:8]), refs[8:12], refs[12:]
    core, odd = idx[2], idx[4]
    for came, hold in zip(layers, holds):
        hold[...] = added(came).astype(F32)
    count = home_mine.shape[0]

    def rows_of(hold, which):
        return hold[pl.ds(pl.multiple_of(which * count, 8), count), :]

    for which, home, away in ((core, home_mine, away_mine), (1 - core, home_other, away_other)):
        lower, upper = rows_of(holds[0], which), rows_of(holds[1], which)
        home[...] = jnp.where(odd == 1, upper, lower).astype(home.dtype)
        away[...] = jnp.where(odd == 1, lower, upper).astype(away.dtype)


def place_kernel(idx, y_in, y_got, g_in, g_got, y_out, g_out, y_v, g_v, sems):
    copies = Copies(sems)
    pending = []
    for got, wide_v, out in ((y_got, y_v, y_out), (g_got, g_v, g_out)):
        wide_v[...] = got[...].astype(F32)
        pending.append(copies.start(wide_v, out.at[1 - idx[3]]))
    for copy in pending:
        copy.wait()


def picked(rows, columns, wanted):
    row = lax.broadcasted_iota(jnp.int32, (rows, columns), 0)
    column = lax.broadcasted_iota(jnp.int32, (rows, columns), 1)
    return row, column, jnp.where(column == wanted(row), 1.0, 0.0)


def prepare_kernel(d, ff, p_in, p_attn, p_down, n_gain, o_bias, u_bias, q_gain, k_gain, shuffle, out):
    share = p_in.shape[0]
    heads_part = p_in.shape[1] - ff
    for at in range(0, ff, WIDE):
        out[:, at : at + WIDE] = mm(p_in[:, heads_part + at : heads_part + at + WIDE], shuffle[...]).astype(BF)
    out[:, ff : ff + heads_part] = p_in[:, :heads_part]
    at = ff + heads_part
    out[:, at : at + d] = p_attn[...]
    down = p_down[...]
    for j in range(4):
        take = picked(share, down.shape[0], lambda row: 4 * row + j)[2].astype(BF)
        out[:, at + d * (j + 1) : at + d * (j + 2)] = mm(take, down).astype(BF)

    def column_of(ref, wanted, where):
        values = ref[...].astype(F32)
        take = picked(share, values.shape[1], wanted)[2]
        lane = lax.broadcasted_iota(jnp.int32, (share, LANES), 1)
        return jnp.where(lane == where, jnp.sum(take * values, axis=1, keepdims=True), 0.0)

    table = column_of(n_gain, lambda row: row, 0) + column_of(o_bias, lambda row: row, 1)
    for j in range(4):
        table = table + column_of(u_bias, lambda row: 4 * row + j, 2 + j)
    table = table + column_of(q_gain, lambda row: row, 6) + column_of(k_gain, lambda row: row, 7)
    out[:, at + 5 * d :] = table.astype(BF)


def smalls_kernel(d, ff, base, stride, g, place, ngain, gains, ubias, obias, t_v, sems):
    copies = Copies(sems)
    loads = [copies.start(g.at[:, pl.ds(base + stride * layer, LANES)], t_v.at[layer]) for layer in range(2)]
    quarter = WIDE // 4
    for layer in range(2):
        loads[layer].wait()
        table = t_v[layer].astype(F32).T
        ngain[layer] = table[0:1]
        obias[layer] = table[1:2]
        pieces = [table[2 + j : 3 + j, quarter * b : quarter * (b + 1)] for b in range(ff // WIDE) for j in range(4)]
        ubias[layer] = jnp.concatenate(pieces, axis=1)
        both = mm(table[0:8].astype(BF), place[...])
        gains[layer, 0] = both[6:7]
        gains[layer, 1] = both[7:8]


def finish_kernel(d, ff, idx, own, a_in, b_in, c_in, shuffle, g_in, g_attn, g_down, g_ng, g_q, g_k, g_ub, g_ob):
    core = idx[2]
    share = own.shape[0]
    mine = own[...] + a_in[...].astype(F32)
    theirs = b_in[...].astype(F32) + c_in[...].astype(F32)
    half0 = jnp.where(core == 0, mine, theirs)
    half1 = jnp.where(core == 0, theirs, mine)
    g_in[:, : 2 * d] = half1[:, ff : ff + 2 * d]
    g_in[:, 2 * d : 3 * d] = half0[:, 5 * d : 6 * d]
    for at in range(0, ff, WIDE):
        g_in[:, 3 * d + at : 3 * d + at + WIDE] = lax.dot_general(
            half1[:, at : at + WIDE], shuffle[...], NT, precision=lax.Precision.HIGHEST, preferred_element_type=F32)
    g_attn[...] = half0[:, 4 * d : 5 * d]
    stacked = jnp.concatenate([half0[:, at : at + d] for at in range(0, 4 * d, d)], axis=0)
    row, column, _ = picked(4 * share, 4 * share, lambda row: row)
    turn = jnp.where(column == lax.rem(row, 4) * share + row // 4, 1.0, 0.0)
    g_down[...] = lax.dot_general(turn, stacked, NN, precision=lax.Precision.HIGHEST, preferred_element_type=F32)
    small = joined_small(half0[:, 6 * d :])
    turned = jnp.concatenate([small, jnp.zeros((LANES - share, LANES), F32)], axis=0).T
    g_ng[...] = turned[0:1, :share]
    g_ob[...] = turned[1:2, :share]
    g_q[...] = turned[6:7, : g_q.shape[1]]
    g_k[...] = turned[7:8, : g_k.shape[1]]
    total = jnp.zeros((8, 4 * share), F32)
    for j in range(4):
        row, column, _ = picked(LANES, 4 * share, lambda row: row)
        spread_out = jnp.where(column == 4 * row + j, 1.0, 0.0)
        total = total + jnp.where(lax.broadcasted_iota(jnp.int32, (8, 4 * share), 0) == 2 + j, 1.0, 0.0) * lax.dot_general(
            turned[0:8], spread_out, NN, precision=lax.Precision.HIGHEST, preferred_element_type=F32)
    g_ub[...] = jnp.sum(total, axis=0, keepdims=True)


ANY = pl.BlockSpec(memory_space=pl.ANY)


def whole(shape):
    return pl.BlockSpec(shape, lambda i, idx: (0,) * len(shape))


def pick(shape):
    return pl.BlockSpec((1,) + shape, lambda i, idx: (idx[2],) + (0,) * len(shape))


def call(kernel, idx, ins, fresh, stashes, scratch, flops):
    outs = pl.pallas_call(
        kernel,
        grid_spec=pltpu.PrefetchScalarGridSpec(
            num_scalar_prefetch=1,
            grid=(1,),
            in_specs=[s for _, s in ins] + [ANY] * len(stashes),
            out_specs=[whole(fresh[0])] + [ANY] * len(stashes),
            scratch_shapes=scratch,
        ),
        out_shape=[jax.ShapeDtypeStruct(*fresh)] + [jax.ShapeDtypeStruct(a.shape, a.dtype) for a in stashes],
        input_output_aliases={1 + len(ins) + i: 1 + i for i in range(len(stashes))},
        compiler_params=pltpu.CompilerParams(dimension_semantics=("arbitrary",), vmem_limit_bytes=VMEM_LIMIT),
        cost_estimate=pl.CostEstimate(flops=flops, bytes_accessed=1 << 10, transcendentals=0),
    )(idx, *[a for a, _ in ins], *stashes)
    return outs[0], list(outs[1:])


def plain(kernel, arrays, specs, out_shapes, out_specs, scratch):
    return pl.pallas_call(
        kernel, grid=(1,), in_specs=specs, out_specs=out_specs, scratch_shapes=scratch, out_shape=out_shapes,
        compiler_params=pltpu.CompilerParams(dimension_semantics=("arbitrary",), vmem_limit_bytes=VMEM_LIMIT),
        cost_estimate=pl.CostEstimate(flops=1 << 10, bytes_accessed=1 << 10, transcendentals=0),
    )(*arrays)


def simple(kernel, idx, arrays, specs, out_shapes, out_specs, scratch, flops=1 << 10):
    return pl.pallas_call(
        kernel,
        grid_spec=pltpu.PrefetchScalarGridSpec(
            num_scalar_prefetch=1, grid=(1,), in_specs=specs, out_specs=out_specs, scratch_shapes=scratch
        ),
        out_shape=out_shapes,
        compiler_params=pltpu.CompilerParams(dimension_semantics=("arbitrary",), vmem_limit_bytes=VMEM_LIMIT),
        cost_estimate=pl.CostEstimate(flops=flops, bytes_accessed=1 << 10, transcendentals=0),
    )(idx, *arrays)


def along(x, step, size, by):
    devices = lax.axis_size("dp")

    def to(i):
        digit = i // step % size
        return i + ((digit + by) % size - digit) * step

    return lax.ppermute(x, "dp", [(i, to(i)) for i in range(devices)])


def paired(x):
    return lax.ppermute(x, "section", [(0, 1), (1, 0), (2, 3), (3, 2)])


def body(tokens, cotangent, lengths, proj_in, proj_attn, proj_down, norm_gain, query_gain, key_gain, up_bias, out_bias):
    ranks = lax.axis_size("dp")
    section = lax.axis_index("section")
    rank = lax.axis_index("dp")
    slots = lengths.shape[0]
    rows = tokens.shape[0] // slots
    d = tokens.shape[1]
    joined = proj_in.shape[2]
    ff = proj_down.shape[1] * ranks
    head = query_gain.shape[1] * ranks
    heads = d // head
    dshare = proj_in.shape[1]
    fshare = proj_down.shape[1] // dshare
    hshare = query_gain.shape[1]
    chunks = 3
    wide = joined + d + ff
    stride = wide + LANES
    side = math.isqrt(ranks // 2)
    core, z, y = lax.rem(rank, 2), lax.rem(rank // 2, side), rank // (2 * side)
    stage, odd = section // 2, lax.rem(section, 2)
    slot = lax.rem(stage + odd, 2)

    place = jnp.arange(WIDE, dtype=jnp.int32)
    source = (place % (WIDE // fshare)) * fshare + place // (WIDE // fshare)
    shuffle = (place[:, None] == source[None, :]).astype(BF)

    def full(a):
        return pl.BlockSpec(a.shape, lambda i: (0,) * a.ndim)

    shares = [proj_in[0], proj_attn[0], proj_down[0], norm_gain, out_bias, up_bias, query_gain, key_gain, shuffle]
    heads_part = joined - ff
    local = jax.ShapeDtypeStruct((dshare, stride), BF)
    local = plain(partial(prepare_kernel, d, ff), shares, [full(a) for a in shares], local, full(local), [])
    other = paired(local)
    both = jnp.where(odd == 0, jnp.concatenate([local, other], axis=1), jnp.concatenate([other, local], axis=1))
    g = lax.all_gather(both, "dp", axis=0, tiled=True)
    g3 = g.reshape(ff // WIDE, WIDE // fshare, g.shape[1])
    element = jnp.arange(d, dtype=jnp.int32) % head
    spread_gain = (jnp.arange(d, dtype=jnp.int32)[:, None] == (element // hshare * dshare + element % hshare)[None, :]).astype(BF)
    tables = [jax.ShapeDtypeStruct(s, F32) for s in ((2, 1, d), (2, 2, 1, d), (2, 1, ff), (2, 1, d))]
    ngain, gains, ubias, obias = plain(
        partial(smalls_kernel, d, ff, wide, stride), [g, spread_gain], [ANY, full(spread_gain)], tables,
        [full(a) for a in tables], [pltpu.VMEM((2, d, LANES), BF), pltpu.SemaphoreType.DMA((2,))],
    )

    def of_layer(a, layer):
        return (a, pl.BlockSpec((None,) + a.shape[1:], lambda i, idx: (layer,) + (0,) * (a.ndim - 1)))

    column = jnp.arange(WIDE, dtype=jnp.int32) // head
    spread = jnp.where(column[:, None] == column[None, :], 1.0 / head, 0.0).astype(BF)

    toks = tokens.reshape(slots, rows, d)
    seeds = cotangent.reshape(slots, rows, d)
    ends = jnp.cumsum(lengths, axis=-1)
    position = jnp.arange(rows, dtype=jnp.int32)
    image = jnp.sum((position[None, :, None] >= ends[:, None, :]).astype(jnp.int32), axis=-1)
    image = jnp.where(position[None, :] < ends[:, 2:3], image, ABSENT + position[None, :])
    ids_col, ids_row = image[:, :, None], image[:, None, :]

    def stash(*shape, dtype=BF):
        return pl.pallas_call(
            lambda out: None, out_shape=jax.ShapeDtypeStruct(shape, dtype), out_specs=pl.BlockSpec(memory_space=pl.ANY)
        )()

    fc = ff // chunks
    groups = ff // WIDE

    def index_of(layer, active_stage):
        return jnp.stack([stage == active_stage, core, slot, odd == layer]).astype(jnp.int32)

    V = pltpu.VMEM
    weights_v = [V((d, heads_part), BF), V((chunks, d, fc), BF), V((groups, fshare, WIDE // fshare, d), BF), V((d, d), BF)]
    sems = [pltpu.SemaphoreType.DMA((48,)), pltpu.SemaphoreType.DMA((48,))]
    stacked = ff + 4 * d
    operands = [[stash(rows, stacked), stash(rows, stacked)] for _ in range(2)]
    kept = [[stash(rows, d) for _ in range(4)] + [stash(rows, 2 * d), stash(rows, 2 * d), stash(chunks, rows, fc),
             stash(heads, rows, rows), stash(16, rows, dtype=F32)] for _ in range(2)]
    results = [stash(slots, rows, d, dtype=F32), stash(rows, d)]
    here_x = toks
    for t in range(4):
        layer = t % 2
        ybf, done = call(
            partial(forward_kernel, d, ff, chunks, stride * layer, t == 0),
            index_of(layer, t // 2),
            [(here_x, ANY), (g, ANY), (g3, ANY), (ids_col, pick((rows, 1))), (ids_row, pick((1, rows))),
             of_layer(ngain, layer), of_layer(gains, layer), of_layer(ubias, layer), of_layer(obias, layer),
             (spread, whole((WIDE, WIDE)))],
            ((rows, d), BF),
            kept[layer][:9] + operands[layer] + results,
            [V((rows, d), BF), V((rows, d), BF)] + weights_v
            + [V((rows, d), BF)] * 3 + [V((rows, 2 * d), BF)] * 2 + [V((chunks, rows, fc), BF)] * 2
            + [V((heads, rows, rows), BF), V((16, rows), F32), V((rows, d), BF), V((rows, d), F32), V((rows, d), F32), V((rows, d), BF)]
            + sems,
            1 << 10,
        )
        kept[layer], operands[layer], results = done[:9], done[9:11], done[11:]
        here_x = lax.ppermute(ybf, "section", [(0, 3), (1, 2)]) if t == 1 else ybf
    y_out, y_send = results
    y_got = paired(y_send)

    results = [stash(slots, rows, d, dtype=F32), stash(rows, d)]
    tables = [stash(1, stacked, dtype=F32) for _ in range(2)]
    width = 6 * d + LANES
    share = 2 * dshare
    position = jnp.arange(LANES, dtype=jnp.int32)[:, None] % head
    place = (position // hshare * dshare + position % hshare == jnp.arange(d, dtype=jnp.int32)[None, :]).astype(F32)
    here = jnp.stack([y, z, core, slot, odd]).astype(jnp.int32)

    def moved(x, leg, by):
        def to(i):
            step = 2 * side if i % 2 == leg else 2
            digit = i // step % side
            return i + ((digit + by) % side - digit) * step

        return lax.ppermute(x, "dp", [(i, to(i)) for i in range(ranks)])

    def grads_by_place(layer, got, table_got):
        return simple(
            partial(weight_grad_kernel, d, ff), here,
            [place, tables[layer], table_got, operands[layer][0], got],
            [whole((LANES, d)), whole(table_got.shape), whole(table_got.shape), ANY, ANY],
            [jax.ShapeDtypeStruct((side * share, width), BF)] * 3 + [jax.ShapeDtypeStruct((side // 2 * share, width), BF)] * 2,
            [ANY] * 5,
            [V((2, rows, ff), BF), V((2, rows, d), BF), V((2, rows, d), BF), V((2, rows, 2 * d), BF), V((d, width), BF),
             pltpu.SemaphoreType.DMA((32,)), pltpu.SemaphoreType.DMA((32,))],
        )

    def halves(made):
        return moved(made[3], 0, 1), moved(made[4], 0, -1)

    def first_leg(made, came):
        own, up, down = made[:3]
        part = (side // 2 * share, width)
        up, down = pl.pallas_call(
            relay_kernel,
            grid_spec=pltpu.PrefetchScalarGridSpec(
                num_scalar_prefetch=1, grid=(1,), in_specs=[ANY, ANY, whole(part), whole(part)], out_specs=[ANY] * 2,
                scratch_shapes=[V(part, BF), V(part, BF), pltpu.SemaphoreType.DMA((2,)), pltpu.SemaphoreType.DMA((2,))],
            ),
            out_shape=[jax.ShapeDtypeStruct(up.shape, BF)] * 2,
            input_output_aliases={1: 0, 2: 1},
            compiler_params=pltpu.CompilerParams(dimension_semantics=("arbitrary",), vmem_limit_bytes=VMEM_LIMIT),
            cost_estimate=pl.CostEstimate(flops=1 << 10, bytes_accessed=1 << 10, transcendentals=0),
        )(here, up, down, *came)
        return [own, moved(up, 0, 1), moved(down, 0, -1)]

    def second_leg(outs):
        far, near, back = (moved(outs[s], 1, s) for s in (2, 1, 3))
        return [outs[0], near, far, back]

    def by_second_axis(came):
        return simple(
            mid_kernel, here, came, [whole(a.shape) for a in came],
            [jax.ShapeDtypeStruct((share, width), BF)] * side, [whole((share, width))] * side, [V((side, share, width), BF)],
        )

    here_g = seeds
    swaps = []
    for t in range(4):
        layer = 1 - t % 2
        gbf, done = call(
            partial(backward_kernel, d, ff, chunks, stride * layer, t == 0),
            index_of(layer, 1 - t // 2),
            [(here_g, ANY), (g, ANY), (g3, ANY), (ids_col, pick((rows, 1))), of_layer(ngain, layer), of_layer(gains, layer),
             (spread, whole((WIDE, WIDE)))] + [(a, ANY) for a in kept[layer]],
            ((rows, d), BF),
            operands[layer] + [tables[layer]] + results,
            [V((rows, d), BF), V((rows, d), BF)] + weights_v
            + [V((rows, d), BF)] * 4 + [V((rows, 2 * d), BF)] * 2
            + [V((chunks, rows, fc), BF), V((heads, rows, rows), BF), V((16, rows), F32)]
            + [V((d, rows), BF), V((d, rows), F32), V((rows, d), F32)]
            + [V((rows, d), BF)] * 3 + [V((chunks, rows, fc), BF), V((rows, d), F32), V((rows, d), F32), V((rows, d), BF), V((1, stacked), F32)]
            + sems,
            1 << 10,
        )
        operands[layer], tables[layer], results = done[:2], done[2], done[3:]
        here_g = lax.ppermute(gbf, "section", [(3, 0), (2, 1)]) if t == 1 else gbf
        if t == 1:
            here_g, y_got = lax.optimization_barrier((here_g, y_got))
        if t == 3:
            operands[layer][1], swaps[0] = lax.optimization_barrier((operands[layer][1], swaps[0]))
        if t >= 2:
            swaps.append((along(operands[layer][1], 1, 2, 1), along(tables[layer], 1, 2, 1)))
    gr_got = paired(results[1])
    upper, gr_got = lax.optimization_barrier((grads_by_place(1, *swaps[0]), gr_got))
    upper_came = halves(upper)
    lower = grads_by_place(0, *swaps[1])
    lower_came = halves(lower)
    legs = [first_leg(upper, upper_came), first_leg(lower, lower_came)]
    arrived = [second_leg(by_second_axis(came)) for came in legs]
    gr_out = results[0]
    y_out, gr_out = pl.pallas_call(
        place_kernel,
        grid_spec=pltpu.PrefetchScalarGridSpec(
            num_scalar_prefetch=1, grid=(1,), in_specs=[ANY, whole((rows, d)), ANY, whole((rows, d))], out_specs=[ANY] * 2,
            scratch_shapes=[V((rows, d), F32), V((rows, d), F32), pltpu.SemaphoreType.DMA((2,))],
        ),
        out_shape=[jax.ShapeDtypeStruct(y_out.shape, F32)] * 2,
        input_output_aliases={1: 0, 3: 1},
    )(here, y_out, y_got, gr_out, gr_got)

    both = arrived[1] + arrived[0]
    home_mine, home_other, away_mine, away_other = simple(
        last_kernel, here, both, [whole(a.shape) for a in both],
        [jax.ShapeDtypeStruct((dshare, width), t) for t in (F32, BF, BF, BF)], [whole((dshare, width))] * 4,
        [V((share, width), F32)] * 2,
    )
    sections = lax.axis_size("section")
    cross = [(s * ranks + i, (s ^ 1) * ranks + (i ^ 1)) for s in range(sections) for i in range(ranks)]
    arrays = [home_mine, paired(away_mine), along(home_other, 1, 2, 1), lax.ppermute(away_other, ("section", "dp"), cross),
              shuffle.astype(F32)]
    shapes = [(dshare, joined), (dshare, d), (dshare * fshare, d), (1, dshare), (1, hshare), (1, hshare), (1, dshare * fshare),
              (1, dshare)]
    g_in, g_attn, g_down, g_ng, g_q, g_k, g_ub, g_ob = simple(
        partial(finish_kernel, d, ff), here, arrays, [whole(a.shape) for a in arrays],
        [jax.ShapeDtypeStruct(s, F32) for s in shapes], [whole(s) for s in shapes], [],
    )
    return (y_out.reshape(1, slots * rows, d), gr_out.reshape(1, slots * rows, d), g_in[None], g_attn[None], g_down[None],
            g_ng, g_q, g_k, g_ub, g_ob)


def solution(mesh):
    in_specs = (P("dp", None),) * 3 + (P("section", "dp", None),) * 3 + (P("section", "dp"),) * 5
    out_specs = (P("section", "dp", None),) * 5 + (P("section", "dp"),) * 5
    return jax.shard_map(body, mesh=mesh, in_specs=in_specs, out_specs=out_specs, check_vma=False)
```

```python
from functools import partial
import math

import jax
import jax.numpy as jnp
from jax import lax
from jax.experimental import pallas as pl
from jax.experimental.pallas import tpu as pltpu
from jax.sharding import PartitionSpec as P

BF = jnp.bfloat16
F32 = jnp.float32
VMEM_LIMIT = 60 * 1024 * 1024
EPS = 1e-06
NN = (((1,), (0,)), ((), ()))
NT = (((1,), (1,)), ((), ()))
TN = (((0,), (0,)), ((), ()))
LANES = 128
WIDE = 256
ABSENT = 16


def mm(a, b, dims=NN):
    return lax.dot_general(a, b, dims, preferred_element_type=F32)


def head_mean(x, spread, exact):
    parts = []
    for at in range(0, x.shape[1], WIDE):
        piece = x[:, at : at + WIDE]
        top = piece.astype(BF)
        total = mm(top, spread)
        if exact:
            total = total + mm((piece - top.astype(F32)).astype(BF), spread)
        parts.append(total)
    return jnp.concatenate(parts, axis=1)


def row_norm(x):
    centered = x - jnp.mean(x, axis=-1, keepdims=True)
    rstd = lax.rsqrt(jnp.mean(centered * centered, axis=-1, keepdims=True) + EPS)
    return centered * rstd, rstd


def norm_back(grad, normal, rstd, spread):
    return rstd * (grad - head_mean(grad, spread, False) - normal * head_mean(grad * normal, spread, False))


def lane_half(x, second):
    lane = lax.broadcasted_iota(jnp.int32, x.shape, 1)
    return jnp.where((lane >= LANES // 2) if second else (lane < LANES // 2), x, jnp.zeros_like(x))


class Copies:
    def __init__(self, sems):
        self.sems, self.used = sems, 0

    def start(self, src, dst):
        copy = pltpu.make_async_copy(src, dst, self.sems.at[self.used])
        self.used += 1
        copy.start()
        return copy

    def from_either(self, flag, yes, no, dst):
        sem = self.sems.at[self.used]
        self.used += 1

        @pl.when(flag == 1)
        def _():
            pltpu.make_async_copy(yes, dst, sem).start()

        @pl.when(flag != 1)
        def _():
            pltpu.make_async_copy(no, dst, sem).start()

        return pltpu.make_async_copy(yes, dst, sem)

    def either(self, flag, src, yes, no):
        sem = self.sems.at[self.used]
        self.used += 1

        @pl.when(flag == 1)
        def _():
            pltpu.make_async_copy(src, yes, sem).start()

        @pl.when(flag != 1)
        def _():
            pltpu.make_async_copy(src, no, sem).start()

        return pltpu.make_async_copy(src, yes, sem)


def result_out(home, value, result, rounded, send, copies):
    sem = copies.sems.at[copies.used]
    copies.used += 1

    @pl.when(home == 1)
    def _():
        copy = pltpu.make_async_copy(value, result, sem)
        copy.start()
        copy.wait()

    @pl.when(home != 1)
    def _():
        copy = pltpu.make_async_copy(rounded, send, sem)
        copy.start()
        copy.wait()


def chosen(home, pair, two):
    return jnp.where(home == 1, pair[0][...], pair[1][...]) if two else pair[0][...]


def weights_from(cin, home, two, mine, theirs):
    def fetch(part, dst):
        if two:
            return cin.from_either(home, part(*mine), part(*theirs), dst)
        return cin.start(part(*mine), dst)

    return fetch


def forward_kernel(d, ff, chunks, kind, idx, *refs):
    @pl.when(idx[0] == 1)
    def _():
        forward_work(d, ff, chunks, kind, idx, *refs)


def forward_work(d, ff, chunks, kind, idx, x_in, x_alt, g, g3, o, o3, ids_col, ids_row, *refs):
    two = kind in ("enter", "pair")
    ngains, gainss, ubiass, obiass, spread, refs = refs[:2], refs[2:4], refs[4:6], refs[6:8], refs[8], refs[9:]
    refs = refs[13:]
    ybf, xs, qs, ks, vs, ns, nrs, gps, es, small, kept, sent, y_out, y_send = refs[:14]
    (x_v, h_v, w_v, u_v, d_v, a_v, q_v, k_v, v_v, n_v, r_v, act_v, gp_v, e_v, rs_v, att_v, acc_v, y_v, yb_v, ins, outs) = refs[14:]
    rows = x_v.shape[0]
    fc = ff // chunks
    core, slot, home = idx[1], idx[2], idx[3]
    cin, cout = Copies(ins), Copies(outs)
    ngain, gains, ubias, obias = (chosen(home, pair, two) for pair in (ngains, gainss, ubiass, obiass))
    if kind == "enter":
        x_copy = cin.from_either(home, x_in, x_alt, x_v)
    else:
        x_copy = cin.start(x_in.at[slot] if kind == "first" else x_in, x_v)
    fetch = weights_from(cin, home, two, (g, g3), (o, o3))
    wq = [fetch(lambda a, _, i=i: a.at[:, pl.ds(ff + d * i, d)], w_v.at[:, pl.ds(d * i, d)]) for i in range(3)]
    groups = fc // WIDE
    wff = []
    for c in range(chunks):
        wff.append([fetch(lambda a, _, c=c: a.at[:, pl.ds(fc * c, fc)], u_v.at[c])] + [
            fetch(lambda _, a, c=c, j=j: a.at[pl.ds(groups * c, groups), :, pl.ds(ff + 4 * d + d * j, d)],
                  d_v.at[pl.ds(groups * c, groups), j])
            for j in range(4)
        ])
    wa = fetch(lambda a, _: a.at[:, pl.ds(ff + 3 * d, d)], a_v)

    pending = []

    def side(i):
        return pl.ds(ff + d * i, d)

    x_copy.wait()
    keep = jnp.where(ids_col[0] < ABSENT, 1.0, 0.0)
    masked = keep * x_v[...].astype(F32)
    h_v[...] = (row_norm(masked)[0] * ngain).astype(BF)
    pending += [cout.start(x_v, xs), cout.start(h_v, kept.at[:, side(2)]), cout.start(h_v, sent.at[:, side(2)])]
    bias_mask = jnp.where(ids_col[0] == ids_row[0], 0.0, -1e9)
    for i in range(3):
        wq[i].wait()
        raw = mm(h_v[...], w_v[:, d * i : d * i + d])
        if i == 2:
            v_v[...] = raw.astype(BF)
            pending.append(cout.start(v_v, vs))
        else:
            centered = raw - head_mean(raw, spread[...], True)
            rstd = lax.rsqrt(head_mean(centered * centered, spread[...], True) + EPS)
            normal = centered * rstd
            scaled = (normal * gains[i]).astype(BF)
            n_v[:, d * i : d * i + d] = normal.astype(BF)
            r_v[:, d * i : d * i + d] = rstd.astype(BF)
            if i == 0:
                q_v[...] = scaled * jnp.asarray(0.125, BF)
                pending.append(cout.start(q_v, qs))
            else:
                k_v[...] = scaled
                pending.append(cout.start(k_v, ks))
    pending += [cout.start(n_v, ns), cout.start(r_v, nrs)]
    ones = jnp.ones((16, rows), BF)
    pairs = d // LANES // chunks
    for c in range(chunks):
        for copy in wff[c]:
            copy.wait()
        pre = mm(h_v[...], u_v[c]) + ubias[:, fc * c : fc * c + fc]
        cdf = 0.5 * (1.0 + lax.erf(pre * (1.0 / math.sqrt(2.0))))
        density = jnp.exp(-0.5 * pre * pre) * (1.0 / math.sqrt(2.0 * math.pi))
        act = (pre * cdf).astype(BF)
        act_v[c] = act
        gp_v[c] = (cdf + pre * density).astype(BF)
        total = mm(act, d_v[groups * c : groups * c + groups].reshape(fc, d))
        if c == 0:
            acc_v[...] = total
        else:
            acc_v[...] += total
        for p in range(pairs * c, pairs * c + pairs):
            cols = slice(LANES * p, LANES * p + LANES)
            vals_t = v_v[:, cols].T
            pair = q_v[:, cols]
            both = []
            for half in range(2):
                h = 2 * p + half
                e = jnp.exp(mm(k_v[:, cols], lane_half(pair, half), NT) + bias_mask).astype(BF)
                e_v[h] = e
                got = mm(jnp.concatenate([vals_t[64 * half : 64 * half + 64], ones], axis=0), e)
                inv = 1.0 / got[64:65]
                rs_v[h : h + 1, :] = inv
                both.append((got[:64] * inv).astype(BF))
            att_v[:, cols] = jnp.concatenate(both, axis=0).T
        span = pl.ds(fc * c, fc)
        pending += [cout.either(core, act_v.at[c], sent.at[:, span], kept.at[:, span]), cout.start(gp_v.at[c], gps.at[c]),
                    cout.start(e_v.at[pl.ds(2 * pairs * c, 2 * pairs)], es.at[pl.ds(2 * pairs * c, 2 * pairs)])]
    pending += [cout.start(rs_v, small), cout.either(core, att_v, sent.at[:, side(3)], kept.at[:, side(3)])]
    wa.wait()
    y = keep * (keep * x_v[...].astype(F32) + acc_v[...] + mm(att_v[...], a_v[...]) + obias)
    y_v[...] = y
    ybf[...] = y.astype(BF)
    yb_v[...] = y.astype(BF)
    result_out(home, y_v, y_out.at[slot], yb_v, y_send, cout)
    for copy in pending:
        copy.wait()


def backward_kernel(d, ff, chunks, kind, idx, *refs):
    @pl.when(idx[0] == 1)
    def _():
        backward_work(d, ff, chunks, kind, idx, *refs)


def backward_work(d, ff, chunks, kind, idx, g_in, g, g3, o, o3, ids_col, *refs):
    two = kind in ("first", "pair")
    ngains, gainss, spread, refs = refs[:2], refs[2:4], refs[4], refs[5:]
    xs, qs, ks, vs, ns, nrs, gps, es, small = refs[:9]
    refs = refs[9 + 5 :]
    gbf, kept, sent, table, gr_out, gr_send = refs[:6]
    (g_v, gb_v, w_v, u_v, d_v, a_v, x_v, q_v, k_v, v_v, n_v, r_v, gp_v, e_v, rs_v, gat_v, gqt_v, gk_v,
     gq_b, gk_b, gv_b, gj_v, acc_v, out_v, ob_v, sm_v, ins, outs) = refs[6:]
    rows = x_v.shape[0]
    fc = ff // chunks
    groups = fc // WIDE
    core, slot, home = idx[1], idx[2], idx[3]
    cin, cout = Copies(ins), Copies(outs)
    ngain, gains = (chosen(home, pair, two) for pair in (ngains, gainss))
    g_copy = cin.start(g_in.at[slot] if kind == "first" else g_in, g_v)
    fetch = weights_from(cin, home, two, (g, g3), (o, o3))
    wa = fetch(lambda a, _: a.at[:, pl.ds(ff + 3 * d, d)], a_v)
    heads = [cin.start(s, v) for s, v in ((small, rs_v), (ks, k_v), (vs, v_v), (qs, q_v))]
    pairs = d // LANES // chunks
    wff = []
    for c in range(chunks):
        wff.append(
            [fetch(lambda _, a, c=c, j=j: a.at[pl.ds(groups * c, groups), :, pl.ds(ff + 4 * d + d * j, d)],
                   d_v.at[pl.ds(groups * c, groups), j])
             for j in range(4)]
            + [cin.start(gps.at[c], gp_v.at[c]), fetch(lambda a, _, c=c: a.at[:, pl.ds(fc * c, fc)], u_v.at[c]),
               cin.start(es.at[pl.ds(2 * pairs * c, 2 * pairs)], e_v.at[pl.ds(2 * pairs * c, 2 * pairs)])]
        )
    norms = [cin.start(ns, n_v), cin.start(nrs, r_v)]
    wq = [fetch(lambda a, _, i=i: a.at[:, pl.ds(ff + d * i, d)], w_v.at[:, pl.ds(d * i, d)]) for i in range(3)]
    rows_in = cin.start(xs, x_v)

    pending = []

    def side(i):
        return pl.ds(ff + d * i, d)

    def summed(at, value):
        sm_v[:, at : at + value.shape[1]] = jnp.sum(value, axis=0, keepdims=True)

    g_copy.wait()
    keep = jnp.where(ids_col[0] < ABSENT, 1.0, 0.0)
    gres = keep * g_v[...].astype(F32)
    summed(d, gres)
    gb_v[...] = gres.astype(BF)
    pending.append(cout.either(core, gb_v, sent.at[:, side(0)], kept.at[:, side(0)]))
    wa.wait()
    gat_v[...] = mm(a_v[...], gb_v[...], NT).astype(BF)
    for copy in heads:
        copy.wait()
    zeros = jnp.zeros((LANES // 2, rows), BF)
    for c in range(chunks):
        for copy in wff[c]:
            copy.wait()
        gup = mm(gb_v[...], d_v[groups * c : groups * c + groups].reshape(fc, d), NT) * gp_v[c].astype(F32)
        summed(4 * d + fc * c, gup)
        gup = gup.astype(BF)
        gj_v[c] = gup
        span = pl.ds(fc * c, fc)
        pending.append(cout.either(core, gj_v.at[c], kept.at[:, span], sent.at[:, span]))
        total = mm(gup, u_v[c], NT)
        if c == 0:
            acc_v[...] = total
        else:
            acc_v[...] += total
        for p in range(pairs * c, pairs * c + pairs):
            cols = slice(LANES * p, LANES * p + LANES)
            keys, vals, pair = k_v[:, cols], v_v[:, cols], q_v[:, cols]
            keys_t = keys.T
            gk, gv = None, None
            for half in range(2):
                h = 2 * p + half
                at_rows = slice(64 * h, 64 * h + 64)
                inv = rs_v[h : h + 1, :]
                ga = (gat_v[at_rows, :].astype(F32) * inv).astype(BF)
                ga = jnp.concatenate([zeros, ga] if half else [ga, zeros], axis=0)
                e = e_v[h]
                ef = e.astype(F32)
                gp = ef * mm(vals, ga)
                dot = jnp.sum(gp, axis=0, keepdims=True) * inv
                gs = (gp - ef * dot).astype(BF)
                gk_h = mm(gs, lane_half(pair, half))
                gv_h = mm(e, ga, NT)
                gk = gk_h if gk is None else gk + gk_h
                gv = gv_h if gv is None else gv + gv_h
                gqt_v[at_rows, :] = mm(keys_t[64 * half : 64 * half + 64], gs) * 0.125
            gk_v[:, cols] = gk
            gv_b[:, cols] = gv.astype(BF)
    pending.append(cout.either(core, gv_b, sent.at[:, side(1)], kept.at[:, side(1)]))
    for copy in norms:
        copy.wait()
    for i, (grad, out) in enumerate(((gqt_v[...].T, gq_b), (gk_v[...], gk_b))):
        normal = n_v[:, d * i : d * i + d].astype(F32)
        summed(2 * d + d * i, grad * normal)
        out[...] = norm_back(grad * gains[i], normal, r_v[:, d * i : d * i + d].astype(F32), spread[...]).astype(BF)
        pending.append(cout.either(core, out, kept.at[:, side(i)], sent.at[:, side(i)]))
    for copy in wq:
        copy.wait()
    ghid = acc_v[...]
    for i, part in enumerate((gq_b, gk_b, gv_b)):
        ghid = ghid + mm(part[...], w_v[:, d * i : d * i + d], NT)
    rows_in.wait()
    xhat, rstd = row_norm(keep * x_v[...].astype(F32))
    summed(0, ghid * xhat)
    pending.append(cout.start(sm_v, table))
    gx = ghid * ngain
    gmask = rstd * (gx - jnp.mean(gx, axis=-1, keepdims=True) - xhat * jnp.mean(gx * xhat, axis=-1, keepdims=True))
    out = keep * (keep * g_v[...].astype(F32) + gmask)
    out_v[...] = out
    gbf[...] = out.astype(BF)
    ob_v[...] = out.astype(BF)
    result_out(home, out_v, gr_out.at[slot], ob_v, gr_send, cout)
    for copy in pending:
        copy.wait()


def split_small(values):
    top = values.astype(BF).astype(F32)
    lane = lax.broadcasted_iota(jnp.int32, values.shape, 1)
    return jnp.where(lane < 8, top, jnp.where(lane < 16, pltpu.roll(values - top, 8, 1), 0.0)).astype(BF)


def joined_small(parts):
    return parts + pltpu.roll(parts, LANES - 8, 1)


def small_table(d, ff, place, tables):
    total = tables[0][...]
    for table in tables[1:]:
        total = total + table[...]
    quarter = WIDE // 4
    ub = total[:, 4 * d :]
    up_rows = []
    for j in range(4):
        pieces = [ub[:, WIDE * b + quarter * j : WIDE * b + quarter * (j + 1)] for b in range(ff // WIDE)]
        up_rows.append(jnp.concatenate(pieces, axis=1))
    head_rows = []
    for i in range(2, 4):
        lanes = total[:, d * i : d * i + LANES]
        for p in range(1, d // LANES):
            lanes = lanes + total[:, d * i + LANES * p : d * i + LANES * (p + 1)]
        head_rows.append(lanes)
    both = jnp.concatenate(head_rows + [jnp.zeros((6, LANES), F32)], axis=0)
    placed = lax.dot_general(both, place[...], NN, precision=lax.Precision.HIGHEST, preferred_element_type=F32)
    rows = [total[:, :d], total[:, d : 2 * d]] + up_rows + [placed[0:1], placed[1:2], jnp.zeros((LANES - 8, d), F32)]
    return jnp.concatenate(rows, axis=0).T


def weight_grad_kernel(d, ff, count, stage, idx, place, *refs):
    tables, sources, refs = refs[:count], refs[count : 2 * count], refs[2 * count :]
    results, (big_v, a_v, b_v, c_v, out_v, ins, outs) = refs[:5], refs[5:]
    rows = sources[0].shape[0]
    tokens = count * rows
    quarter, half, third = WIDE // 4, ff // 2, ff // 3
    blocks = third // WIDE
    share = d // 16
    cut = 3 * d
    y, z, core = idx[0], idx[1], idx[2]

    def load(cin, at, width, to, to_at):
        return [cin.start(src.at[:, pl.ds(at, width)], to.at[i, :, pl.ds(to_at, width)]) for i, src in enumerate(sources)]

    def wait(copies):
        for copy in copies:
            copy.wait()

    def both(ref, at=0, width=d):
        return ref[:, :, at : at + width].reshape(tokens, width)

    def put(rows_at, cols_at, value):
        out_v[rows_at, cols_at] = value.astype(BF)

    def send_by_y(cout, at, width):
        cols = pl.ds(at, width)

        def rows_of(s, first, count):
            return out_v.at[pl.ds(pl.multiple_of(lax.rem(y + s, 4) * 4 * share + first, 16), count), cols]

        return [cout.start(rows_of(2, 0, 2 * share), results[3].at[:, cols]),
                cout.start(rows_of(2, 2 * share, 2 * share), results[4].at[:, cols])] + [
            cout.start(rows_of(s, 0, 4 * share), results[r].at[:, cols]) for r, s in ((1, 1), (2, 3), (0, 0))]

    def send_by_z(cout, at, width):
        cols = pl.ds(at, width)

        def rows_of(i, s):
            return out_v.at[pl.ds(pl.multiple_of((4 * i + lax.rem(z + s, 4)) * share, 16), share), cols]

        return [
            cout.start(rows_of(i, s), results[r].at[pl.ds(share * (i - base), share), cols])
            for r, s, base, count in ((3, 2, 0, 2), (4, 2, 2, 2), (1, 1, 0, 4), (2, 3, 0, 4), (0, 0, 0, 4))
            for i in range(base, base + count)
        ]

    everything = slice(0, d)

    @pl.when((core == 0) & (idx[5] == stage))
    def _():
        cin, cout = Copies(ins), Copies(outs)
        grads = load(cin, ff, d, a_v, 0)
        loads = [load(cin, third * k, third, big_v, third * k) for k in range(3)]
        attended = load(cin, ff + 3 * d, d, b_v, 0)
        hidden, values = load(cin, ff + 2 * d, d, c_v, 0), load(cin, ff + d, d, c_v, d)
        wait(grads)
        gb = both(a_v)
        for k in range(3):
            wait(loads[k])
            found = lax.dot_general(both(big_v, third * k, third), gb, TN, preferred_element_type=F32).astype(BF)
            for b in range(blocks):
                at = quarter * (blocks * k + b)
                for j in range(4):
                    put(slice(at, at + quarter), slice(d * j, d * j + d), found[WIDE * b + quarter * j : WIDE * b + quarter * (j + 1)])
        pending = send_by_y(cout, 0, 4 * d)
        wait(attended)
        put(everything, slice(4 * d, 5 * d), lax.dot_general(both(b_v), gb, TN, preferred_element_type=F32))
        wait(hidden + values)
        put(everything, slice(5 * d, 6 * d), lax.dot_general(both(c_v), both(c_v, d), TN, preferred_element_type=F32))
        put(everything, slice(6 * d, 6 * d + LANES), split_small(small_table(d, ff, place, tables)))
        wait(pending + send_by_y(cout, 4 * d, 2 * d + LANES))

    @pl.when((core == 1) & (idx[5] == stage))
    def _():
        cin, cout = Copies(ins), Copies(outs)
        hidden = load(cin, ff + 2 * d, d, a_v, 0)
        loads = [load(cin, third * k, third, big_v, third * k) for k in range(2)]
        queries = load(cin, ff, d, b_v, 0)
        loads.append(load(cin, 2 * third, third, big_v, 2 * third))
        keys = load(cin, ff + d, d, c_v, 0)
        wait(hidden)
        turned = both(a_v).T
        pending = []
        for k in range(2):
            wait(loads[k])
            put(everything, slice(third * k, third * k + third), mm(turned, both(big_v, third * k, third)))
        pending = send_by_z(cout, 0, 2 * third)
        wait(queries)
        put(everything, slice(ff, ff + d), mm(turned, both(b_v)))
        wait(loads[2])
        put(everything, slice(2 * third, ff), mm(turned, both(big_v, 2 * third, third)))
        wait(keys)
        put(everything, slice(ff + d, ff + 2 * d), mm(turned, both(c_v)))
        out_v[:, 6 * d :] = jnp.zeros((d, LANES), BF)
        wait(pending + send_by_z(cout, 2 * third, 6 * d + LANES - 2 * third))


def added(parts):
    total = parts[0][...].astype(F32)
    for part in parts[1:]:
        total = total + part[...].astype(F32)
    shape = total.shape
    total = total.reshape(-1, shape[-1])
    main, last = total[:, : shape[-1] - LANES], split_small(joined_small(total[:, shape[-1] - LANES :]))
    return jnp.concatenate([main.astype(BF), last], axis=1).reshape(shape)


def relay_kernel(stage, idx, up_in, down_in, up_got, down_got, up, down, hold, ins, outs):
    half = up_got.shape[0]

    @pl.when(idx[5] == stage)
    def _():
        cin, cout = Copies(ins), Copies(outs)
        parts = ((up_in, 0, up_got, up), (down_in, half, down_got, down))
        loads = [[cin.start(block.at[pl.ds(at, half)], hold.at[2 * i]), cin.start(got, hold.at[2 * i + 1])]
                 for i, (block, at, got, _) in enumerate(parts)]
        pending = []
        for i, (_, at, _, out) in enumerate(parts):
            for copy in loads[i]:
                copy.wait()
            hold[2 * i] = added([hold.at[2 * i], hold.at[2 * i + 1]])
            pending.append(cout.start(hold.at[2 * i], out.at[pl.ds(at, half)]))
        for copy in pending:
            copy.wait()


def mid_kernel(stage, idx, *refs):
    came, results, (in_v, out_v, ins, outs) = refs[:3], refs[3:7], refs[7:]
    share = results[0].shape[0]

    @pl.when(idx[5] == stage)
    def _():
        cin, cout = Copies(ins), Copies(outs)
        at = jnp.where(idx[2] == 0, idx[1], idx[0])
        order = [2, 1, 3, 0]
        blocks = [pl.multiple_of(lax.rem(at + s, 4) * share, 16) for s in order]
        loads = [[cin.start(part.at[pl.ds(block, share)], in_v.at[i, p]) for p, part in enumerate(came)]
                 for i, block in enumerate(blocks)]
        pending = []
        for i, s in enumerate(order):
            for copy in loads[i]:
                copy.wait()
            out_v[i] = added([in_v.at[i, p] for p in range(3)])
            pending.append(cout.start(out_v.at[i], results[s]))
        for copy in pending:
            copy.wait()


def last_pair_kernel(idx, *refs):
    came, (home_mine, home_other, away_mine, away_other, in_v, hold, ins) = refs[:8], refs[8:]
    share = home_mine.shape[0]
    core, odd = idx[2], idx[4]

    @pl.when(idx[5] == 1)
    def _():
        sum_of(came, in_v, hold, ins)

        def rows_of(k, which):
            return hold[k, pl.ds(pl.multiple_of(which * share, 8), share), :]

        for which, home, away in ((core, home_mine, away_mine), (1 - core, home_other, away_other)):
            home[...] = jnp.where(odd == 1, rows_of(1, which), rows_of(0, which)).astype(home.dtype)
            away[...] = jnp.where(odd == 1, rows_of(0, which), rows_of(1, which)).astype(away.dtype)


def last_kernel(idx, *refs):
    came, (pair_mine, pair_other, mine, other, in_v, hold, ins) = refs[:4], refs[4:]
    share = mine.shape[0]

    @pl.when(idx[5] == 0)
    def _():
        sum_of(came, in_v, hold, ins)
        for which, out in ((idx[2], mine), (1 - idx[2], other)):
            out[...] = hold[0, pl.ds(pl.multiple_of(which * share, 8), share), :].astype(out.dtype)

    @pl.when(idx[5] != 0)
    def _():
        mine[...] = pair_mine[...]
        other[...] = pair_other[...]


def sum_of(came, in_v, hold, sems):
    copies = Copies(sems)
    loads = [copies.start(part, in_v.at[i]) for i, part in enumerate(came)]
    for k in range(len(came) // 4):
        for copy in loads[4 * k : 4 * k + 4]:
            copy.wait()
        hold[k] = added([in_v.at[4 * k + i] for i in range(4)]).astype(F32)


def place_kernel(idx, y_in, y_got, g_in, g_got, y_out, g_out, y_v, g_v, sems):
    @pl.when(idx[5] == 1)
    def _():
        copies = Copies(sems)
        pending = []
        for got, wide_v, out in ((y_got, y_v, y_out), (g_got, g_v, g_out)):
            wide_v[...] = got[...].astype(F32)
            pending.append(copies.start(wide_v, out.at[1 - idx[3]]))
        for copy in pending:
            copy.wait()


def picked(rows, columns, wanted):
    row = lax.broadcasted_iota(jnp.int32, (rows, columns), 0)
    column = lax.broadcasted_iota(jnp.int32, (rows, columns), 1)
    return row, column, jnp.where(column == wanted(row), 1.0, 0.0)


def prepare_kernel(d, ff, p_in, p_attn, p_down, n_gain, o_bias, u_bias, q_gain, k_gain, shuffle, out):
    share = p_in.shape[0]
    heads_part = p_in.shape[1] - ff
    for at in range(0, ff, WIDE):
        out[:, at : at + WIDE] = mm(p_in[:, heads_part + at : heads_part + at + WIDE], shuffle[...]).astype(BF)
    out[:, ff : ff + heads_part] = p_in[:, :heads_part]
    at = ff + heads_part
    out[:, at : at + d] = p_attn[...]
    down = p_down[...]
    for j in range(4):
        take = picked(share, down.shape[0], lambda row: 4 * row + j)[2].astype(BF)
        out[:, at + d * (j + 1) : at + d * (j + 2)] = mm(take, down).astype(BF)

    def column_of(ref, wanted, where):
        values = ref[...].astype(F32)
        take = picked(share, values.shape[1], wanted)[2]
        lane = lax.broadcasted_iota(jnp.int32, (share, LANES), 1)
        return jnp.where(lane == where, jnp.sum(take * values, axis=1, keepdims=True), 0.0)

    table = column_of(n_gain, lambda row: row, 0) + column_of(o_bias, lambda row: row, 1)
    for j in range(4):
        table = table + column_of(u_bias, lambda row: 4 * row + j, 2 + j)
    table = table + column_of(q_gain, lambda row: row, 6) + column_of(k_gain, lambda row: row, 7)
    out[:, at + 5 * d :] = table.astype(BF)


def smalls_kernel(d, ff, base, g, place, ngain, gains, ubias, obias, t_v, sems):
    copy = Copies(sems).start(g.at[:, pl.ds(base, LANES)], t_v)
    quarter = WIDE // 4
    copy.wait()
    table = t_v[...].astype(F32).T
    ngain[...] = table[0:1]
    obias[...] = table[1:2]
    pieces = [table[2 + j : 3 + j, quarter * b : quarter * (b + 1)] for b in range(ff // WIDE) for j in range(4)]
    ubias[...] = jnp.concatenate(pieces, axis=1)
    both = mm(table[0:8].astype(BF), place[...])
    gains[0] = both[6:7]
    gains[1] = both[7:8]


def finish_kernel(d, ff, idx, own, a_in, b_in, c_in, shuffle, g_in, g_attn, g_down, g_ng, g_q, g_k, g_ub, g_ob):
    core = idx[2]
    share = own.shape[0]
    paired = idx[5] == 1
    mine = own[...] + jnp.where(paired, a_in[...].astype(F32), 0.0)
    theirs = b_in[...].astype(F32) + jnp.where(paired, c_in[...].astype(F32), 0.0)
    half0 = jnp.where(core == 0, mine, theirs)
    half1 = jnp.where(core == 0, theirs, mine)
    g_in[:, : 2 * d] = half1[:, ff : ff + 2 * d]
    g_in[:, 2 * d : 3 * d] = half0[:, 5 * d : 6 * d]
    for at in range(0, ff, WIDE):
        g_in[:, 3 * d + at : 3 * d + at + WIDE] = lax.dot_general(
            half1[:, at : at + WIDE], shuffle[...], NT, precision=lax.Precision.HIGHEST, preferred_element_type=F32)
    g_attn[...] = half0[:, 4 * d : 5 * d]
    stacked = jnp.concatenate([half0[:, at : at + d] for at in range(0, 4 * d, d)], axis=0)
    row, column, _ = picked(4 * share, 4 * share, lambda row: row)
    turn = jnp.where(column == lax.rem(row, 4) * share + row // 4, 1.0, 0.0)
    g_down[...] = lax.dot_general(turn, stacked, NN, precision=lax.Precision.HIGHEST, preferred_element_type=F32)
    small = joined_small(half0[:, 6 * d :])
    turned = jnp.concatenate([small, jnp.zeros((LANES - share, LANES), F32)], axis=0).T
    g_ng[...] = turned[0:1, :share]
    g_ob[...] = turned[1:2, :share]
    g_q[...] = turned[6:7, : g_q.shape[1]]
    g_k[...] = turned[7:8, : g_k.shape[1]]
    total = jnp.zeros((8, 4 * share), F32)
    for j in range(4):
        row, column, _ = picked(LANES, 4 * share, lambda row: row)
        spread_out = jnp.where(column == 4 * row + j, 1.0, 0.0)
        total = total + jnp.where(lax.broadcasted_iota(jnp.int32, (8, 4 * share), 0) == 2 + j, 1.0, 0.0) * lax.dot_general(
            turned[0:8], spread_out, NN, precision=lax.Precision.HIGHEST, preferred_element_type=F32)
    g_ub[...] = jnp.sum(total, axis=0, keepdims=True)


ANY = pl.BlockSpec(memory_space=pl.ANY)


def whole(shape):
    return pl.BlockSpec(shape, lambda i, idx: (0,) * len(shape))


def pick(shape):
    return pl.BlockSpec((1,) + shape, lambda i, idx: (idx[2],) + (0,) * len(shape))


def call(kernel, idx, ins, fresh, stashes, scratch, flops):
    outs = pl.pallas_call(
        kernel,
        grid_spec=pltpu.PrefetchScalarGridSpec(
            num_scalar_prefetch=1,
            grid=(1,),
            in_specs=[s for _, s in ins] + [ANY] * len(stashes),
            out_specs=[whole(fresh[0])] + [ANY] * len(stashes),
            scratch_shapes=scratch,
        ),
        out_shape=[jax.ShapeDtypeStruct(*fresh)] + [jax.ShapeDtypeStruct(a.shape, a.dtype) for a in stashes],
        input_output_aliases={1 + len(ins) + i: 1 + i for i in range(len(stashes))},
        compiler_params=pltpu.CompilerParams(dimension_semantics=("arbitrary",), vmem_limit_bytes=VMEM_LIMIT),
        cost_estimate=pl.CostEstimate(flops=flops, bytes_accessed=1 << 10, transcendentals=0),
    )(idx, *[a for a, _ in ins], *stashes)
    return outs[0], list(outs[1:])


def plain(kernel, arrays, specs, out_shapes, out_specs, scratch):
    return pl.pallas_call(
        kernel, grid=(1,), in_specs=specs, out_specs=out_specs, scratch_shapes=scratch, out_shape=out_shapes,
        compiler_params=pltpu.CompilerParams(dimension_semantics=("arbitrary",), vmem_limit_bytes=VMEM_LIMIT),
        cost_estimate=pl.CostEstimate(flops=1 << 10, bytes_accessed=1 << 10, transcendentals=0),
    )(*arrays)


def simple(kernel, idx, arrays, specs, out_shapes, out_specs, scratch, flops=1 << 10):
    return pl.pallas_call(
        kernel,
        grid_spec=pltpu.PrefetchScalarGridSpec(
            num_scalar_prefetch=1, grid=(1,), in_specs=specs, out_specs=out_specs, scratch_shapes=scratch
        ),
        out_shape=out_shapes,
        compiler_params=pltpu.CompilerParams(dimension_semantics=("arbitrary",), vmem_limit_bytes=VMEM_LIMIT),
        cost_estimate=pl.CostEstimate(flops=flops, bytes_accessed=1 << 10, transcendentals=0),
    )(idx, *arrays)


def moved(x, sections, to_section, to_rank):
    ranks = lax.axis_size("dp")
    pairs = [(s * ranks + i, to_section(s) * ranks + to_rank(i)) for s in sections for i in range(ranks)]
    return lax.ppermute(x, ("section", "dp"), pairs)


def same(i):
    return i


def partner(i):
    return i ^ 1


def body(tokens, cotangent, lengths, proj_in, proj_attn, proj_down, norm_gain, query_gain, key_gain, up_bias, out_bias):
    ranks = lax.axis_size("dp")
    section = lax.axis_index("section")
    rank = lax.axis_index("dp")
    slots = lengths.shape[0]
    rows = tokens.shape[0] // slots
    d = tokens.shape[1]
    joined = proj_in.shape[2]
    ff = proj_down.shape[1] * ranks
    head = query_gain.shape[1] * ranks
    heads = d // head
    dshare = proj_in.shape[1]
    fshare = proj_down.shape[1] // dshare
    hshare = query_gain.shape[1]
    chunks = 3
    wide = joined + d + ff
    stride = wide + LANES
    side = math.isqrt(ranks // 2)
    core, z, y = lax.rem(rank, 2), lax.rem(rank // 2, side), rank // (2 * side)
    stage, odd = section // 2, lax.rem(section, 2)
    slot = odd

    place = jnp.arange(WIDE, dtype=jnp.int32)
    source = (place % (WIDE // fshare)) * fshare + place // (WIDE // fshare)
    shuffle = (place[:, None] == source[None, :]).astype(BF)

    def full(a):
        return pl.BlockSpec(a.shape, lambda i: (0,) * a.ndim)

    shares = [proj_in[0], proj_attn[0], proj_down[0], norm_gain, out_bias, up_bias, query_gain, key_gain, shuffle]
    heads_part = joined - ff
    local = jax.ShapeDtypeStruct((dshare, stride), BF)
    local = plain(partial(prepare_kernel, d, ff), shares, [full(a) for a in shares], local, full(local), [])
    g = lax.all_gather(local, "dp", axis=0, tiled=True)
    o = lax.all_gather(moved(local, (2, 3), partner, same), "dp", axis=0, tiled=True)
    g3, o3 = (a.reshape(ff // WIDE, WIDE // fshare, stride) for a in (g, o))
    element = jnp.arange(d, dtype=jnp.int32) % head
    spread_gain = (jnp.arange(d, dtype=jnp.int32)[:, None] == (element // hshare * dshare + element % hshare)[None, :]).astype(BF)

    def small_rows(a):
        shapes = [jax.ShapeDtypeStruct(s, F32) for s in ((1, d), (2, 1, d), (1, ff), (1, d))]
        return plain(
            partial(smalls_kernel, d, ff, wide), [a, spread_gain], [ANY, full(spread_gain)], shapes,
            [full(s) for s in shapes], [pltpu.VMEM((d, LANES), BF), pltpu.SemaphoreType.DMA((1,))],
        )

    own_rows, pair_rows = small_rows(g), small_rows(o)

    def small_pairs(names, two):
        return [(a, whole(a.shape)) for i in names for a in (own_rows[i], (pair_rows if two else own_rows)[i])]

    column = jnp.arange(WIDE, dtype=jnp.int32) // head
    spread = jnp.where(column[:, None] == column[None, :], 1.0 / head, 0.0).astype(BF)

    toks = tokens.reshape(slots, rows, d)
    seeds = cotangent.reshape(slots, rows, d)
    ends = jnp.cumsum(lengths, axis=-1)
    position = jnp.arange(rows, dtype=jnp.int32)
    image = jnp.sum((position[None, :, None] >= ends[:, None, :]).astype(jnp.int32), axis=-1)
    image = jnp.where(position[None, :] < ends[:, 2:3], image, ABSENT + position[None, :])
    ids_col, ids_row = image[:, :, None], image[:, None, :]

    def stash(*shape, dtype=BF):
        return pl.pallas_call(
            lambda out: None, out_shape=jax.ShapeDtypeStruct(shape, dtype), out_specs=pl.BlockSpec(memory_space=pl.ANY)
        )()

    fc = ff // chunks
    groups = ff // WIDE

    def index_of(active, entry, home):
        return jnp.stack([active, core, jnp.asarray(entry), home]).astype(jnp.int32)

    V = pltpu.VMEM
    weights_v = [V((d, heads_part), BF), V((chunks, d, fc), BF), V((groups, fshare, WIDE // fshare, d), BF), V((d, d), BF)]
    sems = [pltpu.SemaphoreType.DMA((48,)), pltpu.SemaphoreType.DMA((48,))]
    stacked = ff + 4 * d
    operands = [[stash(rows, stacked), stash(rows, stacked)] for _ in range(4)]
    kept = [[stash(rows, d) for _ in range(4)] + [stash(rows, 2 * d), stash(rows, 2 * d), stash(chunks, rows, fc),
             stash(heads, rows, rows), stash(16, rows, dtype=F32)] for _ in range(4)]
    results = [stash(slots, rows, d, dtype=F32), stash(rows, d), stash(rows, d)]

    def forward(kind, keep_in, idx, x_in, x_alt):
        two = kind in ("enter", "pair")
        ybf, done = call(
            partial(forward_kernel, d, ff, chunks, kind), idx,
            [(x_in, ANY), (x_alt, ANY), (g, ANY), (g3, ANY), (o if two else g, ANY), (o3 if two else g3, ANY),
             (ids_col, pick((rows, 1))), (ids_row, pick((1, rows)))] + small_pairs((0, 1, 2, 3), two) + [(spread, whole((WIDE, WIDE)))],
            ((rows, d), BF),
            kept[keep_in] + operands[keep_in] + [results[0], results[1 + keep_in // 2]],
            [V((rows, d), BF), V((rows, d), BF)] + weights_v
            + [V((rows, d), BF)] * 3 + [V((rows, 2 * d), BF)] * 2 + [V((chunks, rows, fc), BF)] * 2
            + [V((heads, rows, rows), BF), V((16, rows), F32), V((rows, d), BF), V((rows, d), F32), V((rows, d), F32), V((rows, d), BF)]
            + sems,
            1 << 10,
        )
        kept[keep_in], operands[keep_in] = done[:9], done[9:11]
        results[0], results[1 + keep_in // 2] = done[11:]
        return ybf

    def hop(x, source, target):
        return lax.ppermute(x, "section", [(source, target)])

    at_home = jnp.asarray(True)
    came = []
    for s in range(slots):
        came.append(hop(forward("first", s, index_of(section == 0, s, at_home), toks, toks), 0, 1))
    sent = []
    for s in range(slots):
        sent.append(hop(forward("next", s, index_of(section == 1, s, at_home), came[s], came[s]), 1, 2 + s))
    here_x = forward("enter", 2, index_of(stage == 1, slot, odd == 0), sent[0], sent[1])
    forward("pair", 3, index_of(stage == 1, slot, odd == 1), here_x, here_x)
    y_out, _, y_send = results
    y_got = moved(y_send, (2, 3), partner, same)

    results = [stash(slots, rows, d, dtype=F32), stash(rows, d), stash(rows, d)]
    tables = [stash(1, stacked, dtype=F32) for _ in range(4)]
    width = 6 * d + LANES
    share = 2 * dshare
    position = jnp.arange(LANES, dtype=jnp.int32)[:, None] % head
    place = (position // hshare * dshare + position % hshare == jnp.arange(d, dtype=jnp.int32)[None, :]).astype(F32)
    here = jnp.stack([y, z, core, slot, odd, stage]).astype(jnp.int32)

    lower, upper = (0, 1), (2, 3)

    def rank_after(leg, by):
        def to(i):
            step = 2 * side if i % 2 == leg else 2
            digit = i // step % side
            return i + ((digit + by) % side - digit) * step

        return to

    def swap_cores(x, sections):
        return moved(x, sections, same, partner)

    def manual(kernel, arrays, specs, shapes, out_specs, scratch, aliases):
        return pl.pallas_call(
            kernel,
            grid_spec=pltpu.PrefetchScalarGridSpec(
                num_scalar_prefetch=1, grid=(1,), in_specs=specs, out_specs=out_specs, scratch_shapes=scratch
            ),
            out_shape=shapes,
            input_output_aliases=aliases,
            compiler_params=pltpu.CompilerParams(dimension_semantics=("arbitrary",), vmem_limit_bytes=VMEM_LIMIT),
            cost_estimate=pl.CostEstimate(flops=1 << 10, bytes_accessed=1 << 10, transcendentals=0),
        )(here, *arrays)

    def grads_by_place(of_stage, entries):
        smalls = [a for k, (_, table_got) in entries for a in (tables[k], table_got)]
        sources = [a for k, (got, _) in entries for a in (operands[k][0], got)]
        n = len(sources)
        return manual(
            partial(weight_grad_kernel, d, ff, n, of_stage),
            [place] + smalls + sources,
            [whole((LANES, d))] + [whole(a.shape) for a in smalls] + [ANY] * n,
            [jax.ShapeDtypeStruct((side * share, width), BF)] * 3 + [jax.ShapeDtypeStruct((side // 2 * share, width), BF)] * 2,
            [ANY] * 5,
            [V((n, rows, ff), BF), V((n, rows, d), BF), V((n, rows, d), BF), V((n, rows, 2 * d), BF), V((d, width), BF),
             pltpu.SemaphoreType.DMA((64,)), pltpu.SemaphoreType.DMA((32,))],
            {},
        )

    def halves(made, sections):
        return moved(made[3], sections, same, rank_after(0, 1)), moved(made[4], sections, same, rank_after(0, -1))

    def relayed(of_stage, made, came):
        own, up, down = made[:3]
        up, down = manual(
            partial(relay_kernel, of_stage), [up, down, *came], [ANY] * 4, [jax.ShapeDtypeStruct(up.shape, BF)] * 2, [ANY] * 2,
            [V((4, side // 2 * share, width), BF), pltpu.SemaphoreType.DMA((4,)), pltpu.SemaphoreType.DMA((2,))],
            {1: 0, 2: 1},
        )
        return [own, up, down]

    def first_leg(blocks, sections):
        own, up, down = blocks
        return [own, moved(up, sections, same, rank_after(0, 1)), moved(down, sections, same, rank_after(0, -1))]

    def second_leg(of_stage, came, sections):
        outs = manual(
            partial(mid_kernel, of_stage), came, [ANY] * 3, [jax.ShapeDtypeStruct((share, width), BF)] * side, [ANY] * side,
            [V((side, 3, share, width), BF), V((side, share, width), BF), pltpu.SemaphoreType.DMA((12,)), pltpu.SemaphoreType.DMA((4,))],
            {},
        )
        far, near, back = (moved(outs[s], sections, same, rank_after(1, s)) for s in (2, 1, 3))
        return [outs[0], near, far, back]

    def backward(kind, kept_in, idx, g_in):
        two = kind in ("first", "pair")
        gbf, done = call(
            partial(backward_kernel, d, ff, chunks, kind), idx,
            [(g_in, ANY), (g, ANY), (g3, ANY), (o if two else g, ANY), (o3 if two else g3, ANY), (ids_col, pick((rows, 1)))]
            + small_pairs((0, 1), two) + [(spread, whole((WIDE, WIDE)))] + [(a, ANY) for a in kept[kept_in]],
            ((rows, d), BF),
            operands[kept_in] + [tables[kept_in], results[0], results[1 + kept_in // 2]],
            [V((rows, d), BF), V((rows, d), BF)] + weights_v
            + [V((rows, d), BF)] * 4 + [V((rows, 2 * d), BF)] * 2
            + [V((chunks, rows, fc), BF), V((heads, rows, rows), BF), V((16, rows), F32)]
            + [V((d, rows), BF), V((d, rows), F32), V((rows, d), F32)]
            + [V((rows, d), BF)] * 3
            + [V((chunks, rows, fc), BF), V((rows, d), F32), V((rows, d), F32), V((rows, d), BF), V((1, stacked), F32)]
            + sems,
            1 << 10,
        )
        operands[kept_in], tables[kept_in] = done[:2], done[2]
        results[0], results[1 + kept_in // 2] = done[3:]
        return gbf

    here_g = backward("first", 3, index_of(stage == 1, slot, odd == 1), seeds)
    here_g = backward("pair", 2, index_of(stage == 1, slot, odd == 0), here_g)
    back = [hop(here_g, 2 + s, 1) for s in range(slots)]

    back = [hop(backward("next", s, index_of(section == 1, s, at_home), back[s]), 1, 0) for s in range(slots)]
    swaps = []
    for s in range(slots):
        if s > 0:
            operands[s - 1][1], back[s] = lax.optimization_barrier((operands[s - 1][1], back[s]))
            swaps.append((swap_cores(operands[s - 1][1], lower), swap_cores(tables[s - 1], lower)))
        backward("next", s, index_of(section == 0, s, at_home), back[s])
        if s > 0:
            operands[s][1], swaps[s - 1] = lax.optimization_barrier((operands[s][1], swaps[s - 1]))
    swaps.append((swap_cores(operands[-3][1], lower), swap_cores(tables[-3], lower)))
    made = grads_by_place(0, list(enumerate(swaps)))
    made = relayed(0, made, halves(made, lower))
    (made, operands[2], operands[3], tables[2], tables[3], gr_send) = lax.optimization_barrier(
        (made, operands[2], operands[3], tables[2], tables[3], results[2]))
    gr_got = moved(gr_send, upper, partner, same)
    swaps = [(swap_cores(operands[k][1], upper), swap_cores(tables[k], upper)) for k in (3, 2)]
    pair_made = [grads_by_place(1, [(k, swap)]) for k, swap in zip((3, 2), swaps)]
    legs = [first_leg(relayed(1, m, halves(m, upper)), upper) for m in pair_made]
    both = [second_leg(1, came, upper) for came in legs]
    both = both[1] + both[0]
    pair_shapes = [jax.ShapeDtypeStruct((dshare, width), t) for t in (F32, BF, BF, BF)]
    pair_mine, pair_other, away_mine, away_other = manual(
        last_pair_kernel, both, [ANY] * 8, pair_shapes, [whole((dshare, width))] * 4,
        [V((8, share, width), BF), V((2, share, width), F32), pltpu.SemaphoreType.DMA((8,))], {},
    )
    away_mine, away_other = moved(away_mine, upper, partner, same), moved(away_other, upper, partner, partner)

    arrived = second_leg(0, first_leg(made, lower), lower)
    mine, other = manual(
        last_kernel, arrived + [pair_mine, pair_other], [ANY] * 4 + [whole((dshare, width))] * 2, pair_shapes[:2],
        [whole((dshare, width))] * 2, [V((4, share, width), BF), V((1, share, width), F32), pltpu.SemaphoreType.DMA((4,))], {},
    )
    gr_out = results[0]
    y_out, gr_out = manual(
        place_kernel, [y_out, y_got, gr_out, gr_got], [ANY, whole((rows, d)), ANY, whole((rows, d))],
        [jax.ShapeDtypeStruct(y_out.shape, F32)] * 2, [ANY] * 2,
        [V((rows, d), F32), V((rows, d), F32), pltpu.SemaphoreType.DMA((2,))], {1: 0, 3: 1},
    )
    arrays = [mine, away_mine, swap_cores(other, range(4)), away_other, shuffle.astype(F32)]
    shapes = [(dshare, joined), (dshare, d), (dshare * fshare, d), (1, dshare), (1, hshare), (1, hshare), (1, dshare * fshare),
              (1, dshare)]
    g_in, g_attn, g_down, g_ng, g_q, g_k, g_ub, g_ob = simple(
        partial(finish_kernel, d, ff), here, arrays, [whole(a.shape) for a in arrays],
        [jax.ShapeDtypeStruct(s, F32) for s in shapes], [whole(s) for s in shapes], [],
    )
    return (y_out.reshape(1, slots * rows, d), gr_out.reshape(1, slots * rows, d), g_in[None], g_attn[None], g_down[None],
            g_ng, g_q, g_k, g_ub, g_ob)


def solution(mesh):
    in_specs = (P("dp", None),) * 3 + (P("section", "dp", None),) * 3 + (P("section", "dp"),) * 5
    out_specs = (P("section", "dp", None),) * 5 + (P("section", "dp"),) * 5
    return jax.shard_map(body, mesh=mesh, in_specs=in_specs, out_specs=out_specs, check_vma=False)
```

```python
from functools import partial
import math

import jax
import jax.numpy as jnp
from jax import lax
from jax.experimental import pallas as pl
from jax.experimental.pallas import tpu as pltpu
from jax.sharding import PartitionSpec as P

BF = jnp.bfloat16
F32 = jnp.float32
VMEM_LIMIT = 60 * 1024 * 1024
EPS = 1e-06
NN = (((1,), (0,)), ((), ()))
NT = (((1,), (1,)), ((), ()))
TN = (((0,), (0,)), ((), ()))
LANES = 128
WIDE = 256
ABSENT = 16


def mm(a, b, dims=NN):
    return lax.dot_general(a, b, dims, preferred_element_type=F32)


def head_mean(x, spread, exact):
    parts = []
    for at in range(0, x.shape[1], WIDE):
        piece = x[:, at : at + WIDE]
        top = piece.astype(BF)
        total = mm(top, spread)
        if exact:
            total = total + mm((piece - top.astype(F32)).astype(BF), spread)
        parts.append(total)
    return jnp.concatenate(parts, axis=1)


def row_norm(x):
    centered = x - jnp.mean(x, axis=-1, keepdims=True)
    rstd = lax.rsqrt(jnp.mean(centered * centered, axis=-1, keepdims=True) + EPS)
    return centered * rstd, rstd


def norm_back(grad, normal, rstd, spread):
    return rstd * (grad - head_mean(grad, spread, False) - normal * head_mean(grad * normal, spread, False))


def lane_half(x, second):
    lane = lax.broadcasted_iota(jnp.int32, x.shape, 1)
    return jnp.where((lane >= LANES // 2) if second else (lane < LANES // 2), x, jnp.zeros_like(x))


class Copies:
    def __init__(self, sems):
        self.sems, self.used = sems, 0

    def start(self, src, dst):
        copy = pltpu.make_async_copy(src, dst, self.sems.at[self.used])
        self.used += 1
        copy.start()
        return copy

    def either(self, flag, src, yes, no):
        sem = self.sems.at[self.used]
        self.used += 1

        @pl.when(flag == 1)
        def _():
            pltpu.make_async_copy(src, yes, sem).start()

        @pl.when(flag != 1)
        def _():
            pltpu.make_async_copy(src, no, sem).start()

        return pltpu.make_async_copy(src, yes, sem)


def result_out(home, value, result, rounded, send, copies):
    sem = copies.sems.at[copies.used]
    copies.used += 1

    @pl.when(home == 1)
    def _():
        copy = pltpu.make_async_copy(value, result, sem)
        copy.start()
        copy.wait()

    @pl.when(home != 1)
    def _():
        copy = pltpu.make_async_copy(rounded, send, sem)
        copy.start()
        copy.wait()


def forward_kernel(d, ff, chunks, layer, base, first, idx, *refs):
    @pl.when(idx[0] == 1)
    def _():
        forward_work(d, ff, chunks, layer, base, first, idx, *refs)


def head_spread(head):
    row = lax.broadcasted_iota(jnp.int32, (WIDE, WIDE), 0) // head
    column = lax.broadcasted_iota(jnp.int32, (WIDE, WIDE), 1) // head
    return jnp.where(row == column, 1.0 / head, 0.0).astype(BF)


def as_column(row):
    return jnp.broadcast_to(row, (LANES, row.shape[1])).T[:, :1]


def forward_work(d, ff, chunks, layer, base, first, idx, x_in, g, g3, ids, smalls, *refs):
    refs = refs[13:]
    ybf, xs, qs, ks, vs, ns, nrs, gps, es, small, kept, sent, y_out, y_send = refs[:14]
    (x_v, h_v, w_v, u_v, d_v, a_v, q_v, k_v, v_v, n_v, r_v, act_v, gp_v, e_v, rs_v, att_v, acc_v, y_v, yb_v, id_v, sm_v, ins, outs) = refs[14:]
    rows = x_v.shape[0]
    body_rows = pl.ds(0, rows)
    fc = ff // chunks
    core, slot, home = idx[1], idx[2], idx[3]
    cin, cout = Copies(ins), Copies(outs)
    x_copy = cin.start(x_in.at[slot] if first else x_in, x_v)
    small_copies = [cin.start(ids.at[slot], id_v), cin.start(smalls.at[layer], sm_v)]
    wq = [cin.start(g.at[:, pl.ds(base + ff + d * i, d)], w_v.at[:, pl.ds(d * i, d)]) for i in range(3)]
    groups = fc // WIDE
    wff = []
    for c in range(chunks):
        wff.append([cin.start(g.at[:, pl.ds(base + fc * c, fc)], u_v.at[c])] + [
            cin.start(g3.at[pl.ds(groups * c, groups), :, pl.ds(base + ff + 4 * d + d * j, d)], d_v.at[pl.ds(groups * c, groups), j])
            for j in range(4)
        ])
    wa = cin.start(g.at[:, pl.ds(base + ff + 3 * d, d)], a_v)

    pending = []

    def side(i):
        return pl.ds(ff + d * i, d)

    spread = head_spread(64)
    for copy in small_copies:
        copy.wait()
    ids_row = id_v[0:1]
    ids_col = as_column(ids_row)
    keep = jnp.where(ids_col < ABSENT, 1.0, 0.0)
    x_copy.wait()
    masked = keep * x_v[...].astype(F32)
    h_v[...] = (row_norm(masked)[0] * sm_v[0:1, :d]).astype(BF)
    pending += [cout.start(x_v, xs), cout.start(h_v, kept.at[body_rows, side(2)]), cout.start(h_v, sent.at[body_rows, side(2)])]
    bias_mask = jnp.where(ids_col == ids_row, 0.0, -1e9)
    for i in range(3):
        wq[i].wait()
        raw = mm(h_v[...], w_v[:, d * i : d * i + d])
        if i == 2:
            v_v[...] = raw.astype(BF)
            pending.append(cout.start(v_v, vs))
        else:
            centered = raw - head_mean(raw, spread, True)
            rstd = lax.rsqrt(head_mean(centered * centered, spread, True) + EPS)
            normal = centered * rstd
            scaled = (normal * sm_v[0:1, d * (2 + i) : d * (3 + i)]).astype(BF)
            n_v[:, d * i : d * i + d] = normal.astype(BF)
            r_v[:, d * i : d * i + d] = rstd.astype(BF)
            if i == 0:
                q_v[...] = scaled * jnp.asarray(0.125, BF)
                pending.append(cout.start(q_v, qs))
            else:
                k_v[...] = scaled
                pending.append(cout.start(k_v, ks))
    pending += [cout.start(n_v, ns), cout.start(r_v, nrs)]
    ones = jnp.ones((16, rows), BF)
    pairs = d // LANES // chunks
    for c in range(chunks):
        for copy in wff[c]:
            copy.wait()
        pre = mm(h_v[...], u_v[c]) + sm_v[1:2, fc * c : fc * c + fc]
        cdf = 0.5 * (1.0 + lax.erf(pre * (1.0 / math.sqrt(2.0))))
        density = jnp.exp(-0.5 * pre * pre) * (1.0 / math.sqrt(2.0 * math.pi))
        act = (pre * cdf).astype(BF)
        act_v[c] = act
        gp_v[c] = (cdf + pre * density).astype(BF)
        total = mm(act, d_v[groups * c : groups * c + groups].reshape(fc, d))
        if c == 0:
            acc_v[...] = total
        else:
            acc_v[...] += total
        for p in range(pairs * c, pairs * c + pairs):
            cols = slice(LANES * p, LANES * p + LANES)
            vals_t = v_v[:, cols].T
            pair = q_v[:, cols]
            both = []
            for half in range(2):
                h = 2 * p + half
                e = jnp.exp(mm(k_v[:, cols], lane_half(pair, half), NT) + bias_mask).astype(BF)
                e_v[h] = e
                got = mm(jnp.concatenate([vals_t[64 * half : 64 * half + 64], ones], axis=0), e)
                inv = 1.0 / got[64:65]
                rs_v[h : h + 1, :] = inv
                both.append((got[:64] * inv).astype(BF))
            att_v[:, cols] = jnp.concatenate(both, axis=0).T
        span = pl.ds(fc * c, fc)
        pending += [cout.either(core, act_v.at[c], sent.at[body_rows, span], kept.at[body_rows, span]), cout.start(gp_v.at[c], gps.at[c]),
                    cout.start(e_v.at[pl.ds(2 * pairs * c, 2 * pairs)], es.at[pl.ds(2 * pairs * c, 2 * pairs)])]
    pending += [cout.start(rs_v, small), cout.either(core, att_v, sent.at[body_rows, side(3)], kept.at[body_rows, side(3)])]
    wa.wait()
    y = keep * (keep * x_v[...].astype(F32) + acc_v[...] + mm(att_v[...], a_v[...]) + sm_v[0:1, d : 2 * d])
    y_v[...] = y
    yb_v[...] = y.astype(BF)
    pending.append(cout.start(yb_v, ybf))
    result_out(home, y_v, y_out.at[slot], yb_v, y_send, cout)
    for copy in pending:
        copy.wait()


def backward_kernel(d, ff, chunks, layer, base, first, idx, *refs):
    @pl.when(idx[0] == 1)
    def _():
        backward_work(d, ff, chunks, layer, base, first, idx, *refs)


def backward_work(d, ff, chunks, layer, base, first, idx, g_in, g, g3, ids, smalls, *refs):
    xs, qs, ks, vs, ns, nrs, gps, es, small = refs[:9]
    refs = refs[9 + 4 :]
    gbf, kept, sent, gr_out, gr_send = refs[:5]
    (g_v, gb_v, w_v, u_v, d_v, a_v, x_v, q_v, k_v, v_v, n_v, r_v, gp_v, e_v, rs_v, gat_v, gqt_v, gk_v,
     gq_b, gk_b, gv_b, gj_v, acc_v, out_v, ob_v, sm_v, sp_v, id_v, gain_v, ins, outs) = refs[5:]
    rows = x_v.shape[0]
    body_rows = pl.ds(0, rows)
    fc = ff // chunks
    groups = fc // WIDE
    core, slot, home = idx[1], idx[2], idx[3]
    cin, cout = Copies(ins), Copies(outs)
    g_copy = cin.start(g_in.at[slot] if first else g_in, g_v)
    small_copies = [cin.start(ids.at[slot], id_v), cin.start(smalls.at[layer], gain_v)]
    wa = cin.start(g.at[:, pl.ds(base + ff + 3 * d, d)], a_v)
    heads = [cin.start(s, v) for s, v in ((small, rs_v), (ks, k_v), (vs, v_v), (qs, q_v))]
    pairs = d // LANES // chunks
    wff = []
    for c in range(chunks):
        wff.append(
            [cin.start(g3.at[pl.ds(groups * c, groups), :, pl.ds(base + ff + 4 * d + d * j, d)], d_v.at[pl.ds(groups * c, groups), j])
             for j in range(4)]
            + [cin.start(gps.at[c], gp_v.at[c]), cin.start(g.at[:, pl.ds(base + fc * c, fc)], u_v.at[c]),
               cin.start(es.at[pl.ds(2 * pairs * c, 2 * pairs)], e_v.at[pl.ds(2 * pairs * c, 2 * pairs)])]
        )
    norms = [cin.start(ns, n_v), cin.start(nrs, r_v)]
    wq = [cin.start(g.at[:, pl.ds(base + ff + d * i, d)], w_v.at[:, pl.ds(d * i, d)]) for i in range(3)]
    rows_in = cin.start(xs, x_v)

    pending = []

    def side(i):
        return pl.ds(ff + d * i, d)

    def summed(at, value):
        sm_v[:, at : at + value.shape[1]] = jnp.sum(value, axis=0, keepdims=True)

    spread = head_spread(64)
    for copy in small_copies:
        copy.wait()
    keep = jnp.where(as_column(id_v[0:1]) < ABSENT, 1.0, 0.0)
    g_copy.wait()
    gres = keep * g_v[...].astype(F32)
    summed(d, gres)
    gb_v[...] = gres.astype(BF)
    pending.append(cout.either(core, gb_v, sent.at[body_rows, side(0)], kept.at[body_rows, side(0)]))
    wa.wait()
    gat_v[...] = mm(a_v[...], gb_v[...], NT).astype(BF)
    for copy in heads:
        copy.wait()
    zeros = jnp.zeros((LANES // 2, rows), BF)
    for c in range(chunks):
        for copy in wff[c]:
            copy.wait()
        gup = mm(gb_v[...], d_v[groups * c : groups * c + groups].reshape(fc, d), NT) * gp_v[c].astype(F32)
        summed(4 * d + fc * c, gup)
        gup = gup.astype(BF)
        gj_v[c] = gup
        span = pl.ds(fc * c, fc)
        pending.append(cout.either(core, gj_v.at[c], kept.at[body_rows, span], sent.at[body_rows, span]))
        total = mm(gup, u_v[c], NT)
        if c == 0:
            acc_v[...] = total
        else:
            acc_v[...] += total
        for p in range(pairs * c, pairs * c + pairs):
            cols = slice(LANES * p, LANES * p + LANES)
            keys, vals, pair = k_v[:, cols], v_v[:, cols], q_v[:, cols]
            keys_t = keys.T
            gk, gv = None, None
            for half in range(2):
                h = 2 * p + half
                at_rows = slice(64 * h, 64 * h + 64)
                inv = rs_v[h : h + 1, :]
                ga = (gat_v[at_rows, :].astype(F32) * inv).astype(BF)
                ga = jnp.concatenate([zeros, ga] if half else [ga, zeros], axis=0)
                e = e_v[h]
                ef = e.astype(F32)
                gp = ef * mm(vals, ga)
                dot = jnp.sum(gp, axis=0, keepdims=True) * inv
                gs = (gp - ef * dot).astype(BF)
                gk_h = mm(gs, lane_half(pair, half))
                gv_h = mm(e, ga, NT)
                gk = gk_h if gk is None else gk + gk_h
                gv = gv_h if gv is None else gv + gv_h
                gqt_v[at_rows, :] = mm(keys_t[64 * half : 64 * half + 64], gs) * 0.125
            gk_v[:, cols] = gk
            gv_b[:, cols] = gv.astype(BF)
    pending.append(cout.either(core, gv_b, sent.at[body_rows, side(1)], kept.at[body_rows, side(1)]))
    for copy in norms:
        copy.wait()
    for i, (grad, out) in enumerate(((gqt_v[...].T, gq_b), (gk_v[...], gk_b))):
        normal = n_v[:, d * i : d * i + d].astype(F32)
        summed(2 * d + d * i, grad * normal)
        gain = gain_v[0:1, d * (2 + i) : d * (3 + i)]
        out[...] = norm_back(grad * gain, normal, r_v[:, d * i : d * i + d].astype(F32), spread).astype(BF)
        pending.append(cout.either(core, out, kept.at[body_rows, side(i)], sent.at[body_rows, side(i)]))
    for copy in wq:
        copy.wait()
    ghid = acc_v[...]
    for i, part in enumerate((gq_b, gk_b, gv_b)):
        ghid = ghid + mm(part[...], w_v[:, d * i : d * i + d], NT)
    rows_in.wait()
    xhat, rstd = row_norm(keep * x_v[...].astype(F32))
    summed(0, ghid * xhat)
    top = sm_v[...].astype(BF).astype(F32)
    sp_v[...] = jnp.concatenate([top, sm_v[...] - top, jnp.zeros((14, top.shape[1]), F32)], axis=0).astype(BF)
    tail = pl.ds(rows, 16)
    pending += [cout.start(sp_v, kept.at[tail]), cout.start(sp_v, sent.at[tail])]
    gx = ghid * gain_v[0:1, :d]
    gmask = rstd * (gx - jnp.mean(gx, axis=-1, keepdims=True) - xhat * jnp.mean(gx * xhat, axis=-1, keepdims=True))
    out = keep * (keep * g_v[...].astype(F32) + gmask)
    out_v[...] = out
    ob_v[...] = out.astype(BF)
    pending.append(cout.start(ob_v, gbf))
    result_out(home, out_v, gr_out.at[slot], ob_v, gr_send, cout)
    for copy in pending:
        copy.wait()


def split_small(values):
    top = values.astype(BF).astype(F32)
    lane = lax.broadcasted_iota(jnp.int32, values.shape, 1)
    return jnp.where(lane < 8, top, jnp.where(lane < 16, pltpu.roll(values - top, 8, 1), 0.0)).astype(BF)


def joined_small(parts):
    return parts + pltpu.roll(parts, LANES - 8, 1)


def small_table(d, ff, tables):
    total = jnp.zeros((1, tables.shape[2]), F32)
    for i in range(tables.shape[0]):
        parts = tables[i].astype(F32)
        total = total + parts[0:1] + parts[1:2]
    lane = lax.broadcasted_iota(jnp.int32, (LANES, d), 0) % 64
    place = jnp.where(lax.broadcasted_iota(jnp.int32, (LANES, d), 1) == lane // 2 * 24 + lane % 2, 1.0, 0.0)
    quarter = WIDE // 4
    ub = total[:, 4 * d :]
    up_rows = []
    for j in range(4):
        pieces = [ub[:, WIDE * b + quarter * j : WIDE * b + quarter * (j + 1)] for b in range(ff // WIDE)]
        up_rows.append(jnp.concatenate(pieces, axis=1))
    head_rows = []
    for i in range(2, 4):
        lanes = total[:, d * i : d * i + LANES]
        for p in range(1, d // LANES):
            lanes = lanes + total[:, d * i + LANES * p : d * i + LANES * (p + 1)]
        head_rows.append(lanes)
    both = jnp.concatenate(head_rows + [jnp.zeros((6, LANES), F32)], axis=0)
    placed = lax.dot_general(both, place, NN, precision=lax.Precision.HIGHEST, preferred_element_type=F32)
    rows = [total[:, :d], total[:, d : 2 * d]] + up_rows + [placed[0:1], placed[1:2], jnp.zeros((LANES - 8, d), F32)]
    return jnp.concatenate(rows, axis=0).T


def weight_grad_kernel(d, ff, idx, kept, got, *refs):
    results, (big_v, a_v, b_v, c_v, out_v, t_v, ins, outs) = refs[:5], refs[5:]
    rows = kept.shape[0] - t_v.shape[1]
    tokens = 2 * rows
    quarter, half, third = WIDE // 4, ff // 2, ff // 3
    blocks = third // WIDE
    share = d // 16
    cut = 3 * d
    y, z, core = idx[0], idx[1], idx[2]

    def load(cin, at, width, to, to_at):
        return [cin.start(src.at[pl.ds(0, rows), pl.ds(at, width)], to.at[i, :, pl.ds(to_at, width)]) for i, src in enumerate((kept, got))]

    def wait(copies):
        for copy in copies:
            copy.wait()

    def both(ref, at=0, width=d):
        return ref[:, :, at : at + width].reshape(tokens, width)

    def put(rows_at, cols_at, value):
        out_v[rows_at, cols_at] = value.astype(BF)

    def send_by_y(cout, at, width):
        cols = pl.ds(at, width)

        def rows_of(s, first, count):
            return out_v.at[pl.ds(pl.multiple_of(lax.rem(y + s, 4) * 4 * share + first, 16), count), cols]

        return [cout.start(rows_of(2, 0, 2 * share), results[3].at[:, cols]),
                cout.start(rows_of(2, 2 * share, 2 * share), results[4].at[:, cols])] + [
            cout.start(rows_of(s, 0, 4 * share), results[r].at[:, cols]) for r, s in ((1, 1), (2, 3), (0, 0))]

    def send_by_z(cout, at, width):
        cols = pl.ds(at, width)

        def rows_of(i, s):
            return out_v.at[pl.ds(pl.multiple_of((4 * i + lax.rem(z + s, 4)) * share, 16), share), cols]

        return [
            cout.start(rows_of(i, s), results[r].at[pl.ds(share * (i - base), share), cols])
            for r, s, base, count in ((3, 2, 0, 2), (4, 2, 2, 2), (1, 1, 0, 4), (2, 3, 0, 4), (0, 0, 0, 4))
            for i in range(base, base + count)
        ]

    everything = slice(0, d)

    @pl.when(core == 0)
    def _():
        cin, cout = Copies(ins), Copies(outs)
        grads = load(cin, ff, d, a_v, 0)
        loads = [load(cin, third * k, third, big_v, third * k) for k in range(3)]
        attended = load(cin, ff + 3 * d, d, b_v, 0)
        hidden, values = load(cin, ff + 2 * d, d, c_v, 0), load(cin, ff + d, d, c_v, d)
        smalls = [cin.start(src.at[pl.ds(rows, t_v.shape[1])], t_v.at[i]) for i, src in enumerate((kept, got))]
        wait(grads)
        gb = both(a_v)
        for k in range(3):
            wait(loads[k])
            found = lax.dot_general(both(big_v, third * k, third), gb, TN, preferred_element_type=F32).astype(BF)
            for b in range(blocks):
                at = quarter * (blocks * k + b)
                for j in range(4):
                    put(slice(at, at + quarter), slice(d * j, d * j + d), found[WIDE * b + quarter * j : WIDE * b + quarter * (j + 1)])
        pending = send_by_y(cout, 0, 4 * d)
        wait(attended)
        put(everything, slice(4 * d, 5 * d), lax.dot_general(both(b_v), gb, TN, preferred_element_type=F32))
        wait(hidden + values + smalls)
        put(everything, slice(5 * d, 6 * d), lax.dot_general(both(c_v), both(c_v, d), TN, preferred_element_type=F32))
        put(everything, slice(6 * d, 6 * d + LANES), split_small(small_table(d, ff, t_v)))
        wait(pending + send_by_y(cout, 4 * d, 2 * d + LANES))

    @pl.when(core == 1)
    def _():
        cin, cout = Copies(ins), Copies(outs)
        hidden = load(cin, ff + 2 * d, d, a_v, 0)
        loads = [load(cin, third * k, third, big_v, third * k) for k in range(2)]
        queries = load(cin, ff, d, b_v, 0)
        loads.append(load(cin, 2 * third, third, big_v, 2 * third))
        keys = load(cin, ff + d, d, c_v, 0)
        wait(hidden)
        turned = both(a_v).T
        pending = []
        for k in range(2):
            wait(loads[k])
            put(everything, slice(third * k, third * k + third), mm(turned, both(big_v, third * k, third)))
        pending = send_by_z(cout, 0, 2 * third)
        wait(queries)
        put(everything, slice(ff, ff + d), mm(turned, both(b_v)))
        wait(loads[2])
        put(everything, slice(2 * third, ff), mm(turned, both(big_v, 2 * third, third)))
        wait(keys)
        put(everything, slice(ff + d, ff + 2 * d), mm(turned, both(c_v)))
        out_v[:, 6 * d :] = jnp.zeros((d, LANES), BF)
        wait(pending + send_by_z(cout, 2 * third, 6 * d + LANES - 2 * third))


def added(parts):
    total = parts[0][...].astype(F32)
    for part in parts[1:]:
        total = total + part[...].astype(F32)
    shape = total.shape
    total = total.reshape(-1, shape[-1])
    main, last = total[:, : shape[-1] - LANES], split_small(joined_small(total[:, shape[-1] - LANES :]))
    return jnp.concatenate([main.astype(BF), last], axis=1).reshape(shape)


def relay_kernel(idx, up_in, down_in, up_got, down_got, up, down, hold, ins, outs):
    half = up_got.shape[0]

    cin, cout = Copies(ins), Copies(outs)
    parts = ((up_in, 0, up_got, up), (down_in, half, down_got, down))
    loads = [[cin.start(block.at[pl.ds(at, half)], hold.at[2 * i]), cin.start(got, hold.at[2 * i + 1])]
             for i, (block, at, got, _) in enumerate(parts)]
    pending = []
    for i, (_, at, _, out) in enumerate(parts):
        for copy in loads[i]:
            copy.wait()
        hold[2 * i] = added([hold.at[2 * i], hold.at[2 * i + 1]])
        pending.append(cout.start(hold.at[2 * i], out.at[pl.ds(at, half)]))
    for copy in pending:
        copy.wait()


def mid_kernel(idx, *refs):
    came, results, (in_v, out_v, ins, outs) = refs[:3], refs[3:7], refs[7:]
    share = results[0].shape[0]

    cin, cout = Copies(ins), Copies(outs)
    at = jnp.where(idx[2] == 0, idx[1], idx[0])
    order = [2, 1, 3, 0]
    blocks = [pl.multiple_of(lax.rem(at + s, 4) * share, 16) for s in order]
    loads = [[cin.start(part.at[pl.ds(block, share)], in_v.at[i, p]) for p, part in enumerate(came)]
             for i, block in enumerate(blocks)]
    pending = []
    for i, s in enumerate(order):
        for copy in loads[i]:
            copy.wait()
        out_v[i] = added([in_v.at[i, p] for p in range(3)])
        pending.append(cout.start(out_v.at[i], results[s]))
    for copy in pending:
        copy.wait()


def last_pair_kernel(idx, *refs):
    came, (home_mine, home_other, away_mine, away_other, in_v, hold, ins) = refs[:8], refs[8:]
    share = home_mine.shape[0]
    core, odd = idx[2], idx[4]

    sum_of(came, in_v, hold, ins)

    def rows_of(k, which):
        return hold[k, pl.ds(pl.multiple_of(which * share, 8), share), :]

    for which, home, away in ((core, home_mine, away_mine), (1 - core, home_other, away_other)):
        home[...] = jnp.where(odd == 1, rows_of(1, which), rows_of(0, which)).astype(home.dtype)
        away[...] = jnp.where(odd == 1, rows_of(0, which), rows_of(1, which)).astype(away.dtype)


def sum_of(came, in_v, hold, sems):
    copies = Copies(sems)
    loads = [copies.start(part, in_v.at[i]) for i, part in enumerate(came)]
    for k in range(len(came) // 4):
        for copy in loads[4 * k : 4 * k + 4]:
            copy.wait()
        hold[k] = added([in_v.at[4 * k + i] for i in range(4)]).astype(F32)


def place_kernel(idx, y_in, y_got, g_in, g_got, y_out, g_out, y_v, g_v, sems):
    copies = Copies(sems)
    pending = []
    for got, wide_v, out in ((y_got, y_v, y_out), (g_got, g_v, g_out)):
        wide_v[...] = got[...].astype(F32)
        pending.append(copies.start(wide_v, out.at[1 - idx[3]]))
    for copy in pending:
        copy.wait()


def picked(rows, columns, wanted):
    row = lax.broadcasted_iota(jnp.int32, (rows, columns), 0)
    column = lax.broadcasted_iota(jnp.int32, (rows, columns), 1)
    return row, column, jnp.where(column == wanted(row), 1.0, 0.0)


def prepare_kernel(d, ff, p_in, p_attn, p_down, n_gain, o_bias, u_bias, q_gain, k_gain, shuffle, out):
    share = p_in.shape[0]
    heads_part = p_in.shape[1] - ff
    for at in range(0, ff, WIDE):
        out[:, at : at + WIDE] = mm(p_in[:, heads_part + at : heads_part + at + WIDE], shuffle[...]).astype(BF)
    out[:, ff : ff + heads_part] = p_in[:, :heads_part]
    at = ff + heads_part
    out[:, at : at + d] = p_attn[...]
    down = p_down[...]
    for j in range(4):
        take = picked(share, down.shape[0], lambda row: 4 * row + j)[2].astype(BF)
        out[:, at + d * (j + 1) : at + d * (j + 2)] = mm(take, down).astype(BF)

    def column_of(ref, wanted, where):
        values = ref[...].astype(F32)
        take = picked(share, values.shape[1], wanted)[2]
        lane = lax.broadcasted_iota(jnp.int32, (share, LANES), 1)
        return jnp.where(lane == where, jnp.sum(take * values, axis=1, keepdims=True), 0.0)

    table = column_of(n_gain, lambda row: row, 0) + column_of(o_bias, lambda row: row, 1)
    for j in range(4):
        table = table + column_of(u_bias, lambda row: 4 * row + j, 2 + j)
    table = table + column_of(q_gain, lambda row: row, 6) + column_of(k_gain, lambda row: row, 7)
    out[:, at + 5 * d :] = table.astype(BF)


def smalls_kernel(d, ff, base, stride, g, place, out, t_v, sems):
    copies = Copies(sems)
    loads = [copies.start(g.at[:, pl.ds(base + stride * layer, LANES)], t_v.at[layer]) for layer in range(2)]
    quarter = WIDE // 4
    for layer in range(2):
        loads[layer].wait()
        table = t_v[layer].astype(F32).T
        pieces = [table[2 + j : 3 + j, quarter * b : quarter * (b + 1)] for b in range(ff // WIDE) for j in range(4)]
        both = mm(table[0:8].astype(BF), place[...])
        first = jnp.concatenate([table[0:1], table[1:2], both[6:7], both[7:8]], axis=1)
        out[layer] = jnp.concatenate([first, jnp.concatenate(pieces, axis=1), jnp.zeros((6, ff), F32)], axis=0)


def finish_kernel(d, ff, idx, own, a_in, b_in, c_in, shuffle, g_in, g_attn, g_down, g_ng, g_q, g_k, g_ub, g_ob):
    core = idx[2]
    share = own.shape[0]
    mine = own[...] + a_in[...].astype(F32)
    theirs = b_in[...].astype(F32) + c_in[...].astype(F32)
    half0 = jnp.where(core == 0, mine, theirs)
    half1 = jnp.where(core == 0, theirs, mine)
    g_in[:, : 2 * d] = half1[:, ff : ff + 2 * d]
    g_in[:, 2 * d : 3 * d] = half0[:, 5 * d : 6 * d]
    for at in range(0, ff, WIDE):
        g_in[:, 3 * d + at : 3 * d + at + WIDE] = lax.dot_general(
            half1[:, at : at + WIDE], shuffle[...], NT, precision=lax.Precision.HIGHEST, preferred_element_type=F32)
    g_attn[...] = half0[:, 4 * d : 5 * d]
    stacked = jnp.concatenate([half0[:, at : at + d] for at in range(0, 4 * d, d)], axis=0)
    row, column, _ = picked(4 * share, 4 * share, lambda row: row)
    turn = jnp.where(column == lax.rem(row, 4) * share + row // 4, 1.0, 0.0)
    g_down[...] = lax.dot_general(turn, stacked, NN, precision=lax.Precision.HIGHEST, preferred_element_type=F32)
    small = joined_small(half0[:, 6 * d :])
    turned = jnp.concatenate([small, jnp.zeros((LANES - share, LANES), F32)], axis=0).T
    g_ng[...] = turned[0:1, :share]
    g_ob[...] = turned[1:2, :share]
    g_q[...] = turned[6:7, : g_q.shape[1]]
    g_k[...] = turned[7:8, : g_k.shape[1]]
    total = jnp.zeros((8, 4 * share), F32)
    for j in range(4):
        row, column, _ = picked(LANES, 4 * share, lambda row: row)
        spread_out = jnp.where(column == 4 * row + j, 1.0, 0.0)
        total = total + jnp.where(lax.broadcasted_iota(jnp.int32, (8, 4 * share), 0) == 2 + j, 1.0, 0.0) * lax.dot_general(
            turned[0:8], spread_out, NN, precision=lax.Precision.HIGHEST, preferred_element_type=F32)
    g_ub[...] = jnp.sum(total, axis=0, keepdims=True)


ANY = pl.BlockSpec(memory_space=pl.ANY)


def whole(shape):
    return pl.BlockSpec(shape, lambda i, idx: (0,) * len(shape))


def pick(shape):
    return pl.BlockSpec((1,) + shape, lambda i, idx: (idx[2],) + (0,) * len(shape))


def call(kernel, idx, ins, fresh, stashes, scratch, flops):
    outs = pl.pallas_call(
        kernel,
        grid_spec=pltpu.PrefetchScalarGridSpec(
            num_scalar_prefetch=1,
            grid=(1,),
            in_specs=[s for _, s in ins] + [ANY] * len(stashes),
            out_specs=[ANY] * (1 + len(stashes)),
            scratch_shapes=scratch,
        ),
        out_shape=[jax.ShapeDtypeStruct(*fresh)] + [jax.ShapeDtypeStruct(a.shape, a.dtype) for a in stashes],
        input_output_aliases={1 + len(ins) + i: 1 + i for i in range(len(stashes))},
        compiler_params=pltpu.CompilerParams(dimension_semantics=("arbitrary",), vmem_limit_bytes=VMEM_LIMIT),
        cost_estimate=pl.CostEstimate(flops=flops, bytes_accessed=1 << 10, transcendentals=0),
    )(idx, *[a for a, _ in ins], *stashes)
    return outs[0], list(outs[1:])


def plain(kernel, arrays, specs, out_shapes, out_specs, scratch):
    return pl.pallas_call(
        kernel, grid=(1,), in_specs=specs, out_specs=out_specs, scratch_shapes=scratch, out_shape=out_shapes,
        compiler_params=pltpu.CompilerParams(dimension_semantics=("arbitrary",), vmem_limit_bytes=VMEM_LIMIT),
        cost_estimate=pl.CostEstimate(flops=1 << 10, bytes_accessed=1 << 10, transcendentals=0),
    )(*arrays)


def simple(kernel, idx, arrays, specs, out_shapes, out_specs, scratch, flops=1 << 10):
    return pl.pallas_call(
        kernel,
        grid_spec=pltpu.PrefetchScalarGridSpec(
            num_scalar_prefetch=1, grid=(1,), in_specs=specs, out_specs=out_specs, scratch_shapes=scratch
        ),
        out_shape=out_shapes,
        compiler_params=pltpu.CompilerParams(dimension_semantics=("arbitrary",), vmem_limit_bytes=VMEM_LIMIT),
        cost_estimate=pl.CostEstimate(flops=flops, bytes_accessed=1 << 10, transcendentals=0),
    )(idx, *arrays)


def along(x, step, size, by):
    devices = lax.axis_size("dp")

    def to(i):
        digit = i // step % size
        return i + ((digit + by) % size - digit) * step

    return lax.ppermute(x, "dp", [(i, to(i)) for i in range(devices)])


def paired(x):
    return lax.ppermute(x, "section", [(0, 1), (1, 0), (2, 3), (3, 2)])


def body(tokens, cotangent, lengths, proj_in, proj_attn, proj_down, norm_gain, query_gain, key_gain, up_bias, out_bias):
    ranks = lax.axis_size("dp")
    section = lax.axis_index("section")
    rank = lax.axis_index("dp")
    slots = lengths.shape[0]
    rows = tokens.shape[0] // slots
    d = tokens.shape[1]
    joined = proj_in.shape[2]
    ff = proj_down.shape[1] * ranks
    head = query_gain.shape[1] * ranks
    heads = d // head
    dshare = proj_in.shape[1]
    fshare = proj_down.shape[1] // dshare
    hshare = query_gain.shape[1]
    chunks = 3
    wide = joined + d + ff
    stride = wide + LANES
    side = math.isqrt(ranks // 2)
    core, z, y = lax.rem(rank, 2), lax.rem(rank // 2, side), rank // (2 * side)
    stage, odd = section // 2, lax.rem(section, 2)
    slot = lax.rem(stage + odd, 2)

    place = jnp.arange(WIDE, dtype=jnp.int32)
    source = (place % (WIDE // fshare)) * fshare + place // (WIDE // fshare)
    shuffle = (place[:, None] == source[None, :]).astype(BF)

    def full(a):
        return pl.BlockSpec(a.shape, lambda i: (0,) * a.ndim)

    shares = [proj_in[0], proj_attn[0], proj_down[0], norm_gain, out_bias, up_bias, query_gain, key_gain, shuffle]
    heads_part = joined - ff
    local = jax.ShapeDtypeStruct((dshare, stride), BF)
    local = plain(partial(prepare_kernel, d, ff), shares, [full(a) for a in shares], local, full(local), [])
    other = paired(local)
    both = jnp.where(odd == 0, jnp.concatenate([local, other], axis=1), jnp.concatenate([other, local], axis=1))
    g = lax.all_gather(both, "dp", axis=0, tiled=True)
    g3 = g.reshape(ff // WIDE, WIDE // fshare, g.shape[1])
    element = jnp.arange(d, dtype=jnp.int32) % head
    spread_gain = (jnp.arange(d, dtype=jnp.int32)[:, None] == (element // hshare * dshare + element % hshare)[None, :]).astype(BF)
    small = jax.ShapeDtypeStruct((2, 8, ff), F32)
    smalls = plain(
        partial(smalls_kernel, d, ff, wide, stride), [g, spread_gain], [ANY, full(spread_gain)], small, full(small),
        [pltpu.VMEM((2, d, LANES), BF), pltpu.SemaphoreType.DMA((2,))],
    )

    toks = tokens.reshape(slots, rows, d)
    seeds = cotangent.reshape(slots, rows, d)
    ends = jnp.cumsum(lengths, axis=-1)
    position = jnp.arange(rows, dtype=jnp.int32)
    image = jnp.sum((position[None, :, None] >= ends[:, None, :]).astype(jnp.int32), axis=-1)
    image = jnp.where(position[None, :] < ends[:, 2:3], image, ABSENT + position[None, :])
    ids = jnp.broadcast_to(image[:, None, :].astype(F32), (slots, 8, rows))

    def stash(*shape, dtype=BF):
        return pl.pallas_call(
            lambda out: None, out_shape=jax.ShapeDtypeStruct(shape, dtype), out_specs=pl.BlockSpec(memory_space=pl.ANY)
        )()

    fc = ff // chunks
    groups = ff // WIDE

    def index_of(layer, active_stage):
        return jnp.stack([stage == active_stage, core, slot, odd == layer]).astype(jnp.int32)

    V = pltpu.VMEM
    weights_v = [V((d, heads_part), BF), V((chunks, d, fc), BF), V((groups, fshare, WIDE // fshare, d), BF), V((d, d), BF)]
    sems = [pltpu.SemaphoreType.DMA((48,)), pltpu.SemaphoreType.DMA((48,))]
    stacked = ff + 4 * d
    operands = [[stash(rows + 16, stacked), stash(rows + 16, stacked)] for _ in range(2)]
    kept = [[stash(rows, d) for _ in range(4)] + [stash(rows, 2 * d), stash(rows, 2 * d), stash(chunks, rows, fc),
             stash(heads, rows, rows), stash(16, rows, dtype=F32)] for _ in range(2)]
    results = [stash(slots, rows, d, dtype=F32), stash(rows, d)]
    here_x = toks
    for t in range(4):
        layer = t % 2
        ybf, done = call(
            partial(forward_kernel, d, ff, chunks, layer, stride * layer, t == 0),
            index_of(layer, t // 2),
            [(a, ANY) for a in (here_x, g, g3, ids, smalls)],
            ((rows, d), BF),
            kept[layer][:9] + operands[layer] + results,
            [V((rows, d), BF), V((rows, d), BF)] + weights_v
            + [V((rows, d), BF)] * 3 + [V((rows, 2 * d), BF)] * 2 + [V((chunks, rows, fc), BF)] * 2
            + [V((heads, rows, rows), BF), V((16, rows), F32), V((rows, d), BF), V((rows, d), F32), V((rows, d), F32), V((rows, d), BF), V((8, rows), F32), V((8, ff), F32)]
            + sems,
            1 << 10,
        )
        kept[layer], operands[layer], results = done[:9], done[9:11], done[11:]
        here_x = lax.ppermute(ybf, "section", [(0, 3), (1, 2)]) if t == 1 else ybf
    y_out, y_send = results
    y_got = paired(y_send)

    results = [stash(slots, rows, d, dtype=F32), stash(rows, d)]
    width = 6 * d + LANES
    share = 2 * dshare
    here = jnp.stack([y, z, core, slot, odd]).astype(jnp.int32)

    def moved(x, leg, by):
        def to(i):
            step = 2 * side if i % 2 == leg else 2
            digit = i // step % side
            return i + ((digit + by) % side - digit) * step

        return lax.ppermute(x, "dp", [(i, to(i)) for i in range(ranks)])

    def grads_by_place(layer, got):
        return simple(
            partial(weight_grad_kernel, d, ff), here,
            [operands[layer][0], got], [ANY] * 2,
            [jax.ShapeDtypeStruct((side * share, width), BF)] * 3 + [jax.ShapeDtypeStruct((side // 2 * share, width), BF)] * 2,
            [ANY] * 5,
            [V((2, rows, ff), BF), V((2, rows, d), BF), V((2, rows, d), BF), V((2, rows, 2 * d), BF), V((d, width), BF), V((2, 16, stacked), BF),
             pltpu.SemaphoreType.DMA((32,)), pltpu.SemaphoreType.DMA((32,))],
        )

    def halves(made):
        return moved(made[3], 0, 1), moved(made[4], 0, -1)

    def first_leg(made, came):
        own, up, down = made[:3]
        part = (side // 2 * share, width)
        up, down = pl.pallas_call(
            relay_kernel,
            grid_spec=pltpu.PrefetchScalarGridSpec(
                num_scalar_prefetch=1, grid=(1,), in_specs=[ANY] * 4, out_specs=[ANY] * 2,
                scratch_shapes=[V((4,) + part, BF), pltpu.SemaphoreType.DMA((4,)), pltpu.SemaphoreType.DMA((2,))],
            ),
            out_shape=[jax.ShapeDtypeStruct(up.shape, BF)] * 2,
            input_output_aliases={1: 0, 2: 1},
            compiler_params=pltpu.CompilerParams(dimension_semantics=("arbitrary",), vmem_limit_bytes=VMEM_LIMIT),
            cost_estimate=pl.CostEstimate(flops=1 << 10, bytes_accessed=1 << 10, transcendentals=0),
        )(here, up, down, *came)
        return [own, moved(up, 0, 1), moved(down, 0, -1)]

    def second_leg(outs):
        far, near, back = (moved(outs[s], 1, s) for s in (2, 1, 3))
        return [outs[0], near, far, back]

    def by_second_axis(came):
        return simple(
            mid_kernel, here, came, [ANY] * 3, [jax.ShapeDtypeStruct((share, width), BF)] * side, [ANY] * side,
            [V((side, 3, share, width), BF), V((side, share, width), BF), pltpu.SemaphoreType.DMA((12,)), pltpu.SemaphoreType.DMA((4,))],
        )

    here_g = seeds
    swaps = []
    for t in range(4):
        layer = 1 - t % 2
        gbf, done = call(
            partial(backward_kernel, d, ff, chunks, layer, stride * layer, t == 0),
            index_of(layer, 1 - t // 2),
            [(a, ANY) for a in [here_g, g, g3, ids, smalls] + kept[layer]],
            ((rows, d), BF),
            operands[layer] + results,
            [V((rows, d), BF), V((rows, d), BF)] + weights_v
            + [V((rows, d), BF)] * 4 + [V((rows, 2 * d), BF)] * 2
            + [V((chunks, rows, fc), BF), V((heads, rows, rows), BF), V((16, rows), F32)]
            + [V((d, rows), BF), V((d, rows), F32), V((rows, d), F32)]
            + [V((rows, d), BF)] * 3 + [V((chunks, rows, fc), BF), V((rows, d), F32), V((rows, d), F32), V((rows, d), BF), V((1, stacked), F32), V((16, stacked), BF), V((8, rows), F32), V((8, ff), F32)]
            + sems,
            1 << 10,
        )
        operands[layer], results = done[:2], done[2:]
        here_g = lax.ppermute(gbf, "section", [(3, 0), (2, 1)]) if t == 1 else gbf
        if t == 1:
            here_g, y_got = lax.optimization_barrier((here_g, y_got))
        if t == 3:
            operands[layer][1], swaps[0] = lax.optimization_barrier((operands[layer][1], swaps[0]))
        if t >= 2:
            swaps.append(along(operands[layer][1], 1, 2, 1))
    gr_got = paired(results[1])
    upper, gr_got = lax.optimization_barrier((grads_by_place(1, swaps[0]), gr_got))
    upper_came = halves(upper)
    lower = grads_by_place(0, swaps[1])
    lower_came = halves(lower)
    legs = [first_leg(upper, upper_came), first_leg(lower, lower_came)]
    arrived = [second_leg(by_second_axis(came)) for came in legs]
    gr_out = results[0]
    y_out, gr_out = pl.pallas_call(
        place_kernel,
        grid_spec=pltpu.PrefetchScalarGridSpec(
            num_scalar_prefetch=1, grid=(1,), in_specs=[ANY, whole((rows, d)), ANY, whole((rows, d))], out_specs=[ANY] * 2,
            scratch_shapes=[V((rows, d), F32), V((rows, d), F32), pltpu.SemaphoreType.DMA((2,))],
        ),
        out_shape=[jax.ShapeDtypeStruct(y_out.shape, F32)] * 2,
        input_output_aliases={1: 0, 3: 1},
    )(here, y_out, y_got, gr_out, gr_got)

    both = arrived[1] + arrived[0]
    home_mine, home_other, away_mine, away_other = simple(
        last_pair_kernel, here, both, [ANY] * 8,
        [jax.ShapeDtypeStruct((dshare, width), t) for t in (F32, BF, BF, BF)], [whole((dshare, width))] * 4,
        [V((8, share, width), BF), V((2, share, width), F32), pltpu.SemaphoreType.DMA((8,))],
    )
    sections = lax.axis_size("section")
    cross = [(s * ranks + i, (s ^ 1) * ranks + (i ^ 1)) for s in range(sections) for i in range(ranks)]
    arrays = [home_mine, paired(away_mine), along(home_other, 1, 2, 1), lax.ppermute(away_other, ("section", "dp"), cross),
              shuffle.astype(F32)]
    shapes = [(dshare, joined), (dshare, d), (dshare * fshare, d), (1, dshare), (1, hshare), (1, hshare), (1, dshare * fshare),
              (1, dshare)]
    g_in, g_attn, g_down, g_ng, g_q, g_k, g_ub, g_ob = simple(
        partial(finish_kernel, d, ff), here, arrays, [whole(a.shape) for a in arrays],
        [jax.ShapeDtypeStruct(s, F32) for s in shapes], [whole(s) for s in shapes], [],
    )
    return (y_out.reshape(1, slots * rows, d), gr_out.reshape(1, slots * rows, d), g_in[None], g_attn[None], g_down[None],
            g_ng, g_q, g_k, g_ub, g_ob)


def solution(mesh):
    in_specs = (P("dp", None),) * 3 + (P("section", "dp", None),) * 3 + (P("section", "dp"),) * 5
    out_specs = (P("section", "dp", None),) * 5 + (P("section", "dp"),) * 5
    return jax.shard_map(body, mesh=mesh, in_specs=in_specs, out_specs=out_specs, check_vma=False)
```

```python
from functools import partial
import math

import jax
import jax.numpy as jnp
from jax import lax
from jax.experimental import pallas as pl
from jax.experimental.pallas import tpu as pltpu
from jax.sharding import PartitionSpec as P

BF = jnp.bfloat16
F32 = jnp.float32
VMEM_LIMIT = 56 * 1024 * 1024
SMALL_LIMIT = 30 * 1024 * 1024
EPS = 1e-06
NN = (((1,), (0,)), ((), ()))
NT = (((1,), (1,)), ((), ()))
TN = (((0,), (0,)), ((), ()))
LANES = 128
WIDE = 256
ABSENT = 16
FIRST, LOCAL, ARRIVED = range(3)


def mm(a, b, dims=NN):
    return lax.dot_general(a, b, dims, preferred_element_type=F32)


def head_mean(x, spread, exact):
    parts = []
    for at in range(0, x.shape[1], WIDE):
        piece = x[:, at : at + WIDE]
        top = piece.astype(BF)
        total = mm(top, spread)
        if exact:
            total = total + mm((piece - top.astype(F32)).astype(BF), spread)
        parts.append(total)
    return jnp.concatenate(parts, axis=1)


def row_norm(x):
    centered = x - jnp.mean(x, axis=-1, keepdims=True)
    rstd = lax.rsqrt(jnp.mean(centered * centered, axis=-1, keepdims=True) + EPS)
    return centered * rstd, rstd


def norm_back(grad, normal, rstd, spread):
    return rstd * (grad - head_mean(grad, spread, False) - normal * head_mean(grad * normal, spread, False))


def lane_half(x, second):
    lane = lax.broadcasted_iota(jnp.int32, x.shape, 1)
    return jnp.where((lane >= LANES // 2) if second else (lane < LANES // 2), x, jnp.zeros_like(x))


class Copies:
    def __init__(self, sems):
        self.sems, self.used = sems, 0

    def start(self, src, dst):
        copy = pltpu.make_async_copy(src, dst, self.sems.at[self.used])
        self.used += 1
        copy.start()
        return copy

    def either(self, flag, src, yes, no):
        sem = self.sems.at[self.used]
        self.used += 1

        @pl.when(flag == 1)
        def _():
            pltpu.make_async_copy(src, yes, sem).start()

        @pl.when(flag != 1)
        def _():
            pltpu.make_async_copy(src, no, sem).start()

        return pltpu.make_async_copy(src, yes, sem)


def result_out(home, value, result, rounded, send, copies):
    sem = copies.sems.at[copies.used]
    copies.used += 1

    @pl.when(home == 1)
    def _():
        copy = pltpu.make_async_copy(value, result, sem)
        copy.start()
        copy.wait()

    @pl.when(home != 1)
    def _():
        copy = pltpu.make_async_copy(rounded, send, sem)
        copy.start()
        copy.wait()


def forward_kernel(d, ff, chunks, layer, base, kind, idx, *refs):
    @pl.when(idx[0] == 1)
    def _():
        forward_work(d, ff, chunks, layer, base, kind, idx, *refs)


def head_spread(head):
    row = lax.broadcasted_iota(jnp.int32, (WIDE, WIDE), 0) // head
    column = lax.broadcasted_iota(jnp.int32, (WIDE, WIDE), 1) // head
    return jnp.where(row == column, 1.0 / head, 0.0).astype(BF)


def as_column(row):
    return jnp.broadcast_to(row, (LANES, row.shape[1])).T[:, :1]


def forward_work(d, ff, chunks, layer, base, kind, idx, x_in, g, g3, ids, smalls, *refs):
    refs = refs[13:]
    ybf, xs, qs, ks, vs, ns, nrs, gps, es, small, kept, sent, y_out, y_send = refs[:14]
    (x_v, h_v, w_v, u_v, d_v, a_v, q_v, k_v, v_v, n_v, r_v, act_v, gp_v, e_v, rs_v, att_v, acc_v, y_v, yb_v, id_v, sm_v, ins, outs) = refs[14:]
    rows = x_v.shape[0]
    body_rows = pl.ds(0, rows)
    fc = ff // chunks
    core, slot, home = idx[1], idx[2], idx[3]
    cin, cout = Copies(ins), Copies(outs)
    x_copy = None if kind == ARRIVED else cin.start(x_in.at[slot] if kind == FIRST else x_in, x_v)
    small_copies = [cin.start(ids.at[slot], id_v), cin.start(smalls.at[layer], sm_v)]
    wq = [cin.start(g.at[:, pl.ds(base + ff + d * i, d)], w_v.at[:, pl.ds(d * i, d)]) for i in range(3)]
    groups = fc // WIDE
    wff = []
    for c in range(chunks):
        wff.append([cin.start(g.at[:, pl.ds(base + fc * c, fc)], u_v.at[c])] + [
            cin.start(g3.at[pl.ds(groups * c, groups), :, pl.ds(base + ff + 4 * d + d * j, d)], d_v.at[pl.ds(groups * c, groups), j])
            for j in range(4)
        ])
    wa = cin.start(g.at[:, pl.ds(base + ff + 3 * d, d)], a_v)

    pending = []

    def side(i):
        return pl.ds(ff + d * i, d)

    spread = head_spread(64)
    for copy in small_copies:
        copy.wait()
    ids_row = id_v[0:1]
    ids_col = as_column(ids_row)
    keep = jnp.where(ids_col < ABSENT, 1.0, 0.0)
    if kind == ARRIVED:
        x_v[...] = x_in[...]
    else:
        x_copy.wait()
    masked = keep * x_v[...].astype(F32)
    h_v[...] = (row_norm(masked)[0] * sm_v[0:1, :d]).astype(BF)
    pending += [cout.start(x_v, xs), cout.start(h_v, kept.at[body_rows, side(2)]), cout.start(h_v, sent.at[body_rows, side(2)])]
    bias_mask = jnp.where(ids_col == ids_row, 0.0, -1e9)
    for i in range(3):
        wq[i].wait()
        raw = mm(h_v[...], w_v[:, d * i : d * i + d])
        if i == 2:
            v_v[...] = raw.astype(BF)
            pending.append(cout.start(v_v, vs))
        else:
            centered = raw - head_mean(raw, spread, True)
            rstd = lax.rsqrt(head_mean(centered * centered, spread, True) + EPS)
            normal = centered * rstd
            scaled = (normal * sm_v[0:1, d * (2 + i) : d * (3 + i)]).astype(BF)
            n_v[:, d * i : d * i + d] = normal.astype(BF)
            r_v[:, d * i : d * i + d] = rstd.astype(BF)
            if i == 0:
                q_v[...] = scaled * jnp.asarray(0.125, BF)
                pending.append(cout.start(q_v, qs))
            else:
                k_v[...] = scaled
                pending.append(cout.start(k_v, ks))
    pending += [cout.start(n_v, ns), cout.start(r_v, nrs)]
    ones = jnp.ones((16, rows), BF)
    pairs = d // LANES // chunks
    for c in range(chunks):
        for copy in wff[c]:
            copy.wait()
        pre = mm(h_v[...], u_v[c]) + sm_v[1:2, fc * c : fc * c + fc]
        cdf = 0.5 * (1.0 + lax.erf(pre * (1.0 / math.sqrt(2.0))))
        density = jnp.exp(-0.5 * pre * pre) * (1.0 / math.sqrt(2.0 * math.pi))
        act = (pre * cdf).astype(BF)
        act_v[c] = act
        gp_v[c] = (cdf + pre * density).astype(BF)
        total = mm(act, d_v[groups * c : groups * c + groups].reshape(fc, d))
        if c == 0:
            acc_v[...] = total
        else:
            acc_v[...] += total
        for p in range(pairs * c, pairs * c + pairs):
            cols = slice(LANES * p, LANES * p + LANES)
            vals_t = v_v[:, cols].T
            pair = q_v[:, cols]
            both = []
            for half in range(2):
                h = 2 * p + half
                e = jnp.exp(mm(k_v[:, cols], lane_half(pair, half), NT) + bias_mask).astype(BF)
                e_v[h] = e
                got = mm(jnp.concatenate([vals_t[64 * half : 64 * half + 64], ones], axis=0), e)
                inv = 1.0 / got[64:65]
                rs_v[h : h + 1, :] = inv
                both.append((got[:64] * inv).astype(BF))
            att_v[:, cols] = jnp.concatenate(both, axis=0).T
        span = pl.ds(fc * c, fc)
        pending += [cout.either(core, act_v.at[c], sent.at[body_rows, span], kept.at[body_rows, span]), cout.start(gp_v.at[c], gps.at[c]),
                    cout.start(e_v.at[pl.ds(2 * pairs * c, 2 * pairs)], es.at[pl.ds(2 * pairs * c, 2 * pairs)])]
    pending += [cout.start(rs_v, small), cout.either(core, att_v, sent.at[body_rows, side(3)], kept.at[body_rows, side(3)])]
    wa.wait()
    y = keep * (keep * x_v[...].astype(F32) + acc_v[...] + mm(att_v[...], a_v[...]) + sm_v[0:1, d : 2 * d])
    y_v[...] = y
    yb_v[...] = y.astype(BF)
    pending.append(cout.start(yb_v, ybf))
    result_out(home, y_v, y_out.at[slot], yb_v, y_send, cout)
    for copy in pending:
        copy.wait()


def backward_kernel(d, ff, chunks, layer, base, kind, idx, *refs):
    @pl.when(idx[0] == 1)
    def _():
        backward_work(d, ff, chunks, layer, base, kind, idx, *refs)


def backward_work(d, ff, chunks, layer, base, kind, idx, g_in, g, g3, ids, smalls, *refs):
    xs, qs, ks, vs, ns, nrs, gps, es, small = refs[:9]
    refs = refs[9 + 4 :]
    gbf, kept, sent, gr_out, gr_send = refs[:5]
    (g_v, gb_v, w_v, u_v, d_v, a_v, x_v, q_v, k_v, v_v, n_v, r_v, gp_v, e_v, rs_v, gat_v, gqt_v, gk_v,
     gq_b, gk_b, gv_b, gj_v, acc_v, out_v, ob_v, sm_v, sp_v, id_v, gain_v, ins, outs) = refs[5:]
    rows = x_v.shape[0]
    body_rows = pl.ds(0, rows)
    fc = ff // chunks
    groups = fc // WIDE
    core, slot, home = idx[1], idx[2], idx[3]
    cin, cout = Copies(ins), Copies(outs)
    g_copy = None if kind == ARRIVED else cin.start(g_in.at[slot] if kind == FIRST else g_in, g_v)
    small_copies = [cin.start(ids.at[slot], id_v), cin.start(smalls.at[layer], gain_v)]
    wa = cin.start(g.at[:, pl.ds(base + ff + 3 * d, d)], a_v)
    heads = [cin.start(s, v) for s, v in ((small, rs_v), (ks, k_v), (vs, v_v), (qs, q_v))]
    pairs = d // LANES // chunks
    wff = []
    for c in range(chunks):
        wff.append(
            [cin.start(g3.at[pl.ds(groups * c, groups), :, pl.ds(base + ff + 4 * d + d * j, d)], d_v.at[pl.ds(groups * c, groups), j])
             for j in range(4)]
            + [cin.start(gps.at[c], gp_v.at[c]), cin.start(g.at[:, pl.ds(base + fc * c, fc)], u_v.at[c]),
               cin.start(es.at[pl.ds(2 * pairs * c, 2 * pairs)], e_v.at[pl.ds(2 * pairs * c, 2 * pairs)])]
        )
    norms = [cin.start(ns, n_v), cin.start(nrs, r_v)]
    wq = [cin.start(g.at[:, pl.ds(base + ff + d * i, d)], w_v.at[:, pl.ds(d * i, d)]) for i in range(3)]
    rows_in = cin.start(xs, x_v)

    pending = []

    def side(i):
        return pl.ds(ff + d * i, d)

    def summed(at, value):
        sm_v[:, at : at + value.shape[1]] = jnp.sum(value, axis=0, keepdims=True)

    spread = head_spread(64)
    for copy in small_copies:
        copy.wait()
    keep = jnp.where(as_column(id_v[0:1]) < ABSENT, 1.0, 0.0)
    if kind == ARRIVED:
        g_v[...] = g_in[...]
    else:
        g_copy.wait()
    gres = keep * g_v[...].astype(F32)
    summed(d, gres)
    gb_v[...] = gres.astype(BF)
    pending.append(cout.either(core, gb_v, sent.at[body_rows, side(0)], kept.at[body_rows, side(0)]))
    wa.wait()
    gat_v[...] = mm(a_v[...], gb_v[...], NT).astype(BF)
    for copy in heads:
        copy.wait()
    zeros = jnp.zeros((LANES // 2, rows), BF)
    for c in range(chunks):
        for copy in wff[c]:
            copy.wait()
        gup = mm(gb_v[...], d_v[groups * c : groups * c + groups].reshape(fc, d), NT) * gp_v[c].astype(F32)
        summed(4 * d + fc * c, gup)
        gup = gup.astype(BF)
        gj_v[c] = gup
        span = pl.ds(fc * c, fc)
        pending.append(cout.either(core, gj_v.at[c], kept.at[body_rows, span], sent.at[body_rows, span]))
        total = mm(gup, u_v[c], NT)
        if c == 0:
            acc_v[...] = total
        else:
            acc_v[...] += total
        for p in range(pairs * c, pairs * c + pairs):
            cols = slice(LANES * p, LANES * p + LANES)
            keys, vals, pair = k_v[:, cols], v_v[:, cols], q_v[:, cols]
            keys_t = keys.T
            gk, gv = None, None
            for half in range(2):
                h = 2 * p + half
                at_rows = slice(64 * h, 64 * h + 64)
                inv = rs_v[h : h + 1, :]
                ga = (gat_v[at_rows, :].astype(F32) * inv).astype(BF)
                ga = jnp.concatenate([zeros, ga] if half else [ga, zeros], axis=0)
                e = e_v[h]
                ef = e.astype(F32)
                gp = ef * mm(vals, ga)
                dot = jnp.sum(gp, axis=0, keepdims=True) * inv
                gs = (gp - ef * dot).astype(BF)
                gk_h = mm(gs, lane_half(pair, half))
                gv_h = mm(e, ga, NT)
                gk = gk_h if gk is None else gk + gk_h
                gv = gv_h if gv is None else gv + gv_h
                gqt_v[at_rows, :] = mm(keys_t[64 * half : 64 * half + 64], gs) * 0.125
            gk_v[:, cols] = gk
            gv_b[:, cols] = gv.astype(BF)
    pending.append(cout.either(core, gv_b, sent.at[body_rows, side(1)], kept.at[body_rows, side(1)]))
    for copy in norms:
        copy.wait()
    for i, (grad, out) in enumerate(((gqt_v[...].T, gq_b), (gk_v[...], gk_b))):
        normal = n_v[:, d * i : d * i + d].astype(F32)
        summed(2 * d + d * i, grad * normal)
        gain = gain_v[0:1, d * (2 + i) : d * (3 + i)]
        out[...] = norm_back(grad * gain, normal, r_v[:, d * i : d * i + d].astype(F32), spread).astype(BF)
        pending.append(cout.either(core, out, kept.at[body_rows, side(i)], sent.at[body_rows, side(i)]))
    for copy in wq:
        copy.wait()
    ghid = acc_v[...]
    for i, part in enumerate((gq_b, gk_b, gv_b)):
        ghid = ghid + mm(part[...], w_v[:, d * i : d * i + d], NT)
    rows_in.wait()
    xhat, rstd = row_norm(keep * x_v[...].astype(F32))
    summed(0, ghid * xhat)
    top = sm_v[...].astype(BF).astype(F32)
    sp_v[...] = jnp.concatenate([top, sm_v[...] - top, jnp.zeros((14, top.shape[1]), F32)], axis=0).astype(BF)
    tail = pl.ds(rows, 16)
    pending += [cout.start(sp_v, kept.at[tail]), cout.start(sp_v, sent.at[tail])]
    gx = ghid * gain_v[0:1, :d]
    gmask = rstd * (gx - jnp.mean(gx, axis=-1, keepdims=True) - xhat * jnp.mean(gx * xhat, axis=-1, keepdims=True))
    out = keep * (keep * g_v[...].astype(F32) + gmask)
    out_v[...] = out
    ob_v[...] = out.astype(BF)
    pending.append(cout.start(ob_v, gbf))
    result_out(home, out_v, gr_out.at[slot], ob_v, gr_send, cout)
    for copy in pending:
        copy.wait()


def split_small(values):
    top = values.astype(BF).astype(F32)
    lane = lax.broadcasted_iota(jnp.int32, values.shape, 1)
    return jnp.where(lane < 8, top, jnp.where(lane < 16, pltpu.roll(values - top, 8, 1), 0.0)).astype(BF)


def joined_small(parts):
    return parts + pltpu.roll(parts, LANES - 8, 1)


def small_table(d, ff, tables):
    total = jnp.zeros((1, tables.shape[2]), F32)
    for i in range(tables.shape[0]):
        parts = tables[i].astype(F32)
        total = total + parts[0:1] + parts[1:2]
    lane = lax.broadcasted_iota(jnp.int32, (LANES, d), 0) % 64
    place = jnp.where(lax.broadcasted_iota(jnp.int32, (LANES, d), 1) == lane // 2 * 24 + lane % 2, 1.0, 0.0)
    quarter = WIDE // 4
    ub = total[:, 4 * d :]
    up_rows = []
    for j in range(4):
        pieces = [ub[:, WIDE * b + quarter * j : WIDE * b + quarter * (j + 1)] for b in range(ff // WIDE)]
        up_rows.append(jnp.concatenate(pieces, axis=1))
    head_rows = []
    for i in range(2, 4):
        lanes = total[:, d * i : d * i + LANES]
        for p in range(1, d // LANES):
            lanes = lanes + total[:, d * i + LANES * p : d * i + LANES * (p + 1)]
        head_rows.append(lanes)
    both = jnp.concatenate(head_rows + [jnp.zeros((6, LANES), F32)], axis=0)
    placed = lax.dot_general(both, place, NN, precision=lax.Precision.HIGHEST, preferred_element_type=F32)
    rows = [total[:, :d], total[:, d : 2 * d]] + up_rows + [placed[0:1], placed[1:2], jnp.zeros((LANES - 8, d), F32)]
    return jnp.concatenate(rows, axis=0).T


def weight_grad_kernel(d, ff, idx, kept, got, *refs):
    results, (big_v, a_v, b_v, c_v, out_v, t_v, ins, outs) = refs[:5], refs[5:]
    rows = kept.shape[0] - t_v.shape[1]
    tokens = 2 * rows
    quarter, half, third = WIDE // 4, ff // 2, ff // 3
    blocks = third // WIDE
    share = d // 16
    cut = 3 * d
    y, z, core = idx[0], idx[1], idx[2]

    def load(cin, at, width, to, to_at):
        return [cin.start(src.at[pl.ds(0, rows), pl.ds(at, width)], to.at[i, :, pl.ds(to_at, width)]) for i, src in enumerate((kept, got))]

    def wait(copies):
        for copy in copies:
            copy.wait()

    def both(ref, at=0, width=d):
        return ref[:, :, at : at + width].reshape(tokens, width)

    def put(rows_at, cols_at, value):
        out_v[rows_at, cols_at] = value.astype(BF)

    def send_by_y(cout, at, width):
        cols = pl.ds(at, width)

        def rows_of(s, first, count):
            return out_v.at[pl.ds(pl.multiple_of(lax.rem(y + s, 4) * 4 * share + first, 16), count), cols]

        return [cout.start(rows_of(2, 0, 2 * share), results[3].at[:, cols]),
                cout.start(rows_of(2, 2 * share, 2 * share), results[4].at[:, cols])] + [
            cout.start(rows_of(s, 0, 4 * share), results[r].at[:, cols]) for r, s in ((1, 1), (2, 3), (0, 0))]

    def send_by_z(cout, at, width):
        cols = pl.ds(at, width)

        def rows_of(i, s):
            return out_v.at[pl.ds(pl.multiple_of((4 * i + lax.rem(z + s, 4)) * share, 16), share), cols]

        return [
            cout.start(rows_of(i, s), results[r].at[pl.ds(share * (i - base), share), cols])
            for r, s, base, count in ((3, 2, 0, 2), (4, 2, 2, 2), (1, 1, 0, 4), (2, 3, 0, 4), (0, 0, 0, 4))
            for i in range(base, base + count)
        ]

    everything = slice(0, d)

    @pl.when(core == 0)
    def _():
        cin, cout = Copies(ins), Copies(outs)
        grads = load(cin, ff, d, a_v, 0)
        loads = [load(cin, third * k, third, big_v, third * k) for k in range(3)]
        attended = load(cin, ff + 3 * d, d, b_v, 0)
        hidden, values = load(cin, ff + 2 * d, d, c_v, 0), load(cin, ff + d, d, c_v, d)
        smalls = [cin.start(src.at[pl.ds(rows, t_v.shape[1])], t_v.at[i]) for i, src in enumerate((kept, got))]
        wait(grads)
        gb = both(a_v)
        for k in range(3):
            wait(loads[k])
            found = lax.dot_general(both(big_v, third * k, third), gb, TN, preferred_element_type=F32).astype(BF)
            for b in range(blocks):
                at = quarter * (blocks * k + b)
                for j in range(4):
                    put(slice(at, at + quarter), slice(d * j, d * j + d), found[WIDE * b + quarter * j : WIDE * b + quarter * (j + 1)])
        pending = send_by_y(cout, 0, 4 * d)
        wait(attended)
        put(everything, slice(4 * d, 5 * d), lax.dot_general(both(b_v), gb, TN, preferred_element_type=F32))
        wait(hidden + values + smalls)
        put(everything, slice(5 * d, 6 * d), lax.dot_general(both(c_v), both(c_v, d), TN, preferred_element_type=F32))
        put(everything, slice(6 * d, 6 * d + LANES), split_small(small_table(d, ff, t_v)))
        wait(pending + send_by_y(cout, 4 * d, 2 * d + LANES))

    @pl.when(core == 1)
    def _():
        cin, cout = Copies(ins), Copies(outs)
        hidden = load(cin, ff + 2 * d, d, a_v, 0)
        loads = [load(cin, third * k, third, big_v, third * k) for k in range(2)]
        queries = load(cin, ff, d, b_v, 0)
        loads.append(load(cin, 2 * third, third, big_v, 2 * third))
        keys = load(cin, ff + d, d, c_v, 0)
        wait(hidden)
        turned = both(a_v).T
        pending = []
        for k in range(2):
            wait(loads[k])
            put(everything, slice(third * k, third * k + third), mm(turned, both(big_v, third * k, third)))
        pending = send_by_z(cout, 0, 2 * third)
        wait(queries)
        put(everything, slice(ff, ff + d), mm(turned, both(b_v)))
        wait(loads[2])
        put(everything, slice(2 * third, ff), mm(turned, both(big_v, 2 * third, third)))
        wait(keys)
        put(everything, slice(ff + d, ff + 2 * d), mm(turned, both(c_v)))
        out_v[:, 6 * d :] = jnp.zeros((d, LANES), BF)
        wait(pending + send_by_z(cout, 2 * third, 6 * d + LANES - 2 * third))


def added(parts):
    total = parts[0][...].astype(F32)
    for part in parts[1:]:
        total = total + part[...].astype(F32)
    shape = total.shape
    total = total.reshape(-1, shape[-1])
    main, last = total[:, : shape[-1] - LANES], split_small(joined_small(total[:, shape[-1] - LANES :]))
    return jnp.concatenate([main.astype(BF), last], axis=1).reshape(shape)


def relay_kernel(idx, up_in, down_in, up_got, down_got, up, down, hold, ins, outs):
    half = up_got.shape[0]
    cin, cout = Copies(ins), Copies(outs)
    parts = ((up_in, 0, up_got, up), (down_in, half, down_got, down))
    loads = [cin.start(block.at[pl.ds(at, half)], hold.at[i]) for i, (block, at, _, _) in enumerate(parts)]
    pending = []
    for i, (_, at, got, out) in enumerate(parts):
        loads[i].wait()
        hold[i] = added([hold.at[i], got])
        pending.append(cout.start(hold.at[i], out.at[pl.ds(at, half)]))
    for copy in pending:
        copy.wait()


def mid_kernel(idx, *refs):
    came, results, (in_v, out_v, ins, outs) = refs[:3], refs[3:7], refs[7:]
    share = results[0].shape[0]

    cin, cout = Copies(ins), Copies(outs)
    at = jnp.where(idx[2] == 0, idx[1], idx[0])
    order = [2, 1, 3, 0]
    blocks = [pl.multiple_of(lax.rem(at + s, 4) * share, 16) for s in order]
    loads = [[cin.start(part.at[pl.ds(block, share)], in_v.at[i, p]) for p, part in enumerate(came)]
             for i, block in enumerate(blocks)]
    pending = []
    for i, s in enumerate(order):
        for copy in loads[i]:
            copy.wait()
        out_v[i] = added([in_v.at[i, p] for p in range(3)])
        pending.append(cout.start(out_v.at[i], results[s]))
    for copy in pending:
        copy.wait()


def last_pair_kernel(idx, *refs):
    came, (home_mine, home_other, away_mine, away_other, in_v, hold, ins) = refs[:8], refs[8:]
    share = home_mine.shape[0]
    core, odd = idx[2], idx[4]

    sum_of(came, in_v, hold, ins)

    def rows_of(k, which):
        return hold[k, pl.ds(pl.multiple_of(which * share, 8), share), :]

    for which, home, away in ((core, home_mine, away_mine), (1 - core, home_other, away_other)):
        home[...] = jnp.where(odd == 1, rows_of(1, which), rows_of(0, which)).astype(home.dtype)
        away[...] = jnp.where(odd == 1, rows_of(0, which), rows_of(1, which)).astype(away.dtype)


def sum_of(came, in_v, hold, sems):
    copies = Copies(sems)
    loads = [copies.start(came[4 * k], in_v.at[k]) for k in range(len(came) // 4)]
    for k, load in enumerate(loads):
        load.wait()
        hold[k] = added([in_v.at[k]] + list(came[4 * k + 1 : 4 * k + 4])).astype(F32)


def place_kernel(idx, y_in, y_got, g_in, g_got, y_out, g_out, y_v, g_v, sems):
    copies = Copies(sems)
    pending = []
    for got, wide_v, out in ((y_got, y_v, y_out), (g_got, g_v, g_out)):
        wide_v[...] = got[...].astype(F32)
        pending.append(copies.start(wide_v, out.at[1 - idx[3]]))
    for copy in pending:
        copy.wait()


def picked(rows, columns, wanted):
    row = lax.broadcasted_iota(jnp.int32, (rows, columns), 0)
    column = lax.broadcasted_iota(jnp.int32, (rows, columns), 1)
    return row, column, jnp.where(column == wanted(row), 1.0, 0.0)


def prepare_kernel(d, ff, p_in, p_attn, p_down, n_gain, o_bias, u_bias, q_gain, k_gain, shuffle, out):
    share = p_in.shape[0]
    heads_part = p_in.shape[1] - ff
    for at in range(0, ff, WIDE):
        out[:, at : at + WIDE] = mm(p_in[:, heads_part + at : heads_part + at + WIDE], shuffle[...]).astype(BF)
    out[:, ff : ff + heads_part] = p_in[:, :heads_part]
    at = ff + heads_part
    out[:, at : at + d] = p_attn[...]
    down = p_down[...]
    for j in range(4):
        take = picked(share, down.shape[0], lambda row: 4 * row + j)[2].astype(BF)
        out[:, at + d * (j + 1) : at + d * (j + 2)] = mm(take, down).astype(BF)

    def column_of(ref, wanted, where):
        values = ref[...].astype(F32)
        take = picked(share, values.shape[1], wanted)[2]
        lane = lax.broadcasted_iota(jnp.int32, (share, LANES), 1)
        return jnp.where(lane == where, jnp.sum(take * values, axis=1, keepdims=True), 0.0)

    table = column_of(n_gain, lambda row: row, 0) + column_of(o_bias, lambda row: row, 1)
    for j in range(4):
        table = table + column_of(u_bias, lambda row: 4 * row + j, 2 + j)
    table = table + column_of(q_gain, lambda row: row, 6) + column_of(k_gain, lambda row: row, 7)
    out[:, at + 5 * d :] = table.astype(BF)


def smalls_kernel(d, ff, base, stride, g, place, out, t_v, sems):
    copies = Copies(sems)
    loads = [copies.start(g.at[:, pl.ds(base + stride * layer, LANES)], t_v.at[layer]) for layer in range(2)]
    quarter = WIDE // 4
    for layer in range(2):
        loads[layer].wait()
        table = t_v[layer].astype(F32).T
        pieces = [table[2 + j : 3 + j, quarter * b : quarter * (b + 1)] for b in range(ff // WIDE) for j in range(4)]
        both = mm(table[0:8].astype(BF), place[...])
        first = jnp.concatenate([table[0:1], table[1:2], both[6:7], both[7:8]], axis=1)
        out[layer] = jnp.concatenate([first, jnp.concatenate(pieces, axis=1), jnp.zeros((6, ff), F32)], axis=0)


def in_parts(x):
    top = x.astype(BF)
    rest = x - top.astype(F32)
    middle = rest.astype(BF)
    return top, middle, (rest - middle.astype(F32)).astype(BF)


def finish_kernel(d, ff, idx, own, a_in, b_in, c_in, shuffle, g_in, g_attn, g_down, g_ng, g_q, g_k, g_ub, g_ob):
    core = idx[2]
    share = own.shape[0]
    mine = own[...] + a_in[...].astype(F32)
    theirs = b_in[...].astype(F32) + c_in[...].astype(F32)
    half0 = jnp.where(core == 0, mine, theirs)
    half1 = jnp.where(core == 0, theirs, mine)
    g_in[:, : 2 * d] = half1[:, ff : ff + 2 * d]
    g_in[:, 2 * d : 3 * d] = half0[:, 5 * d : 6 * d]
    for at in range(0, ff, WIDE):
        g_in[:, 3 * d + at : 3 * d + at + WIDE] = sum(mm(part, shuffle[...], NT) for part in in_parts(half1[:, at : at + WIDE]))
    g_attn[...] = half0[:, 4 * d : 5 * d]
    stacked = jnp.concatenate([half0[:, at : at + d] for at in range(0, 4 * d, d)], axis=0)
    row, column, _ = picked(4 * share, 4 * share, lambda row: row)
    turn = jnp.where(column == lax.rem(row, 4) * share + row // 4, 1.0, 0.0).astype(BF)
    g_down[...] = sum(mm(turn, part) for part in in_parts(stacked))
    small = joined_small(half0[:, 6 * d :])
    turned = jnp.concatenate([small, jnp.zeros((LANES - share, LANES), F32)], axis=0).T
    g_ng[...] = turned[0:1, :share]
    g_ob[...] = turned[1:2, :share]
    g_q[...] = turned[6:7, : g_q.shape[1]]
    g_k[...] = turned[7:8, : g_k.shape[1]]
    total = jnp.zeros((8, 4 * share), F32)
    for j in range(4):
        row, column, _ = picked(LANES, 4 * share, lambda row: row)
        spread_out = jnp.where(column == 4 * row + j, 1.0, 0.0)
        total = total + jnp.where(lax.broadcasted_iota(jnp.int32, (8, 4 * share), 0) == 2 + j, 1.0, 0.0) * lax.dot_general(
            turned[0:8], spread_out, NN, precision=lax.Precision.HIGHEST, preferred_element_type=F32)
    g_ub[...] = jnp.sum(total, axis=0, keepdims=True)


ANY = pl.BlockSpec(memory_space=pl.ANY)
HERE = pl.BlockSpec(memory_space=pltpu.VMEM)


def whole(shape):
    return pl.BlockSpec(shape, lambda i, idx: (0,) * len(shape))


def pick(shape):
    return pl.BlockSpec((1,) + shape, lambda i, idx: (idx[2],) + (0,) * len(shape))


def call(kernel, idx, ins, fresh, stashes, scratch, flops):
    outs = pl.pallas_call(
        kernel,
        grid_spec=pltpu.PrefetchScalarGridSpec(
            num_scalar_prefetch=1,
            grid=(1,),
            in_specs=[s for _, s in ins] + [ANY] * len(stashes),
            out_specs=[ANY] * (1 + len(stashes)),
            scratch_shapes=scratch,
        ),
        out_shape=[jax.ShapeDtypeStruct(*fresh)] + [jax.ShapeDtypeStruct(a.shape, a.dtype) for a in stashes],
        input_output_aliases={1 + len(ins) + i: 1 + i for i in range(len(stashes))},
        compiler_params=pltpu.CompilerParams(dimension_semantics=("arbitrary",), vmem_limit_bytes=VMEM_LIMIT),
        cost_estimate=pl.CostEstimate(flops=flops, bytes_accessed=1 << 10, transcendentals=0),
    )(idx, *[a for a, _ in ins], *stashes)
    return outs[0], list(outs[1:])


def plain(kernel, arrays, specs, out_shapes, out_specs, scratch):
    return pl.pallas_call(
        kernel, grid=(1,), in_specs=specs, out_specs=out_specs, scratch_shapes=scratch, out_shape=out_shapes,
        compiler_params=pltpu.CompilerParams(dimension_semantics=("arbitrary",), vmem_limit_bytes=VMEM_LIMIT),
        cost_estimate=pl.CostEstimate(flops=1 << 10, bytes_accessed=1 << 10, transcendentals=0),
    )(*arrays)


def simple(kernel, idx, arrays, specs, out_shapes, out_specs, scratch, limit=VMEM_LIMIT):
    return pl.pallas_call(
        kernel,
        grid_spec=pltpu.PrefetchScalarGridSpec(
            num_scalar_prefetch=1, grid=(1,), in_specs=specs, out_specs=out_specs, scratch_shapes=scratch
        ),
        out_shape=out_shapes,
        compiler_params=pltpu.CompilerParams(dimension_semantics=("arbitrary",), vmem_limit_bytes=limit),
        cost_estimate=pl.CostEstimate(flops=1 << 10, bytes_accessed=1 << 10, transcendentals=0),
    )(idx, *arrays)


def along(x, step, size, by):
    devices = lax.axis_size("dp")

    def to(i):
        digit = i // step % size
        return i + ((digit + by) % size - digit) * step

    return lax.ppermute(x, "dp", [(i, to(i)) for i in range(devices)])


def paired(x):
    return lax.ppermute(x, "section", [(0, 1), (1, 0), (2, 3), (3, 2)])


def body(tokens, cotangent, lengths, proj_in, proj_attn, proj_down, norm_gain, query_gain, key_gain, up_bias, out_bias):
    ranks = lax.axis_size("dp")
    section = lax.axis_index("section")
    rank = lax.axis_index("dp")
    slots = lengths.shape[0]
    rows = tokens.shape[0] // slots
    d = tokens.shape[1]
    joined = proj_in.shape[2]
    ff = proj_down.shape[1] * ranks
    head = query_gain.shape[1] * ranks
    heads = d // head
    dshare = proj_in.shape[1]
    fshare = proj_down.shape[1] // dshare
    hshare = query_gain.shape[1]
    chunks = 3
    wide = joined + d + ff
    stride = wide + LANES
    side = math.isqrt(ranks // 2)
    core, z, y = lax.rem(rank, 2), lax.rem(rank // 2, side), rank // (2 * side)
    stage, odd = section // 2, lax.rem(section, 2)
    slot = lax.rem(stage + odd, 2)

    place = jnp.arange(WIDE, dtype=jnp.int32)
    source = (place % (WIDE // fshare)) * fshare + place // (WIDE // fshare)
    shuffle = (place[:, None] == source[None, :]).astype(BF)

    def full(a):
        return pl.BlockSpec(a.shape, lambda i: (0,) * a.ndim)

    shares = [proj_in[0], proj_attn[0], proj_down[0], norm_gain, out_bias, up_bias, query_gain, key_gain, shuffle]
    heads_part = joined - ff
    local = jax.ShapeDtypeStruct((dshare, stride), BF)
    local = plain(partial(prepare_kernel, d, ff), shares, [full(a) for a in shares], local, full(local), [])
    other = paired(local)
    both = jnp.where(odd == 0, jnp.concatenate([local, other], axis=1), jnp.concatenate([other, local], axis=1))
    g = lax.all_gather(both, "dp", axis=0, tiled=True)
    toks = tokens.reshape(slots, rows, d)
    seeds = cotangent.reshape(slots, rows, d)
    ends = jnp.cumsum(lengths, axis=-1)
    position = jnp.arange(rows, dtype=jnp.int32)
    image = jnp.sum((position[None, :, None] >= ends[:, None, :]).astype(jnp.int32), axis=-1)
    image = jnp.where(position[None, :] < ends[:, 2:3], image, ABSENT + position[None, :])
    ids = jnp.broadcast_to(image[:, None, :].astype(F32), (slots, 8, rows))

    def index_of(layer, active_stage):
        return jnp.stack([stage == active_stage, core, slot, odd == layer]).astype(jnp.int32)

    indices = [[index_of(layer, active) for active in range(2)] for layer in range(2)]
    here = jnp.stack([y, z, core, slot, odd]).astype(jnp.int32)
    element = jnp.arange(d, dtype=jnp.int32) % head
    spread_gain = (jnp.arange(d, dtype=jnp.int32)[:, None] == (element // hshare * dshare + element % hshare)[None, :]).astype(BF)
    g, indices, here, ids, spread_gain = lax.optimization_barrier((g, indices, here, ids, spread_gain))
    g3 = g.reshape(ff // WIDE, WIDE // fshare, g.shape[1])
    small = jax.ShapeDtypeStruct((2, 8, ff), F32)
    smalls = plain(
        partial(smalls_kernel, d, ff, wide, stride), [g, spread_gain], [ANY, full(spread_gain)], small, full(small),
        [pltpu.VMEM((2, d, LANES), BF), pltpu.SemaphoreType.DMA((2,))],
    )

    def stash(*shape, dtype=BF):
        return pl.pallas_call(
            lambda out: None, out_shape=jax.ShapeDtypeStruct(shape, dtype), out_specs=pl.BlockSpec(memory_space=pl.ANY)
        )()

    fc = ff // chunks
    groups = ff // WIDE

    V = pltpu.VMEM
    weights_v = [V((d, heads_part), BF), V((chunks, d, fc), BF), V((groups, fshare, WIDE // fshare, d), BF), V((d, d), BF)]
    sems = [pltpu.SemaphoreType.DMA((48,)), pltpu.SemaphoreType.DMA((48,))]
    stacked = ff + 4 * d
    operands = [[stash(rows + 16, stacked), stash(rows + 16, stacked)] for _ in range(2)]
    kept = [[stash(rows, d) for _ in range(4)] + [stash(rows, 2 * d), stash(rows, 2 * d), stash(chunks, rows, fc),
             stash(heads, rows, rows), stash(16, rows, dtype=F32)] for _ in range(2)]
    results = [stash(slots, rows, d, dtype=F32), stash(rows, d)]
    here_x = toks
    for t in range(4):
        layer = t % 2
        ybf, done = call(
            partial(forward_kernel, d, ff, chunks, layer, stride * layer, (FIRST, LOCAL, ARRIVED, LOCAL)[t]),
            indices[layer][t // 2],
            [(here_x, HERE if t == 2 else ANY)] + [(a, ANY) for a in (g, g3, ids, smalls)],
            ((rows, d), BF),
            kept[layer][:9] + operands[layer] + results,
            [V((rows, d), BF), V((rows, d), BF)] + weights_v
            + [V((rows, d), BF)] * 3 + [V((rows, 2 * d), BF)] * 2 + [V((chunks, rows, fc), BF)] * 2
            + [V((heads, rows, rows), BF), V((16, rows), F32), V((rows, d), BF), V((rows, d), F32), V((rows, d), F32), V((rows, d), BF), V((8, rows), F32), V((8, ff), F32)]
            + sems,
            1 << 10,
        )
        kept[layer], operands[layer], results = done[:9], done[9:11], done[11:]
        here_x = lax.ppermute(ybf, "section", [(0, 3), (1, 2)]) if t == 1 else ybf
    y_out, y_send = results
    y_got = paired(y_send)

    results = [stash(slots, rows, d, dtype=F32), stash(rows, d)]
    width = 6 * d + LANES
    share = 2 * dshare

    def moved(x, leg, by):
        def to(i):
            step = 2 * side if i % 2 == leg else 2
            digit = i // step % side
            return i + ((digit + by) % side - digit) * step

        return lax.ppermute(x, "dp", [(i, to(i)) for i in range(ranks)])

    def grads_by_place(layer, got):
        return simple(
            partial(weight_grad_kernel, d, ff), here,
            [operands[layer][0], got], [ANY] * 2,
            [jax.ShapeDtypeStruct((side * share, width), BF)] * 3 + [jax.ShapeDtypeStruct((side // 2 * share, width), BF)] * 2,
            [ANY] * 5,
            [V((2, rows, ff), BF), V((2, rows, d), BF), V((2, rows, d), BF), V((2, rows, 2 * d), BF), V((d, width), BF), V((2, 16, stacked), BF),
             pltpu.SemaphoreType.DMA((32,)), pltpu.SemaphoreType.DMA((32,))],
        )

    def halves(made):
        return moved(made[3], 0, 1), moved(made[4], 0, -1)

    def first_leg(made, came):
        own, up, down = made[:3]
        part = (side // 2 * share, width)
        up, down = pl.pallas_call(
            relay_kernel,
            grid_spec=pltpu.PrefetchScalarGridSpec(
                num_scalar_prefetch=1, grid=(1,), in_specs=[ANY, ANY, HERE, HERE], out_specs=[ANY] * 2,
                scratch_shapes=[V((2,) + part, BF), pltpu.SemaphoreType.DMA((2,)), pltpu.SemaphoreType.DMA((2,))],
            ),
            out_shape=[jax.ShapeDtypeStruct(up.shape, BF)] * 2,
            input_output_aliases={1: 0, 2: 1},
            compiler_params=pltpu.CompilerParams(dimension_semantics=("arbitrary",), vmem_limit_bytes=SMALL_LIMIT),
            cost_estimate=pl.CostEstimate(flops=1 << 10, bytes_accessed=1 << 10, transcendentals=0),
        )(here, up, down, *came)
        return [own, moved(up, 0, 1), moved(down, 0, -1)]

    def second_leg(outs):
        far, near, back = (moved(outs[s], 1, s) for s in (2, 1, 3))
        return [outs[0], near, far, back]

    def by_second_axis(came):
        return simple(
            mid_kernel, here, came, [ANY] * 3, [jax.ShapeDtypeStruct((share, width), BF)] * side, [ANY] * side,
            [V((side, 3, share, width), BF), V((side, share, width), BF), pltpu.SemaphoreType.DMA((12,)), pltpu.SemaphoreType.DMA((4,))],
        )

    here_g = seeds
    swaps = []
    for t in range(4):
        layer = 1 - t % 2
        gbf, done = call(
            partial(backward_kernel, d, ff, chunks, layer, stride * layer, (FIRST, LOCAL, ARRIVED, LOCAL)[t]),
            indices[layer][1 - t // 2],
            [(here_g, HERE if t == 2 else ANY)] + [(a, ANY) for a in [g, g3, ids, smalls] + kept[layer]],
            ((rows, d), BF),
            operands[layer] + results,
            [V((rows, d), BF), V((rows, d), BF)] + weights_v
            + [V((rows, d), BF)] * 4 + [V((rows, 2 * d), BF)] * 2
            + [V((chunks, rows, fc), BF), V((heads, rows, rows), BF), V((16, rows), F32)]
            + [V((d, rows), BF), V((d, rows), F32), V((rows, d), F32)]
            + [V((rows, d), BF)] * 3 + [V((chunks, rows, fc), BF), V((rows, d), F32), V((rows, d), F32), V((rows, d), BF), V((1, stacked), F32), V((16, stacked), BF), V((8, rows), F32), V((8, ff), F32)]
            + sems,
            1 << 10,
        )
        operands[layer], results = done[:2], done[2:]
        here_g = lax.ppermute(gbf, "section", [(3, 0), (2, 1)]) if t == 1 else gbf
        if t == 1:
            here_g, y_got = lax.optimization_barrier((here_g, y_got))
        if t == 3:
            operands[layer][1], swaps[0] = lax.optimization_barrier((operands[layer][1], swaps[0]))
        if t >= 2:
            swaps.append(along(operands[layer][1], 1, 2, 1))
    gr_got = paired(results[1])
    upper, gr_got = lax.optimization_barrier((grads_by_place(1, swaps[0]), gr_got))
    upper_came = halves(upper)
    lower = grads_by_place(0, swaps[1])
    lower_came = halves(lower)
    legs = [first_leg(upper, upper_came), first_leg(lower, lower_came)]
    arrived = [second_leg(by_second_axis(came)) for came in legs]
    gr_out = results[0]
    y_out, gr_out = pl.pallas_call(
        place_kernel,
        grid_spec=pltpu.PrefetchScalarGridSpec(
            num_scalar_prefetch=1, grid=(1,), in_specs=[ANY, whole((rows, d)), ANY, whole((rows, d))], out_specs=[ANY] * 2,
            scratch_shapes=[V((rows, d), F32), V((rows, d), F32), pltpu.SemaphoreType.DMA((2,))],
        ),
        out_shape=[jax.ShapeDtypeStruct(y_out.shape, F32)] * 2,
        input_output_aliases={1: 0, 3: 1},
    )(here, y_out, y_got, gr_out, gr_got)

    both = arrived[1] + arrived[0]
    home_mine, home_other, away_mine, away_other = simple(
        last_pair_kernel, here, both, [ANY, HERE, HERE, HERE] * 2,
        [jax.ShapeDtypeStruct((dshare, width), t) for t in (F32, BF, BF, BF)], [whole((dshare, width))] * 4,
        [V((2, share, width), BF), V((2, share, width), F32), pltpu.SemaphoreType.DMA((2,))], SMALL_LIMIT,
    )
    sections = lax.axis_size("section")
    cross = [(s * ranks + i, (s ^ 1) * ranks + (i ^ 1)) for s in range(sections) for i in range(ranks)]
    arrays = [home_mine, paired(away_mine), along(home_other, 1, 2, 1), lax.ppermute(away_other, ("section", "dp"), cross),
              shuffle]
    shapes = [(dshare, joined), (dshare, d), (dshare * fshare, d), (1, dshare), (1, hshare), (1, hshare), (1, dshare * fshare),
              (1, dshare)]
    g_in, g_attn, g_down, g_ng, g_q, g_k, g_ub, g_ob = simple(
        partial(finish_kernel, d, ff), here, arrays, [whole(a.shape) for a in arrays],
        [jax.ShapeDtypeStruct(s, F32) for s in shapes], [whole(s) for s in shapes], [],
    )
    return (y_out.reshape(1, slots * rows, d), gr_out.reshape(1, slots * rows, d), g_in[None], g_attn[None], g_down[None],
            g_ng, g_q, g_k, g_ub, g_ob)


def solution(mesh):
    in_specs = (P("dp", None),) * 3 + (P("section", "dp", None),) * 3 + (P("section", "dp"),) * 5
    out_specs = (P("section", "dp", None),) * 5 + (P("section", "dp"),) * 5
    return jax.shard_map(body, mesh=mesh, in_specs=in_specs, out_specs=out_specs, check_vma=False)
```

```python
from functools import partial
import math

import jax
import jax.numpy as jnp
from jax import lax
from jax.experimental import pallas as pl
from jax.experimental.pallas import tpu as pltpu
from jax.sharding import PartitionSpec as P

BF = jnp.bfloat16
F32 = jnp.float32
VMEM_LIMIT = 56 * 1024 * 1024
SMALL_LIMIT = 30 * 1024 * 1024
EPS = 1e-06
NN = (((1,), (0,)), ((), ()))
NT = (((1,), (1,)), ((), ()))
TN = (((0,), (0,)), ((), ()))
LANES = 128
WIDE = 256
ABSENT = 16
FIRST, LOCAL, ARRIVED = range(3)


def mm(a, b, dims=NN):
    return lax.dot_general(a, b, dims, preferred_element_type=F32)


def head_mean(x, spread, exact):
    parts = []
    for at in range(0, x.shape[1], WIDE):
        piece = x[:, at : at + WIDE]
        top = piece.astype(BF)
        total = mm(top, spread)
        if exact:
            total = total + mm((piece - top.astype(F32)).astype(BF), spread)
        parts.append(total)
    return jnp.concatenate(parts, axis=1)


def row_norm(x):
    centered = x - jnp.mean(x, axis=-1, keepdims=True)
    rstd = lax.rsqrt(jnp.mean(centered * centered, axis=-1, keepdims=True) + EPS)
    return centered * rstd, rstd


def norm_back(grad, normal, rstd, spread):
    return rstd * (grad - head_mean(grad, spread, False) - normal * head_mean(grad * normal, spread, False))


def lane_half(x, second):
    lane = lax.broadcasted_iota(jnp.int32, x.shape, 1)
    return jnp.where((lane >= LANES // 2) if second else (lane < LANES // 2), x, jnp.zeros_like(x))


class Copies:
    def __init__(self, sems):
        self.sems, self.used = sems, 0

    def start(self, src, dst):
        copy = pltpu.make_async_copy(src, dst, self.sems.at[self.used])
        self.used += 1
        copy.start()
        return copy

    def either(self, flag, src, yes, no):
        sem = self.sems.at[self.used]
        self.used += 1

        @pl.when(flag == 1)
        def _():
            pltpu.make_async_copy(src, yes, sem).start()

        @pl.when(flag != 1)
        def _():
            pltpu.make_async_copy(src, no, sem).start()

        return pltpu.make_async_copy(src, yes, sem)


def result_out(home, value, result, rounded, send, copies):
    sem = copies.sems.at[copies.used]
    copies.used += 1

    @pl.when(home == 1)
    def _():
        copy = pltpu.make_async_copy(value, result, sem)
        copy.start()
        copy.wait()

    @pl.when(home != 1)
    def _():
        copy = pltpu.make_async_copy(rounded, send, sem)
        copy.start()
        copy.wait()


def forward_kernel(d, ff, chunks, stride, kind, idx, *refs):
    @pl.when(idx[0] == 1)
    def _():
        forward_work(d, ff, chunks, stride, kind, idx, *refs)


def head_spread(head):
    row = lax.broadcasted_iota(jnp.int32, (WIDE, WIDE), 0) // head
    column = lax.broadcasted_iota(jnp.int32, (WIDE, WIDE), 1) // head
    return jnp.where(row == column, 1.0 / head, 0.0).astype(BF)


def as_column(row):
    return jnp.broadcast_to(row, (LANES, row.shape[1])).T[:, :1]


def forward_work(d, ff, chunks, stride, kind, idx, x_in, g, g3, ids, smalls, *refs):
    refs = refs[13:]
    ybf, xs, qs, ks, vs, ns, nrs, gps, es, small, kept, sent, y_out, y_send = refs[:14]
    (x_v, h_v, w_v, u_v, d_v, a_v, q_v, k_v, v_v, n_v, r_v, act_v, gp_v, e_v, rs_v, att_v, acc_v, y_v, yb_v, id_v, sm_v, ins, outs) = refs[14:]
    rows = x_v.shape[0]
    body_rows = pl.ds(0, rows)
    fc = ff // chunks
    core, slot, home = idx[1], idx[2], idx[3]
    base = jnp.where(home == 1, 0, stride)

    def columns(at, width):
        return pl.ds(pl.multiple_of(base + at, LANES), width)

    cin, cout = Copies(ins), Copies(outs)
    x_copy = None if kind == ARRIVED else cin.start(x_in.at[slot] if kind == FIRST else x_in, x_v)
    small_copies = [cin.start(ids.at[slot], id_v), cin.start(smalls.at[1 - home], sm_v)]
    wq = [cin.start(g.at[:, columns(ff + d * i, d)], w_v.at[:, pl.ds(d * i, d)]) for i in range(3)]
    groups = fc // WIDE
    wff = []
    for c in range(chunks):
        wff.append([cin.start(g.at[:, columns(fc * c, fc)], u_v.at[c])] + [
            cin.start(g3.at[pl.ds(groups * c, groups), :, columns(ff + 4 * d + d * j, d)], d_v.at[pl.ds(groups * c, groups), j])
            for j in range(4)
        ])
    wa = cin.start(g.at[:, columns(ff + 3 * d, d)], a_v)

    pending = []

    def side(i):
        return pl.ds(ff + d * i, d)

    spread = head_spread(64)
    for copy in small_copies:
        copy.wait()
    ids_row = id_v[0:1]
    ids_col = as_column(ids_row)
    keep = jnp.where(ids_col < ABSENT, 1.0, 0.0)
    if kind == ARRIVED:
        x_v[...] = x_in[...]
    else:
        x_copy.wait()
    masked = keep * x_v[...].astype(F32)
    h_v[...] = (row_norm(masked)[0] * sm_v[0:1, :d]).astype(BF)
    pending += [cout.start(x_v, xs), cout.start(h_v, kept.at[body_rows, side(2)]), cout.start(h_v, sent.at[body_rows, side(2)])]
    bias_mask = jnp.where(ids_col == ids_row, 0.0, -1e9)
    for i in range(3):
        wq[i].wait()
        raw = mm(h_v[...], w_v[:, d * i : d * i + d])
        if i == 2:
            v_v[...] = raw.astype(BF)
            pending.append(cout.start(v_v, vs))
        else:
            centered = raw - head_mean(raw, spread, True)
            rstd = lax.rsqrt(head_mean(centered * centered, spread, True) + EPS)
            normal = centered * rstd
            scaled = (normal * sm_v[0:1, d * (2 + i) : d * (3 + i)]).astype(BF)
            n_v[:, d * i : d * i + d] = normal.astype(BF)
            r_v[:, d * i : d * i + d] = rstd.astype(BF)
            if i == 0:
                q_v[...] = scaled * jnp.asarray(0.125, BF)
                pending.append(cout.start(q_v, qs))
            else:
                k_v[...] = scaled
                pending.append(cout.start(k_v, ks))
    pending += [cout.start(n_v, ns), cout.start(r_v, nrs)]
    ones = jnp.ones((16, rows), BF)
    pairs = d // LANES // chunks
    for c in range(chunks):
        for copy in wff[c]:
            copy.wait()
        pre = mm(h_v[...], u_v[c]) + sm_v[1:2, fc * c : fc * c + fc]
        cdf = 0.5 * (1.0 + lax.erf(pre * (1.0 / math.sqrt(2.0))))
        density = jnp.exp(-0.5 * pre * pre) * (1.0 / math.sqrt(2.0 * math.pi))
        act = (pre * cdf).astype(BF)
        act_v[c] = act
        gp_v[c] = (cdf + pre * density).astype(BF)
        total = mm(act, d_v[groups * c : groups * c + groups].reshape(fc, d))
        if c == 0:
            acc_v[...] = total
        else:
            acc_v[...] += total
        for p in range(pairs * c, pairs * c + pairs):
            cols = slice(LANES * p, LANES * p + LANES)
            vals_t = v_v[:, cols].T
            pair = q_v[:, cols]
            both = []
            for half in range(2):
                h = 2 * p + half
                e = jnp.exp(mm(k_v[:, cols], lane_half(pair, half), NT) + bias_mask).astype(BF)
                e_v[h] = e
                got = mm(jnp.concatenate([vals_t[64 * half : 64 * half + 64], ones], axis=0), e)
                inv = 1.0 / got[64:65]
                rs_v[h : h + 1, :] = inv
                both.append((got[:64] * inv).astype(BF))
            att_v[:, cols] = jnp.concatenate(both, axis=0).T
        span = pl.ds(fc * c, fc)
        pending += [cout.either(core, act_v.at[c], sent.at[body_rows, span], kept.at[body_rows, span]), cout.start(gp_v.at[c], gps.at[c]),
                    cout.start(e_v.at[pl.ds(2 * pairs * c, 2 * pairs)], es.at[pl.ds(2 * pairs * c, 2 * pairs)])]
    pending += [cout.start(rs_v, small), cout.either(core, att_v, sent.at[body_rows, side(3)], kept.at[body_rows, side(3)])]
    wa.wait()
    y = keep * (keep * x_v[...].astype(F32) + acc_v[...] + mm(att_v[...], a_v[...]) + sm_v[0:1, d : 2 * d])
    y_v[...] = y
    yb_v[...] = y.astype(BF)
    pending.append(cout.start(yb_v, ybf))
    result_out(home, y_v, y_out.at[slot], yb_v, y_send, cout)
    for copy in pending:
        copy.wait()


def backward_kernel(d, ff, chunks, stride, kind, idx, *refs):
    @pl.when(idx[0] == 1)
    def _():
        backward_work(d, ff, chunks, stride, kind, idx, *refs)


def backward_work(d, ff, chunks, stride, kind, idx, g_in, g, g3, ids, smalls, *refs):
    xs, qs, ks, vs, ns, nrs, gps, es, small = refs[:9]
    refs = refs[9 + 4 :]
    gbf, kept, sent, gr_out, gr_send = refs[:5]
    (g_v, gb_v, w_v, u_v, d_v, a_v, x_v, q_v, k_v, v_v, n_v, r_v, gp_v, e_v, rs_v, gat_v, gqt_v, gk_v,
     gq_b, gk_b, gv_b, gj_v, acc_v, out_v, ob_v, sm_v, sp_v, id_v, gain_v, ins, outs) = refs[5:]
    rows = x_v.shape[0]
    body_rows = pl.ds(0, rows)
    fc = ff // chunks
    groups = fc // WIDE
    core, slot, home = idx[1], idx[2], idx[3]
    base = jnp.where(home == 1, 0, stride)

    def columns(at, width):
        return pl.ds(pl.multiple_of(base + at, LANES), width)

    cin, cout = Copies(ins), Copies(outs)
    g_copy = None if kind == ARRIVED else cin.start(g_in.at[slot] if kind == FIRST else g_in, g_v)
    small_copies = [cin.start(ids.at[slot], id_v), cin.start(smalls.at[1 - home], gain_v)]
    wa = cin.start(g.at[:, columns(ff + 3 * d, d)], a_v)
    heads = [cin.start(s, v) for s, v in ((small, rs_v), (ks, k_v), (vs, v_v), (qs, q_v))]
    pairs = d // LANES // chunks
    wff = []
    for c in range(chunks):
        wff.append(
            [cin.start(g3.at[pl.ds(groups * c, groups), :, columns(ff + 4 * d + d * j, d)], d_v.at[pl.ds(groups * c, groups), j])
             for j in range(4)]
            + [cin.start(gps.at[c], gp_v.at[c]), cin.start(g.at[:, columns(fc * c, fc)], u_v.at[c]),
               cin.start(es.at[pl.ds(2 * pairs * c, 2 * pairs)], e_v.at[pl.ds(2 * pairs * c, 2 * pairs)])]
        )
    norms = [cin.start(ns, n_v), cin.start(nrs, r_v)]
    wq = [cin.start(g.at[:, columns(ff + d * i, d)], w_v.at[:, pl.ds(d * i, d)]) for i in range(3)]
    rows_in = cin.start(xs, x_v)

    pending = []

    def side(i):
        return pl.ds(ff + d * i, d)

    def summed(at, value):
        sm_v[:, at : at + value.shape[1]] = jnp.sum(value, axis=0, keepdims=True)

    spread = head_spread(64)
    for copy in small_copies:
        copy.wait()
    keep = jnp.where(as_column(id_v[0:1]) < ABSENT, 1.0, 0.0)
    if kind == ARRIVED:
        g_v[...] = g_in[...]
    else:
        g_copy.wait()
    gres = keep * g_v[...].astype(F32)
    summed(d, gres)
    gb_v[...] = gres.astype(BF)
    pending.append(cout.either(core, gb_v, sent.at[body_rows, side(0)], kept.at[body_rows, side(0)]))
    wa.wait()
    gat_v[...] = mm(a_v[...], gb_v[...], NT).astype(BF)
    for copy in heads:
        copy.wait()
    zeros = jnp.zeros((LANES // 2, rows), BF)
    for c in range(chunks):
        for copy in wff[c]:
            copy.wait()
        gup = mm(gb_v[...], d_v[groups * c : groups * c + groups].reshape(fc, d), NT) * gp_v[c].astype(F32)
        summed(4 * d + fc * c, gup)
        gup = gup.astype(BF)
        gj_v[c] = gup
        span = pl.ds(fc * c, fc)
        pending.append(cout.either(core, gj_v.at[c], kept.at[body_rows, span], sent.at[body_rows, span]))
        total = mm(gup, u_v[c], NT)
        if c == 0:
            acc_v[...] = total
        else:
            acc_v[...] += total
        for p in range(pairs * c, pairs * c + pairs):
            cols = slice(LANES * p, LANES * p + LANES)
            keys, vals, pair = k_v[:, cols], v_v[:, cols], q_v[:, cols]
            keys_t = keys.T
            gk, gv = None, None
            for half in range(2):
                h = 2 * p + half
                at_rows = slice(64 * h, 64 * h + 64)
                inv = rs_v[h : h + 1, :]
                ga = (gat_v[at_rows, :].astype(F32) * inv).astype(BF)
                ga = jnp.concatenate([zeros, ga] if half else [ga, zeros], axis=0)
                e = e_v[h]
                ef = e.astype(F32)
                gp = ef * mm(vals, ga)
                dot = jnp.sum(gp, axis=0, keepdims=True) * inv
                gs = (gp - ef * dot).astype(BF)
                gk_h = mm(gs, lane_half(pair, half))
                gv_h = mm(e, ga, NT)
                gk = gk_h if gk is None else gk + gk_h
                gv = gv_h if gv is None else gv + gv_h
                gqt_v[at_rows, :] = mm(keys_t[64 * half : 64 * half + 64], gs) * 0.125
            gk_v[:, cols] = gk
            gv_b[:, cols] = gv.astype(BF)
    pending.append(cout.either(core, gv_b, sent.at[body_rows, side(1)], kept.at[body_rows, side(1)]))
    for copy in norms:
        copy.wait()
    for i, (grad, out) in enumerate(((gqt_v[...].T, gq_b), (gk_v[...], gk_b))):
        normal = n_v[:, d * i : d * i + d].astype(F32)
        summed(2 * d + d * i, grad * normal)
        gain = gain_v[0:1, d * (2 + i) : d * (3 + i)]
        out[...] = norm_back(grad * gain, normal, r_v[:, d * i : d * i + d].astype(F32), spread).astype(BF)
        pending.append(cout.either(core, out, kept.at[body_rows, side(i)], sent.at[body_rows, side(i)]))
    for copy in wq:
        copy.wait()
    ghid = acc_v[...]
    for i, part in enumerate((gq_b, gk_b, gv_b)):
        ghid = ghid + mm(part[...], w_v[:, d * i : d * i + d], NT)
    rows_in.wait()
    xhat, rstd = row_norm(keep * x_v[...].astype(F32))
    summed(0, ghid * xhat)
    top = sm_v[...].astype(BF).astype(F32)
    sp_v[...] = jnp.concatenate([top, sm_v[...] - top, jnp.zeros((14, top.shape[1]), F32)], axis=0).astype(BF)
    tail = pl.ds(rows, 16)
    pending += [cout.start(sp_v, kept.at[tail]), cout.start(sp_v, sent.at[tail])]
    gx = ghid * gain_v[0:1, :d]
    gmask = rstd * (gx - jnp.mean(gx, axis=-1, keepdims=True) - xhat * jnp.mean(gx * xhat, axis=-1, keepdims=True))
    out = keep * (keep * g_v[...].astype(F32) + gmask)
    out_v[...] = out
    ob_v[...] = out.astype(BF)
    pending.append(cout.start(ob_v, gbf))
    result_out(home, out_v, gr_out.at[slot], ob_v, gr_send, cout)
    for copy in pending:
        copy.wait()


def split_small(values):
    top = values.astype(BF).astype(F32)
    lane = lax.broadcasted_iota(jnp.int32, values.shape, 1)
    return jnp.where(lane < 8, top, jnp.where(lane < 16, pltpu.roll(values - top, 8, 1), 0.0)).astype(BF)


def joined_small(parts):
    return parts + pltpu.roll(parts, LANES - 8, 1)


def small_table(d, ff, tables):
    total = jnp.zeros((1, tables.shape[2]), F32)
    for i in range(tables.shape[0]):
        parts = tables[i].astype(F32)
        total = total + parts[0:1] + parts[1:2]
    lane = lax.broadcasted_iota(jnp.int32, (LANES, d), 0) % 64
    place = jnp.where(lax.broadcasted_iota(jnp.int32, (LANES, d), 1) == lane // 2 * 24 + lane % 2, 1.0, 0.0)
    quarter = WIDE // 4
    ub = total[:, 4 * d :]
    up_rows = []
    for j in range(4):
        pieces = [ub[:, WIDE * b + quarter * j : WIDE * b + quarter * (j + 1)] for b in range(ff // WIDE)]
        up_rows.append(jnp.concatenate(pieces, axis=1))
    head_rows = []
    for i in range(2, 4):
        lanes = total[:, d * i : d * i + LANES]
        for p in range(1, d // LANES):
            lanes = lanes + total[:, d * i + LANES * p : d * i + LANES * (p + 1)]
        head_rows.append(lanes)
    both = jnp.concatenate(head_rows + [jnp.zeros((6, LANES), F32)], axis=0)
    placed = lax.dot_general(both, place, NN, precision=lax.Precision.HIGHEST, preferred_element_type=F32)
    rows = [total[:, :d], total[:, d : 2 * d]] + up_rows + [placed[0:1], placed[1:2], jnp.zeros((LANES - 8, d), F32)]
    return jnp.concatenate(rows, axis=0).T


def weight_grad_kernel(d, ff, idx, kept, got, *refs):
    results, (big_v, a_v, b_v, c_v, out_v, t_v, ins, outs) = refs[:5], refs[5:]
    rows = kept.shape[0] - t_v.shape[1]
    tokens = 2 * rows
    quarter, half, third = WIDE // 4, ff // 2, ff // 3
    blocks = third // WIDE
    share = d // 16
    cut = 3 * d
    y, z, core = idx[0], idx[1], idx[2]

    def load(cin, at, width, to, to_at):
        return [cin.start(src.at[pl.ds(0, rows), pl.ds(at, width)], to.at[i, :, pl.ds(to_at, width)]) for i, src in enumerate((kept, got))]

    def wait(copies):
        for copy in copies:
            copy.wait()

    def both(ref, at=0, width=d):
        return ref[:, :, at : at + width].reshape(tokens, width)

    def put(rows_at, cols_at, value):
        out_v[rows_at, cols_at] = value.astype(BF)

    def send_by_y(cout, at, width):
        cols = pl.ds(at, width)

        def rows_of(s, first, count):
            return out_v.at[pl.ds(pl.multiple_of(lax.rem(y + s, 4) * 4 * share + first, 16), count), cols]

        return [cout.start(rows_of(2, 0, 2 * share), results[3].at[:, cols]),
                cout.start(rows_of(2, 2 * share, 2 * share), results[4].at[:, cols])] + [
            cout.start(rows_of(s, 0, 4 * share), results[r].at[:, cols]) for r, s in ((1, 1), (2, 3), (0, 0))]

    def send_by_z(cout, at, width):
        cols = pl.ds(at, width)

        def rows_of(i, s):
            return out_v.at[pl.ds(pl.multiple_of((4 * i + lax.rem(z + s, 4)) * share, 16), share), cols]

        return [
            cout.start(rows_of(i, s), results[r].at[pl.ds(share * (i - base), share), cols])
            for r, s, base, count in ((3, 2, 0, 2), (4, 2, 2, 2), (1, 1, 0, 4), (2, 3, 0, 4), (0, 0, 0, 4))
            for i in range(base, base + count)
        ]

    everything = slice(0, d)

    @pl.when(core == 0)
    def _():
        cin, cout = Copies(ins), Copies(outs)
        grads = load(cin, ff, d, a_v, 0)
        loads = [load(cin, third * k, third, big_v, third * k) for k in range(3)]
        attended = load(cin, ff + 3 * d, d, b_v, 0)
        hidden, values = load(cin, ff + 2 * d, d, c_v, 0), load(cin, ff + d, d, c_v, d)
        smalls = [cin.start(src.at[pl.ds(rows, t_v.shape[1])], t_v.at[i]) for i, src in enumerate((kept, got))]
        wait(grads)
        gb = both(a_v)
        for k in range(3):
            wait(loads[k])
            found = lax.dot_general(both(big_v, third * k, third), gb, TN, preferred_element_type=F32).astype(BF)
            for b in range(blocks):
                at = quarter * (blocks * k + b)
                for j in range(4):
                    put(slice(at, at + quarter), slice(d * j, d * j + d), found[WIDE * b + quarter * j : WIDE * b + quarter * (j + 1)])
        pending = send_by_y(cout, 0, 4 * d)
        wait(attended)
        put(everything, slice(4 * d, 5 * d), lax.dot_general(both(b_v), gb, TN, preferred_element_type=F32))
        wait(hidden + values + smalls)
        put(everything, slice(5 * d, 6 * d), lax.dot_general(both(c_v), both(c_v, d), TN, preferred_element_type=F32))
        put(everything, slice(6 * d, 6 * d + LANES), split_small(small_table(d, ff, t_v)))
        wait(pending + send_by_y(cout, 4 * d, 2 * d + LANES))

    @pl.when(core == 1)
    def _():
        cin, cout = Copies(ins), Copies(outs)
        hidden = load(cin, ff + 2 * d, d, a_v, 0)
        loads = [load(cin, third * k, third, big_v, third * k) for k in range(2)]
        queries = load(cin, ff, d, b_v, 0)
        loads.append(load(cin, 2 * third, third, big_v, 2 * third))
        keys = load(cin, ff + d, d, c_v, 0)
        wait(hidden)
        turned = both(a_v).T
        pending = []
        for k in range(2):
            wait(loads[k])
            put(everything, slice(third * k, third * k + third), mm(turned, both(big_v, third * k, third)))
        pending = send_by_z(cout, 0, 2 * third)
        wait(queries)
        put(everything, slice(ff, ff + d), mm(turned, both(b_v)))
        wait(loads[2])
        put(everything, slice(2 * third, ff), mm(turned, both(big_v, 2 * third, third)))
        wait(keys)
        put(everything, slice(ff + d, ff + 2 * d), mm(turned, both(c_v)))
        out_v[:, 6 * d :] = jnp.zeros((d, LANES), BF)
        wait(pending + send_by_z(cout, 2 * third, 6 * d + LANES - 2 * third))


def added(parts):
    total = parts[0][...].astype(F32)
    for part in parts[1:]:
        total = total + part[...].astype(F32)
    shape = total.shape
    total = total.reshape(-1, shape[-1])
    main, last = total[:, : shape[-1] - LANES], split_small(joined_small(total[:, shape[-1] - LANES :]))
    return jnp.concatenate([main.astype(BF), last], axis=1).reshape(shape)


def relay_kernel(idx, up_in, down_in, up_got, down_got, up, down, hold, ins, outs):
    half = up_got.shape[0]
    cin, cout = Copies(ins), Copies(outs)
    parts = ((up_in, 0, up_got, up), (down_in, half, down_got, down))
    loads = [cin.start(block.at[pl.ds(at, half)], hold.at[i]) for i, (block, at, _, _) in enumerate(parts)]
    pending = []
    for i, (_, at, got, out) in enumerate(parts):
        loads[i].wait()
        hold[i] = added([hold.at[i], got])
        pending.append(cout.start(hold.at[i], out.at[pl.ds(at, half)]))
    for copy in pending:
        copy.wait()


def mid_kernel(idx, *refs):
    came, results, (in_v, out_v, ins, outs) = refs[:3], refs[3:7], refs[7:]
    share = results[0].shape[0]

    cin, cout = Copies(ins), Copies(outs)
    at = jnp.where(idx[2] == 0, idx[1], idx[0])
    order = [2, 1, 3, 0]
    blocks = [pl.multiple_of(lax.rem(at + s, 4) * share, 16) for s in order]
    loads = [[cin.start(part.at[pl.ds(block, share)], in_v.at[i, p]) for p, part in enumerate(came)]
             for i, block in enumerate(blocks)]
    pending = []
    for i, s in enumerate(order):
        for copy in loads[i]:
            copy.wait()
        out_v[i] = added([in_v.at[i, p] for p in range(3)])
        pending.append(cout.start(out_v.at[i], results[s]))
    for copy in pending:
        copy.wait()


def last_pair_kernel(idx, *refs):
    came, (home_mine, home_other, away_mine, away_other, in_v, hold, ins) = refs[:8], refs[8:]
    share = home_mine.shape[0]
    core, odd = idx[2], idx[4]

    sum_of(came, in_v, hold, ins)

    def rows_of(k, which):
        return hold[k, pl.ds(pl.multiple_of(which * share, 8), share), :]

    for which, home, away in ((core, home_mine, away_mine), (1 - core, home_other, away_other)):
        home[...] = jnp.where(odd == 1, rows_of(1, which), rows_of(0, which)).astype(home.dtype)
        away[...] = jnp.where(odd == 1, rows_of(0, which), rows_of(1, which)).astype(away.dtype)


def sum_of(came, in_v, hold, sems):
    copies = Copies(sems)
    loads = [copies.start(came[4 * k], in_v.at[k]) for k in range(len(came) // 4)]
    for k, load in enumerate(loads):
        load.wait()
        hold[k] = added([in_v.at[k]] + list(came[4 * k + 1 : 4 * k + 4])).astype(F32)


def place_kernel(idx, y_in, y_got, g_in, g_got, y_out, g_out, y_v, g_v, sems):
    copies = Copies(sems)
    pending = []
    for got, wide_v, out in ((y_got, y_v, y_out), (g_got, g_v, g_out)):
        wide_v[...] = got[...].astype(F32)
        pending.append(copies.start(wide_v, out.at[1 - idx[3]]))
    for copy in pending:
        copy.wait()


def picked(rows, columns, wanted):
    row = lax.broadcasted_iota(jnp.int32, (rows, columns), 0)
    column = lax.broadcasted_iota(jnp.int32, (rows, columns), 1)
    return row, column, jnp.where(column == wanted(row), 1.0, 0.0)


def prepare_kernel(d, ff, p_in, p_attn, p_down, n_gain, o_bias, u_bias, q_gain, k_gain, shuffle, out):
    share = p_in.shape[0]
    heads_part = p_in.shape[1] - ff
    for at in range(0, ff, WIDE):
        out[:, at : at + WIDE] = mm(p_in[:, heads_part + at : heads_part + at + WIDE], shuffle[...]).astype(BF)
    out[:, ff : ff + heads_part] = p_in[:, :heads_part]
    at = ff + heads_part
    out[:, at : at + d] = p_attn[...]
    down = p_down[...]
    for j in range(4):
        take = picked(share, down.shape[0], lambda row: 4 * row + j)[2].astype(BF)
        out[:, at + d * (j + 1) : at + d * (j + 2)] = mm(take, down).astype(BF)

    def column_of(ref, wanted, where):
        values = ref[...].astype(F32)
        take = picked(share, values.shape[1], wanted)[2]
        lane = lax.broadcasted_iota(jnp.int32, (share, LANES), 1)
        return jnp.where(lane == where, jnp.sum(take * values, axis=1, keepdims=True), 0.0)

    table = column_of(n_gain, lambda row: row, 0) + column_of(o_bias, lambda row: row, 1)
    for j in range(4):
        table = table + column_of(u_bias, lambda row: 4 * row + j, 2 + j)
    table = table + column_of(q_gain, lambda row: row, 6) + column_of(k_gain, lambda row: row, 7)
    out[:, at + 5 * d :] = table.astype(BF)


def smalls_kernel(d, ff, shares, place, out):
    quarter = WIDE // 4
    for layer in range(2):
        table = shares[:, LANES * layer : LANES * (layer + 1)].astype(F32).T
        pieces = [table[2 + j : 3 + j, quarter * b : quarter * (b + 1)] for b in range(ff // WIDE) for j in range(4)]
        both = mm(table[0:8].astype(BF), place[...])
        first = jnp.concatenate([table[0:1], table[1:2], both[6:7], both[7:8]], axis=1)
        out[layer] = jnp.concatenate([first, jnp.concatenate(pieces, axis=1), jnp.zeros((6, ff), F32)], axis=0)


def in_parts(x):
    top = x.astype(BF)
    rest = x - top.astype(F32)
    middle = rest.astype(BF)
    return top, middle, (rest - middle.astype(F32)).astype(BF)


def finish_kernel(d, ff, idx, own, a_in, b_in, c_in, shuffle, g_in, g_attn, g_down, g_ng, g_q, g_k, g_ub, g_ob):
    core = idx[2]
    share = own.shape[0]
    mine = own[...] + a_in[...].astype(F32)
    theirs = b_in[...].astype(F32) + c_in[...].astype(F32)
    half0 = jnp.where(core == 0, mine, theirs)
    half1 = jnp.where(core == 0, theirs, mine)
    g_in[:, : 2 * d] = half1[:, ff : ff + 2 * d]
    g_in[:, 2 * d : 3 * d] = half0[:, 5 * d : 6 * d]
    for at in range(0, ff, WIDE):
        g_in[:, 3 * d + at : 3 * d + at + WIDE] = sum(mm(part, shuffle[...], NT) for part in in_parts(half1[:, at : at + WIDE]))
    g_attn[...] = half0[:, 4 * d : 5 * d]
    stacked = jnp.concatenate([half0[:, at : at + d] for at in range(0, 4 * d, d)], axis=0)
    row, column, _ = picked(4 * share, 4 * share, lambda row: row)
    turn = jnp.where(column == lax.rem(row, 4) * share + row // 4, 1.0, 0.0).astype(BF)
    g_down[...] = sum(mm(turn, part) for part in in_parts(stacked))
    small = joined_small(half0[:, 6 * d :])
    turned = jnp.concatenate([small, jnp.zeros((LANES - share, LANES), F32)], axis=0).T
    g_ng[...] = turned[0:1, :share]
    g_ob[...] = turned[1:2, :share]
    g_q[...] = turned[6:7, : g_q.shape[1]]
    g_k[...] = turned[7:8, : g_k.shape[1]]
    total = jnp.zeros((8, 4 * share), F32)
    for j in range(4):
        row, column, _ = picked(LANES, 4 * share, lambda row: row)
        spread_out = jnp.where(column == 4 * row + j, 1.0, 0.0)
        total = total + jnp.where(lax.broadcasted_iota(jnp.int32, (8, 4 * share), 0) == 2 + j, 1.0, 0.0) * lax.dot_general(
            turned[0:8], spread_out, NN, precision=lax.Precision.HIGHEST, preferred_element_type=F32)
    g_ub[...] = jnp.sum(total, axis=0, keepdims=True)


ANY = pl.BlockSpec(memory_space=pl.ANY)
HERE = pl.BlockSpec(memory_space=pltpu.VMEM)


def whole(shape):
    return pl.BlockSpec(shape, lambda i, idx: (0,) * len(shape))


def pick(shape):
    return pl.BlockSpec((1,) + shape, lambda i, idx: (idx[2],) + (0,) * len(shape))


def call(kernel, idx, ins, fresh, stashes, scratch, flops):
    outs = pl.pallas_call(
        kernel,
        grid_spec=pltpu.PrefetchScalarGridSpec(
            num_scalar_prefetch=1,
            grid=(1,),
            in_specs=[s for _, s in ins] + [ANY] * len(stashes),
            out_specs=[ANY] * (1 + len(stashes)),
            scratch_shapes=scratch,
        ),
        out_shape=[jax.ShapeDtypeStruct(*fresh)] + [jax.ShapeDtypeStruct(a.shape, a.dtype) for a in stashes],
        input_output_aliases={1 + len(ins) + i: 1 + i for i in range(len(stashes))},
        compiler_params=pltpu.CompilerParams(dimension_semantics=("arbitrary",), vmem_limit_bytes=VMEM_LIMIT),
        cost_estimate=pl.CostEstimate(flops=flops, bytes_accessed=1 << 10, transcendentals=0),
    )(idx, *[a for a, _ in ins], *stashes)
    return outs[0], list(outs[1:])


def plain(kernel, arrays, specs, out_shapes, out_specs, scratch):
    return pl.pallas_call(
        kernel, grid=(1,), in_specs=specs, out_specs=out_specs, scratch_shapes=scratch, out_shape=out_shapes,
        compiler_params=pltpu.CompilerParams(dimension_semantics=("arbitrary",), vmem_limit_bytes=VMEM_LIMIT),
        cost_estimate=pl.CostEstimate(flops=1 << 10, bytes_accessed=1 << 10, transcendentals=0),
    )(*arrays)


def simple(kernel, idx, arrays, specs, out_shapes, out_specs, scratch, limit=VMEM_LIMIT):
    return pl.pallas_call(
        kernel,
        grid_spec=pltpu.PrefetchScalarGridSpec(
            num_scalar_prefetch=1, grid=(1,), in_specs=specs, out_specs=out_specs, scratch_shapes=scratch
        ),
        out_shape=out_shapes,
        compiler_params=pltpu.CompilerParams(dimension_semantics=("arbitrary",), vmem_limit_bytes=limit),
        cost_estimate=pl.CostEstimate(flops=1 << 10, bytes_accessed=1 << 10, transcendentals=0),
    )(idx, *arrays)


def along(x, step, size, by):
    devices = lax.axis_size("dp")

    def to(i):
        digit = i // step % size
        return i + ((digit + by) % size - digit) * step

    return lax.ppermute(x, "dp", [(i, to(i)) for i in range(devices)])


def paired(x):
    return lax.ppermute(x, "section", [(0, 1), (1, 0), (2, 3), (3, 2)])


def body(tokens, cotangent, lengths, proj_in, proj_attn, proj_down, norm_gain, query_gain, key_gain, up_bias, out_bias):
    ranks = lax.axis_size("dp")
    section = lax.axis_index("section")
    rank = lax.axis_index("dp")
    slots = lengths.shape[0]
    rows = tokens.shape[0] // slots
    d = tokens.shape[1]
    joined = proj_in.shape[2]
    ff = proj_down.shape[1] * ranks
    head = query_gain.shape[1] * ranks
    heads = d // head
    dshare = proj_in.shape[1]
    fshare = proj_down.shape[1] // dshare
    hshare = query_gain.shape[1]
    chunks = 3
    wide = joined + d + ff
    stride = wide + LANES
    side = math.isqrt(ranks // 2)
    core, z, y = lax.rem(rank, 2), lax.rem(rank // 2, side), rank // (2 * side)
    stage, odd = section // 2, lax.rem(section, 2)
    slot = lax.rem(stage + odd, 2)

    place = jnp.arange(WIDE, dtype=jnp.int32)
    source = (place % (WIDE // fshare)) * fshare + place // (WIDE // fshare)
    shuffle = (place[:, None] == source[None, :]).astype(BF)

    def full(a):
        return pl.BlockSpec(a.shape, lambda i: (0,) * a.ndim)

    shares = [proj_in[0], proj_attn[0], proj_down[0], norm_gain, out_bias, up_bias, query_gain, key_gain, shuffle]
    heads_part = joined - ff
    local = jax.ShapeDtypeStruct((dshare, stride), BF)
    local = plain(partial(prepare_kernel, d, ff), shares, [full(a) for a in shares], local, full(local), [])
    other = paired(local)
    g = lax.all_gather(jnp.concatenate([local, other], axis=1), "dp", axis=0).reshape(d, 2 * stride)
    shares = jnp.concatenate([local[:, wide:], other[:, wide:]], axis=1)
    step = 1
    while step < ranks:
        got = lax.ppermute(shares, "dp", [(i, i ^ step) for i in range(ranks)])
        low = lax.rem(rank // step, 2) == 0
        shares = jnp.where(low, jnp.concatenate([shares, got]), jnp.concatenate([got, shares]))
        step *= 2
    toks = tokens.reshape(slots, rows, d)
    seeds = cotangent.reshape(slots, rows, d)
    ends = jnp.cumsum(lengths, axis=-1)
    position = jnp.arange(rows, dtype=jnp.int32)
    image = jnp.sum((position[None, :, None] >= ends[:, None, :]).astype(jnp.int32), axis=-1)
    image = jnp.where(position[None, :] < ends[:, 2:3], image, ABSENT + position[None, :])
    ids = jnp.broadcast_to(image[:, None, :].astype(F32), (slots, 8, rows))

    def index_of(layer, active_stage):
        return jnp.stack([stage == active_stage, core, slot, odd == layer]).astype(jnp.int32)

    indices = [[index_of(layer, active) for active in range(2)] for layer in range(2)]
    here = jnp.stack([y, z, core, slot, odd]).astype(jnp.int32)
    element = jnp.arange(d, dtype=jnp.int32) % head
    spread_gain = (jnp.arange(d, dtype=jnp.int32)[:, None] == (element // hshare * dshare + element % hshare)[None, :]).astype(BF)
    small = jax.ShapeDtypeStruct((2, 8, ff), F32)
    smalls = plain(
        partial(smalls_kernel, d, ff), [shares, spread_gain], [full(shares), full(spread_gain)], small, full(small), [],
    )
    g, indices, here, ids, smalls = lax.optimization_barrier((g, indices, here, ids, smalls))
    g3 = g.reshape(ff // WIDE, WIDE // fshare, g.shape[1])
    def stash(*shape, dtype=BF):
        return pl.pallas_call(
            lambda out: None, out_shape=jax.ShapeDtypeStruct(shape, dtype), out_specs=pl.BlockSpec(memory_space=pl.ANY)
        )()

    fc = ff // chunks
    groups = ff // WIDE

    V = pltpu.VMEM
    weights_v = [V((d, heads_part), BF), V((chunks, d, fc), BF), V((groups, fshare, WIDE // fshare, d), BF), V((d, d), BF)]
    sems = [pltpu.SemaphoreType.DMA((48,)), pltpu.SemaphoreType.DMA((48,))]
    stacked = ff + 4 * d
    operands = [[stash(rows + 16, stacked), stash(rows + 16, stacked)] for _ in range(2)]
    kept = [[stash(rows, d) for _ in range(4)] + [stash(rows, 2 * d), stash(rows, 2 * d), stash(chunks, rows, fc),
             stash(heads, rows, rows), stash(16, rows, dtype=F32)] for _ in range(2)]
    results = [stash(slots, rows, d, dtype=F32), stash(rows, d)]
    here_x = toks
    for t in range(4):
        layer = t % 2
        ybf, done = call(
            partial(forward_kernel, d, ff, chunks, stride, (FIRST, LOCAL, ARRIVED, LOCAL)[t]),
            indices[layer][t // 2],
            [(here_x, HERE if t == 2 else ANY)] + [(a, ANY) for a in (g, g3, ids, smalls)],
            ((rows, d), BF),
            kept[layer][:9] + operands[layer] + results,
            [V((rows, d), BF), V((rows, d), BF)] + weights_v
            + [V((rows, d), BF)] * 3 + [V((rows, 2 * d), BF)] * 2 + [V((chunks, rows, fc), BF)] * 2
            + [V((heads, rows, rows), BF), V((16, rows), F32), V((rows, d), BF), V((rows, d), F32), V((rows, d), F32), V((rows, d), BF), V((8, rows), F32), V((8, ff), F32)]
            + sems,
            1 << 10,
        )
        kept[layer], operands[layer], results = done[:9], done[9:11], done[11:]
        here_x = lax.ppermute(ybf, "section", [(0, 3), (1, 2)]) if t == 1 else ybf
    y_out, y_send = results
    y_got = paired(y_send)

    results = [stash(slots, rows, d, dtype=F32), stash(rows, d)]
    width = 6 * d + LANES
    share = 2 * dshare

    def moved(x, leg, by):
        def to(i):
            step = 2 * side if i % 2 == leg else 2
            digit = i // step % side
            return i + ((digit + by) % side - digit) * step

        return lax.ppermute(x, "dp", [(i, to(i)) for i in range(ranks)])

    def grads_by_place(layer, got):
        return simple(
            partial(weight_grad_kernel, d, ff), here,
            [operands[layer][0], got], [ANY] * 2,
            [jax.ShapeDtypeStruct((side * share, width), BF)] * 3 + [jax.ShapeDtypeStruct((side // 2 * share, width), BF)] * 2,
            [ANY] * 5,
            [V((2, rows, ff), BF), V((2, rows, d), BF), V((2, rows, d), BF), V((2, rows, 2 * d), BF), V((d, width), BF), V((2, 16, stacked), BF),
             pltpu.SemaphoreType.DMA((32,)), pltpu.SemaphoreType.DMA((32,))],
        )

    def halves(made):
        return moved(made[3], 0, 1), moved(made[4], 0, -1)

    def first_leg(made, came):
        own, up, down = made[:3]
        part = (side // 2 * share, width)
        up, down = pl.pallas_call(
            relay_kernel,
            grid_spec=pltpu.PrefetchScalarGridSpec(
                num_scalar_prefetch=1, grid=(1,), in_specs=[ANY, ANY, HERE, HERE], out_specs=[ANY] * 2,
                scratch_shapes=[V((2,) + part, BF), pltpu.SemaphoreType.DMA((2,)), pltpu.SemaphoreType.DMA((2,))],
            ),
            out_shape=[jax.ShapeDtypeStruct(up.shape, BF)] * 2,
            input_output_aliases={1: 0, 2: 1},
            compiler_params=pltpu.CompilerParams(dimension_semantics=("arbitrary",), vmem_limit_bytes=SMALL_LIMIT),
            cost_estimate=pl.CostEstimate(flops=1 << 10, bytes_accessed=1 << 10, transcendentals=0),
        )(here, up, down, *came)
        return [own, moved(up, 0, 1), moved(down, 0, -1)]

    def second_leg(outs):
        far, near, back = (moved(outs[s], 1, s) for s in (2, 1, 3))
        return [outs[0], near, far, back]

    def by_second_axis(came):
        return simple(
            mid_kernel, here, came, [ANY] * 3, [jax.ShapeDtypeStruct((share, width), BF)] * side, [ANY] * side,
            [V((side, 3, share, width), BF), V((side, share, width), BF), pltpu.SemaphoreType.DMA((12,)), pltpu.SemaphoreType.DMA((4,))],
        )

    here_g = seeds
    swaps = []
    for t in range(4):
        layer = 1 - t % 2
        gbf, done = call(
            partial(backward_kernel, d, ff, chunks, stride, (FIRST, LOCAL, ARRIVED, LOCAL)[t]),
            indices[layer][1 - t // 2],
            [(here_g, HERE if t == 2 else ANY)] + [(a, ANY) for a in [g, g3, ids, smalls] + kept[layer]],
            ((rows, d), BF),
            operands[layer] + results,
            [V((rows, d), BF), V((rows, d), BF)] + weights_v
            + [V((rows, d), BF)] * 4 + [V((rows, 2 * d), BF)] * 2
            + [V((chunks, rows, fc), BF), V((heads, rows, rows), BF), V((16, rows), F32)]
            + [V((d, rows), BF), V((d, rows), F32), V((rows, d), F32)]
            + [V((rows, d), BF)] * 3 + [V((chunks, rows, fc), BF), V((rows, d), F32), V((rows, d), F32), V((rows, d), BF), V((1, stacked), F32), V((16, stacked), BF), V((8, rows), F32), V((8, ff), F32)]
            + sems,
            1 << 10,
        )
        operands[layer], results = done[:2], done[2:]
        here_g = lax.ppermute(gbf, "section", [(3, 0), (2, 1)]) if t == 1 else gbf
        if t == 1:
            here_g, y_got = lax.optimization_barrier((here_g, y_got))
        if t == 3:
            operands[layer][1], swaps[0] = lax.optimization_barrier((operands[layer][1], swaps[0]))
        if t >= 2:
            swaps.append(along(operands[layer][1], 1, 2, 1))
    gr_got = paired(results[1])
    upper, gr_got = lax.optimization_barrier((grads_by_place(1, swaps[0]), gr_got))
    upper_came = halves(upper)
    lower = grads_by_place(0, swaps[1])
    lower_came = halves(lower)
    legs = [first_leg(upper, upper_came), first_leg(lower, lower_came)]
    arrived = [second_leg(by_second_axis(came)) for came in legs]
    gr_out = results[0]
    y_out, gr_out = pl.pallas_call(
        place_kernel,
        grid_spec=pltpu.PrefetchScalarGridSpec(
            num_scalar_prefetch=1, grid=(1,), in_specs=[ANY, whole((rows, d)), ANY, whole((rows, d))], out_specs=[ANY] * 2,
            scratch_shapes=[V((rows, d), F32), V((rows, d), F32), pltpu.SemaphoreType.DMA((2,))],
        ),
        out_shape=[jax.ShapeDtypeStruct(y_out.shape, F32)] * 2,
        input_output_aliases={1: 0, 3: 1},
    )(here, y_out, y_got, gr_out, gr_got)

    both = arrived[1] + arrived[0]
    home_mine, home_other, away_mine, away_other = simple(
        last_pair_kernel, here, both, [ANY, HERE, HERE, HERE] * 2,
        [jax.ShapeDtypeStruct((dshare, width), t) for t in (F32, BF, BF, BF)], [whole((dshare, width))] * 4,
        [V((2, share, width), BF), V((2, share, width), F32), pltpu.SemaphoreType.DMA((2,))], SMALL_LIMIT,
    )
    sections = lax.axis_size("section")
    cross = [(s * ranks + i, (s ^ 1) * ranks + (i ^ 1)) for s in range(sections) for i in range(ranks)]
    arrays = [home_mine, paired(away_mine), along(home_other, 1, 2, 1), lax.ppermute(away_other, ("section", "dp"), cross),
              shuffle]
    shapes = [(dshare, joined), (dshare, d), (dshare * fshare, d), (1, dshare), (1, hshare), (1, hshare), (1, dshare * fshare),
              (1, dshare)]
    g_in, g_attn, g_down, g_ng, g_q, g_k, g_ub, g_ob = simple(
        partial(finish_kernel, d, ff), here, arrays, [whole(a.shape) for a in arrays],
        [jax.ShapeDtypeStruct(s, F32) for s in shapes], [whole(s) for s in shapes], [],
    )
    return (y_out.reshape(1, slots * rows, d), gr_out.reshape(1, slots * rows, d), g_in[None], g_attn[None], g_down[None],
            g_ng, g_q, g_k, g_ub, g_ob)


def solution(mesh):
    in_specs = (P("dp", None),) * 3 + (P("section", "dp", None),) * 3 + (P("section", "dp"),) * 5
    out_specs = (P("section", "dp", None),) * 5 + (P("section", "dp"),) * 5
    return jax.shard_map(body, mesh=mesh, in_specs=in_specs, out_specs=out_specs, check_vma=False)
```

```python
from functools import partial
import math

import jax
import jax.numpy as jnp
from jax import lax
from jax.experimental import pallas as pl
from jax.experimental.pallas import tpu as pltpu
from jax.sharding import PartitionSpec as P

BF = jnp.bfloat16
F32 = jnp.float32
VMEM_LIMIT = 56 * 1024 * 1024
SMALL_LIMIT = 30 * 1024 * 1024
EPS = 1e-06
NN = (((1,), (0,)), ((), ()))
NT = (((1,), (1,)), ((), ()))
TN = (((0,), (0,)), ((), ()))
LANES = 128
WIDE = 256
ABSENT = 16
FIRST, LOCAL, ARRIVED = range(3)


def mm(a, b, dims=NN):
    return lax.dot_general(a, b, dims, preferred_element_type=F32)


def head_mean(x, spread, exact):
    parts = []
    for at in range(0, x.shape[1], WIDE):
        piece = x[:, at : at + WIDE]
        top = piece.astype(BF)
        total = mm(top, spread)
        if exact:
            total = total + mm((piece - top.astype(F32)).astype(BF), spread)
        parts.append(total)
    return jnp.concatenate(parts, axis=1)


def row_norm(x):
    centered = x - jnp.mean(x, axis=-1, keepdims=True)
    rstd = lax.rsqrt(jnp.mean(centered * centered, axis=-1, keepdims=True) + EPS)
    return centered * rstd, rstd


def norm_back(grad, normal, rstd, spread):
    return rstd * (grad - head_mean(grad, spread, False) - normal * head_mean(grad * normal, spread, False))


def lane_half(x, second):
    lane = lax.broadcasted_iota(jnp.int32, x.shape, 1)
    return jnp.where((lane >= LANES // 2) if second else (lane < LANES // 2), x, jnp.zeros_like(x))


class Copies:
    def __init__(self, sems):
        self.sems, self.used = sems, 0

    def start(self, src, dst):
        copy = pltpu.make_async_copy(src, dst, self.sems.at[self.used])
        self.used += 1
        copy.start()
        return copy

    def either(self, flag, src, yes, no):
        sem = self.sems.at[self.used]
        self.used += 1

        @pl.when(flag == 1)
        def _():
            pltpu.make_async_copy(src, yes, sem).start()

        @pl.when(flag != 1)
        def _():
            pltpu.make_async_copy(src, no, sem).start()

        return pltpu.make_async_copy(src, yes, sem)


def result_out(home, value, result, rounded, send, copies):
    sem = copies.sems.at[copies.used]
    copies.used += 1

    @pl.when(home == 1)
    def _():
        copy = pltpu.make_async_copy(value, result, sem)
        copy.start()
        copy.wait()

    @pl.when(home != 1)
    def _():
        copy = pltpu.make_async_copy(rounded, send, sem)
        copy.start()
        copy.wait()


def forward_kernel(d, ff, chunks, stride, kind, idx, *refs):
    @pl.when(idx[0] == 1)
    def _():
        forward_work(d, ff, chunks, stride, kind, idx, *refs)


def head_spread(head):
    row = lax.broadcasted_iota(jnp.int32, (WIDE, WIDE), 0) // head
    column = lax.broadcasted_iota(jnp.int32, (WIDE, WIDE), 1) // head
    return jnp.where(row == column, 1.0 / head, 0.0).astype(BF)


def as_column(row):
    return jnp.broadcast_to(row, (LANES, row.shape[1])).T[:, :1]


def forward_work(d, ff, chunks, stride, kind, idx, x_in, g, g3, ids, smalls, *refs):
    refs = refs[13:]
    ybf, xs, qs, ks, vs, ns, nrs, gps, es, small, kept, sent, y_out, y_send = refs[:14]
    (x_v, h_v, w_v, u_v, d_v, a_v, q_v, k_v, v_v, n_v, r_v, act_v, gp_v, e_v, rs_v, att_v, acc_v, y_v, yb_v, id_v, sm_v, ins, outs) = refs[14:]
    rows = x_v.shape[0]
    body_rows = pl.ds(0, rows)
    fc = ff // chunks
    core, slot, home = idx[1], idx[2], idx[3]
    base = jnp.where(home == 1, 0, stride)

    def columns(at, width):
        return pl.ds(pl.multiple_of(base + at, LANES), width)

    cin, cout = Copies(ins), Copies(outs)
    x_copy = None if kind == ARRIVED else cin.start(x_in.at[slot] if kind == FIRST else x_in, x_v)
    small_copies = [cin.start(ids.at[slot], id_v), cin.start(smalls.at[1 - home], sm_v)]
    wq = [cin.start(g.at[:, columns(ff + d * i, d)], w_v.at[:, pl.ds(d * i, d)]) for i in range(3)]
    groups = fc // WIDE
    wff = []
    for c in range(chunks):
        wff.append([cin.start(g.at[:, columns(fc * c, fc)], u_v.at[c])] + [
            cin.start(g3.at[pl.ds(groups * c, groups), :, columns(ff + 4 * d + d * j, d)], d_v.at[pl.ds(groups * c, groups), j])
            for j in range(4)
        ])
    wa = cin.start(g.at[:, columns(ff + 3 * d, d)], a_v)

    pending = []

    def side(i):
        return pl.ds(ff + d * i, d)

    spread = head_spread(64)
    for copy in small_copies:
        copy.wait()
    ids_row = id_v[...]
    ids_col = as_column(ids_row)
    keep = jnp.where(ids_col < ABSENT, 1.0, 0.0)
    if kind == ARRIVED:
        x_v[...] = x_in[...]
    else:
        x_copy.wait()
    masked = keep * x_v[...].astype(F32)
    h_v[...] = (row_norm(masked)[0] * sm_v[0:1, :d]).astype(BF)
    pending += [cout.start(x_v, xs), cout.start(h_v, kept.at[body_rows, side(2)]), cout.start(h_v, sent.at[body_rows, side(2)])]
    bias_mask = jnp.where(ids_col == ids_row, 0.0, -1e9)
    for i in range(3):
        wq[i].wait()
        raw = mm(h_v[...], w_v[:, d * i : d * i + d])
        if i == 2:
            v_v[...] = raw.astype(BF)
            pending.append(cout.start(v_v, vs))
        else:
            centered = raw - head_mean(raw, spread, True)
            rstd = lax.rsqrt(head_mean(centered * centered, spread, True) + EPS)
            normal = centered * rstd
            scaled = (normal * sm_v[0:1, d * (2 + i) : d * (3 + i)]).astype(BF)
            n_v[:, d * i : d * i + d] = normal.astype(BF)
            r_v[:, d * i : d * i + d] = rstd.astype(BF)
            if i == 0:
                q_v[...] = scaled * jnp.asarray(0.125, BF)
                pending.append(cout.start(q_v, qs))
            else:
                k_v[...] = scaled
                pending.append(cout.start(k_v, ks))
    pending += [cout.start(n_v, ns), cout.start(r_v, nrs)]
    ones = jnp.ones((16, rows), BF)
    pairs = d // LANES // chunks
    for c in range(chunks):
        for copy in wff[c]:
            copy.wait()
        pre = mm(h_v[...], u_v[c]) + sm_v[1:2, fc * c : fc * c + fc]
        cdf = 0.5 * (1.0 + lax.erf(pre * (1.0 / math.sqrt(2.0))))
        density = jnp.exp(-0.5 * pre * pre) * (1.0 / math.sqrt(2.0 * math.pi))
        act = (pre * cdf).astype(BF)
        act_v[c] = act
        gp_v[c] = (cdf + pre * density).astype(BF)
        total = mm(act, d_v[groups * c : groups * c + groups].reshape(fc, d))
        if c == 0:
            acc_v[...] = total
        else:
            acc_v[...] += total
        for p in range(pairs * c, pairs * c + pairs):
            cols = slice(LANES * p, LANES * p + LANES)
            vals_t = v_v[:, cols].T
            pair = q_v[:, cols]
            both = []
            for half in range(2):
                h = 2 * p + half
                e = jnp.exp(mm(k_v[:, cols], lane_half(pair, half), NT) + bias_mask).astype(BF)
                e_v[h] = e
                got = mm(jnp.concatenate([vals_t[64 * half : 64 * half + 64], ones], axis=0), e)
                inv = 1.0 / got[64:65]
                rs_v[h : h + 1, :] = inv
                both.append((got[:64] * inv).astype(BF))
            att_v[:, cols] = jnp.concatenate(both, axis=0).T
        span = pl.ds(fc * c, fc)
        pending += [cout.either(core, act_v.at[c], sent.at[body_rows, span], kept.at[body_rows, span]), cout.start(gp_v.at[c], gps.at[c]),
                    cout.start(e_v.at[pl.ds(2 * pairs * c, 2 * pairs)], es.at[pl.ds(2 * pairs * c, 2 * pairs)])]
    pending += [cout.start(rs_v, small), cout.either(core, att_v, sent.at[body_rows, side(3)], kept.at[body_rows, side(3)])]
    wa.wait()
    y = keep * (keep * x_v[...].astype(F32) + acc_v[...] + mm(att_v[...], a_v[...]) + sm_v[0:1, d : 2 * d])
    y_v[...] = y
    yb_v[...] = y.astype(BF)
    pending.append(cout.start(yb_v, ybf))
    result_out(home, y_v, y_out.at[slot], yb_v, y_send, cout)
    for copy in pending:
        copy.wait()


def backward_kernel(d, ff, chunks, stride, kind, idx, *refs):
    @pl.when(idx[0] == 1)
    def _():
        backward_work(d, ff, chunks, stride, kind, idx, *refs)


def backward_work(d, ff, chunks, stride, kind, idx, g_in, g, g3, ids, smalls, *refs):
    xs, qs, ks, vs, ns, nrs, gps, es, small = refs[:9]
    refs = refs[9 + 4 :]
    gbf, kept, sent, gr_out, gr_send = refs[:5]
    (g_v, gb_v, w_v, u_v, d_v, a_v, x_v, q_v, k_v, v_v, n_v, r_v, gp_v, e_v, rs_v, gat_v, gqt_v, gk_v,
     gq_b, gk_b, gv_b, gj_v, acc_v, out_v, ob_v, sm_v, sp_v, id_v, gain_v, ins, outs) = refs[5:]
    rows = x_v.shape[0]
    body_rows = pl.ds(0, rows)
    fc = ff // chunks
    groups = fc // WIDE
    core, slot, home = idx[1], idx[2], idx[3]
    base = jnp.where(home == 1, 0, stride)

    def columns(at, width):
        return pl.ds(pl.multiple_of(base + at, LANES), width)

    cin, cout = Copies(ins), Copies(outs)
    g_copy = None if kind == ARRIVED else cin.start(g_in.at[slot] if kind == FIRST else g_in, g_v)
    small_copies = [cin.start(ids.at[slot], id_v), cin.start(smalls.at[1 - home], gain_v)]
    wa = cin.start(g.at[:, columns(ff + 3 * d, d)], a_v)
    heads = [cin.start(s, v) for s, v in ((small, rs_v), (ks, k_v), (vs, v_v), (qs, q_v))]
    pairs = d // LANES // chunks
    wff = []
    for c in range(chunks):
        wff.append(
            [cin.start(g3.at[pl.ds(groups * c, groups), :, columns(ff + 4 * d + d * j, d)], d_v.at[pl.ds(groups * c, groups), j])
             for j in range(4)]
            + [cin.start(gps.at[c], gp_v.at[c]), cin.start(g.at[:, columns(fc * c, fc)], u_v.at[c]),
               cin.start(es.at[pl.ds(2 * pairs * c, 2 * pairs)], e_v.at[pl.ds(2 * pairs * c, 2 * pairs)])]
        )
    norms = [cin.start(ns, n_v), cin.start(nrs, r_v)]
    wq = [cin.start(g.at[:, columns(ff + d * i, d)], w_v.at[:, pl.ds(d * i, d)]) for i in range(3)]
    rows_in = cin.start(xs, x_v)

    pending = []

    def side(i):
        return pl.ds(ff + d * i, d)

    def summed(at, value):
        sm_v[:, at : at + value.shape[1]] = jnp.sum(value, axis=0, keepdims=True)

    spread = head_spread(64)
    for copy in small_copies:
        copy.wait()
    keep = jnp.where(as_column(id_v[...]) < ABSENT, 1.0, 0.0)
    if kind == ARRIVED:
        g_v[...] = g_in[...]
    else:
        g_copy.wait()
    gres = keep * g_v[...].astype(F32)
    summed(d, gres)
    gb_v[...] = gres.astype(BF)
    pending.append(cout.either(core, gb_v, sent.at[body_rows, side(0)], kept.at[body_rows, side(0)]))
    wa.wait()
    gat_v[...] = mm(a_v[...], gb_v[...], NT).astype(BF)
    for copy in heads:
        copy.wait()
    zeros = jnp.zeros((LANES // 2, rows), BF)
    for c in range(chunks):
        for copy in wff[c]:
            copy.wait()
        gup = mm(gb_v[...], d_v[groups * c : groups * c + groups].reshape(fc, d), NT) * gp_v[c].astype(F32)
        summed(4 * d + fc * c, gup)
        gup = gup.astype(BF)
        gj_v[c] = gup
        span = pl.ds(fc * c, fc)
        pending.append(cout.either(core, gj_v.at[c], kept.at[body_rows, span], sent.at[body_rows, span]))
        total = mm(gup, u_v[c], NT)
        if c == 0:
            acc_v[...] = total
        else:
            acc_v[...] += total
        for p in range(pairs * c, pairs * c + pairs):
            cols = slice(LANES * p, LANES * p + LANES)
            keys, vals, pair = k_v[:, cols], v_v[:, cols], q_v[:, cols]
            keys_t = keys.T
            gk, gv = None, None
            for half in range(2):
                h = 2 * p + half
                at_rows = slice(64 * h, 64 * h + 64)
                inv = rs_v[h : h + 1, :]
                ga = (gat_v[at_rows, :].astype(F32) * inv).astype(BF)
                ga = jnp.concatenate([zeros, ga] if half else [ga, zeros], axis=0)
                e = e_v[h]
                ef = e.astype(F32)
                gp = ef * mm(vals, ga)
                dot = jnp.sum(gp, axis=0, keepdims=True) * inv
                gs = (gp - ef * dot).astype(BF)
                gk_h = mm(gs, lane_half(pair, half))
                gv_h = mm(e, ga, NT)
                gk = gk_h if gk is None else gk + gk_h
                gv = gv_h if gv is None else gv + gv_h
                gqt_v[at_rows, :] = mm(keys_t[64 * half : 64 * half + 64], gs) * 0.125
            gk_v[:, cols] = gk
            gv_b[:, cols] = gv.astype(BF)
    pending.append(cout.either(core, gv_b, sent.at[body_rows, side(1)], kept.at[body_rows, side(1)]))
    for copy in norms:
        copy.wait()
    for i, (grad, out) in enumerate(((gqt_v[...].T, gq_b), (gk_v[...], gk_b))):
        normal = n_v[:, d * i : d * i + d].astype(F32)
        summed(2 * d + d * i, grad * normal)
        gain = gain_v[0:1, d * (2 + i) : d * (3 + i)]
        out[...] = norm_back(grad * gain, normal, r_v[:, d * i : d * i + d].astype(F32), spread).astype(BF)
        pending.append(cout.either(core, out, kept.at[body_rows, side(i)], sent.at[body_rows, side(i)]))
    for copy in wq:
        copy.wait()
    ghid = acc_v[...]
    for i, part in enumerate((gq_b, gk_b, gv_b)):
        ghid = ghid + mm(part[...], w_v[:, d * i : d * i + d], NT)
    rows_in.wait()
    xhat, rstd = row_norm(keep * x_v[...].astype(F32))
    summed(0, ghid * xhat)
    top = sm_v[...].astype(BF).astype(F32)
    sp_v[...] = jnp.concatenate([top, sm_v[...] - top, jnp.zeros((14, top.shape[1]), F32)], axis=0).astype(BF)
    tail = pl.ds(rows, 16)
    pending += [cout.start(sp_v, kept.at[tail]), cout.start(sp_v, sent.at[tail])]
    gx = ghid * gain_v[0:1, :d]
    gmask = rstd * (gx - jnp.mean(gx, axis=-1, keepdims=True) - xhat * jnp.mean(gx * xhat, axis=-1, keepdims=True))
    out = keep * (keep * g_v[...].astype(F32) + gmask)
    out_v[...] = out
    ob_v[...] = out.astype(BF)
    pending.append(cout.start(ob_v, gbf))
    result_out(home, out_v, gr_out.at[slot], ob_v, gr_send, cout)
    for copy in pending:
        copy.wait()


def split_small(values):
    top = values.astype(BF).astype(F32)
    lane = lax.broadcasted_iota(jnp.int32, values.shape, 1)
    return jnp.where(lane < 8, top, jnp.where(lane < 16, pltpu.roll(values - top, 8, 1), 0.0)).astype(BF)


def joined_small(parts):
    return parts + pltpu.roll(parts, LANES - 8, 1)


def small_table(d, ff, tables):
    total = jnp.zeros((1, tables.shape[2]), F32)
    for i in range(tables.shape[0]):
        parts = tables[i].astype(F32)
        total = total + parts[0:1] + parts[1:2]
    lane = lax.broadcasted_iota(jnp.int32, (LANES, d), 0) % 64
    place = jnp.where(lax.broadcasted_iota(jnp.int32, (LANES, d), 1) == lane // 2 * 24 + lane % 2, 1.0, 0.0)
    quarter = WIDE // 4
    ub = total[:, 4 * d :]
    up_rows = []
    for j in range(4):
        pieces = [ub[:, WIDE * b + quarter * j : WIDE * b + quarter * (j + 1)] for b in range(ff // WIDE)]
        up_rows.append(jnp.concatenate(pieces, axis=1))
    head_rows = []
    for i in range(2, 4):
        lanes = total[:, d * i : d * i + LANES]
        for p in range(1, d // LANES):
            lanes = lanes + total[:, d * i + LANES * p : d * i + LANES * (p + 1)]
        head_rows.append(lanes)
    both = jnp.concatenate(head_rows + [jnp.zeros((6, LANES), F32)], axis=0)
    placed = lax.dot_general(both, place, NN, precision=lax.Precision.HIGHEST, preferred_element_type=F32)
    rows = [total[:, :d], total[:, d : 2 * d]] + up_rows + [placed[0:1], placed[1:2], jnp.zeros((LANES - 8, d), F32)]
    return jnp.concatenate(rows, axis=0).T


def weight_grad_kernel(d, ff, idx, kept, got, *refs):
    results, (big_v, a_v, b_v, c_v, out_v, t_v, ins, outs) = refs[:5], refs[5:]
    rows = kept.shape[0] - t_v.shape[1]
    tokens = 2 * rows
    quarter, half, third = WIDE // 4, ff // 2, ff // 3
    blocks = third // WIDE
    share = d // 16
    cut = 3 * d
    y, z, core = idx[0], idx[1], idx[2]

    def load(cin, at, width, to, to_at):
        return [cin.start(src.at[pl.ds(0, rows), pl.ds(at, width)], to.at[i, :, pl.ds(to_at, width)]) for i, src in enumerate((kept, got))]

    def wait(copies):
        for copy in copies:
            copy.wait()

    def both(ref, at=0, width=d):
        return ref[:, :, at : at + width].reshape(tokens, width)

    def put(rows_at, cols_at, value):
        out_v[rows_at, cols_at] = value.astype(BF)

    def send_by_y(cout, at, width):
        cols = pl.ds(at, width)

        def rows_of(s, first, count):
            return out_v.at[pl.ds(pl.multiple_of(lax.rem(y + s, 4) * 4 * share + first, 16), count), cols]

        return [cout.start(rows_of(2, 0, 2 * share), results[3].at[:, cols]),
                cout.start(rows_of(2, 2 * share, 2 * share), results[4].at[:, cols])] + [
            cout.start(rows_of(s, 0, 4 * share), results[r].at[:, cols]) for r, s in ((1, 1), (2, 3), (0, 0))]

    def send_by_z(cout, at, width):
        cols = pl.ds(at, width)

        def rows_of(i, s):
            return out_v.at[pl.ds(pl.multiple_of((4 * i + lax.rem(z + s, 4)) * share, 16), share), cols]

        return [
            cout.start(rows_of(i, s), results[r].at[pl.ds(share * (i - base), share), cols])
            for r, s, base, count in ((3, 2, 0, 2), (4, 2, 2, 2), (1, 1, 0, 4), (2, 3, 0, 4), (0, 0, 0, 4))
            for i in range(base, base + count)
        ]

    everything = slice(0, d)

    @pl.when(core == 0)
    def _():
        cin, cout = Copies(ins), Copies(outs)
        grads = load(cin, ff, d, a_v, 0)
        loads = [load(cin, third * k, third, big_v, third * k) for k in range(3)]
        attended = load(cin, ff + 3 * d, d, b_v, 0)
        hidden, values = load(cin, ff + 2 * d, d, c_v, 0), load(cin, ff + d, d, c_v, d)
        smalls = [cin.start(src.at[pl.ds(rows, t_v.shape[1])], t_v.at[i]) for i, src in enumerate((kept, got))]
        wait(grads)
        gb = both(a_v)
        for k in range(3):
            wait(loads[k])
            found = lax.dot_general(both(big_v, third * k, third), gb, TN, preferred_element_type=F32).astype(BF)
            for b in range(blocks):
                at = quarter * (blocks * k + b)
                for j in range(4):
                    put(slice(at, at + quarter), slice(d * j, d * j + d), found[WIDE * b + quarter * j : WIDE * b + quarter * (j + 1)])
        pending = send_by_y(cout, 0, 4 * d)
        wait(attended)
        put(everything, slice(4 * d, 5 * d), lax.dot_general(both(b_v), gb, TN, preferred_element_type=F32))
        wait(hidden + values + smalls)
        put(everything, slice(5 * d, 6 * d), lax.dot_general(both(c_v), both(c_v, d), TN, preferred_element_type=F32))
        put(everything, slice(6 * d, 6 * d + LANES), split_small(small_table(d, ff, t_v)))
        wait(pending + send_by_y(cout, 4 * d, 2 * d + LANES))

    @pl.when(core == 1)
    def _():
        cin, cout = Copies(ins), Copies(outs)
        hidden = load(cin, ff + 2 * d, d, a_v, 0)
        loads = [load(cin, third * k, third, big_v, third * k) for k in range(2)]
        queries = load(cin, ff, d, b_v, 0)
        loads.append(load(cin, 2 * third, third, big_v, 2 * third))
        keys = load(cin, ff + d, d, c_v, 0)
        wait(hidden)
        turned = both(a_v).T
        pending = []
        for k in range(2):
            wait(loads[k])
            put(everything, slice(third * k, third * k + third), mm(turned, both(big_v, third * k, third)))
        pending = send_by_z(cout, 0, 2 * third)
        wait(queries)
        put(everything, slice(ff, ff + d), mm(turned, both(b_v)))
        wait(loads[2])
        put(everything, slice(2 * third, ff), mm(turned, both(big_v, 2 * third, third)))
        wait(keys)
        put(everything, slice(ff + d, ff + 2 * d), mm(turned, both(c_v)))
        out_v[:, 6 * d :] = jnp.zeros((d, LANES), BF)
        wait(pending + send_by_z(cout, 2 * third, 6 * d + LANES - 2 * third))


def added(parts):
    total = parts[0][...].astype(F32)
    for part in parts[1:]:
        total = total + part[...].astype(F32)
    shape = total.shape
    total = total.reshape(-1, shape[-1])
    main, last = total[:, : shape[-1] - LANES], split_small(joined_small(total[:, shape[-1] - LANES :]))
    return jnp.concatenate([main.astype(BF), last], axis=1).reshape(shape)


def relay_kernel(idx, up_in, down_in, up_got, down_got, up, down, hold, ins, outs):
    half = up_got.shape[0]
    cin, cout = Copies(ins), Copies(outs)
    parts = ((up_in, 0, up_got, up), (down_in, half, down_got, down))
    loads = [cin.start(block.at[pl.ds(at, half)], hold.at[i]) for i, (block, at, _, _) in enumerate(parts)]
    pending = []
    for i, (_, at, got, out) in enumerate(parts):
        loads[i].wait()
        hold[i] = added([hold.at[i], got])
        pending.append(cout.start(hold.at[i], out.at[pl.ds(at, half)]))
    for copy in pending:
        copy.wait()


def mid_kernel(idx, *refs):
    came, results, (in_v, out_v, ins, outs) = refs[:3], refs[3:7], refs[7:]
    share = results[0].shape[0]

    cin, cout = Copies(ins), Copies(outs)
    at = jnp.where(idx[2] == 0, idx[1], idx[0])
    order = [2, 1, 3, 0]
    blocks = [pl.multiple_of(lax.rem(at + s, 4) * share, 16) for s in order]
    loads = [[cin.start(part.at[pl.ds(block, share)], in_v.at[i, p]) for p, part in enumerate(came)]
             for i, block in enumerate(blocks)]
    pending = []
    for i, s in enumerate(order):
        for copy in loads[i]:
            copy.wait()
        out_v[i] = added([in_v.at[i, p] for p in range(3)])
        pending.append(cout.start(out_v.at[i], results[s]))
    for copy in pending:
        copy.wait()


def last_pair_kernel(idx, *refs):
    came, (home_mine, home_other, away_mine, away_other, in_v, hold, ins) = refs[:8], refs[8:]
    share = home_mine.shape[0]
    core, odd = idx[2], idx[4]

    sum_of(came, in_v, hold, ins)

    def rows_of(k, which):
        return hold[k, pl.ds(pl.multiple_of(which * share, 8), share), :]

    for which, home, away in ((core, home_mine, away_mine), (1 - core, home_other, away_other)):
        home[...] = jnp.where(odd == 1, rows_of(1, which), rows_of(0, which)).astype(home.dtype)
        away[...] = jnp.where(odd == 1, rows_of(0, which), rows_of(1, which)).astype(away.dtype)


def sum_of(came, in_v, hold, sems):
    copies = Copies(sems)
    loads = [copies.start(came[4 * k], in_v.at[k]) for k in range(len(came) // 4)]
    for k, load in enumerate(loads):
        load.wait()
        hold[k] = added([in_v.at[k]] + list(came[4 * k + 1 : 4 * k + 4])).astype(F32)


def place_kernel(idx, y_in, y_got, g_in, g_got, y_out, g_out, y_v, g_v, sems):
    copies = Copies(sems)
    pending = []
    for got, wide_v, out in ((y_got, y_v, y_out), (g_got, g_v, g_out)):
        wide_v[...] = got[...].astype(F32)
        pending.append(copies.start(wide_v, out.at[1 - idx[3]]))
    for copy in pending:
        copy.wait()


def picked(rows, columns, wanted):
    row = lax.broadcasted_iota(jnp.int32, (rows, columns), 0)
    column = lax.broadcasted_iota(jnp.int32, (rows, columns), 1)
    return row, column, jnp.where(column == wanted(row), 1.0, 0.0)


def prepare_kernel(d, ff, p_in, p_attn, p_down, n_gain, o_bias, u_bias, q_gain, k_gain, shuffle, out):
    share = p_in.shape[0]
    heads_part = p_in.shape[1] - ff
    for at in range(0, ff, WIDE):
        out[:, at : at + WIDE] = mm(p_in[:, heads_part + at : heads_part + at + WIDE], shuffle[...]).astype(BF)
    out[:, ff : ff + heads_part] = p_in[:, :heads_part]
    at = ff + heads_part
    out[:, at : at + d] = p_attn[...]
    down = p_down[...]
    for j in range(4):
        take = picked(share, down.shape[0], lambda row: 4 * row + j)[2].astype(BF)
        out[:, at + d * (j + 1) : at + d * (j + 2)] = mm(take, down).astype(BF)

    def column_of(ref, wanted, where):
        values = ref[...].astype(F32)
        take = picked(share, values.shape[1], wanted)[2]
        lane = lax.broadcasted_iota(jnp.int32, (share, LANES), 1)
        return jnp.where(lane == where, jnp.sum(take * values, axis=1, keepdims=True), 0.0)

    table = column_of(n_gain, lambda row: row, 0) + column_of(o_bias, lambda row: row, 1)
    for j in range(4):
        table = table + column_of(u_bias, lambda row: 4 * row + j, 2 + j)
    table = table + column_of(q_gain, lambda row: row, 6) + column_of(k_gain, lambda row: row, 7)
    out[:, at + 5 * d :] = table.astype(BF)


def smalls_kernel(d, ff, base, stride, g, place, out, t_v, sems):
    copies = Copies(sems)
    loads = [copies.start(g.at[:, pl.ds(base + stride * layer, LANES)], t_v.at[layer]) for layer in range(2)]
    quarter = WIDE // 4
    for layer in range(2):
        loads[layer].wait()
        table = t_v[layer].astype(F32).T
        pieces = [table[2 + j : 3 + j, quarter * b : quarter * (b + 1)] for b in range(ff // WIDE) for j in range(4)]
        both = mm(table[0:8].astype(BF), place[...])
        first = jnp.concatenate([table[0:1], table[1:2], both[6:7], both[7:8]], axis=1)
        out[layer] = jnp.concatenate([first, jnp.concatenate(pieces, axis=1), jnp.zeros((6, ff), F32)], axis=0)


def in_parts(x):
    top = x.astype(BF)
    rest = x - top.astype(F32)
    middle = rest.astype(BF)
    return top, middle, (rest - middle.astype(F32)).astype(BF)


def finish_kernel(d, ff, idx, own, a_in, b_in, c_in, shuffle, g_in, g_attn, g_down, g_ng, g_q, g_k, g_ub, g_ob):
    core = idx[2]
    share = own.shape[0]
    mine = own[...] + a_in[...].astype(F32)
    theirs = b_in[...].astype(F32) + c_in[...].astype(F32)
    half0 = jnp.where(core == 0, mine, theirs)
    half1 = jnp.where(core == 0, theirs, mine)
    g_in[:, : 2 * d] = half1[:, ff : ff + 2 * d]
    g_in[:, 2 * d : 3 * d] = half0[:, 5 * d : 6 * d]
    for at in range(0, ff, WIDE):
        g_in[:, 3 * d + at : 3 * d + at + WIDE] = sum(mm(part, shuffle[...], NT) for part in in_parts(half1[:, at : at + WIDE]))
    g_attn[...] = half0[:, 4 * d : 5 * d]
    stacked = jnp.concatenate([half0[:, at : at + d] for at in range(0, 4 * d, d)], axis=0)
    row, column, _ = picked(4 * share, 4 * share, lambda row: row)
    turn = jnp.where(column == lax.rem(row, 4) * share + row // 4, 1.0, 0.0).astype(BF)
    g_down[...] = sum(mm(turn, part) for part in in_parts(stacked))
    small = joined_small(half0[:, 6 * d :])
    turned = jnp.concatenate([small, jnp.zeros((LANES - share, LANES), F32)], axis=0).T
    g_ng[...] = turned[0:1, :share]
    g_ob[...] = turned[1:2, :share]
    g_q[...] = turned[6:7, : g_q.shape[1]]
    g_k[...] = turned[7:8, : g_k.shape[1]]
    total = jnp.zeros((8, 4 * share), F32)
    for j in range(4):
        row, column, _ = picked(LANES, 4 * share, lambda row: row)
        spread_out = jnp.where(column == 4 * row + j, 1.0, 0.0)
        total = total + jnp.where(lax.broadcasted_iota(jnp.int32, (8, 4 * share), 0) == 2 + j, 1.0, 0.0) * lax.dot_general(
            turned[0:8], spread_out, NN, precision=lax.Precision.HIGHEST, preferred_element_type=F32)
    g_ub[...] = jnp.sum(total, axis=0, keepdims=True)


ANY = pl.BlockSpec(memory_space=pl.ANY)
HERE = pl.BlockSpec(memory_space=pltpu.VMEM)


def whole(shape):
    return pl.BlockSpec(shape, lambda i, idx: (0,) * len(shape))


def pick(shape):
    return pl.BlockSpec((1,) + shape, lambda i, idx: (idx[2],) + (0,) * len(shape))


def call(kernel, idx, ins, fresh, stashes, scratch, flops):
    outs = pl.pallas_call(
        kernel,
        grid_spec=pltpu.PrefetchScalarGridSpec(
            num_scalar_prefetch=1,
            grid=(1,),
            in_specs=[s for _, s in ins] + [ANY] * len(stashes),
            out_specs=[ANY] * (1 + len(stashes)),
            scratch_shapes=scratch,
        ),
        out_shape=[jax.ShapeDtypeStruct(*fresh)] + [jax.ShapeDtypeStruct(a.shape, a.dtype) for a in stashes],
        input_output_aliases={1 + len(ins) + i: 1 + i for i in range(len(stashes))},
        compiler_params=pltpu.CompilerParams(dimension_semantics=("arbitrary",), vmem_limit_bytes=VMEM_LIMIT),
        cost_estimate=pl.CostEstimate(flops=flops, bytes_accessed=1 << 10, transcendentals=0),
    )(idx, *[a for a, _ in ins], *stashes)
    return outs[0], list(outs[1:])


def plain(kernel, arrays, specs, out_shapes, out_specs, scratch):
    return pl.pallas_call(
        kernel, grid=(1,), in_specs=specs, out_specs=out_specs, scratch_shapes=scratch, out_shape=out_shapes,
        compiler_params=pltpu.CompilerParams(dimension_semantics=("arbitrary",), vmem_limit_bytes=VMEM_LIMIT),
        cost_estimate=pl.CostEstimate(flops=1 << 10, bytes_accessed=1 << 10, transcendentals=0),
    )(*arrays)


def simple(kernel, idx, arrays, specs, out_shapes, out_specs, scratch, limit=VMEM_LIMIT):
    return pl.pallas_call(
        kernel,
        grid_spec=pltpu.PrefetchScalarGridSpec(
            num_scalar_prefetch=1, grid=(1,), in_specs=specs, out_specs=out_specs, scratch_shapes=scratch
        ),
        out_shape=out_shapes,
        compiler_params=pltpu.CompilerParams(dimension_semantics=("arbitrary",), vmem_limit_bytes=limit),
        cost_estimate=pl.CostEstimate(flops=1 << 10, bytes_accessed=1 << 10, transcendentals=0),
    )(idx, *arrays)


def along(x, step, size, by):
    devices = lax.axis_size("dp")

    def to(i):
        digit = i // step % size
        return i + ((digit + by) % size - digit) * step

    return lax.ppermute(x, "dp", [(i, to(i)) for i in range(devices)])


def paired(x):
    return lax.ppermute(x, "section", [(0, 1), (1, 0), (2, 3), (3, 2)])


def body(tokens, cotangent, lengths, proj_in, proj_attn, proj_down, norm_gain, query_gain, key_gain, up_bias, out_bias):
    ranks = lax.axis_size("dp")
    section = lax.axis_index("section")
    rank = lax.axis_index("dp")
    slots = lengths.shape[0]
    rows = tokens.shape[0] // slots
    d = tokens.shape[1]
    joined = proj_in.shape[2]
    ff = proj_down.shape[1] * ranks
    head = query_gain.shape[1] * ranks
    heads = d // head
    dshare = proj_in.shape[1]
    fshare = proj_down.shape[1] // dshare
    hshare = query_gain.shape[1]
    chunks = 3
    wide = joined + d + ff
    stride = wide + LANES
    side = math.isqrt(ranks // 2)
    core, z, y = lax.rem(rank, 2), lax.rem(rank // 2, side), rank // (2 * side)
    stage, odd = section // 2, lax.rem(section, 2)
    slot = lax.rem(stage + odd, 2)

    place = jnp.arange(WIDE, dtype=jnp.int32)
    source = (place % (WIDE // fshare)) * fshare + place // (WIDE // fshare)
    shuffle = (place[:, None] == source[None, :]).astype(BF)

    def full(a):
        return pl.BlockSpec(a.shape, lambda i: (0,) * a.ndim)

    shares = [proj_in[0], proj_attn[0], proj_down[0], norm_gain, out_bias, up_bias, query_gain, key_gain, shuffle]
    heads_part = joined - ff
    local = jax.ShapeDtypeStruct((dshare, stride), BF)
    local = plain(partial(prepare_kernel, d, ff), shares, [full(a) for a in shares], local, full(local), [])
    other = paired(local)
    g = lax.all_gather(jnp.concatenate([local, other], axis=1), "dp", axis=0).reshape(d, 2 * stride)
    toks = tokens.reshape(slots, rows, d)
    seeds = cotangent.reshape(slots, rows, d)
    ends = jnp.cumsum(lengths, axis=-1)
    position = jnp.arange(rows, dtype=jnp.int32)
    image = jnp.sum((position[None, :, None] >= ends[:, None, :]).astype(jnp.int32), axis=-1)
    image = jnp.where(position[None, :] < ends[:, 2:3], image, ABSENT + position[None, :])
    ids = image[:, None, :].astype(F32)

    def index_of(layer, active_stage):
        return jnp.stack([stage == active_stage, core, slot, odd == layer]).astype(jnp.int32)

    indices = [[index_of(layer, active) for active in range(2)] for layer in range(2)]
    here = jnp.stack([y, z, core, slot, odd]).astype(jnp.int32)
    element = jnp.arange(d, dtype=jnp.int32) % head
    spread_gain = (jnp.arange(d, dtype=jnp.int32)[:, None] == (element // hshare * dshare + element % hshare)[None, :]).astype(BF)
    g, indices, here, ids, spread_gain = lax.optimization_barrier((g, indices, here, ids, spread_gain))
    small = jax.ShapeDtypeStruct((2, 8, ff), F32)
    smalls = plain(
        partial(smalls_kernel, d, ff, wide, stride), [g, spread_gain], [ANY, full(spread_gain)], small, full(small),
        [pltpu.VMEM((2, d, LANES), BF), pltpu.SemaphoreType.DMA((2,))],
    )
    g3 = g.reshape(ff // WIDE, WIDE // fshare, g.shape[1])
    def stash(*shape, dtype=BF):
        return pl.pallas_call(
            lambda out: None, out_shape=jax.ShapeDtypeStruct(shape, dtype), out_specs=pl.BlockSpec(memory_space=pl.ANY)
        )()

    fc = ff // chunks
    groups = ff // WIDE

    V = pltpu.VMEM
    weights_v = [V((d, heads_part), BF), V((chunks, d, fc), BF), V((groups, fshare, WIDE // fshare, d), BF), V((d, d), BF)]
    sems = [pltpu.SemaphoreType.DMA((48,)), pltpu.SemaphoreType.DMA((48,))]
    stacked = ff + 4 * d
    operands = [[stash(rows + 16, stacked), stash(rows + 16, stacked)] for _ in range(2)]
    kept = [[stash(rows, d) for _ in range(4)] + [stash(rows, 2 * d), stash(rows, 2 * d), stash(chunks, rows, fc),
             stash(heads, rows, rows), stash(16, rows, dtype=F32)] for _ in range(2)]
    results = [stash(slots, rows, d, dtype=F32), stash(rows, d)]
    here_x = toks
    for t in range(4):
        layer = t % 2
        ybf, done = call(
            partial(forward_kernel, d, ff, chunks, stride, (FIRST, LOCAL, ARRIVED, LOCAL)[t]),
            indices[layer][t // 2],
            [(here_x, HERE if t == 2 else ANY)] + [(a, ANY) for a in (g, g3, ids, smalls)],
            ((rows, d), BF),
            kept[layer][:9] + operands[layer] + results,
            [V((rows, d), BF), V((rows, d), BF)] + weights_v
            + [V((rows, d), BF)] * 3 + [V((rows, 2 * d), BF)] * 2 + [V((chunks, rows, fc), BF)] * 2
            + [V((heads, rows, rows), BF), V((16, rows), F32), V((rows, d), BF), V((rows, d), F32), V((rows, d), F32), V((rows, d), BF), V((1, rows), F32), V((8, ff), F32)]
            + sems,
            1 << 10,
        )
        kept[layer], operands[layer], results = done[:9], done[9:11], done[11:]
        here_x = lax.ppermute(ybf, "section", [(0, 3), (1, 2)]) if t == 1 else ybf
    y_out, y_send = results
    y_got = paired(y_send)

    results = [stash(slots, rows, d, dtype=F32), stash(rows, d)]
    width = 6 * d + LANES
    share = 2 * dshare

    def moved(x, leg, by):
        def to(i):
            step = 2 * side if i % 2 == leg else 2
            digit = i // step % side
            return i + ((digit + by) % side - digit) * step

        return lax.ppermute(x, "dp", [(i, to(i)) for i in range(ranks)])

    def grads_by_place(layer, got):
        return simple(
            partial(weight_grad_kernel, d, ff), here,
            [operands[layer][0], got], [ANY] * 2,
            [jax.ShapeDtypeStruct((side * share, width), BF)] * 3 + [jax.ShapeDtypeStruct((side // 2 * share, width), BF)] * 2,
            [ANY] * 5,
            [V((2, rows, ff), BF), V((2, rows, d), BF), V((2, rows, d), BF), V((2, rows, 2 * d), BF), V((d, width), BF), V((2, 16, stacked), BF),
             pltpu.SemaphoreType.DMA((32,)), pltpu.SemaphoreType.DMA((32,))],
        )

    def halves(made):
        return moved(made[3], 0, 1), moved(made[4], 0, -1)

    def first_leg(made, came):
        own, up, down = made[:3]
        part = (side // 2 * share, width)
        up, down = pl.pallas_call(
            relay_kernel,
            grid_spec=pltpu.PrefetchScalarGridSpec(
                num_scalar_prefetch=1, grid=(1,), in_specs=[ANY, ANY, HERE, HERE], out_specs=[ANY] * 2,
                scratch_shapes=[V((2,) + part, BF), pltpu.SemaphoreType.DMA((2,)), pltpu.SemaphoreType.DMA((2,))],
            ),
            out_shape=[jax.ShapeDtypeStruct(up.shape, BF)] * 2,
            input_output_aliases={1: 0, 2: 1},
            compiler_params=pltpu.CompilerParams(dimension_semantics=("arbitrary",), vmem_limit_bytes=SMALL_LIMIT),
            cost_estimate=pl.CostEstimate(flops=1 << 10, bytes_accessed=1 << 10, transcendentals=0),
        )(here, up, down, *came)
        return [own, moved(up, 0, 1), moved(down, 0, -1)]

    def second_leg(outs):
        far, near, back = (moved(outs[s], 1, s) for s in (2, 1, 3))
        return [outs[0], near, far, back]

    def by_second_axis(came):
        return simple(
            mid_kernel, here, came, [ANY] * 3, [jax.ShapeDtypeStruct((share, width), BF)] * side, [ANY] * side,
            [V((side, 3, share, width), BF), V((side, share, width), BF), pltpu.SemaphoreType.DMA((12,)), pltpu.SemaphoreType.DMA((4,))],
        )

    here_g = seeds
    swaps = []
    for t in range(4):
        layer = 1 - t % 2
        gbf, done = call(
            partial(backward_kernel, d, ff, chunks, stride, (FIRST, LOCAL, ARRIVED, LOCAL)[t]),
            indices[layer][1 - t // 2],
            [(here_g, HERE if t == 2 else ANY)] + [(a, ANY) for a in [g, g3, ids, smalls] + kept[layer]],
            ((rows, d), BF),
            operands[layer] + results,
            [V((rows, d), BF), V((rows, d), BF)] + weights_v
            + [V((rows, d), BF)] * 4 + [V((rows, 2 * d), BF)] * 2
            + [V((chunks, rows, fc), BF), V((heads, rows, rows), BF), V((16, rows), F32)]
            + [V((d, rows), BF), V((d, rows), F32), V((rows, d), F32)]
            + [V((rows, d), BF)] * 3 + [V((chunks, rows, fc), BF), V((rows, d), F32), V((rows, d), F32), V((rows, d), BF), V((1, stacked), F32), V((16, stacked), BF), V((1, rows), F32), V((8, ff), F32)]
            + sems,
            1 << 10,
        )
        operands[layer], results = done[:2], done[2:]
        here_g = lax.ppermute(gbf, "section", [(3, 0), (2, 1)]) if t == 1 else gbf
        if t == 1:
            here_g, y_got = lax.optimization_barrier((here_g, y_got))
        if t == 3:
            operands[layer][1], swaps[0] = lax.optimization_barrier((operands[layer][1], swaps[0]))
        if t >= 2:
            swaps.append(along(operands[layer][1], 1, 2, 1))
    gr_got = paired(results[1])
    upper, gr_got = lax.optimization_barrier((grads_by_place(1, swaps[0]), gr_got))
    upper_came = halves(upper)
    lower = grads_by_place(0, swaps[1])
    lower_came = halves(lower)
    legs = [first_leg(upper, upper_came), first_leg(lower, lower_came)]
    arrived = [second_leg(by_second_axis(came)) for came in legs]
    gr_out = results[0]
    y_out, gr_out = pl.pallas_call(
        place_kernel,
        grid_spec=pltpu.PrefetchScalarGridSpec(
            num_scalar_prefetch=1, grid=(1,), in_specs=[ANY, whole((rows, d)), ANY, whole((rows, d))], out_specs=[ANY] * 2,
            scratch_shapes=[V((rows, d), F32), V((rows, d), F32), pltpu.SemaphoreType.DMA((2,))],
        ),
        out_shape=[jax.ShapeDtypeStruct(y_out.shape, F32)] * 2,
        input_output_aliases={1: 0, 3: 1},
    )(here, y_out, y_got, gr_out, gr_got)

    both = arrived[1] + arrived[0]
    home_mine, home_other, away_mine, away_other = simple(
        last_pair_kernel, here, both, [ANY, HERE, HERE, HERE] * 2,
        [jax.ShapeDtypeStruct((dshare, width), t) for t in (F32, BF, BF, BF)], [whole((dshare, width))] * 4,
        [V((2, share, width), BF), V((2, share, width), F32), pltpu.SemaphoreType.DMA((2,))], SMALL_LIMIT,
    )
    sections = lax.axis_size("section")
    cross = [(s * ranks + i, (s ^ 1) * ranks + (i ^ 1)) for s in range(sections) for i in range(ranks)]
    arrays = [home_mine, paired(away_mine), along(home_other, 1, 2, 1), lax.ppermute(away_other, ("section", "dp"), cross),
              shuffle]
    shapes = [(dshare, joined), (dshare, d), (dshare * fshare, d), (1, dshare), (1, hshare), (1, hshare), (1, dshare * fshare),
              (1, dshare)]
    g_in, g_attn, g_down, g_ng, g_q, g_k, g_ub, g_ob = simple(
        partial(finish_kernel, d, ff), here, arrays, [whole(a.shape) for a in arrays],
        [jax.ShapeDtypeStruct(s, F32) for s in shapes], [whole(s) for s in shapes], [],
    )
    return (y_out.reshape(1, slots * rows, d), gr_out.reshape(1, slots * rows, d), g_in[None], g_attn[None], g_down[None],
            g_ng, g_q, g_k, g_ub, g_ob)


def solution(mesh):
    in_specs = (P("dp", None),) * 3 + (P("section", "dp", None),) * 3 + (P("section", "dp"),) * 5
    out_specs = (P("section", "dp", None),) * 5 + (P("section", "dp"),) * 5
    return jax.shard_map(body, mesh=mesh, in_specs=in_specs, out_specs=out_specs, check_vma=False)
```

```python
from functools import partial
import math

import jax
import jax.numpy as jnp
from jax import lax
from jax.experimental import pallas as pl
from jax.experimental.pallas import tpu as pltpu
from jax.sharding import PartitionSpec as P

BF = jnp.bfloat16
F32 = jnp.float32
VMEM_LIMIT = 56 * 1024 * 1024
SMALL_LIMIT = 30 * 1024 * 1024
EPS = 1e-06
NN = (((1,), (0,)), ((), ()))
NT = (((1,), (1,)), ((), ()))
TN = (((0,), (0,)), ((), ()))
LANES = 128
WIDE = 256
ABSENT = 16
FIRST, LOCAL, ARRIVED = range(3)


def mm(a, b, dims=NN):
    return lax.dot_general(a, b, dims, preferred_element_type=F32)


def head_mean(x, spread, exact):
    parts = []
    for at in range(0, x.shape[1], WIDE):
        piece = x[:, at : at + WIDE]
        top = piece.astype(BF)
        total = mm(top, spread)
        if exact:
            total = total + mm((piece - top.astype(F32)).astype(BF), spread)
        parts.append(total)
    return jnp.concatenate(parts, axis=1)


def row_norm(x):
    centered = x - jnp.mean(x, axis=-1, keepdims=True)
    rstd = lax.rsqrt(jnp.mean(centered * centered, axis=-1, keepdims=True) + EPS)
    return centered * rstd, rstd


def norm_back(grad, normal, rstd, spread):
    return rstd * (grad - head_mean(grad, spread, False) - normal * head_mean(grad * normal, spread, False))


def lane_half(x, second):
    lane = lax.broadcasted_iota(jnp.int32, x.shape, 1)
    return jnp.where((lane >= LANES // 2) if second else (lane < LANES // 2), x, jnp.zeros_like(x))


class Copies:
    def __init__(self, sems):
        self.sems, self.used = sems, 0

    def start(self, src, dst):
        copy = pltpu.make_async_copy(src, dst, self.sems.at[self.used])
        self.used += 1
        copy.start()
        return copy

    def either(self, flag, src, yes, no):
        sem = self.sems.at[self.used]
        self.used += 1

        @pl.when(flag == 1)
        def _():
            pltpu.make_async_copy(src, yes, sem).start()

        @pl.when(flag != 1)
        def _():
            pltpu.make_async_copy(src, no, sem).start()

        return pltpu.make_async_copy(src, yes, sem)


def result_out(home, value, result, rounded, send, copies):
    sem = copies.sems.at[copies.used]
    copies.used += 1

    @pl.when(home == 1)
    def _():
        copy = pltpu.make_async_copy(value, result, sem)
        copy.start()
        copy.wait()

    @pl.when(home != 1)
    def _():
        copy = pltpu.make_async_copy(rounded, send, sem)
        copy.start()
        copy.wait()


def forward_kernel(d, ff, chunks, stride, kind, idx, *refs):
    @pl.when(idx[0] == 1)
    def _():
        forward_work(d, ff, chunks, stride, kind, idx, *refs)


def head_spread(head):
    row = lax.broadcasted_iota(jnp.int32, (WIDE, WIDE), 0) // head
    column = lax.broadcasted_iota(jnp.int32, (WIDE, WIDE), 1) // head
    return jnp.where(row == column, 1.0 / head, 0.0).astype(BF)


def as_column(row):
    return jnp.broadcast_to(row, (LANES, row.shape[1])).T[:, :1]


def forward_work(d, ff, chunks, stride, kind, idx, x_in, g, g3, ids, smalls, *refs):
    refs = refs[13:]
    ybf, xs, qs, ks, vs, ns, nrs, gps, es, small, kept, sent, y_out, y_send = refs[:14]
    (x_v, h_v, w_v, u_v, d_v, a_v, q_v, k_v, v_v, n_v, r_v, act_v, gp_v, e_v, rs_v, att_v, acc_v, y_v, yb_v, id_v, sm_v, ins, outs) = refs[14:]
    rows = x_v.shape[0]
    body_rows = pl.ds(0, rows)
    fc = ff // chunks
    core, slot, home = idx[1], idx[2], idx[3]
    base = jnp.where(home == 1, 0, stride)

    def columns(at, width):
        return pl.ds(pl.multiple_of(base + at, LANES), width)

    cin, cout = Copies(ins), Copies(outs)
    x_copy = None if kind == ARRIVED else cin.start(x_in.at[slot] if kind == FIRST else x_in, x_v)
    small_copies = [cin.start(ids.at[slot], id_v), cin.start(smalls.at[1 - home], sm_v)]
    wq = [cin.start(g.at[:, columns(ff + d * i, d)], w_v.at[:, pl.ds(d * i, d)]) for i in range(3)]
    groups = fc // WIDE
    wff = []
    for c in range(chunks):
        wff.append([cin.start(g.at[:, columns(fc * c, fc)], u_v.at[c])] + [
            cin.start(g3.at[pl.ds(groups * c, groups), :, columns(ff + 4 * d + d * j, d)], d_v.at[pl.ds(groups * c, groups), j])
            for j in range(4)
        ])
    wa = cin.start(g.at[:, columns(ff + 3 * d, d)], a_v)

    pending = []

    def side(i):
        return pl.ds(ff + d * i, d)

    spread = head_spread(64)
    for copy in small_copies:
        copy.wait()
    ids_row = id_v[...]
    ids_col = as_column(ids_row)
    keep = jnp.where(ids_col < ABSENT, 1.0, 0.0)
    if kind == ARRIVED:
        x_v[...] = x_in[...]
    else:
        x_copy.wait()
    masked = keep * x_v[...].astype(F32)
    h_v[...] = (row_norm(masked)[0] * sm_v[0:1, :d]).astype(BF)
    pending += [cout.start(x_v, xs), cout.start(h_v, kept.at[body_rows, side(2)]), cout.start(h_v, sent.at[body_rows, side(2)])]
    bias_mask = jnp.where(ids_col == ids_row, 0.0, -1e9)
    for i in range(3):
        wq[i].wait()
        raw = mm(h_v[...], w_v[:, d * i : d * i + d])
        if i == 2:
            v_v[...] = raw.astype(BF)
            pending.append(cout.start(v_v, vs))
        else:
            centered = raw - head_mean(raw, spread, True)
            rstd = lax.rsqrt(head_mean(centered * centered, spread, True) + EPS)
            normal = centered * rstd
            scaled = (normal * sm_v[0:1, d * (2 + i) : d * (3 + i)]).astype(BF)
            n_v[:, d * i : d * i + d] = normal.astype(BF)
            r_v[:, d * i : d * i + d] = rstd.astype(BF)
            if i == 0:
                q_v[...] = scaled * jnp.asarray(0.125, BF)
                pending.append(cout.start(q_v, qs))
            else:
                k_v[...] = scaled
                pending.append(cout.start(k_v, ks))
    pending += [cout.start(n_v, ns), cout.start(r_v, nrs)]
    ones = jnp.ones((16, rows), BF)
    pairs = d // LANES // chunks
    for c in range(chunks):
        for copy in wff[c]:
            copy.wait()
        pre = mm(h_v[...], u_v[c]) + sm_v[1:2, fc * c : fc * c + fc]
        cdf = 0.5 * (1.0 + lax.erf(pre * (1.0 / math.sqrt(2.0))))
        density = jnp.exp(-0.5 * pre * pre) * (1.0 / math.sqrt(2.0 * math.pi))
        act = (pre * cdf).astype(BF)
        act_v[c] = act
        gp_v[c] = (cdf + pre * density).astype(BF)
        total = mm(act, d_v[groups * c : groups * c + groups].reshape(fc, d))
        if c == 0:
            acc_v[...] = total
        else:
            acc_v[...] += total
        for p in range(pairs * c, pairs * c + pairs):
            cols = slice(LANES * p, LANES * p + LANES)
            vals_t = v_v[:, cols].T
            pair = q_v[:, cols]
            both = []
            for half in range(2):
                h = 2 * p + half
                e = jnp.exp(mm(k_v[:, cols], lane_half(pair, half), NT) + bias_mask).astype(BF)
                e_v[h] = e
                got = mm(jnp.concatenate([vals_t[64 * half : 64 * half + 64], ones], axis=0), e)
                inv = 1.0 / got[64:65]
                rs_v[h : h + 1, :] = inv
                both.append((got[:64] * inv).astype(BF))
            att_v[:, cols] = jnp.concatenate(both, axis=0).T
        span = pl.ds(fc * c, fc)
        pending += [cout.either(core, act_v.at[c], sent.at[body_rows, span], kept.at[body_rows, span]), cout.start(gp_v.at[c], gps.at[c]),
                    cout.start(e_v.at[pl.ds(2 * pairs * c, 2 * pairs)], es.at[pl.ds(2 * pairs * c, 2 * pairs)])]
    pending += [cout.start(rs_v, small), cout.either(core, att_v, sent.at[body_rows, side(3)], kept.at[body_rows, side(3)])]
    wa.wait()
    y = keep * (keep * x_v[...].astype(F32) + acc_v[...] + mm(att_v[...], a_v[...]) + sm_v[0:1, d : 2 * d])
    y_v[...] = y
    yb_v[...] = y.astype(BF)
    pending.append(cout.start(yb_v, ybf))
    result_out(home, y_v, y_out.at[slot], yb_v, y_send, cout)
    for copy in pending:
        copy.wait()


def backward_kernel(d, ff, chunks, stride, kind, idx, *refs):
    @pl.when(idx[0] == 1)
    def _():
        backward_work(d, ff, chunks, stride, kind, idx, *refs)


def backward_work(d, ff, chunks, stride, kind, idx, g_in, g, g3, ids, smalls, *refs):
    xs, qs, ks, vs, ns, nrs, gps, es, small = refs[:9]
    refs = refs[9 + 4 :]
    gbf, kept, sent, gr_out, gr_send = refs[:5]
    (g_v, gb_v, w_v, u_v, d_v, a_v, x_v, q_v, k_v, v_v, n_v, r_v, gp_v, e_v, rs_v, gat_v, gqt_v, gk_v,
     gq_b, gk_b, gv_b, gj_v, acc_v, out_v, ob_v, sm_v, sp_v, id_v, gain_v, ins, outs) = refs[5:]
    rows = x_v.shape[0]
    body_rows = pl.ds(0, rows)
    fc = ff // chunks
    groups = fc // WIDE
    core, slot, home = idx[1], idx[2], idx[3]
    base = jnp.where(home == 1, 0, stride)

    def columns(at, width):
        return pl.ds(pl.multiple_of(base + at, LANES), width)

    cin, cout = Copies(ins), Copies(outs)
    g_copy = None if kind == ARRIVED else cin.start(g_in.at[slot] if kind == FIRST else g_in, g_v)
    small_copies = [cin.start(ids.at[slot], id_v), cin.start(smalls.at[1 - home], gain_v)]
    wa = cin.start(g.at[:, columns(ff + 3 * d, d)], a_v)
    heads = [cin.start(s, v) for s, v in ((small, rs_v), (ks, k_v), (vs, v_v), (qs, q_v))]
    pairs = d // LANES // chunks
    wff = []
    for c in range(chunks):
        wff.append(
            [cin.start(g3.at[pl.ds(groups * c, groups), :, columns(ff + 4 * d + d * j, d)], d_v.at[pl.ds(groups * c, groups), j])
             for j in range(4)]
            + [cin.start(gps.at[c], gp_v.at[c]), cin.start(g.at[:, columns(fc * c, fc)], u_v.at[c]),
               cin.start(es.at[pl.ds(2 * pairs * c, 2 * pairs)], e_v.at[pl.ds(2 * pairs * c, 2 * pairs)])]
        )
    norms = [cin.start(ns, n_v), cin.start(nrs, r_v)]
    wq = [cin.start(g.at[:, columns(ff + d * i, d)], w_v.at[:, pl.ds(d * i, d)]) for i in range(3)]
    rows_in = cin.start(xs, x_v)

    pending = []

    def side(i):
        return pl.ds(ff + d * i, d)

    def summed(at, value):
        sm_v[:, at : at + value.shape[1]] = jnp.sum(value, axis=0, keepdims=True)

    spread = head_spread(64)
    for copy in small_copies:
        copy.wait()
    keep = jnp.where(as_column(id_v[...]) < ABSENT, 1.0, 0.0)
    if kind == ARRIVED:
        g_v[...] = g_in[...]
    else:
        g_copy.wait()
    gres = keep * g_v[...].astype(F32)
    summed(d, gres)
    gb_v[...] = gres.astype(BF)
    pending.append(cout.either(core, gb_v, sent.at[body_rows, side(0)], kept.at[body_rows, side(0)]))
    wa.wait()
    gat_v[...] = mm(a_v[...], gb_v[...], NT).astype(BF)
    for copy in heads:
        copy.wait()
    zeros = jnp.zeros((LANES // 2, rows), BF)
    for c in range(chunks):
        for copy in wff[c]:
            copy.wait()
        gup = mm(gb_v[...], d_v[groups * c : groups * c + groups].reshape(fc, d), NT) * gp_v[c].astype(F32)
        summed(4 * d + fc * c, gup)
        gup = gup.astype(BF)
        gj_v[c] = gup
        span = pl.ds(fc * c, fc)
        pending.append(cout.either(core, gj_v.at[c], kept.at[body_rows, span], sent.at[body_rows, span]))
        total = mm(gup, u_v[c], NT)
        if c == 0:
            acc_v[...] = total
        else:
            acc_v[...] += total
        for p in range(pairs * c, pairs * c + pairs):
            cols = slice(LANES * p, LANES * p + LANES)
            keys, vals, pair = k_v[:, cols], v_v[:, cols], q_v[:, cols]
            keys_t = keys.T
            gk, gv = None, None
            for half in range(2):
                h = 2 * p + half
                at_rows = slice(64 * h, 64 * h + 64)
                inv = rs_v[h : h + 1, :]
                ga = (gat_v[at_rows, :].astype(F32) * inv).astype(BF)
                ga = jnp.concatenate([zeros, ga] if half else [ga, zeros], axis=0)
                e = e_v[h]
                ef = e.astype(F32)
                gp = ef * mm(vals, ga)
                dot = jnp.sum(gp, axis=0, keepdims=True) * inv
                gs = (gp - ef * dot).astype(BF)
                gk_h = mm(gs, lane_half(pair, half))
                gv_h = mm(e, ga, NT)
                gk = gk_h if gk is None else gk + gk_h
                gv = gv_h if gv is None else gv + gv_h
                gqt_v[at_rows, :] = mm(keys_t[64 * half : 64 * half + 64], gs) * 0.125
            gk_v[:, cols] = gk
            gv_b[:, cols] = gv.astype(BF)
    pending.append(cout.either(core, gv_b, sent.at[body_rows, side(1)], kept.at[body_rows, side(1)]))
    for copy in norms:
        copy.wait()
    for i, (grad, out) in enumerate(((gqt_v[...].T, gq_b), (gk_v[...], gk_b))):
        normal = n_v[:, d * i : d * i + d].astype(F32)
        summed(2 * d + d * i, grad * normal)
        gain = gain_v[0:1, d * (2 + i) : d * (3 + i)]
        out[...] = norm_back(grad * gain, normal, r_v[:, d * i : d * i + d].astype(F32), spread).astype(BF)
        pending.append(cout.either(core, out, kept.at[body_rows, side(i)], sent.at[body_rows, side(i)]))
    for copy in wq:
        copy.wait()
    ghid = acc_v[...]
    for i, part in enumerate((gq_b, gk_b, gv_b)):
        ghid = ghid + mm(part[...], w_v[:, d * i : d * i + d], NT)
    rows_in.wait()
    xhat, rstd = row_norm(keep * x_v[...].astype(F32))
    summed(0, ghid * xhat)
    top = sm_v[...].astype(BF).astype(F32)
    sp_v[...] = jnp.concatenate([top, sm_v[...] - top, jnp.zeros((14, top.shape[1]), F32)], axis=0).astype(BF)
    tail = pl.ds(rows, 16)
    pending += [cout.start(sp_v, kept.at[tail]), cout.start(sp_v, sent.at[tail])]
    gx = ghid * gain_v[0:1, :d]
    gmask = rstd * (gx - jnp.mean(gx, axis=-1, keepdims=True) - xhat * jnp.mean(gx * xhat, axis=-1, keepdims=True))
    out = keep * (keep * g_v[...].astype(F32) + gmask)
    out_v[...] = out
    ob_v[...] = out.astype(BF)
    pending.append(cout.start(ob_v, gbf))
    result_out(home, out_v, gr_out.at[slot], ob_v, gr_send, cout)
    for copy in pending:
        copy.wait()


def split_small(values):
    top = values.astype(BF).astype(F32)
    lane = lax.broadcasted_iota(jnp.int32, values.shape, 1)
    return jnp.where(lane < 8, top, jnp.where(lane < 16, pltpu.roll(values - top, 8, 1), 0.0)).astype(BF)


def joined_small(parts):
    return parts + pltpu.roll(parts, LANES - 8, 1)


def small_table(d, ff, tables):
    total = jnp.zeros((1, tables.shape[2]), F32)
    for i in range(tables.shape[0]):
        parts = tables[i].astype(F32)
        total = total + parts[0:1] + parts[1:2]
    lane = lax.broadcasted_iota(jnp.int32, (LANES, d), 0) % 64
    place = jnp.where(lax.broadcasted_iota(jnp.int32, (LANES, d), 1) == lane // 2 * 24 + lane % 2, 1.0, 0.0)
    quarter = WIDE // 4
    ub = total[:, 4 * d :]
    up_rows = []
    for j in range(4):
        pieces = [ub[:, WIDE * b + quarter * j : WIDE * b + quarter * (j + 1)] for b in range(ff // WIDE)]
        up_rows.append(jnp.concatenate(pieces, axis=1))
    head_rows = []
    for i in range(2, 4):
        lanes = total[:, d * i : d * i + LANES]
        for p in range(1, d // LANES):
            lanes = lanes + total[:, d * i + LANES * p : d * i + LANES * (p + 1)]
        head_rows.append(lanes)
    both = jnp.concatenate(head_rows + [jnp.zeros((6, LANES), F32)], axis=0)
    placed = lax.dot_general(both, place, NN, precision=lax.Precision.HIGHEST, preferred_element_type=F32)
    rows = [total[:, :d], total[:, d : 2 * d]] + up_rows + [placed[0:1], placed[1:2], jnp.zeros((LANES - 8, d), F32)]
    return jnp.concatenate(rows, axis=0).T


def weight_grad_kernel(d, ff, idx, kept, got, *refs):
    results, (big_v, a_v, b_v, c_v, out_v, t_v, ins, outs) = refs[:5], refs[5:]
    rows = kept.shape[0] - t_v.shape[1]
    tokens = 2 * rows
    quarter, half, third = WIDE // 4, ff // 2, ff // 3
    blocks = third // WIDE
    share = d // 16
    cut = 3 * d
    y, z, core = idx[0], idx[1], idx[2]

    def load(cin, at, width, to, to_at):
        return [cin.start(src.at[pl.ds(0, rows), pl.ds(at, width)], to.at[i, :, pl.ds(to_at, width)]) for i, src in enumerate((kept, got))]

    def wait(copies):
        for copy in copies:
            copy.wait()

    def both(ref, at=0, width=d):
        return ref[:, :, at : at + width].reshape(tokens, width)

    def put(rows_at, cols_at, value):
        out_v[rows_at, cols_at] = value.astype(BF)

    def send_by_y(cout, at, width):
        cols = pl.ds(at, width)

        def rows_of(s, first, count):
            return out_v.at[pl.ds(pl.multiple_of(lax.rem(y + s, 4) * 4 * share + first, 16), count), cols]

        return [cout.start(rows_of(2, 0, 2 * share), results[3].at[:, cols]),
                cout.start(rows_of(2, 2 * share, 2 * share), results[4].at[:, cols])] + [
            cout.start(rows_of(s, 0, 4 * share), results[r].at[:, cols]) for r, s in ((1, 1), (2, 3), (0, 0))]

    def send_by_z(cout, at, width):
        cols = pl.ds(at, width)

        def rows_of(i, s):
            return out_v.at[pl.ds(pl.multiple_of((4 * i + lax.rem(z + s, 4)) * share, 16), share), cols]

        return [
            cout.start(rows_of(i, s), results[r].at[pl.ds(share * (i - base), share), cols])
            for r, s, base, count in ((3, 2, 0, 2), (4, 2, 2, 2), (1, 1, 0, 4), (2, 3, 0, 4), (0, 0, 0, 4))
            for i in range(base, base + count)
        ]

    everything = slice(0, d)

    @pl.when(core == 0)
    def _():
        cin, cout = Copies(ins), Copies(outs)
        grads = load(cin, ff, d, a_v, 0)
        loads = [load(cin, third * k, third, big_v, third * k) for k in range(3)]
        attended = load(cin, ff + 3 * d, d, b_v, 0)
        hidden, values = load(cin, ff + 2 * d, d, c_v, 0), load(cin, ff + d, d, c_v, d)
        smalls = [cin.start(src.at[pl.ds(rows, t_v.shape[1])], t_v.at[i]) for i, src in enumerate((kept, got))]
        wait(grads)
        gb = both(a_v)
        for k in range(3):
            wait(loads[k])
            found = lax.dot_general(both(big_v, third * k, third), gb, TN, preferred_element_type=F32).astype(BF)
            for b in range(blocks):
                at = quarter * (blocks * k + b)
                for j in range(4):
                    put(slice(at, at + quarter), slice(d * j, d * j + d), found[WIDE * b + quarter * j : WIDE * b + quarter * (j + 1)])
        pending = send_by_y(cout, 0, 4 * d)
        wait(attended)
        put(everything, slice(4 * d, 5 * d), lax.dot_general(both(b_v), gb, TN, preferred_element_type=F32))
        wait(hidden + values + smalls)
        put(everything, slice(5 * d, 6 * d), lax.dot_general(both(c_v), both(c_v, d), TN, preferred_element_type=F32))
        put(everything, slice(6 * d, 6 * d + LANES), split_small(small_table(d, ff, t_v)))
        wait(pending + send_by_y(cout, 4 * d, 2 * d + LANES))

    @pl.when(core == 1)
    def _():
        cin, cout = Copies(ins), Copies(outs)
        hidden = load(cin, ff + 2 * d, d, a_v, 0)
        loads = [load(cin, third * k, third, big_v, third * k) for k in range(2)]
        queries = load(cin, ff, d, b_v, 0)
        loads.append(load(cin, 2 * third, third, big_v, 2 * third))
        keys = load(cin, ff + d, d, c_v, 0)
        wait(hidden)
        turned = both(a_v).T
        pending = []
        for k in range(2):
            wait(loads[k])
            put(everything, slice(third * k, third * k + third), mm(turned, both(big_v, third * k, third)))
        pending = send_by_z(cout, 0, 2 * third)
        wait(queries)
        put(everything, slice(ff, ff + d), mm(turned, both(b_v)))
        wait(loads[2])
        put(everything, slice(2 * third, ff), mm(turned, both(big_v, 2 * third, third)))
        wait(keys)
        put(everything, slice(ff + d, ff + 2 * d), mm(turned, both(c_v)))
        out_v[:, 6 * d :] = jnp.zeros((d, LANES), BF)
        wait(pending + send_by_z(cout, 2 * third, 6 * d + LANES - 2 * third))


def added(parts):
    total = parts[0][...].astype(F32)
    for part in parts[1:]:
        total = total + part[...].astype(F32)
    shape = total.shape
    total = total.reshape(-1, shape[-1])
    main, last = total[:, : shape[-1] - LANES], split_small(joined_small(total[:, shape[-1] - LANES :]))
    return jnp.concatenate([main.astype(BF), last], axis=1).reshape(shape)


def relay_kernel(idx, up_in, down_in, up_got, down_got, up, down, hold, ins, outs):
    half = up_got.shape[0]
    cin, cout = Copies(ins), Copies(outs)
    parts = ((up_in, 0, up_got, up), (down_in, half, down_got, down))
    loads = [cin.start(block.at[pl.ds(at, half)], hold.at[i]) for i, (block, at, _, _) in enumerate(parts)]
    pending = []
    for i, (_, at, got, out) in enumerate(parts):
        loads[i].wait()
        hold[i] = added([hold.at[i], got])
        pending.append(cout.start(hold.at[i], out.at[pl.ds(at, half)]))
    for copy in pending:
        copy.wait()


def mid_kernel(idx, *refs):
    came, results, (in_v, out_v, ins, outs) = refs[:3], refs[3:7], refs[7:]
    share = results[0].shape[0]

    cin, cout = Copies(ins), Copies(outs)
    at = jnp.where(idx[2] == 0, idx[1], idx[0])
    order = [2, 1, 3, 0]
    blocks = [pl.multiple_of(lax.rem(at + s, 4) * share, 16) for s in order]
    loads = [[cin.start(part.at[pl.ds(block, share)], in_v.at[i, p]) for p, part in enumerate(came)]
             for i, block in enumerate(blocks)]
    pending = []
    for i, s in enumerate(order):
        for copy in loads[i]:
            copy.wait()
        out_v[i] = added([in_v.at[i, p] for p in range(3)])
        pending.append(cout.start(out_v.at[i], results[s]))
    for copy in pending:
        copy.wait()


def last_pair_kernel(idx, *refs):
    came, (home_mine, home_other, away_mine, away_other, in_v, hold, ins) = refs[:8], refs[8:]
    share = home_mine.shape[0]
    core, odd = idx[2], idx[4]

    sum_of(came, in_v, hold, ins)

    def rows_of(k, which):
        return hold[k, pl.ds(pl.multiple_of(which * share, 8), share), :]

    for which, home, away in ((core, home_mine, away_mine), (1 - core, home_other, away_other)):
        home[...] = jnp.where(odd == 1, rows_of(1, which), rows_of(0, which)).astype(home.dtype)
        away[...] = jnp.where(odd == 1, rows_of(0, which), rows_of(1, which)).astype(away.dtype)


def sum_of(came, in_v, hold, sems):
    copies = Copies(sems)
    loads = [copies.start(came[4 * k], in_v.at[k]) for k in range(len(came) // 4)]
    for k, load in enumerate(loads):
        load.wait()
        hold[k] = added([in_v.at[k]] + list(came[4 * k + 1 : 4 * k + 4])).astype(F32)


def place_kernel(idx, y_in, y_got, g_in, g_got, y_out, g_out, y_v, g_v, sems):
    copies = Copies(sems)
    pending = []
    for got, wide_v, out in ((y_got, y_v, y_out), (g_got, g_v, g_out)):
        wide_v[...] = got[...].astype(F32)
        pending.append(copies.start(wide_v, out.at[1 - idx[3]]))
    for copy in pending:
        copy.wait()


def picked(rows, columns, wanted):
    row = lax.broadcasted_iota(jnp.int32, (rows, columns), 0)
    column = lax.broadcasted_iota(jnp.int32, (rows, columns), 1)
    return row, column, jnp.where(column == wanted(row), 1.0, 0.0)


def prepare_kernel(d, ff, p_in, p_attn, p_down, n_gain, o_bias, u_bias, q_gain, k_gain, shuffle, out):
    share = p_in.shape[0]
    heads_part = p_in.shape[1] - ff
    for at in range(0, ff, WIDE):
        out[:, at : at + WIDE] = mm(p_in[:, heads_part + at : heads_part + at + WIDE], shuffle[...]).astype(BF)
    out[:, ff : ff + heads_part] = p_in[:, :heads_part]
    at = ff + heads_part
    out[:, at : at + d] = p_attn[...]
    down = p_down[...]
    for j in range(4):
        take = picked(share, down.shape[0], lambda row: 4 * row + j)[2].astype(BF)
        out[:, at + d * (j + 1) : at + d * (j + 2)] = mm(take, down).astype(BF)

    def column_of(ref, wanted, where):
        values = ref[...].astype(F32)
        take = picked(share, values.shape[1], wanted)[2]
        lane = lax.broadcasted_iota(jnp.int32, (share, LANES), 1)
        return jnp.where(lane == where, jnp.sum(take * values, axis=1, keepdims=True), 0.0)

    table = column_of(n_gain, lambda row: row, 0) + column_of(o_bias, lambda row: row, 1)
    for j in range(4):
        table = table + column_of(u_bias, lambda row: 4 * row + j, 2 + j)
    table = table + column_of(q_gain, lambda row: row, 6) + column_of(k_gain, lambda row: row, 7)
    out[:, at + 5 * d :] = table.astype(BF)


def smalls_kernel(d, ff, shares, place, out):
    quarter = WIDE // 4
    for layer in range(2):
        table = shares[:, LANES * layer : LANES * (layer + 1)].astype(F32).T
        pieces = [table[2 + j : 3 + j, quarter * b : quarter * (b + 1)] for b in range(ff // WIDE) for j in range(4)]
        both = mm(table[0:8].astype(BF), place[...])
        first = jnp.concatenate([table[0:1], table[1:2], both[6:7], both[7:8]], axis=1)
        out[layer] = jnp.concatenate([first, jnp.concatenate(pieces, axis=1), jnp.zeros((6, ff), F32)], axis=0)


def in_parts(x):
    top = x.astype(BF)
    rest = x - top.astype(F32)
    middle = rest.astype(BF)
    return top, middle, (rest - middle.astype(F32)).astype(BF)


def finish_kernel(d, ff, idx, own, a_in, b_in, c_in, shuffle, g_in, g_attn, g_down, g_ng, g_q, g_k, g_ub, g_ob):
    core = idx[2]
    share = own.shape[0]
    mine = own[...] + a_in[...].astype(F32)
    theirs = b_in[...].astype(F32) + c_in[...].astype(F32)
    half0 = jnp.where(core == 0, mine, theirs)
    half1 = jnp.where(core == 0, theirs, mine)
    g_in[:, : 2 * d] = half1[:, ff : ff + 2 * d]
    g_in[:, 2 * d : 3 * d] = half0[:, 5 * d : 6 * d]
    for at in range(0, ff, WIDE):
        g_in[:, 3 * d + at : 3 * d + at + WIDE] = sum(mm(part, shuffle[...], NT) for part in in_parts(half1[:, at : at + WIDE]))
    g_attn[...] = half0[:, 4 * d : 5 * d]
    stacked = jnp.concatenate([half0[:, at : at + d] for at in range(0, 4 * d, d)], axis=0)
    row, column, _ = picked(4 * share, 4 * share, lambda row: row)
    turn = jnp.where(column == lax.rem(row, 4) * share + row // 4, 1.0, 0.0).astype(BF)
    g_down[...] = sum(mm(turn, part) for part in in_parts(stacked))
    small = joined_small(half0[:, 6 * d :])
    turned = jnp.concatenate([small, jnp.zeros((LANES - share, LANES), F32)], axis=0).T
    g_ng[...] = turned[0:1, :share]
    g_ob[...] = turned[1:2, :share]
    g_q[...] = turned[6:7, : g_q.shape[1]]
    g_k[...] = turned[7:8, : g_k.shape[1]]
    total = jnp.zeros((8, 4 * share), F32)
    for j in range(4):
        row, column, _ = picked(LANES, 4 * share, lambda row: row)
        spread_out = jnp.where(column == 4 * row + j, 1.0, 0.0)
        total = total + jnp.where(lax.broadcasted_iota(jnp.int32, (8, 4 * share), 0) == 2 + j, 1.0, 0.0) * lax.dot_general(
            turned[0:8], spread_out, NN, precision=lax.Precision.HIGHEST, preferred_element_type=F32)
    g_ub[...] = jnp.sum(total, axis=0, keepdims=True)


ANY = pl.BlockSpec(memory_space=pl.ANY)
HERE = pl.BlockSpec(memory_space=pltpu.VMEM)


def whole(shape):
    return pl.BlockSpec(shape, lambda i, idx: (0,) * len(shape))


def pick(shape):
    return pl.BlockSpec((1,) + shape, lambda i, idx: (idx[2],) + (0,) * len(shape))


def call(kernel, idx, ins, fresh, stashes, scratch, flops):
    outs = pl.pallas_call(
        kernel,
        grid_spec=pltpu.PrefetchScalarGridSpec(
            num_scalar_prefetch=1,
            grid=(1,),
            in_specs=[s for _, s in ins] + [ANY] * len(stashes),
            out_specs=[ANY] * (1 + len(stashes)),
            scratch_shapes=scratch,
        ),
        out_shape=[jax.ShapeDtypeStruct(*fresh)] + [jax.ShapeDtypeStruct(a.shape, a.dtype) for a in stashes],
        input_output_aliases={1 + len(ins) + i: 1 + i for i in range(len(stashes))},
        compiler_params=pltpu.CompilerParams(dimension_semantics=("arbitrary",), vmem_limit_bytes=VMEM_LIMIT),
        cost_estimate=pl.CostEstimate(flops=flops, bytes_accessed=1 << 10, transcendentals=0),
    )(idx, *[a for a, _ in ins], *stashes)
    return outs[0], list(outs[1:])


def plain(kernel, arrays, specs, out_shapes, out_specs, scratch):
    return pl.pallas_call(
        kernel, grid=(1,), in_specs=specs, out_specs=out_specs, scratch_shapes=scratch, out_shape=out_shapes,
        compiler_params=pltpu.CompilerParams(dimension_semantics=("arbitrary",), vmem_limit_bytes=VMEM_LIMIT),
        cost_estimate=pl.CostEstimate(flops=1 << 10, bytes_accessed=1 << 10, transcendentals=0),
    )(*arrays)


def simple(kernel, idx, arrays, specs, out_shapes, out_specs, scratch, limit=VMEM_LIMIT):
    return pl.pallas_call(
        kernel,
        grid_spec=pltpu.PrefetchScalarGridSpec(
            num_scalar_prefetch=1, grid=(1,), in_specs=specs, out_specs=out_specs, scratch_shapes=scratch
        ),
        out_shape=out_shapes,
        compiler_params=pltpu.CompilerParams(dimension_semantics=("arbitrary",), vmem_limit_bytes=limit),
        cost_estimate=pl.CostEstimate(flops=1 << 10, bytes_accessed=1 << 10, transcendentals=0),
    )(idx, *arrays)


def along(x, step, size, by):
    devices = lax.axis_size("dp")

    def to(i):
        digit = i // step % size
        return i + ((digit + by) % size - digit) * step

    return lax.ppermute(x, "dp", [(i, to(i)) for i in range(devices)])


def paired(x):
    return lax.ppermute(x, "section", [(0, 1), (1, 0), (2, 3), (3, 2)])


def body(tokens, cotangent, lengths, proj_in, proj_attn, proj_down, norm_gain, query_gain, key_gain, up_bias, out_bias):
    ranks = lax.axis_size("dp")
    section = lax.axis_index("section")
    rank = lax.axis_index("dp")
    slots = lengths.shape[0]
    rows = tokens.shape[0] // slots
    d = tokens.shape[1]
    joined = proj_in.shape[2]
    ff = proj_down.shape[1] * ranks
    head = query_gain.shape[1] * ranks
    heads = d // head
    dshare = proj_in.shape[1]
    fshare = proj_down.shape[1] // dshare
    hshare = query_gain.shape[1]
    chunks = 3
    wide = joined + d + ff
    stride = wide + LANES
    side = math.isqrt(ranks // 2)
    core, z, y = lax.rem(rank, 2), lax.rem(rank // 2, side), rank // (2 * side)
    stage, odd = section // 2, lax.rem(section, 2)
    slot = lax.rem(stage + odd, 2)

    place = jnp.arange(WIDE, dtype=jnp.int32)
    source = (place % (WIDE // fshare)) * fshare + place // (WIDE // fshare)
    shuffle = (place[:, None] == source[None, :]).astype(BF)

    def full(a):
        return pl.BlockSpec(a.shape, lambda i: (0,) * a.ndim)

    shares = [proj_in[0], proj_attn[0], proj_down[0], norm_gain, out_bias, up_bias, query_gain, key_gain, shuffle]
    heads_part = joined - ff
    local = jax.ShapeDtypeStruct((dshare, stride), BF)
    local = plain(partial(prepare_kernel, d, ff), shares, [full(a) for a in shares], local, full(local), [])
    other = paired(local)
    g = lax.all_gather(jnp.concatenate([local, other], axis=1), "dp", axis=0).reshape(d, 2 * stride)
    shares = jnp.concatenate([a[:, wide : wide + 8].reshape(1, 8 * dshare) for a in (local, other)], axis=1)
    step = 1
    while step < ranks:
        got = lax.ppermute(shares, "dp", [(i, i ^ step) for i in range(ranks)])
        low = lax.rem(rank // step, 2) == 0
        shares = jnp.where(low, jnp.concatenate([shares, got]), jnp.concatenate([got, shares]))
        step *= 2
    shares = shares.reshape(ranks, 2, dshare, 8).transpose(0, 2, 1, 3).reshape(d, 2, 8)
    shares = jnp.pad(shares, ((0, 0), (0, 0), (0, LANES - 8))).reshape(d, 2 * LANES)
    toks = tokens.reshape(slots, rows, d)
    seeds = cotangent.reshape(slots, rows, d)
    ends = jnp.cumsum(lengths, axis=-1)
    position = jnp.arange(rows, dtype=jnp.int32)
    image = jnp.sum((position[None, :, None] >= ends[:, None, :]).astype(jnp.int32), axis=-1)
    image = jnp.where(position[None, :] < ends[:, 2:3], image, ABSENT + position[None, :])
    ids = image[:, None, :].astype(F32)

    def index_of(layer, active_stage):
        return jnp.stack([stage == active_stage, core, slot, odd == layer]).astype(jnp.int32)

    indices = [[index_of(layer, active) for active in range(2)] for layer in range(2)]
    here = jnp.stack([y, z, core, slot, odd]).astype(jnp.int32)
    element = jnp.arange(d, dtype=jnp.int32) % head
    spread_gain = (jnp.arange(d, dtype=jnp.int32)[:, None] == (element // hshare * dshare + element % hshare)[None, :]).astype(BF)
    small = jax.ShapeDtypeStruct((2, 8, ff), F32)
    smalls = plain(
        partial(smalls_kernel, d, ff), [shares, spread_gain], [full(shares), full(spread_gain)], small, full(small), [],
    )
    g, indices, here, ids, smalls = lax.optimization_barrier((g, indices, here, ids, smalls))
    g3 = g.reshape(ff // WIDE, WIDE // fshare, g.shape[1])
    def stash(*shape, dtype=BF):
        return pl.pallas_call(
            lambda out: None, out_shape=jax.ShapeDtypeStruct(shape, dtype), out_specs=pl.BlockSpec(memory_space=pl.ANY)
        )()

    fc = ff // chunks
    groups = ff // WIDE

    V = pltpu.VMEM
    weights_v = [V((d, heads_part), BF), V((chunks, d, fc), BF), V((groups, fshare, WIDE // fshare, d), BF), V((d, d), BF)]
    sems = [pltpu.SemaphoreType.DMA((48,)), pltpu.SemaphoreType.DMA((48,))]
    stacked = ff + 4 * d
    operands = [[stash(rows + 16, stacked), stash(rows + 16, stacked)] for _ in range(2)]
    kept = [[stash(rows, d) for _ in range(4)] + [stash(rows, 2 * d), stash(rows, 2 * d), stash(chunks, rows, fc),
             stash(heads, rows, rows), stash(16, rows, dtype=F32)] for _ in range(2)]
    results = [stash(slots, rows, d, dtype=F32), stash(rows, d)]
    here_x = toks
    for t in range(4):
        layer = t % 2
        ybf, done = call(
            partial(forward_kernel, d, ff, chunks, stride, (FIRST, LOCAL, ARRIVED, LOCAL)[t]),
            indices[layer][t // 2],
            [(here_x, HERE if t == 2 else ANY)] + [(a, ANY) for a in (g, g3, ids, smalls)],
            ((rows, d), BF),
            kept[layer][:9] + operands[layer] + results,
            [V((rows, d), BF), V((rows, d), BF)] + weights_v
            + [V((rows, d), BF)] * 3 + [V((rows, 2 * d), BF)] * 2 + [V((chunks, rows, fc), BF)] * 2
            + [V((heads, rows, rows), BF), V((16, rows), F32), V((rows, d), BF), V((rows, d), F32), V((rows, d), F32), V((rows, d), BF), V((1, rows), F32), V((8, ff), F32)]
            + sems,
            1 << 10,
        )
        kept[layer], operands[layer], results = done[:9], done[9:11], done[11:]
        here_x = lax.ppermute(ybf, "section", [(0, 3), (1, 2)]) if t == 1 else ybf
    y_out, y_send = results
    y_got = paired(y_send)

    results = [stash(slots, rows, d, dtype=F32), stash(rows, d)]
    width = 6 * d + LANES
    share = 2 * dshare

    def moved(x, leg, by):
        def to(i):
            step = 2 * side if i % 2 == leg else 2
            digit = i // step % side
            return i + ((digit + by) % side - digit) * step

        return lax.ppermute(x, "dp", [(i, to(i)) for i in range(ranks)])

    def grads_by_place(layer, got):
        return simple(
            partial(weight_grad_kernel, d, ff), here,
            [operands[layer][0], got], [ANY] * 2,
            [jax.ShapeDtypeStruct((side * share, width), BF)] * 3 + [jax.ShapeDtypeStruct((side // 2 * share, width), BF)] * 2,
            [ANY] * 5,
            [V((2, rows, ff), BF), V((2, rows, d), BF), V((2, rows, d), BF), V((2, rows, 2 * d), BF), V((d, width), BF), V((2, 16, stacked), BF),
             pltpu.SemaphoreType.DMA((32,)), pltpu.SemaphoreType.DMA((32,))],
        )

    def halves(made):
        return moved(made[3], 0, 1), moved(made[4], 0, -1)

    def first_leg(made, came):
        own, up, down = made[:3]
        part = (side // 2 * share, width)
        up, down = pl.pallas_call(
            relay_kernel,
            grid_spec=pltpu.PrefetchScalarGridSpec(
                num_scalar_prefetch=1, grid=(1,), in_specs=[ANY, ANY, HERE, HERE], out_specs=[ANY] * 2,
                scratch_shapes=[V((2,) + part, BF), pltpu.SemaphoreType.DMA((2,)), pltpu.SemaphoreType.DMA((2,))],
            ),
            out_shape=[jax.ShapeDtypeStruct(up.shape, BF)] * 2,
            input_output_aliases={1: 0, 2: 1},
            compiler_params=pltpu.CompilerParams(dimension_semantics=("arbitrary",), vmem_limit_bytes=SMALL_LIMIT),
            cost_estimate=pl.CostEstimate(flops=1 << 10, bytes_accessed=1 << 10, transcendentals=0),
        )(here, up, down, *came)
        return [own, moved(up, 0, 1), moved(down, 0, -1)]

    def second_leg(outs):
        far, near, back = (moved(outs[s], 1, s) for s in (2, 1, 3))
        return [outs[0], near, far, back]

    def by_second_axis(came):
        return simple(
            mid_kernel, here, came, [ANY] * 3, [jax.ShapeDtypeStruct((share, width), BF)] * side, [ANY] * side,
            [V((side, 3, share, width), BF), V((side, share, width), BF), pltpu.SemaphoreType.DMA((12,)), pltpu.SemaphoreType.DMA((4,))],
        )

    here_g = seeds
    swaps = []
    for t in range(4):
        layer = 1 - t % 2
        gbf, done = call(
            partial(backward_kernel, d, ff, chunks, stride, (FIRST, LOCAL, ARRIVED, LOCAL)[t]),
            indices[layer][1 - t // 2],
            [(here_g, HERE if t == 2 else ANY)] + [(a, ANY) for a in [g, g3, ids, smalls] + kept[layer]],
            ((rows, d), BF),
            operands[layer] + results,
            [V((rows, d), BF), V((rows, d), BF)] + weights_v
            + [V((rows, d), BF)] * 4 + [V((rows, 2 * d), BF)] * 2
            + [V((chunks, rows, fc), BF), V((heads, rows, rows), BF), V((16, rows), F32)]
            + [V((d, rows), BF), V((d, rows), F32), V((rows, d), F32)]
            + [V((rows, d), BF)] * 3 + [V((chunks, rows, fc), BF), V((rows, d), F32), V((rows, d), F32), V((rows, d), BF), V((1, stacked), F32), V((16, stacked), BF), V((1, rows), F32), V((8, ff), F32)]
            + sems,
            1 << 10,
        )
        operands[layer], results = done[:2], done[2:]
        here_g = lax.ppermute(gbf, "section", [(3, 0), (2, 1)]) if t == 1 else gbf
        if t == 1:
            here_g, y_got = lax.optimization_barrier((here_g, y_got))
        if t == 3:
            operands[layer][1], swaps[0] = lax.optimization_barrier((operands[layer][1], swaps[0]))
        if t >= 2:
            swaps.append(along(operands[layer][1], 1, 2, 1))
    gr_got = paired(results[1])
    upper, gr_got = lax.optimization_barrier((grads_by_place(1, swaps[0]), gr_got))
    upper_came = halves(upper)
    lower = grads_by_place(0, swaps[1])
    lower_came = halves(lower)
    legs = [first_leg(upper, upper_came), first_leg(lower, lower_came)]
    arrived = [second_leg(by_second_axis(came)) for came in legs]
    gr_out = results[0]
    y_out, gr_out = pl.pallas_call(
        place_kernel,
        grid_spec=pltpu.PrefetchScalarGridSpec(
            num_scalar_prefetch=1, grid=(1,), in_specs=[ANY, whole((rows, d)), ANY, whole((rows, d))], out_specs=[ANY] * 2,
            scratch_shapes=[V((rows, d), F32), V((rows, d), F32), pltpu.SemaphoreType.DMA((2,))],
        ),
        out_shape=[jax.ShapeDtypeStruct(y_out.shape, F32)] * 2,
        input_output_aliases={1: 0, 3: 1},
    )(here, y_out, y_got, gr_out, gr_got)

    both = arrived[1] + arrived[0]
    home_mine, home_other, away_mine, away_other = simple(
        last_pair_kernel, here, both, [ANY, HERE, HERE, HERE] * 2,
        [jax.ShapeDtypeStruct((dshare, width), t) for t in (F32, BF, BF, BF)], [whole((dshare, width))] * 4,
        [V((2, share, width), BF), V((2, share, width), F32), pltpu.SemaphoreType.DMA((2,))], SMALL_LIMIT,
    )
    sections = lax.axis_size("section")
    cross = [(s * ranks + i, (s ^ 1) * ranks + (i ^ 1)) for s in range(sections) for i in range(ranks)]
    arrays = [home_mine, paired(away_mine), along(home_other, 1, 2, 1), lax.ppermute(away_other, ("section", "dp"), cross),
              shuffle]
    shapes = [(dshare, joined), (dshare, d), (dshare * fshare, d), (1, dshare), (1, hshare), (1, hshare), (1, dshare * fshare),
              (1, dshare)]
    g_in, g_attn, g_down, g_ng, g_q, g_k, g_ub, g_ob = simple(
        partial(finish_kernel, d, ff), here, arrays, [whole(a.shape) for a in arrays],
        [jax.ShapeDtypeStruct(s, F32) for s in shapes], [whole(s) for s in shapes], [],
    )
    return (y_out.reshape(1, slots * rows, d), gr_out.reshape(1, slots * rows, d), g_in[None], g_attn[None], g_down[None],
            g_ng, g_q, g_k, g_ub, g_ob)


def solution(mesh):
    in_specs = (P("dp", None),) * 3 + (P("section", "dp", None),) * 3 + (P("section", "dp"),) * 5
    out_specs = (P("section", "dp", None),) * 5 + (P("section", "dp"),) * 5
    return jax.shard_map(body, mesh=mesh, in_specs=in_specs, out_specs=out_specs, check_vma=False)
```
